32 devices in a mesh: dp: 16 (over z, y, core), mp: 2 (over x).
Axes of the slice: x: 2, y: 2, z: 4, core: 2. Of those that a mesh axis runs over, the one named last changes fastest.
Arguments:
- state: bfloat16 [32768, 512], P('dp'), may hold values from -6 to 6
- lengths: int32 [32], P('dp'), may hold values from 256 to 1024, as said below
- halt_mask: int32 [32768], P('dp'), may hold values 0 or 1
- w_query: bfloat16 [512, 512], P(None, 'mp'), may hold values from -0.25 to 0.25
- w_key: bfloat16 [512, 512], P(None, 'mp'), may hold values from -0.25 to 0.25
- w_value: bfloat16 [512, 512], P(None, 'mp'), may hold values from -0.25 to 0.25
- w_output: bfloat16 [512, 512], P('mp'), may hold values from -1 to 1
- first_norm_gain: float32 [512], replicated, may hold values from 0.1 to 1.9
- first_norm_bias: float32 [512], replicated, may hold values from -3 to 3
- w_inner: bfloat16 [512, 2048], P(None, 'mp'), may hold values from -0.25 to 0.25
- w_outer: bfloat16 [2048, 512], P('mp'), may hold values from -0.125 to 0.125
- second_norm_gain: float32 [512], replicated, may hold values from 0.1 to 1.9
- second_norm_bias: float32 [512], replicated, may hold values from -3 to 3
- halt_weight: float32 [512], replicated, may hold values from -0.25 to 0.25
- cotangent: bfloat16 [32768, 512], P('dp'), may hold values from -6 to 6
Outputs:
- new_state: float32 [32768, 512], P('dp')
- grad_state: float32 [32768, 512], P('dp')
- grad_query: float32 [512, 512], P(None, 'mp')
- grad_key: float32 [512, 512], P(None, 'mp')
- grad_value: float32 [512, 512], P(None, 'mp')
- grad_output: float32 [512, 512], P('mp')
- first_gain_gradient: float32 [512], replicated
- grad_bias1: float32 [512], replicated
- grad_inner: float32 [512, 2048], P(None, 'mp')
- grad_outer: float32 [2048, 512], P('mp')
- second_gain_gradient: float32 [512], replicated
- grad_bias2: float32 [512], replicated
- grad_halt: float32 [512], replicated
The draws below stay inside these ranges and needn't reach their ends.
Inputs may be any that keep to these rules, and one draw needn't show every extreme that they name: Tokens of sequence s at positions lengths[s] and beyond are padding; some sequence has exactly 1024 real tokens.
All inputs are finite; a program needn't handle non-finite values. No bound on the sum of `halt_mask` on one device may be relied on, other than what follows from the above.
Results may differ from the reference program's by a relative error of at most 0.017.
The reference program's roundings to bfloat16 on the way count: a program that leaves them out, or rounds other values in their place, can miss the bound.
Values sent between devices are 32-bit elements; how exact they have to be, the bound alone decides.
No kernel may reach another device: no remote copies, remote signals or barrier semaphores. Data moves between devices by JAX's collectives and lax.ppermute only.
A program may use at most 256 MiB of HBM per device.

```python
import math
import jax
import jax.numpy as jnp
from jax import lax

D = 512
FF = 2048
HEAD = 64
HEADS = 8
LEN = 1024
STEP = 2
SEQS = 32
TOKENS = 32768


def draw_lengths(key, part):
    key = jax.random.fold_in(key, 7)
    first, second = jax.random.split(key)
    base = jax.random.randint(first, (SEQS,), LEN // 4, LEN + 1)
    longest = jax.random.randint(second, (), 0, SEQS)
    return jnp.where(jnp.arange(SEQS) == longest, LEN, base).astype(jnp.int32)


def place_ends(values, key, smallest, top_value):
    extent = values.shape
    place = [jax.random.randint(jax.random.fold_in(key, axis), (), 0, extent[axis]) for axis in range(len(extent))]
    values = values.at[tuple(place)].set(smallest)
    longest = extent.index(max(extent))
    place[longest] = (place[longest] + 1) % extent[longest]
    return values.at[tuple(place)].set(top_value)


def levels(rng, shape, cuts, smallest, largest):
    loudness = 1.0
    for axis_at, blocks in cuts:
        heights = jax.random.uniform(jax.random.fold_in(jax.random.fold_in(rng, 6), axis_at), (blocks,), jnp.float32, smallest / len(cuts), largest / len(cuts))
        loudness = loudness * jnp.repeat(jnp.exp(heights), shape[axis_at] // blocks).reshape((-1,) + (1,) * (len(shape) - 1 - axis_at))
    return loudness


def noise(own_key, dims, scale, limit, shards=(), kind=jnp.bfloat16):
    array = scale * jax.random.normal(own_key, dims, jnp.float32)
    if shards:
        array = array * levels(own_key, dims, shards, -0.22, 0.18)
    return jnp.clip(array, -limit, limit).astype(kind)


def setup_inputs(seed: int = 0) -> dict:
    arg_keys = jax.random.split(jax.random.key(seed), 16)
    state = noise(arg_keys[0], (TOKENS, D), 1.0, 6.0, ((0, 16),))
    lengths = draw_lengths(jax.random.fold_in(arg_keys[15], 71), 0)
    halt_mask = place_ends((jax.random.randint(arg_keys[2], (TOKENS,), 0, 4) < 3).astype(jnp.int32), jax.random.fold_in(arg_keys[2], 1), 0, 1)
    w_query = noise(arg_keys[3], (D, D), D ** -0.5, 0.25, ((1, 2),))
    w_key = noise(arg_keys[4], (D, D), D ** -0.5, 0.25, ((1, 2),))
    w_value = noise(arg_keys[5], (D, D), D ** -0.5, 0.25, ((1, 2),))
    w_output = noise(arg_keys[6], (D, D), (D // 16) ** -0.5, 1.0, ((0, 2),))
    first_norm_gain = jnp.clip(1.0 + 0.18 * jax.random.normal(arg_keys[7], (D,), jnp.float32), 0.1, 1.9)
    first_norm_bias = noise(arg_keys[8], (D,), 0.5, 3.0, (), jnp.float32)
    w_inner = noise(arg_keys[9], (D, FF), D ** -0.5, 0.25, ((1, 2),))
    w_outer = noise(arg_keys[10], (FF, D), FF ** -0.5, 0.125, ((0, 2),))
    second_norm_gain = jnp.clip(1.0 + 0.18 * jax.random.normal(arg_keys[11], (D,), jnp.float32), 0.1, 1.9)
    second_norm_bias = noise(arg_keys[12], (D,), 0.5, 3.0, (), jnp.float32)
    halt_weight = noise(arg_keys[13], (D,), D ** -0.5, 0.25, (), jnp.float32)
    cotangent = noise(arg_keys[14], (TOKENS, D), 1.0, 6.0, ((0, 16),))
    return dict(state=state, lengths=lengths, halt_mask=halt_mask, w_query=w_query, w_key=w_key, w_value=w_value, w_output=w_output, first_norm_gain=first_norm_gain, first_norm_bias=first_norm_bias, w_inner=w_inner, w_outer=w_outer, second_norm_gain=second_norm_gain, second_norm_bias=second_norm_bias, halt_weight=halt_weight, cotangent=cotangent)


@jax.custom_vjp
def low(v):
    return lax.optimization_barrier(v.astype(jnp.bfloat16)).astype(jnp.float32)

@jax.custom_vjp
def low_back(v):
    return v

def low_keep(v):
    return (low(v), None)

def low_pass(kept, grad):
    return (grad,)

def back_keep(v):
    return (v, None)

def back_low(kept, grad):
    return (low(grad),)
low.defvjp(low_keep, low_pass)
low_back.defvjp(back_keep, back_low)
HIGH = lax.Precision.HIGHEST

def signal_rows(positions, width):
    half = width // 2
    rates = jnp.exp(-math.log(10000.0) * jnp.arange(half, dtype=jnp.float32) / (half - 1))
    angles = positions[:, None] * rates[None, :]
    return jnp.concatenate([jnp.sin(angles), jnp.cos(angles)], axis=1)

def layer_norm_apply(values):
    centre = values - lax.optimization_barrier(jnp.mean(values, axis=-1, keepdims=True))
    inverse_deviation = lax.rsqrt(lax.optimization_barrier(jnp.mean(centre * centre, axis=-1, keepdims=True)) + 1e-05)
    return centre * inverse_deviation

def attend(query, key, value, valid):
    scores = jnp.einsum('qhd,khd->hqk', query, key, precision=HIGH) / jnp.sqrt(jnp.float32(HEAD))
    scores = jnp.where(valid[None, None, :], scores, jnp.float32(-1e+30))
    scores = low_back(scores)
    probs = low(jax.nn.softmax(scores, axis=-1))
    mixed = jnp.einsum('hqk,khd->qhd', probs, value, precision=HIGH)
    return mixed.reshape(LEN, D)

def block(state, valid, running, w_query, w_key, w_value, w_output, gain1, bias1, w_inner, w_outer, gain2, bias2, halt_weight):
    count = state.shape[0]
    positions = jnp.arange(LEN, dtype=jnp.float32)
    timing = signal_rows(positions, D) + signal_rows(jnp.full((1,), STEP, jnp.float32), D)
    embedded_input = state + timing[None]
    flat_low = low(embedded_input.reshape(count * LEN, D))

    def project(weight):
        return low(low_back(jnp.dot(flat_low, weight, precision=HIGH))).reshape(count, LEN, HEADS, HEAD)
    query, key, value = (project(w_query), project(w_key), project(w_value))
    mixed = lax.map(lambda item: jax.checkpoint(attend)(*item), (query, key, value, valid))
    mixed = low(low_back(mixed.reshape(count * LEN, D)))
    attention_output = low_back(jnp.dot(mixed, w_output, precision=HIGH))
    hidden1 = embedded_input.reshape(count * LEN, D) + attention_output
    first_normed_rows = layer_norm_apply(hidden1) * gain1 + bias1
    inner = low_back(jnp.dot(low(first_normed_rows), w_inner, precision=HIGH))
    activated = low(jax.nn.gelu(inner))
    outer_projection = low_back(jnp.dot(activated, w_outer, precision=HIGH))
    block_output = layer_norm_apply(first_normed_rows + outer_projection) * gain2 + bias2
    halt_prob = jax.nn.sigmoid(lax.optimization_barrier(jnp.sum(block_output * halt_weight, axis=-1)))
    flat_state = state.reshape(count * LEN, D)
    weight = (running.reshape(count * LEN) * halt_prob)[:, None]
    return (flat_state + weight * (block_output - flat_state)).reshape(count, LEN, D)

def reference(state, lengths, halt_mask, w_query, w_key, w_value, w_output, first_norm_gain, first_norm_bias, w_inner, w_outer, second_norm_gain, second_norm_bias, halt_weight, cotangent):
    group = math.gcd(SEQS, max(1, 4096 // LEN))
    steps = SEQS // group
    states = state.astype(jnp.float32).reshape(steps, group, LEN, D)
    grads_in = cotangent.astype(jnp.float32).reshape(steps, group, LEN, D)
    runs = halt_mask.astype(jnp.float32).reshape(steps, group, LEN)
    lens = lengths.astype(jnp.int32).reshape(steps, group)
    weights = (w_query.astype(jnp.float32), w_key.astype(jnp.float32), w_value.astype(jnp.float32), w_output.astype(jnp.float32), first_norm_gain.astype(jnp.float32), first_norm_bias.astype(jnp.float32), w_inner.astype(jnp.float32), w_outer.astype(jnp.float32), second_norm_gain.astype(jnp.float32), second_norm_bias.astype(jnp.float32), halt_weight.astype(jnp.float32))

    def one_group(totals, item):
        block_state, block_len, block_run, block_grad = item
        valid = jnp.arange(LEN, dtype=jnp.int32)[None, :] < block_len[:, None]
        result, pull = jax.vjp(lambda xs, *ws: block(xs, valid, block_run, *ws), block_state, *weights)
        grads = pull(block_grad)
        totals = tuple((a + b for a, b in zip(totals, grads[1:])))
        return (totals, (result, grads[0]))
    start = tuple((jnp.zeros_like(w) for w in weights))
    totals, (results, state_grads) = lax.scan(one_group, start, (states, lens, runs, grads_in))
    return (results.reshape(TOKENS, D), state_grads.reshape(TOKENS, D)) + tuple(totals)
```

```python
import functools
import math

import jax
import jax.numpy as jnp
import numpy as np
from jax import lax
from jax.experimental import pallas as pl
from jax.experimental.pallas import tpu as pltpu
from jax.sharding import PartitionSpec as P

HEAD = 64
LEN = 1024
STEP = 2
LOG2E = 1.4426950408889634
BF = jnp.bfloat16
F32 = jnp.float32
NN = (((1,), (0,)), ((), ()))
NT = (((1,), (1,)), ((), ()))
TN = (((0,), (0,)), ((), ()))
TT = (((0,), (1,)), ((), ()))
VMEM_LIMIT = 60 << 20
CHUNK = 256


def mm(a, b, dims=NN):
    return lax.dot_general(a, b, dims, preferred_element_type=F32)


def params():
    return pltpu.CompilerParams(vmem_limit_bytes=VMEM_LIMIT)


def whole(shape):
    zeros = (0,) * len(shape)
    return pl.BlockSpec(shape, lambda *_: zeros)


def timing_rows(width):
    half = width // 2
    rates = np.exp(-math.log(10000.0) * np.arange(half, dtype=np.float64) / (half - 1))

    def rows(positions):
        angles = positions[:, None] * rates[None, :]
        return np.concatenate([np.sin(angles), np.cos(angles)], axis=1)

    return (rows(np.arange(LEN, dtype=np.float64)) + rows(np.array([float(STEP)]))).astype(
        np.float32
    )


def split_low(value):
    high = value.astype(BF)
    return high, (value - high.astype(F32)).astype(BF)


def rolled(pair):
    return jnp.concatenate([pair[:, HEAD:], pair[:, :HEAD]], axis=1)


def lane_index(shape):
    return lax.broadcasted_iota(jnp.int32, shape, 1)


def row_index(shape):
    return lax.broadcasted_iota(jnp.int32, shape, 0)


def attention_forward_kernel(
    lengths, state, timing, wq, wk, wv, e_out, mixed_out, r_out,
    kaug, qaug, vaug, sa, sb, ma, mb, *, seqs, heads
):
    count = seqs * heads
    j = pl.program_id(0)
    pieces = LEN // CHUNK

    def score_piece(i, c, target):
        rows = slice(c * CHUNK, (c + 1) * CHUNK)
        s = mm(kaug[i, rows], qaug[i])
        target[rows] = s
        return jnp.max(s.reshape(CHUNK // 8, 8, LEN), axis=0)

    @pl.when(j == 0)
    def _():
        for s in range(seqs):
            x = (state[s * LEN : (s + 1) * LEN].astype(F32) + timing[...]).astype(BF)
            query = mm(wq[...], x, TT).astype(BF).astype(F32) * (LOG2E / math.sqrt(HEAD))
            high, rest = split_low(query)
            key = mm(x, wk[...]).astype(BF)
            value = mm(wv[...], x, TT).astype(BF)
            shape = (LEN, 2 * HEAD)
            lane = lane_index(shape)
            padded = row_index(shape) >= lengths[s]
            mask = jnp.where(padded & ((lane == 0) | (lane == HEAD)), -1e30, 0.0).astype(BF)
            first = row_index((HEAD, LEN)) == 0
            ones = jnp.where(first, 1.0, 0.0).astype(BF)
            zeros = jnp.zeros((HEAD, LEN), BF)
            for h in range(heads):
                i = s * heads + h
                pair = key[:, (h // 2) * 128 : (h // 2) * 128 + 128]
                turned = rolled(pair)
                mine = slice(h * HEAD, (h + 1) * HEAD)
                kaug[i, :, 0:128] = pair
                if h % 2 == 0:
                    kaug[i, :, 128:256] = jnp.where(lane < HEAD, mask, turned)
                    parts = (high[mine], zeros, ones, rest[mine])
                else:
                    kaug[i, :, 128:256] = jnp.where(lane < HEAD, turned, mask)
                    parts = (zeros, high[mine], rest[mine], ones)
                for n, part in enumerate(parts):
                    qaug[i, n * HEAD : (n + 1) * HEAD] = part
                vaug[i, 0:HEAD] = value[mine]
                vaug[i, HEAD : HEAD + 16] = jnp.ones((16, LEN), BF)
        top = None
        for c in range(pieces):
            m = score_piece(0, c, sa)
            top = m if top is None else jnp.maximum(top, m)
        ma[...] = jnp.max(top, axis=0, keepdims=True)

    def step(slot, cur, cur_m, nxt, nxt_m):
        i = 2 * j + slot
        following = lax.rem(i + 1, count)
        shift = cur_m[...]
        top = None
        out = None
        for c in range(pieces):
            rows = slice(c * CHUNK, (c + 1) * CHUNK)
            m = score_piece(following, c, nxt)
            top = m if top is None else jnp.maximum(top, m)
            e = jnp.exp2(cur[rows] - shift).astype(BF)
            e_out[slot, rows] = e
            o = mm(vaug[i, :, rows], e)
            out = o if out is None else out + o
        nxt_m[...] = jnp.max(top, axis=0, keepdims=True)
        r = 1.0 / out[HEAD : HEAD + 1]
        mixed_out[slot * HEAD : (slot + 1) * HEAD] = (out[:HEAD] * r).astype(BF)
        r_out[slot] = r

    step(0, sa, ma, sb, mb)
    step(1, sb, mb, sa, ma)


def attention_forward(lengths, state, timing, wq, wk, wv):
    rows, width = state.shape
    seqs, local = rows // LEN, wq.shape[1]
    heads = local // HEAD
    count, half = seqs * heads, heads // 2
    return pl.pallas_call(
        functools.partial(attention_forward_kernel, seqs=seqs, heads=heads),
        grid=(count // 2,),
        in_specs=[
            pl.BlockSpec(memory_space=pltpu.SMEM),
            whole((rows, width)),
            whole((LEN, width)),
            whole((width, local)),
            whole((width, local)),
            whole((width, local)),
        ],
        out_specs=[
            pl.BlockSpec((2, LEN, LEN), lambda j: (j, 0, 0)),
            pl.BlockSpec((2 * HEAD, LEN), lambda j: (j % half, j // half)),
            pl.BlockSpec((2, 1, LEN), lambda j: (j, 0, 0)),
        ],
        out_shape=[
            jax.ShapeDtypeStruct((count, LEN, LEN), BF),
            jax.ShapeDtypeStruct((local, rows), BF),
            jax.ShapeDtypeStruct((count, 1, LEN), F32),
        ],
        scratch_shapes=[
            pltpu.VMEM((count, LEN, 256), BF),
            pltpu.VMEM((count, 256, LEN), BF),
            pltpu.VMEM((count, HEAD + 16, LEN), BF),
            pltpu.VMEM((LEN, LEN), F32),
            pltpu.VMEM((LEN, LEN), F32),
            pltpu.VMEM((1, LEN), F32),
            pltpu.VMEM((1, LEN), F32),
        ],
        compiler_params=params(),
        cost_estimate=pl.CostEstimate(
            flops=8 * 2 * count * LEN * LEN * HEAD,
            bytes_accessed=2 * count * LEN * LEN,
            transcendentals=count * LEN * LEN,
        ),
        name="attention_forward",
    )(lengths, state, timing, wq, wk, wv)


def row_mean(v):
    return jnp.mean(v, axis=-1, keepdims=True)


def norm_rows(v):
    centre = v - row_mean(v)
    deviation = lax.rsqrt(row_mean(centre * centre) + 1e-05)
    return centre * deviation, deviation


def norm_back(e, xhat, deviation):
    return deviation * (e - row_mean(e) - xhat * row_mean(e * xhat))


def fold_rows(v):
    return jnp.sum(v.reshape(v.shape[0] // 8, 8, v.shape[1]), axis=0)


def middle_kernel(
    state, timing, cot, run, mix_a, mix_b, r_a, r_b, wo_a, wo_b, wi_a, wi_b, wu_a, wu_b,
    vectors, new_state, gs, do_a, do_b, dl_a, dl_b, grads, act, slope, fold, *, heads
):
    t = pl.program_id(0)
    last = pl.num_programs(0) - 1
    ff = wi_a.shape[1]
    local = wo_a.shape[0]
    width = state.shape[1]
    gain1, bias1, gain2, bias2, halt_w = (vectors[n : n + 1] for n in range(5))

    @pl.when(t == 0)
    def _():
        grads[...] = jnp.zeros(grads.shape, F32)
        fold[...] = jnp.zeros(fold.shape, F32)

    old = state[...].astype(F32)
    embedded = old + timing[...]
    attended = mm(mix_a[...], wo_a[...], TN) + mm(mix_b[...], wo_b[...], TN)
    xhat1, dev1 = norm_rows(embedded + attended)
    normed1 = xhat1 * gain1 + bias1
    low1 = normed1.astype(BF)
    c0 = math.sqrt(2.0 / math.pi)
    outer = None
    for n, (wi, wu) in enumerate(((wi_a, wu_a), (wi_b, wu_b))):
        v = mm(low1, wi[...])
        square = v * v
        h = 0.5 + 0.5 * jnp.tanh(v * (c0 + (c0 * 0.044715) * square))
        g = v * h
        act[n] = g.astype(BF)
        slope[n] = (
            h + g * (1.0 - h) * (2.0 * c0 + (6.0 * c0 * 0.044715) * square)
        ).astype(slope.dtype)
        o = mm(act[n], wu[...])
        outer = o if outer is None else outer + o
    xhat2, dev2 = norm_rows(normed1 + outer)
    block = xhat2 * gain2 + bias2
    halt = jax.nn.sigmoid(jnp.sum(block * halt_w, axis=-1, keepdims=True))
    running = run[...].astype(F32)
    gate = running * halt
    new_state[...] = old + gate * (block - old)
    g_in = cot[...].astype(F32)
    d_prob = running * jnp.sum(g_in * (block - old), axis=-1, keepdims=True)
    d_logit = d_prob * halt * (1.0 - halt)
    d_block = gate * g_in + d_logit * halt_w
    fold[4] += fold_rows(d_logit * block)
    fold[2] += fold_rows(d_block * xhat2)
    fold[3] += fold_rows(d_block)
    d_hidden2 = norm_back(d_block * gain2, xhat2, dev2)
    d_outer = d_hidden2.astype(BF)
    d_normed1 = d_hidden2
    for n, (wi, wu) in enumerate(((wi_a, wu_a), (wi_b, wu_b))):
        d_act = mm(d_outer, wu[...], NT)
        d_inner = (d_act * slope[n].astype(F32)).astype(BF)
        d_normed1 = d_normed1 + mm(d_inner, wi[...], NT)
        if n == 0:
            grads[0:ff] += mm(act[0], d_outer, TN)
            gi = mm(low1, d_inner, TN)
            for p in range(ff // width):
                grads[ff + p * width : ff + (p + 1) * width] += gi[
                    :, p * width : (p + 1) * width
                ]
    fold[0] += fold_rows(d_normed1 * xhat1)
    fold[1] += fold_rows(d_normed1)
    d_hidden1 = norm_back(d_normed1 * gain1, xhat1, dev1)
    d_att = d_hidden1.astype(BF)
    gs[...] = g_in * (1.0 - gate) + d_hidden1
    grads[2 * ff : 2 * ff + local] += mm(mix_a[...], d_att)
    for mix, r, wo, do, dl in (
        (mix_a, r_a, wo_a, do_a, dl_a),
        (mix_b, r_b, wo_b, do_b, dl_b),
    ):
        d_mixed = mm(wo[...], d_att, NT).astype(BF).astype(F32)
        for h in range(heads):
            mine = slice(h * HEAD, (h + 1) * HEAD)
            part = d_mixed[mine]
            scale = r[h]
            do[mine] = part * scale
            total = jnp.sum(part * mix[mine].astype(F32), axis=0, keepdims=True)
            dl[h] = total * scale

    @pl.when(t == last)
    def _():
        base = 2 * ff + local
        for n in range(5):
            grads[base + n : base + n + 1] = jnp.sum(fold[n], axis=0, keepdims=True)


def middle(state, timing, cot, run, mix_a, mix_b, r_a, r_b, wo_a, wo_b, wi_a, wi_b, wu_a,
           wu_b, vectors):
    rows, width = state.shape
    local, ff = wo_a.shape[0], wi_a.shape[1]
    heads = local // HEAD
    tile = 512
    per = LEN // tile
    grad_rows = 2 * ff + local + 8
    by_rows = pl.BlockSpec((tile, width), lambda t: (t, 0))
    by_columns = pl.BlockSpec((local, tile), lambda t: (0, t))
    per_head = pl.BlockSpec((heads, 1, tile), lambda t: (t // per, 0, t % per))
    return pl.pallas_call(
        functools.partial(middle_kernel, heads=heads),
        grid=(rows // tile,),
        in_specs=[
            by_rows,
            pl.BlockSpec((tile, width), lambda t: (t % per, 0)),
            by_rows,
            pl.BlockSpec((tile, 1), lambda t: (t, 0)),
            by_columns,
            by_columns,
            per_head,
            per_head,
            whole((local, width)),
            whole((local, width)),
            whole((width, ff)),
            whole((width, ff)),
            whole((ff, width)),
            whole((ff, width)),
            whole((8, width)),
        ],
        out_specs=[
            by_rows,
            by_rows,
            by_columns,
            by_columns,
            per_head,
            per_head,
            whole((grad_rows, width)),
        ],
        out_shape=[
            jax.ShapeDtypeStruct((rows, width), F32),
            jax.ShapeDtypeStruct((rows, width), F32),
            jax.ShapeDtypeStruct((local, rows), F32),
            jax.ShapeDtypeStruct((local, rows), F32),
            jax.ShapeDtypeStruct((rows // LEN * heads, 1, LEN), F32),
            jax.ShapeDtypeStruct((rows // LEN * heads, 1, LEN), F32),
            jax.ShapeDtypeStruct((grad_rows, width), F32),
        ],
        scratch_shapes=[
            pltpu.VMEM((2, tile, ff), BF),
            pltpu.VMEM((2, tile, ff), F32),
            pltpu.VMEM((8, 8, width), F32),
        ],
        compiler_params=params(),
        cost_estimate=pl.CostEstimate(
            flops=2 * rows * width * ff * 10 + 2 * rows * width * local * 6,
            bytes_accessed=rows * width * 20,
            transcendentals=2 * rows * ff,
        ),
        name="middle",
    )(state, timing, cot, run, mix_a, mix_b, r_a, r_b, wo_a, wo_b, wi_a, wi_b, wu_a, wu_b,
      vectors)


def attention_backward_kernel(
    e_in, do_in, dl_in, state, timing, wq, wk, wv, gs_in, gs_out, *rest, heads, own
):
    if own:
        gq, gk, gv, x_s, qt, kt, vaug, dq, dk, dv, aq, akv = rest
    else:
        x_s, qt, kt, vaug, dq, dk, dv = rest
    i = pl.program_id(0)
    h = lax.rem(i, heads)
    factor = 1.0 / math.sqrt(HEAD)
    pieces = LEN // CHUNK
    local = wq.shape[1]

    @pl.when(h == 0)
    def _():
        x = (state[...].astype(F32) + timing[...]).astype(BF)
        x_s[...] = x
        query = mm(wq[...], x, TT).astype(BF)
        key = mm(wk[...], x, TT).astype(BF)
        value = mm(x, wv[...]).astype(BF)
        lane = lane_index((LEN, 2 * HEAD))
        ones = jnp.where((lane % HEAD) < 3, 1.0, 0.0).astype(BF)
        for n in range(heads):
            mine = slice(n * HEAD, (n + 1) * HEAD)
            qt[n] = query[mine]
            kt[n] = key[mine]
            pair = value[:, (n // 2) * 128 : (n // 2) * 128 + 128]
            turned = rolled(pair)
            if n % 2 == 0:
                vaug[n, :, 0:128] = jnp.where(lane < HEAD, pair, turned)
            else:
                vaug[n, :, 0:128] = jnp.where(lane < HEAD, turned, pair)
            vaug[n, :, 128:256] = ones

    high, low = split_low(do_in[...])
    delta = -dl_in[0]
    d1 = delta.astype(BF)
    left = delta - d1.astype(F32)
    d2 = left.astype(BF)
    d3 = (left - d2.astype(F32)).astype(BF)
    index = row_index((2 * HEAD, LEN))
    tail = jnp.where(
        index == 0,
        d1.astype(F32),
        jnp.where(index == 1, d2.astype(F32), jnp.where(index == 2, d3.astype(F32), 0.0)),
    ).astype(BF)
    right = jnp.concatenate([high, low, tail], axis=0)
    query = qt[h]
    out = None
    for c in range(pieces):
        rows = slice(c * CHUNK, (c + 1) * CHUNK)
        d_probs = mm(vaug[h, rows], right)
        e = e_in[0, rows]
        d_scores = (e.astype(F32) * d_probs).astype(BF)
        dv[h, rows] = mm(e, high, NT).astype(BF)
        dk[h, rows] = (mm(d_scores, query, NT) * factor).astype(BF)
        o = mm(kt[h, :, rows], d_scores)
        out = o if out is None else out + o
    dq[pl.ds(pl.multiple_of(h * HEAD, HEAD), HEAD)] = (out * factor).astype(BF)

    @pl.when(h == heads - 1)
    def _():
        x = x_s[...]
        d_query = dq[...]
        d_key = jnp.concatenate([dk[n] for n in range(heads)], axis=1)
        d_value = jnp.concatenate([dv[n] for n in range(heads)], axis=1)
        total = mm(d_query, wq[...], TT)
        total = total + mm(d_key, wk[...], NT)
        total = total + mm(d_value, wv[...], NT)
        gs_out[...] = gs_in[...] + total
        if own:
            g1 = mm(d_query, x)
            g2 = mm(x, jnp.concatenate([d_key, d_value], axis=1), TN)

            @pl.when(i < heads)
            def _():
                aq[...] = g1
                akv[...] = g2

            @pl.when(i >= heads)
            def _():
                aq[...] += g1
                akv[...] += g2

            @pl.when(i == pl.num_programs(0) - 1)
            def _():
                gq[...] = aq[...].T
                gk[...] = akv[:, :local]
                gv[...] = akv[:, local:]


def attention_backward(e, do, dl, state, timing, wq, wk, wv, gs, own):
    rows, width = state.shape
    seqs, local = rows // LEN, wq.shape[1]
    heads = local // HEAD
    count = seqs * heads
    by_rows = pl.BlockSpec((LEN, width), lambda i: (i // heads, 0))
    out_specs = [by_rows]
    out_shape = [jax.ShapeDtypeStruct((rows, width), F32)]
    scratch = [
        pltpu.VMEM((LEN, width), BF),
        pltpu.VMEM((heads, HEAD, LEN), BF),
        pltpu.VMEM((heads, HEAD, LEN), BF),
        pltpu.VMEM((heads, LEN, 256), BF),
        pltpu.VMEM((local, LEN), BF),
        pltpu.VMEM((heads, LEN, HEAD), BF),
        pltpu.VMEM((heads, LEN, HEAD), BF),
    ]
    if own:
        out_specs += [whole((width, local))] * 3
        out_shape += [jax.ShapeDtypeStruct((width, local), F32)] * 3
        scratch += [pltpu.VMEM((local, width), F32), pltpu.VMEM((width, 2 * local), F32)]
    return pl.pallas_call(
        functools.partial(attention_backward_kernel, heads=heads, own=own),
        grid=(count,),
        in_specs=[
            pl.BlockSpec((1, LEN, LEN), lambda i: (i, 0, 0)),
            pl.BlockSpec((HEAD, LEN), lambda i: (i % heads, i // heads)),
            pl.BlockSpec((1, 1, LEN), lambda i: (i, 0, 0)),
            by_rows,
            whole((LEN, width)),
            whole((width, local)),
            whole((width, local)),
            whole((width, local)),
            by_rows,
        ],
        out_specs=out_specs,
        out_shape=out_shape,
        scratch_shapes=scratch,
        compiler_params=params(),
        input_output_aliases={8: 0},
        cost_estimate=pl.CostEstimate(
            flops=16 * 2 * count * LEN * LEN * HEAD,
            bytes_accessed=2 * count * LEN * LEN,
            transcendentals=0,
        ),
        name="attention_backward_own" if own else "attention_backward_other",
    )(e, do, dl, state, timing, wq, wk, wv, gs)


def pack_kernel(place, wq, wk, wv, wo, wi, wu, out_a, out_b):
    p = place[0]
    width, local = wq.shape
    quarter = width // 4

    def cut(ref, size):
        return ref[pl.ds(pl.multiple_of(p * size, size), size)].astype(F32)

    for n, ref in enumerate((wq, wk, wv)):
        out_a[:, n * local : (n + 1) * local] = cut(ref, quarter)
    inner = cut(wi, quarter)
    for n in range(wi.shape[1] // width):
        out_b[n * quarter : (n + 1) * quarter] = inner[:, n * width : (n + 1) * width]
    base = quarter * (wi.shape[1] // width)
    fourth = wu.shape[0] // 4
    out_b[base : base + fourth] = cut(wu, fourth)
    out_b[base + fourth :] = cut(wo, wo.shape[0] // 4)


def pack(place, wq, wk, wv, wo, wi, wu):
    width, local = wq.shape
    ff = wi.shape[1]
    return pl.pallas_call(
        pack_kernel,
        in_specs=[pl.BlockSpec(memory_space=pltpu.SMEM)]
        + [pl.BlockSpec(memory_space=pltpu.VMEM)] * 6,
        out_specs=[pl.BlockSpec(memory_space=pltpu.VMEM)] * 2,
        out_shape=[
            jax.ShapeDtypeStruct((width // 4, 3 * local), F32),
            jax.ShapeDtypeStruct((ff // 2 + local // 4, width), F32),
        ],
        compiler_params=params(),
        name="pack",
    )(place, wq, wk, wv, wo, wi, wu)


def unpack_qkv_kernel(place, a, b, c, d, wq, wk, wv):
    quarter = a.shape[0]
    local = wq.shape[1]
    for flip, ref in ((0, a), (2, b), (1, c), (3, d)):
        p = place[flip]
        rows = pl.ds(pl.multiple_of(p * quarter, quarter), quarter)
        for n, out in enumerate((wq, wk, wv)):
            out[rows] = ref[:, n * local : (n + 1) * local].astype(BF)


def unpack_qkv(place, parts, width, local):
    return pl.pallas_call(
        unpack_qkv_kernel,
        in_specs=[pl.BlockSpec(memory_space=pltpu.SMEM)]
        + [pl.BlockSpec(memory_space=pltpu.VMEM)] * 4,
        out_specs=[pl.BlockSpec(memory_space=pltpu.VMEM)] * 3,
        out_shape=[jax.ShapeDtypeStruct((width, local), BF)] * 3,
        compiler_params=params(),
        name="unpack_qkv",
    )(place, *parts)


def unpack_ff_kernel(place, a, b, c, d, wo, wi, wu):
    width, ff = wi.shape
    quarter, fourth, few = width // 4, ff // 4, wo.shape[0] // 4
    for flip, ref in ((0, a), (2, b), (1, c), (3, d)):
        p = place[flip]
        rows = pl.ds(pl.multiple_of(p * quarter, quarter), quarter)
        for n in range(ff // width):
            wi[rows, n * width : (n + 1) * width] = ref[
                n * quarter : (n + 1) * quarter
            ].astype(BF)
        base = quarter * (ff // width)
        wu[pl.ds(pl.multiple_of(p * fourth, fourth), fourth)] = ref[
            base : base + fourth
        ].astype(BF)
        wo[pl.ds(pl.multiple_of(p * few, few), few)] = ref[base + fourth :].astype(BF)


def unpack_ff(place, parts, width, local, ff):
    return pl.pallas_call(
        unpack_ff_kernel,
        in_specs=[pl.BlockSpec(memory_space=pltpu.SMEM)]
        + [pl.BlockSpec(memory_space=pltpu.VMEM)] * 4,
        out_specs=[pl.BlockSpec(memory_space=pltpu.VMEM)] * 3,
        out_shape=[
            jax.ShapeDtypeStruct((local, width), BF),
            jax.ShapeDtypeStruct((width, ff), BF),
            jax.ShapeDtypeStruct((ff, width), BF),
        ],
        compiler_params=params(),
        name="unpack_ff",
    )(place, *parts)


def flipped(size, bit):
    return [(i, i ^ bit) for i in range(size)]


def spread(chunk, dp):
    a = lax.ppermute(chunk, "mp", [(0, 1), (1, 0)])
    b = lax.ppermute(a, "dp", flipped(dp, 2))
    c = lax.ppermute(a, "dp", flipped(dp, 1))
    d = lax.ppermute(b, "dp", flipped(dp, 1))
    return a, b, c, d


def shards(
    dp, state, lengths, halt_mask, wq, wk, wv, wo, gain1, bias1, wi, wu, gain2, bias2,
    halt_weight, cotangent
):
    rows, width = state.shape
    local, ff = wq.shape[1], wi.shape[1]
    timing = jnp.asarray(timing_rows(width))
    me = lax.rem(lax.axis_index("dp"), 4).astype(jnp.int32)
    places = jnp.bitwise_xor(me, jnp.arange(4, dtype=jnp.int32))
    chunk_a, chunk_b = pack(places, wq, wk, wv, wo, wi, wu)
    parts_a = spread(chunk_a, dp)
    parts_b = spread(chunk_b, dp)
    e_a, mix_a, r_a = attention_forward(lengths, state, timing, wq, wk, wv)
    wq2, wk2, wv2 = unpack_qkv(places, parts_a, width, local)
    e_b, mix_b, r_b = attention_forward(lengths, state, timing, wq2, wk2, wv2)
    wo2, wi2, wu2 = unpack_ff(places, parts_b, width, local, ff)
    vectors = jnp.stack([gain1, bias1, gain2, bias2, halt_weight] + [gain1] * 3)
    new_state, gs, do_a, do_b, dl_a, dl_b, grads = middle(
        state, timing, cotangent, halt_mask[:, None], mix_a, mix_b, r_a, r_b, wo, wo2, wi,
        wi2, wu, wu2, vectors
    )
    gs, gq, gk, gv = attention_backward(e_a, do_a, dl_a, state, timing, wq, wk, wv, gs, True)
    (gs,) = attention_backward(e_b, do_b, dl_b, state, timing, wq2, wk2, wv2, gs, False)
    grads, gq, gk, gv = lax.psum((grads, gq, gk, gv), "dp")
    gi = jnp.concatenate([grads[ff + n * width : ff + (n + 1) * width] for n in range(ff // width)], axis=1)
    base = 2 * ff + local
    return (
        new_state,
        gs,
        gq,
        gk,
        gv,
        grads[2 * ff : base],
        grads[base],
        grads[base + 1],
        gi,
        grads[:ff],
        grads[base + 2],
        grads[base + 3],
        grads[base + 4],
    )


def solution(mesh):
    rows, columns, parts = P("dp", None), P(None, "mp"), P("mp", None)
    return jax.shard_map(
        functools.partial(shards, mesh.shape["dp"]),
        mesh=mesh,
        in_specs=(
            rows, P("dp"), P("dp"), columns, columns, columns, parts, P(), P(), columns,
            parts, P(), P(), P(), rows
        ),
        out_specs=(
            rows, rows, columns, columns, columns, parts, P(), P(), columns, parts, P(), P(),
            P()
        ),
        check_vma=False,
    )
```

```python
import functools
import math

import jax
import jax.numpy as jnp
import numpy as np
from jax import lax
from jax.experimental import pallas as pl
from jax.experimental.pallas import tpu as pltpu
from jax.sharding import PartitionSpec as P

HEAD = 64
LEN = 1024
STEP = 2
LOG2E = 1.4426950408889634
BF = jnp.bfloat16
F32 = jnp.float32
NN = (((1,), (0,)), ((), ()))
NT = (((1,), (1,)), ((), ()))
TN = (((0,), (0,)), ((), ()))
TT = (((0,), (1,)), ((), ()))
VMEM_LIMIT = 60 << 20
CHUNK = 256


def mm(a, b, dims=NN):
    return lax.dot_general(a, b, dims, preferred_element_type=F32)


def params():
    return pltpu.CompilerParams(vmem_limit_bytes=VMEM_LIMIT)


def whole(shape):
    zeros = (0,) * len(shape)
    return pl.BlockSpec(shape, lambda *_: zeros)


def timing_rows(width):
    half = width // 2
    rates = np.exp(-math.log(10000.0) * np.arange(half, dtype=np.float64) / (half - 1))

    def rows(positions):
        angles = positions[:, None] * rates[None, :]
        return np.concatenate([np.sin(angles), np.cos(angles)], axis=1)

    return (rows(np.arange(LEN, dtype=np.float64)) + rows(np.array([float(STEP)]))).astype(
        np.float32
    )


def split_low(value):
    high = value.astype(BF)
    return high, (value - high.astype(F32)).astype(BF)


def rolled(pair):
    return jnp.concatenate([pair[:, HEAD:], pair[:, :HEAD]], axis=1)


def lane_index(shape):
    return lax.broadcasted_iota(jnp.int32, shape, 1)


def row_index(shape):
    return lax.broadcasted_iota(jnp.int32, shape, 0)


def attention_forward_kernel(
    lengths, state, timing, wq, wk, wv, *rest, seqs, heads
):
    e_out, mixed_out, r_out, kaug, qaug, vaug, sa, sb, ma, mb = rest[-10:]
    count = seqs * heads
    j = pl.program_id(0)
    pieces = LEN // CHUNK

    def score_piece(i, c, target):
        rows = slice(c * CHUNK, (c + 1) * CHUNK)
        s = mm(kaug[i, rows], qaug[i])
        target[rows] = s
        return jnp.max(s.reshape(CHUNK // 8, 8, LEN), axis=0)

    @pl.when(j == 0)
    def _():
        for s in range(seqs):
            x = (state[s * LEN : (s + 1) * LEN].astype(F32) + timing[...]).astype(BF)
            query = mm(wq[...], x, TT).astype(BF).astype(F32) * (LOG2E / math.sqrt(HEAD))
            high, rest = split_low(query)
            key = mm(x, wk[...]).astype(BF)
            value = mm(wv[...], x, TT).astype(BF)
            shape = (LEN, 2 * HEAD)
            lane = lane_index(shape)
            padded = row_index(shape) >= lengths[s]
            mask = jnp.where(padded & ((lane == 0) | (lane == HEAD)), -1e30, 0.0).astype(BF)
            first = row_index((HEAD, LEN)) == 0
            ones = jnp.where(first, 1.0, 0.0).astype(BF)
            zeros = jnp.zeros((HEAD, LEN), BF)
            for h in range(heads):
                i = s * heads + h
                pair = key[:, (h // 2) * 128 : (h // 2) * 128 + 128]
                turned = rolled(pair)
                mine = slice(h * HEAD, (h + 1) * HEAD)
                kaug[i, :, 0:128] = pair
                if h % 2 == 0:
                    kaug[i, :, 128:256] = jnp.where(lane < HEAD, mask, turned)
                    parts = (high[mine], zeros, ones, rest[mine])
                else:
                    kaug[i, :, 128:256] = jnp.where(lane < HEAD, turned, mask)
                    parts = (zeros, high[mine], rest[mine], ones)
                for n, part in enumerate(parts):
                    qaug[i, n * HEAD : (n + 1) * HEAD] = part
                vaug[i, 0:HEAD] = value[mine]
                vaug[i, HEAD : HEAD + 16] = jnp.ones((16, LEN), BF)
        top = None
        for c in range(pieces):
            m = score_piece(0, c, sa)
            top = m if top is None else jnp.maximum(top, m)
        ma[...] = jnp.max(top, axis=0, keepdims=True)

    def step(slot, cur, cur_m, nxt, nxt_m):
        i = 2 * j + slot
        following = lax.rem(i + 1, count)
        shift = cur_m[...]
        top = None
        out = None
        for c in range(pieces):
            rows = slice(c * CHUNK, (c + 1) * CHUNK)
            m = score_piece(following, c, nxt)
            top = m if top is None else jnp.maximum(top, m)
            e = jnp.exp2(cur[rows] - shift).astype(BF)
            e_out[slot, rows] = e
            o = mm(vaug[i, :, rows], e)
            out = o if out is None else out + o
        nxt_m[...] = jnp.max(top, axis=0, keepdims=True)
        r = 1.0 / out[HEAD : HEAD + 1]
        mixed_out[slot * HEAD : (slot + 1) * HEAD] = (out[:HEAD] * r).astype(BF)
        r_out[slot] = r

    step(0, sa, ma, sb, mb)
    step(1, sb, mb, sa, ma)


def attention_forward(part, lengths, state, timing, wq, wk, wv, earlier=()):
    rows, width = state.shape
    seqs, local = rows // LEN, wq.shape[1]
    heads, parts = 2, local // 128
    count, total = seqs * heads, seqs * local // HEAD
    columns = pl.BlockSpec((width, 128), lambda j: (0, part))
    return pl.pallas_call(
        functools.partial(attention_forward_kernel, seqs=seqs, heads=heads),
        grid=(seqs,),
        in_specs=[
            pl.BlockSpec(memory_space=pltpu.SMEM),
            whole((rows, width)),
            whole((LEN, width)),
            columns,
            columns,
            columns,
        ]
        + [pl.BlockSpec(memory_space=pl.ANY)] * len(earlier),
        out_specs=[
            pl.BlockSpec((2, LEN, LEN), lambda j: (j * parts + part, 0, 0)),
            pl.BlockSpec((2 * HEAD, LEN), lambda j: (part, j)),
            pl.BlockSpec((2, 1, LEN), lambda j: (j * parts + part, 0, 0)),
        ],
        out_shape=[
            jax.ShapeDtypeStruct((total, LEN, LEN), BF),
            jax.ShapeDtypeStruct((local, rows), BF),
            jax.ShapeDtypeStruct((total, 1, LEN), F32),
        ],
        scratch_shapes=[
            pltpu.VMEM((count, LEN, 256), BF),
            pltpu.VMEM((count, 256, LEN), BF),
            pltpu.VMEM((count, HEAD + 16, LEN), BF),
            pltpu.VMEM((LEN, LEN), F32),
            pltpu.VMEM((LEN, LEN), F32),
            pltpu.VMEM((1, LEN), F32),
            pltpu.VMEM((1, LEN), F32),
        ],
        compiler_params=params(),
        input_output_aliases={6 + n: n for n in range(len(earlier))},
        cost_estimate=pl.CostEstimate(
            flops=8 * 2 * count * LEN * LEN * HEAD,
            bytes_accessed=2 * count * LEN * LEN,
            transcendentals=count * LEN * LEN,
        ),
        name="attention_forward",
    )(lengths, state, timing, wq, wk, wv, *earlier)


def row_mean(v):
    return jnp.mean(v, axis=-1, keepdims=True)


def norm_rows(v):
    centre = v - row_mean(v)
    deviation = lax.rsqrt(row_mean(centre * centre) + 1e-05)
    return centre * deviation, deviation


def norm_back(e, xhat, deviation):
    return deviation * (e - row_mean(e) - xhat * row_mean(e * xhat))


def fold_rows(v):
    return jnp.sum(v.reshape(v.shape[0] // 8, 8, v.shape[1]), axis=0)


def middle_kernel(
    state, timing, cot, run, mix_a, mix_b, r_a, r_b, wo_a, wo_b, wi_a, wi_b, wu_a, wu_b,
    vectors, new_state, gs, do_a, do_b, dl_a, dl_b, grads, act, slope, fold, *, heads
):
    t = pl.program_id(0)
    last = pl.num_programs(0) - 1
    ff = wi_a.shape[1]
    local = wo_a.shape[0]
    width = state.shape[1]
    gain1, bias1, gain2, bias2, halt_w = (vectors[n : n + 1] for n in range(5))

    @pl.when(t == 0)
    def _():
        grads[...] = jnp.zeros(grads.shape, F32)
        fold[...] = jnp.zeros(fold.shape, F32)

    old = state[...].astype(F32)
    embedded = old + timing[...]
    attended = mm(mix_a[...], wo_a[...], TN) + mm(mix_b[...], wo_b[...], TN)
    xhat1, dev1 = norm_rows(embedded + attended)
    normed1 = xhat1 * gain1 + bias1
    low1 = normed1.astype(BF)
    c0 = math.sqrt(2.0 / math.pi)
    outer = None
    for n, (wi, wu) in enumerate(((wi_a, wu_a), (wi_b, wu_b))):
        v = mm(low1, wi[...])
        square = v * v
        h = 0.5 + 0.5 * jnp.tanh(v * (c0 + (c0 * 0.044715) * square))
        g = v * h
        act[n] = g.astype(BF)
        slope[n] = (
            h + g * (1.0 - h) * (2.0 * c0 + (6.0 * c0 * 0.044715) * square)
        ).astype(slope.dtype)
        o = mm(act[n], wu[...])
        outer = o if outer is None else outer + o
    xhat2, dev2 = norm_rows(normed1 + outer)
    block = xhat2 * gain2 + bias2
    halt = jax.nn.sigmoid(jnp.sum(block * halt_w, axis=-1, keepdims=True))
    running = run[...].astype(F32)
    gate = running * halt
    new_state[...] = old + gate * (block - old)
    g_in = cot[...].astype(F32)
    d_prob = running * jnp.sum(g_in * (block - old), axis=-1, keepdims=True)
    d_logit = d_prob * halt * (1.0 - halt)
    d_block = gate * g_in + d_logit * halt_w
    fold[4] += fold_rows(d_logit * block)
    fold[2] += fold_rows(d_block * xhat2)
    fold[3] += fold_rows(d_block)
    d_hidden2 = norm_back(d_block * gain2, xhat2, dev2)
    d_outer = d_hidden2.astype(BF)
    d_normed1 = d_hidden2
    for n, (wi, wu) in enumerate(((wi_a, wu_a), (wi_b, wu_b))):
        d_act = mm(d_outer, wu[...], NT)
        d_inner = (d_act * slope[n].astype(F32)).astype(BF)
        d_normed1 = d_normed1 + mm(d_inner, wi[...], NT)
        if n == 0:
            gu = mm(act[0], d_outer, TN)
            gi = mm(low1, d_inner, TN)
            half, quarter = ff // 2, width // 2
            for c in range(2):
                grads[c, 0:half] += gu[c * half : (c + 1) * half]
                for p in range(ff // width):
                    base = half + p * quarter
                    grads[c, base : base + quarter] += gi[
                        c * quarter : (c + 1) * quarter, p * width : (p + 1) * width
                    ]
    fold[0] += fold_rows(d_normed1 * xhat1)
    fold[1] += fold_rows(d_normed1)
    d_hidden1 = norm_back(d_normed1 * gain1, xhat1, dev1)
    d_att = d_hidden1.astype(BF)
    gs[...] = g_in * (1.0 - gate) + d_hidden1
    go = mm(mix_a[...], d_att)
    for c in range(2):
        grads[c, ff : ff + local // 2] += go[c * local // 2 : (c + 1) * local // 2]
    for mix, r, wo, do, dl in (
        (mix_a, r_a, wo_a, do_a, dl_a),
        (mix_b, r_b, wo_b, do_b, dl_b),
    ):
        d_mixed = mm(wo[...], d_att, NT).astype(BF).astype(F32)
        for h in range(heads):
            mine = slice(h * HEAD, (h + 1) * HEAD)
            part = d_mixed[mine]
            scale = r[h]
            do[mine] = part * scale
            total = jnp.sum(part * mix[mine].astype(F32), axis=0, keepdims=True)
            dl[h] = total * scale

    @pl.when(t == last)
    def _():
        base = ff + local // 2
        for n in range(5):
            grads[0, base + n : base + n + 1] = jnp.sum(fold[n], axis=0, keepdims=True)


def middle(state, timing, cot, run, mix_a, mix_b, r_a, r_b, wo_a, wo_b, wi_a, wi_b, wu_a,
           wu_b, vectors):
    rows, width = state.shape
    local, ff = wo_a.shape[0], wi_a.shape[1]
    heads = local // HEAD
    tile = 512
    per = LEN // tile
    grad_rows = ff + local // 2 + 64
    by_rows = pl.BlockSpec((tile, width), lambda t: (t, 0))
    by_columns = pl.BlockSpec((local, tile), lambda t: (0, t))
    per_head = pl.BlockSpec((heads, 1, tile), lambda t: (t // per, 0, t % per))
    return pl.pallas_call(
        functools.partial(middle_kernel, heads=heads),
        grid=(rows // tile,),
        in_specs=[
            by_rows,
            pl.BlockSpec((tile, width), lambda t: (t % per, 0)),
            by_rows,
            pl.BlockSpec((tile, 1), lambda t: (t, 0)),
            by_columns,
            by_columns,
            per_head,
            per_head,
            whole((local, width)),
            whole((local, width)),
            whole((width, ff)),
            whole((width, ff)),
            whole((ff, width)),
            whole((ff, width)),
            whole((8, width)),
        ],
        out_specs=[
            by_rows,
            by_rows,
            by_columns,
            by_columns,
            per_head,
            per_head,
            whole((2, grad_rows, width)),
        ],
        out_shape=[
            jax.ShapeDtypeStruct((rows, width), F32),
            jax.ShapeDtypeStruct((rows, width), F32),
            jax.ShapeDtypeStruct((local, rows), F32),
            jax.ShapeDtypeStruct((local, rows), F32),
            jax.ShapeDtypeStruct((rows // LEN * heads, 1, LEN), F32),
            jax.ShapeDtypeStruct((rows // LEN * heads, 1, LEN), F32),
            jax.ShapeDtypeStruct((2, grad_rows, width), F32),
        ],
        scratch_shapes=[
            pltpu.VMEM((2, tile, ff), BF),
            pltpu.VMEM((2, tile, ff), F32),
            pltpu.VMEM((8, 8, width), F32),
        ],
        compiler_params=params(),
        cost_estimate=pl.CostEstimate(
            flops=2 * rows * width * ff * 10 + 2 * rows * width * local * 6,
            bytes_accessed=rows * width * 20,
            transcendentals=2 * rows * ff,
        ),
        name="middle",
    )(state, timing, cot, run, mix_a, mix_b, r_a, r_b, wo_a, wo_b, wi_a, wi_b, wu_a, wu_b,
      vectors)


def attention_backward_kernel(
    e_in, do_in, dl_in, state, timing, wq, wk, wv, gs_in, gs_out, *rest, heads, own
):
    if own:
        gqkv, x_s, qt, kt, vaug, dq, dk, dv, aq, akv = rest
    else:
        x_s, qt, kt, vaug, dq, dk, dv = rest
    i = pl.program_id(0)
    h = lax.rem(i, heads)
    factor = 1.0 / math.sqrt(HEAD)
    pieces = LEN // CHUNK
    local = wq.shape[1]

    @pl.when(h == 0)
    def _():
        x = (state[...].astype(F32) + timing[...]).astype(BF)
        x_s[...] = x
        query = mm(wq[...], x, TT).astype(BF)
        key = mm(wk[...], x, TT).astype(BF)
        value = mm(x, wv[...]).astype(BF)
        lane = lane_index((LEN, 2 * HEAD))
        ones = jnp.where((lane % HEAD) < 3, 1.0, 0.0).astype(BF)
        for n in range(heads):
            mine = slice(n * HEAD, (n + 1) * HEAD)
            qt[n] = query[mine]
            kt[n] = key[mine]
            pair = value[:, (n // 2) * 128 : (n // 2) * 128 + 128]
            turned = rolled(pair)
            if n % 2 == 0:
                vaug[n, :, 0:128] = jnp.where(lane < HEAD, pair, turned)
            else:
                vaug[n, :, 0:128] = jnp.where(lane < HEAD, turned, pair)
            vaug[n, :, 128:256] = ones

    high, low = split_low(do_in[...])
    delta = -dl_in[0]
    d1 = delta.astype(BF)
    left = delta - d1.astype(F32)
    d2 = left.astype(BF)
    d3 = (left - d2.astype(F32)).astype(BF)
    index = row_index((2 * HEAD, LEN))
    tail = jnp.where(
        index == 0,
        d1.astype(F32),
        jnp.where(index == 1, d2.astype(F32), jnp.where(index == 2, d3.astype(F32), 0.0)),
    ).astype(BF)
    right = jnp.concatenate([high, low, tail], axis=0)
    query = qt[h]
    out = None
    for c in range(pieces):
        rows = slice(c * CHUNK, (c + 1) * CHUNK)
        d_probs = mm(vaug[h, rows], right)
        e = e_in[0, rows]
        d_scores = (e.astype(F32) * d_probs).astype(BF)
        dv[h, rows] = mm(e, high, NT).astype(BF)
        dk[h, rows] = (mm(d_scores, query, NT) * factor).astype(BF)
        o = mm(kt[h, :, rows], d_scores)
        out = o if out is None else out + o
    dq[pl.ds(pl.multiple_of(h * HEAD, HEAD), HEAD)] = (out * factor).astype(BF)

    @pl.when(h == heads - 1)
    def _():
        x = x_s[...]
        d_query = dq[...]
        d_key = jnp.concatenate([dk[n] for n in range(heads)], axis=1)
        d_value = jnp.concatenate([dv[n] for n in range(heads)], axis=1)
        total = mm(d_query, wq[...], TT)
        total = total + mm(d_key, wk[...], NT)
        total = total + mm(d_value, wv[...], NT)
        gs_out[...] = gs_in[...] + total
        if own:
            g1 = mm(d_query, x)
            g2 = mm(x, jnp.concatenate([d_key, d_value], axis=1), TN)

            @pl.when(i < heads)
            def _():
                aq[...] = g1
                akv[...] = g2

            @pl.when(i >= heads)
            def _():
                aq[...] += g1
                akv[...] += g2

            @pl.when(i == pl.num_programs(0) - 1)
            def _():
                gqkv[:, :local] = aq[...].T
                gqkv[:, local:] = akv[...]


def attention_backward(part, e, do, dl, state, timing, wq, wk, wv, gs, own):
    rows, width = state.shape
    seqs = rows // LEN
    heads, local = 2, 128
    every = wq.shape[1] // HEAD
    count = seqs * heads

    def at(i):
        return (i // heads) * every + part * heads + i % heads

    by_rows = pl.BlockSpec((LEN, width), lambda i: (i // heads, 0))
    columns = pl.BlockSpec((width, local), lambda i: (0, part))
    out_specs = [by_rows]
    out_shape = [jax.ShapeDtypeStruct((rows, width), F32)]
    scratch = [
        pltpu.VMEM((LEN, width), BF),
        pltpu.VMEM((heads, HEAD, LEN), BF),
        pltpu.VMEM((heads, HEAD, LEN), BF),
        pltpu.VMEM((heads, LEN, 256), BF),
        pltpu.VMEM((local, LEN), BF),
        pltpu.VMEM((heads, LEN, HEAD), BF),
        pltpu.VMEM((heads, LEN, HEAD), BF),
    ]
    if own:
        out_specs += [whole((width, 3 * local))]
        out_shape += [jax.ShapeDtypeStruct((width, 3 * local), F32)]
        scratch += [pltpu.VMEM((local, width), F32), pltpu.VMEM((width, 2 * local), F32)]
    return pl.pallas_call(
        functools.partial(attention_backward_kernel, heads=heads, own=own),
        grid=(count,),
        in_specs=[
            pl.BlockSpec((1, LEN, LEN), lambda i: (at(i), 0, 0)),
            pl.BlockSpec((HEAD, LEN), lambda i: (part * heads + i % heads, i // heads)),
            pl.BlockSpec((1, 1, LEN), lambda i: (at(i), 0, 0)),
            by_rows,
            whole((LEN, width)),
            columns,
            columns,
            columns,
            by_rows,
        ],
        out_specs=out_specs,
        out_shape=out_shape,
        scratch_shapes=scratch,
        compiler_params=params(),
        input_output_aliases={8: 0},
        cost_estimate=pl.CostEstimate(
            flops=16 * 2 * count * LEN * LEN * HEAD,
            bytes_accessed=2 * count * LEN * LEN,
            transcendentals=0,
        ),
        name="attention_backward_own" if own else "attention_backward_other",
    )(e, do, dl, state, timing, wq, wk, wv, gs)


def rows_at(index, size):
    return pl.ds(pl.multiple_of(index * size, size), size)


def local_kernel(fn, count, place, *refs):
    fn(place, refs[:count], refs[count:])


def local_call(name, fn, place, ins, outs):
    return pl.pallas_call(
        functools.partial(local_kernel, fn, len(ins)),
        in_specs=[pl.BlockSpec(memory_space=pltpu.SMEM)]
        + [pl.BlockSpec(memory_space=pltpu.VMEM)] * len(ins),
        out_specs=[pl.BlockSpec(memory_space=pltpu.VMEM)] * len(outs),
        out_shape=[jax.ShapeDtypeStruct(shape, kind) for shape, kind in outs],
        compiler_params=params(),
        name=name,
    )(place, *ins)


def flipped(size, bit):
    return [(i, i ^ bit) for i in range(size)]


CORE, Y, Z = 4, 5, 6


def pack(place, ins, outs):
    wq, wk, wv, wo, wi, wu = ins
    out_a, out_b, out_c = outs
    p = place[0]
    width, local = wq.shape
    quarter = width // 4

    def cut(ref, size):
        return ref[rows_at(p, size)].astype(F32)

    for n, ref in enumerate((wq, wk, wv)):
        out_a[:, n * local : (n + 1) * local] = cut(ref, quarter)
    inner = cut(wi, quarter)
    blocks = wi.shape[1] // width
    for n in range(blocks):
        out_b[n * quarter : (n + 1) * quarter] = inner[:, n * width : (n + 1) * width]
    out_b[blocks * quarter :] = cut(wo, wo.shape[0] // 4)
    out_c[...] = cut(wu, wu.shape[0] // 4)


def unpack_qkv(place, ins, outs):
    local = outs[0].shape[1]
    for p, ref in zip((0, 2, 1, 3), ins):
        rows = rows_at(place[p], ref.shape[0])
        for n, out in enumerate(outs):
            out[rows] = ref[:, n * local : (n + 1) * local].astype(BF)


def unpack_inner(place, ins, outs):
    wo, wi = outs
    width = wi.shape[0]
    quarter, blocks = width // 4, wi.shape[1] // width
    for p, ref in zip((0, 2, 1, 3), ins):
        rows = rows_at(place[p], quarter)
        for n in range(blocks):
            wi[rows, n * width : (n + 1) * width] = ref[
                n * quarter : (n + 1) * quarter
            ].astype(BF)
        wo[rows_at(place[p], wo.shape[0] // 4)] = ref[blocks * quarter :].astype(BF)


def unpack_outer(place, ins, outs):
    for p, ref in zip((0, 2, 1, 3), ins):
        outs[0][rows_at(place[p], ref.shape[0])] = ref[...].astype(BF)


def pair_cut(place, bit, value, keep, send):
    half = value.shape[0] // 2
    keep[...] = value[rows_at(place[bit], half)]
    send[...] = value[rows_at(1 - place[bit], half)]


def quad_cut(place, value, outs):
    size = value.shape[0] // 4
    for d, out in enumerate(outs):
        out[...] = value[rows_at(jnp.bitwise_xor(place[Z], d), size)]


def pair_join(place, bit, mine, theirs, out):
    half = mine.shape[0]
    out[rows_at(place[bit], half)] = mine[...]
    out[rows_at(1 - place[bit], half)] = theirs[...]


def quad_join(place, parts, out):
    size = parts[0].shape[0]
    for d, part in enumerate(parts):
        out[rows_at(jnp.bitwise_xor(place[Z], d), size)] = part[...]


def total(refs):
    out = refs[0][...]
    for ref in refs[1:]:
        out = out + ref[...]
    return out


def f32s(*shapes):
    return [(shape, F32) for shape in shapes]


def shards(
    dp, state, lengths, halt_mask, wq, wk, wv, wo, gain1, bias1, wi, wu, gain2, bias2,
    halt_weight, cotangent
):
    rows, width = state.shape
    local, ff = wq.shape[1], wi.shape[1]
    timing = jnp.asarray(timing_rows(width))
    me = lax.axis_index("dp").astype(jnp.int32)
    shift = np.array([0, 0, 0, 0, 0, 1, 2], np.int32)
    mask = np.array([3, 3, 3, 3, 1, 1, 3], np.int32)
    flip = np.array([0, 1, 2, 3, 0, 0, 0], np.int32)
    place = jnp.bitwise_xor(jnp.bitwise_and(jnp.right_shift(me, shift), mask), flip)
    bits = dp.bit_length() - 1

    def across(v):
        return lax.ppermute(v, "mp", [(0, 1), (1, 0)])

    def core(v):
        return lax.ppermute(v, "dp", flipped(dp, 1))

    def along_y(v):
        return lax.ppermute(v, "dp", flipped(dp, 2))

    def along_z(values):
        return [lax.ppermute(v, "dp", flipped(dp, 4 * d)) for d, v in zip((1, 2, 3), values)]

    def beyond(v):
        for bit in range(4, bits):
            v = v + lax.ppermute(v, "dp", flipped(dp, 1 << bit))
        return v

    tie = lax.optimization_barrier
    call = functools.partial(local_call, place=place)

    quarter = width // 4
    chunk_a, chunk_b, chunk_c = call(
        "pack", pack, ins=(wq, wk, wv, wo, wi, wu),
        outs=f32s((quarter, 3 * local), (ff // 4 + local // 4, width), (ff // 4, width)),
    )
    qkv0 = across(chunk_a)
    fwd = attention_forward(0, lengths, state, timing, wq, wk, wv)
    qkv0, chunk_b, fwd = tie((qkv0, chunk_b, fwd))
    qkv1 = along_y(qkv0)
    in0 = across(chunk_b)
    fwd = attention_forward(1, lengths, state, timing, wq, wk, wv, fwd)
    qkv1, fwd = tie((qkv1, fwd))
    qkv2, qkv3 = core(qkv0), core(qkv1)
    wq2, wk2, wv2 = call(
        "unpack_qkv", unpack_qkv, ins=(qkv0, qkv1, qkv2, qkv3),
        outs=[((width, local), BF)] * 3,
    )
    in0, chunk_c, wq2, wk2, wv2 = tie((in0, chunk_c, wq2, wk2, wv2))
    in1 = along_y(in0)
    out0 = across(chunk_c)
    fwd2 = attention_forward(0, lengths, state, timing, wq2, wk2, wv2)
    fwd2 = attention_forward(1, lengths, state, timing, wq2, wk2, wv2, fwd2)
    in1, out0, fwd2 = tie((in1, out0, fwd2))
    in2, in3 = core(in0), core(in1)
    out1 = along_y(out0)
    wo2, wi2 = call(
        "unpack_inner", unpack_inner, ins=(in0, in1, in2, in3),
        outs=[((local, width), BF), ((width, ff), BF)],
    )
    out2, out3 = core(out0), core(out1)
    (wu2,) = call(
        "unpack_outer", unpack_outer, ins=(out0, out1, out2, out3), outs=[((ff, width), BF)]
    )
    e_a, mix_a, r_a = fwd
    e_b, mix_b, r_b = fwd2
    vectors = jnp.stack([gain1, bias1, gain2, bias2, halt_weight] + [gain1] * 3)
    new_state, gs, do_a, do_b, dl_a, dl_b, grads = middle(
        state, timing, cotangent, halt_mask[:, None], mix_a, mix_b, r_a, r_b, wo, wo2, wi,
        wi2, wu, wu2, vectors
    )

    long = grads.shape[1]
    na, nb = 768, long - 768
    send = lax.dynamic_index_in_dim(grads, 1 - place[CORE], 0, False)
    got = core(send)

    def first(place, ins, outs):
        full, got = ins
        value = full[place[CORE]] + got[...]
        pair_cut_value(place, Y, value, outs[0], outs[1], outs[6])
        quad_cut_value(place, value[na:], outs[2:6], outs[7])

    def pair_cut_value(place, bit, value, keep, send, hold):
        hold[...] = value[:na]
        pair_cut(place, bit, hold, keep, send)

    def quad_cut_value(place, value, outs, hold):
        hold[...] = value
        quad_cut(place, hold, outs)

    a_keep, a_send, *b_parts = call(
        "sum_core", first, ins=(grads, got),
        outs=f32s(*[(na // 2, width)] * 2, *[(nb // 4, width)] * 4, (na, width), (nb, width)),
    )[:6]
    a_got = along_y(a_send)
    b_got = along_z(b_parts[1:])
    back = functools.partial(attention_backward, state=state, timing=timing)
    own = dict(e=e_a, do=do_a, dl=dl_a, wq=wq, wk=wk, wv=wv, own=True)
    other = dict(e=e_b, do=do_b, dl=dl_b, wq=wq2, wk=wk2, wv=wv2, own=False)
    gs, g0 = back(0, gs=gs, **own)
    a_got, b_got, gs, g0 = tie((a_got, b_got, gs, g0))

    def second(place, ins, outs):
        a = ins[:2]
        b = ins[2:]
        outs[6][...] = total(a)
        quad_cut(place, outs[6], outs[:4])
        outs[7][...] = total(b)
        pair_cut(place, Y, outs[7], outs[4], outs[5])

    *a_parts, b_keep, b_send = call(
        "sum_first", second, ins=(a_keep, a_got, b_parts[0], *b_got),
        outs=f32s(*[(na // 8, width)] * 4, *[(nb // 8, width)] * 2, (na // 2, width),
                  (nb // 4, width)),
    )[:6]
    a_got = along_z(a_parts[1:])
    b_got = along_y(b_send)
    gs, g1 = back(1, gs=gs, **own)
    a_got, b_got, gs, g1 = tie((a_got, b_got, gs, g1))

    def third(place, ins, outs):
        outs[0][...] = total(ins[:4])
        outs[1][...] = total(ins[4:6])
        half = width // 2
        for n, ref in enumerate(ins[6:]):
            size = ref.shape[1]
            columns = slice(n * size, (n + 1) * size)
            outs[2][:, columns] = ref[rows_at(place[CORE], half)]
            outs[3][:, columns] = ref[rows_at(1 - place[CORE], half)]

    a_sum, b_sum, q_keep, q_send = call(
        "sum_second", third, ins=(a_parts[0], *a_got, b_keep, b_got, g0, g1),
        outs=f32s((na // 8, width), (nb // 8, width), *[(width // 2, 3 * local)] * 2),
    )
    a_sum, b_sum = beyond(a_sum), beyond(b_sum)
    q_got = core(q_send)
    a_got = along_z([a_sum] * 3)
    b_got = along_y(b_sum)

    def q_first(place, ins, outs):
        outs[2][...] = total(ins)
        pair_cut(place, Y, outs[2], outs[0], outs[1])

    q_keep, q_send = call(
        "sum_core_qkv", q_first, ins=(q_keep, q_got),
        outs=f32s(*[(width // 4, 3 * local)] * 2, (width // 2, 3 * local)),
    )[:2]
    q_got = along_y(q_send)
    (gs,) = back(0, gs=gs, **other)
    a_got, b_got, q_got, gs = tie((a_got, b_got, q_got, gs))

    def fourth(place, ins, outs):
        quad_join(place, ins[:4], outs[0])
        pair_join(place, Y, ins[4], ins[5], outs[1])
        outs[6][...] = total(ins[6:])
        quad_cut(place, outs[6], outs[2:6])

    a_half, b_half, *q_parts = call(
        "join_first", fourth, ins=(a_sum, *a_got, b_sum, b_got, q_keep, q_got),
        outs=f32s((na // 2, width), (nb // 4, width), *[(width // 16, 3 * local)] * 4,
                  (width // 4, 3 * local)),
    )[:6]
    a_got = along_y(a_half)
    b_got = along_z([b_half] * 3)
    q_got = along_z(q_parts[1:])
    (gs,) = back(1, gs=gs, **other)
    a_got, b_got, q_got, gs = tie((a_got, b_got, q_got, gs))

    def fifth(place, ins, outs):
        pair_join(place, Y, ins[0], ins[1], outs[0])
        quad_join(place, ins[2:6], outs[1])
        outs[2][...] = total(ins[6:])

    a_full, b_full, q_sum = call(
        "join_second", fifth, ins=(a_half, a_got, b_half, *b_got, q_parts[0], *q_got),
        outs=f32s((na, width), (nb, width), (width // 16, 3 * local)),
    )
    q_sum = beyond(q_sum)
    q_got = along_z([q_sum] * 3)
    a_got, b_got = core(a_full), core(b_full)

    def finish_ff(place, ins, outs):
        gu, gi, go, vec = outs
        half, small, few = ff // 2, width // 2, local // 2
        for flip, (a, b) in ((0, ins[:2]), (1, ins[2:])):
            c = jnp.bitwise_xor(place[CORE], flip)
            gu[rows_at(c, half)] = a[:half]
            gi[rows_at(c, small), :width] = a[half:]
            gi[rows_at(c, small), width:] = b[:small]
            go[rows_at(c, few)] = b[small : small + few]

            @pl.when(c == 0)
            def _():
                vec[...] = b[small + few : small + few + 8]

    gu, gi, go, vec = call(
        "finish_ff", finish_ff, ins=(a_full, b_full, a_got, b_got),
        outs=f32s((ff, width), (width, ff), (local, width), (8, width)),
    )

    def q_join(place, ins, outs):
        quad_join(place, ins, outs[0])

    (q_half,) = call(
        "join_z_qkv", q_join, ins=(q_sum, *q_got), outs=f32s((width // 4, 3 * local))
    )
    q_got = along_y(q_half)

    def q_join2(place, ins, outs):
        pair_join(place, Y, ins[0], ins[1], outs[0])

    (q_full,) = call(
        "join_y_qkv", q_join2, ins=(q_half, q_got), outs=f32s((width // 2, 3 * local))
    )
    q_got = core(q_full)

    def finish_qkv(place, ins, outs):
        for flip, ref in enumerate(ins):
            rows = rows_at(jnp.bitwise_xor(place[CORE], flip), width // 2)
            for part in range(local // 128):
                for n, out in enumerate(outs):
                    at = part * 384 + n * 128
                    out[rows, part * 128 : (part + 1) * 128] = ref[:, at : at + 128]

    gq, gk, gv = call(
        "finish_qkv", finish_qkv, ins=(q_full, q_got), outs=f32s(*[(width, local)] * 3)
    )
    return (
        new_state, gs, gq, gk, gv, go, vec[0], vec[1], gi, gu, vec[2], vec[3], vec[4]
    )


def solution(mesh):
    rows, columns, parts = P("dp", None), P(None, "mp"), P("mp", None)
    return jax.shard_map(
        functools.partial(shards, mesh.shape["dp"]),
        mesh=mesh,
        in_specs=(
            rows, P("dp"), P("dp"), columns, columns, columns, parts, P(), P(), columns,
            parts, P(), P(), P(), rows
        ),
        out_specs=(
            rows, rows, columns, columns, columns, parts, P(), P(), columns, parts, P(), P(),
            P()
        ),
        check_vma=False,
    )
```

```python
import functools
import math

import jax
import jax.numpy as jnp
import numpy as np
from jax import lax
from jax.experimental import pallas as pl
from jax.experimental.pallas import tpu as pltpu
from jax.sharding import PartitionSpec as P

HEAD = 64
LEN = 1024
STEP = 2
LOG2E = 1.4426950408889634
BF = jnp.bfloat16
F32 = jnp.float32
NN = (((1,), (0,)), ((), ()))
NT = (((1,), (1,)), ((), ()))
TN = (((0,), (0,)), ((), ()))
TT = (((0,), (1,)), ((), ()))
VMEM_LIMIT = 60 << 20
CHUNK = 256


def mm(a, b, dims=NN):
    return lax.dot_general(a, b, dims, preferred_element_type=F32)


def params():
    return pltpu.CompilerParams(vmem_limit_bytes=VMEM_LIMIT)


def whole(shape):
    zeros = (0,) * len(shape)
    return pl.BlockSpec(shape, lambda *_: zeros)


def timing_rows(width):
    half = width // 2
    rates = np.exp(-math.log(10000.0) * np.arange(half, dtype=np.float64) / (half - 1))

    def rows(positions):
        angles = positions[:, None] * rates[None, :]
        return np.concatenate([np.sin(angles), np.cos(angles)], axis=1)

    return (rows(np.arange(LEN, dtype=np.float64)) + rows(np.array([float(STEP)]))).astype(
        np.float32
    )


def split_low(value):
    high = value.astype(BF)
    return high, (value - high.astype(F32)).astype(BF)


def rolled(pair):
    return jnp.concatenate([pair[:, HEAD:], pair[:, :HEAD]], axis=1)


def lane_index(shape):
    return lax.broadcasted_iota(jnp.int32, shape, 1)


def row_index(shape):
    return lax.broadcasted_iota(jnp.int32, shape, 0)


def attention_forward_kernel(seq, lengths, x_in, wq, wk, wv, *rest, heads):
    e_out, mixed_out, r_out, kaug, qaug, vaug, sa, sb, ma, mb = rest[-10:]
    j = pl.program_id(0)
    last = heads // 2 - 1
    pieces = LEN // CHUNK

    def score_piece(i, c, target):
        rows = slice(c * CHUNK, (c + 1) * CHUNK)
        s = mm(kaug[i, rows], qaug[i])
        target[rows] = s
        return jnp.max(s.reshape(CHUNK // 8, 8, LEN), axis=0)

    @pl.when(j == 0)
    def _():
        x = x_in[...]
        query = mm(wq[...], x, TT).astype(BF).astype(F32) * (LOG2E / math.sqrt(HEAD))
        high, rest = split_low(query)
        key = mm(x, wk[...]).astype(BF)
        value = mm(wv[...], x, TT).astype(BF)
        shape = (LEN, 2 * HEAD)
        lane = lane_index(shape)
        padded = row_index(shape) >= lengths[seq]
        mask = jnp.where(padded & ((lane == 0) | (lane == HEAD)), -1e30, 0.0).astype(BF)
        first = row_index((HEAD, LEN)) == 0
        ones = jnp.where(first, 1.0, 0.0).astype(BF)
        zeros = jnp.zeros((HEAD, LEN), BF)
        for i in range(heads):
            pair = key[:, (i // 2) * 128 : (i // 2) * 128 + 128]
            turned = rolled(pair)
            mine = slice(i * HEAD, (i + 1) * HEAD)
            kaug[i, :, 0:128] = pair
            if i % 2 == 0:
                kaug[i, :, 128:256] = jnp.where(lane < HEAD, mask, turned)
                parts = (high[mine], zeros, ones, rest[mine])
            else:
                kaug[i, :, 128:256] = jnp.where(lane < HEAD, turned, mask)
                parts = (zeros, high[mine], rest[mine], ones)
            for n, part in enumerate(parts):
                qaug[i, n * HEAD : (n + 1) * HEAD] = part
            vaug[i, 0:HEAD] = value[mine]
            vaug[i, HEAD : HEAD + 16] = jnp.ones((16, LEN), BF)
        top = None
        for c in range(pieces):
            m = score_piece(0, c, sa)
            top = m if top is None else jnp.maximum(top, m)
        ma[...] = jnp.max(top, axis=0, keepdims=True)

    def step(slot, cur, cur_m, nxt, nxt_m, ahead=True):
        i = 2 * j + slot
        shift = cur_m[...]
        top = None
        out = None
        for c in range(pieces):
            rows = slice(c * CHUNK, (c + 1) * CHUNK)
            if ahead:
                m = score_piece(i + 1, c, nxt)
                top = m if top is None else jnp.maximum(top, m)
            e = jnp.exp2(cur[rows] - shift).astype(BF)
            e_out[slot, rows] = e
            o = mm(vaug[i, :, rows], e)
            out = o if out is None else out + o
        if ahead:
            nxt_m[...] = jnp.max(top, axis=0, keepdims=True)
        r = 1.0 / out[HEAD : HEAD + 1]
        mixed_out[slot * HEAD : (slot + 1) * HEAD] = (out[:HEAD] * r).astype(BF)
        r_out[slot] = r

    step(0, sa, ma, sb, mb)

    @pl.when(j < last)
    def _():
        step(1, sb, mb, sa, ma)

    @pl.when(j == last)
    def _():
        step(1, sb, mb, sa, ma, ahead=False)


def attention_forward(seq, lengths, x, wq, wk, wv, earlier=()):
    rows, width = x.shape
    local = wq.shape[1]
    heads = local // HEAD
    steps, total = heads // 2, rows // LEN * heads
    return pl.pallas_call(
        functools.partial(attention_forward_kernel, seq, heads=heads),
        grid=(steps,),
        in_specs=[
            pl.BlockSpec(memory_space=pltpu.SMEM),
            pl.BlockSpec((LEN, width), lambda j: (seq, 0)),
            whole((width, local)),
            whole((width, local)),
            whole((width, local)),
        ]
        + [pl.BlockSpec(memory_space=pl.ANY)] * len(earlier),
        out_specs=[
            pl.BlockSpec((2, LEN, LEN), lambda j: (seq * steps + j, 0, 0)),
            pl.BlockSpec((2 * HEAD, LEN), lambda j: (j, seq)),
            pl.BlockSpec((2, 1, LEN), lambda j: (seq * steps + j, 0, 0)),
        ],
        out_shape=[
            jax.ShapeDtypeStruct((total, LEN, LEN), BF),
            jax.ShapeDtypeStruct((local, rows), BF),
            jax.ShapeDtypeStruct((total, 1, LEN), F32),
        ],
        scratch_shapes=[
            pltpu.VMEM((heads, LEN, 256), BF),
            pltpu.VMEM((heads, 256, LEN), BF),
            pltpu.VMEM((heads, HEAD + 16, LEN), BF),
            pltpu.VMEM((LEN, LEN), F32),
            pltpu.VMEM((LEN, LEN), F32),
            pltpu.VMEM((1, LEN), F32),
            pltpu.VMEM((1, LEN), F32),
        ],
        compiler_params=params(),
        input_output_aliases={5 + n: n for n in range(len(earlier))},
        cost_estimate=pl.CostEstimate(
            flops=8 * 2 * heads * LEN * LEN * HEAD,
            bytes_accessed=2 * heads * LEN * LEN,
            transcendentals=heads * LEN * LEN,
        ),
        name="attention_forward",
    )(lengths, x, wq, wk, wv, *earlier)


def row_mean(v):
    return jnp.mean(v, axis=-1, keepdims=True)


def norm_rows(v):
    centre = v - row_mean(v)
    deviation = lax.rsqrt(row_mean(centre * centre) + 1e-05)
    return centre * deviation, deviation


def norm_back(e, xhat, deviation):
    return deviation * (e - row_mean(e) - xhat * row_mean(e * xhat))


def fold_rows(v):
    return jnp.sum(v.reshape(v.shape[0] // 8, 8, v.shape[1]), axis=0)


def middle_kernel(
    state, timing, cot, run, mix_a, mix_b, r_a, r_b, wo_a, wo_b, wi_a, wi_b, wu_a, wu_b,
    vectors, new_state, gs, do_a, do_b, dl_a, dl_b, grads, act, slope, fold, *, heads
):
    t = pl.program_id(0)
    last = pl.num_programs(0) - 1
    ff = wi_a.shape[1]
    local = wo_a.shape[0]
    width = state.shape[1]
    gain1, bias1, gain2, bias2, halt_w = (vectors[n : n + 1] for n in range(5))

    @pl.when(t == 0)
    def _():
        grads[...] = jnp.zeros(grads.shape, F32)
        fold[...] = jnp.zeros(fold.shape, F32)

    old = state[...].astype(F32)
    embedded = old + timing[...]
    attended = mm(mix_a[...], wo_a[...], TN) + mm(mix_b[...], wo_b[...], TN)
    xhat1, dev1 = norm_rows(embedded + attended)
    normed1 = xhat1 * gain1 + bias1
    low1 = normed1.astype(BF)
    c0 = math.sqrt(2.0 / math.pi)
    outer = None
    for n, (wi, wu) in enumerate(((wi_a, wu_a), (wi_b, wu_b))):
        v = mm(low1, wi[...])
        square = v * v
        h = 0.5 + 0.5 * jnp.tanh(v * (c0 + (c0 * 0.044715) * square))
        g = v * h
        act[n] = g.astype(BF)
        slope[n] = (
            h + g * (1.0 - h) * (2.0 * c0 + (6.0 * c0 * 0.044715) * square)
        ).astype(slope.dtype)
        o = mm(act[n], wu[...])
        outer = o if outer is None else outer + o
    xhat2, dev2 = norm_rows(normed1 + outer)
    block = xhat2 * gain2 + bias2
    halt = jax.nn.sigmoid(jnp.sum(block * halt_w, axis=-1, keepdims=True))
    running = run[...].astype(F32)
    gate = running * halt
    new_state[...] = old + gate * (block - old)
    g_in = cot[...].astype(F32)
    d_prob = running * jnp.sum(g_in * (block - old), axis=-1, keepdims=True)
    d_logit = d_prob * halt * (1.0 - halt)
    d_block = gate * g_in + d_logit * halt_w
    fold[4] += fold_rows(d_logit * block)
    fold[2] += fold_rows(d_block * xhat2)
    fold[3] += fold_rows(d_block)
    d_hidden2 = norm_back(d_block * gain2, xhat2, dev2)
    d_outer = d_hidden2.astype(BF)
    d_normed1 = d_hidden2
    for n, (wi, wu) in enumerate(((wi_a, wu_a), (wi_b, wu_b))):
        d_act = mm(d_outer, wu[...], NT)
        d_inner = (d_act * slope[n].astype(F32)).astype(BF)
        d_normed1 = d_normed1 + mm(d_inner, wi[...], NT)
        if n == 0:
            gu = mm(act[0], d_outer, TN)
            gi = mm(low1, d_inner, TN)
            half, quarter = ff // 2, width // 2
            for c in range(2):
                grads[c, 0:half] += gu[c * half : (c + 1) * half]
                for p in range(ff // width):
                    base = half + p * quarter
                    grads[c, base : base + quarter] += gi[
                        c * quarter : (c + 1) * quarter, p * width : (p + 1) * width
                    ]
    fold[0] += fold_rows(d_normed1 * xhat1)
    fold[1] += fold_rows(d_normed1)
    d_hidden1 = norm_back(d_normed1 * gain1, xhat1, dev1)
    d_att = d_hidden1.astype(BF)
    gs[...] = g_in * (1.0 - gate) + d_hidden1
    go = mm(mix_a[...], d_att)
    for c in range(2):
        grads[c, ff : ff + local // 2] += go[c * local // 2 : (c + 1) * local // 2]
    for mix, r, wo, do, dl in (
        (mix_a, r_a, wo_a, do_a, dl_a),
        (mix_b, r_b, wo_b, do_b, dl_b),
    ):
        d_mixed = mm(wo[...], d_att, NT).astype(BF).astype(F32)
        for h in range(heads):
            mine = slice(h * HEAD, (h + 1) * HEAD)
            part = d_mixed[mine]
            scale = r[h]
            do[mine] = part * scale
            total = jnp.sum(part * mix[mine].astype(F32), axis=0, keepdims=True)
            dl[h] = total * scale

    @pl.when(t == last)
    def _():
        base = ff + local // 2
        for n in range(5):
            grads[0, base + n : base + n + 1] = jnp.sum(fold[n], axis=0, keepdims=True)


def middle(state, timing, cot, run, mix_a, mix_b, r_a, r_b, wo_a, wo_b, wi_a, wi_b, wu_a,
           wu_b, vectors):
    rows, width = state.shape
    local, ff = wo_a.shape[0], wi_a.shape[1]
    heads = local // HEAD
    tile = 512
    per = LEN // tile
    grad_rows = ff + local // 2 + 64
    by_rows = pl.BlockSpec((tile, width), lambda t: (t, 0))
    by_columns = pl.BlockSpec((local, tile), lambda t: (0, t))
    per_head = pl.BlockSpec((heads, 1, tile), lambda t: (t // per, 0, t % per))
    return pl.pallas_call(
        functools.partial(middle_kernel, heads=heads),
        grid=(rows // tile,),
        in_specs=[
            by_rows,
            pl.BlockSpec((tile, width), lambda t: (t % per, 0)),
            by_rows,
            pl.BlockSpec((tile, 1), lambda t: (t, 0)),
            by_columns,
            by_columns,
            per_head,
            per_head,
            whole((local, width)),
            whole((local, width)),
            whole((width, ff)),
            whole((width, ff)),
            whole((ff, width)),
            whole((ff, width)),
            whole((8, width)),
        ],
        out_specs=[
            by_rows,
            by_rows,
            by_columns,
            by_columns,
            per_head,
            per_head,
            whole((2, grad_rows, width)),
        ],
        out_shape=[
            jax.ShapeDtypeStruct((rows, width), F32),
            jax.ShapeDtypeStruct((rows, width), F32),
            jax.ShapeDtypeStruct((local, rows), F32),
            jax.ShapeDtypeStruct((local, rows), F32),
            jax.ShapeDtypeStruct((rows // LEN * heads, 1, LEN), F32),
            jax.ShapeDtypeStruct((rows // LEN * heads, 1, LEN), F32),
            jax.ShapeDtypeStruct((2, grad_rows, width), F32),
        ],
        scratch_shapes=[
            pltpu.VMEM((2, tile, ff), BF),
            pltpu.VMEM((2, tile, ff), F32),
            pltpu.VMEM((8, 8, width), F32),
        ],
        compiler_params=params(),
        cost_estimate=pl.CostEstimate(
            flops=2 * rows * width * ff * 10 + 2 * rows * width * local * 6,
            bytes_accessed=rows * width * 20,
            transcendentals=2 * rows * ff,
        ),
        name="middle",
    )(state, timing, cot, run, mix_a, mix_b, r_a, r_b, wo_a, wo_b, wi_a, wi_b, wu_a, wu_b,
      vectors)


def attention_backward_kernel(
    e_in, do_in, dl_in, x_in, wq, wk, wv, gs_in, *rest, heads, own, more
):
    if own:
        before, gs_out, gqkv, qt, kt, vaug, dq, dk, dv = rest if more else (None, *rest)
    else:
        gs_out, qt, kt, vaug, dq, dk, dv = rest
    h = pl.program_id(0)
    factor = 1.0 / math.sqrt(HEAD)
    pieces = LEN // CHUNK
    local = wq.shape[1]

    @pl.when(h == 0)
    def _():
        x = x_in[...]
        query = mm(wq[...], x, TT).astype(BF)
        key = mm(wk[...], x, TT).astype(BF)
        value = mm(x, wv[...]).astype(BF)
        lane = lane_index((LEN, 2 * HEAD))
        ones = jnp.where((lane % HEAD) < 3, 1.0, 0.0).astype(BF)
        for n in range(heads):
            mine = slice(n * HEAD, (n + 1) * HEAD)
            qt[n] = query[mine]
            kt[n] = key[mine]
            pair = value[:, (n // 2) * 128 : (n // 2) * 128 + 128]
            turned = rolled(pair)
            if n % 2 == 0:
                vaug[n, :, 0:128] = jnp.where(lane < HEAD, pair, turned)
            else:
                vaug[n, :, 0:128] = jnp.where(lane < HEAD, turned, pair)
            vaug[n, :, 128:256] = ones

    high, low = split_low(do_in[...])
    delta = -dl_in[0]
    d1 = delta.astype(BF)
    left = delta - d1.astype(F32)
    d2 = left.astype(BF)
    d3 = (left - d2.astype(F32)).astype(BF)
    index = row_index((2 * HEAD, LEN))
    tail = jnp.where(
        index == 0,
        d1.astype(F32),
        jnp.where(index == 1, d2.astype(F32), jnp.where(index == 2, d3.astype(F32), 0.0)),
    ).astype(BF)
    right = jnp.concatenate([high, low, tail], axis=0)
    query = qt[h]
    out = None
    for c in range(pieces):
        rows = slice(c * CHUNK, (c + 1) * CHUNK)
        d_probs = mm(vaug[h, rows], right)
        e = e_in[0, rows]
        d_scores = (e.astype(F32) * d_probs).astype(BF)
        dv[h, rows] = mm(e, high, NT).astype(BF)
        dk[h, rows] = (mm(d_scores, query, NT) * factor).astype(BF)
        o = mm(kt[h, :, rows], d_scores)
        out = o if out is None else out + o
    dq[pl.ds(pl.multiple_of(h * HEAD, HEAD), HEAD)] = (out * factor).astype(BF)

    @pl.when(h == heads - 1)
    def _():
        d_query = dq[...]
        d_key = jnp.concatenate([dk[n] for n in range(heads)], axis=1)
        d_value = jnp.concatenate([dv[n] for n in range(heads)], axis=1)
        total = mm(d_query, wq[...], TT)
        total = total + mm(d_key, wk[...], NT)
        total = total + mm(d_value, wv[...], NT)
        gs_out[...] = gs_in[...] + total
        if own:
            x = x_in[...]
            g1 = mm(d_query, x).T
            g2 = mm(x, jnp.concatenate([d_key, d_value], axis=1), TN)
            if more:
                g1 = g1 + before[:, :local]
                g2 = g2 + before[:, local:]
            gqkv[:, :local] = g1
            gqkv[:, local:] = g2


def attention_backward(seq, e, do, dl, x, wq, wk, wv, gs, own, before=None):
    rows, width = x.shape
    local = wq.shape[1]
    heads = local // HEAD
    more = before is not None
    by_rows = pl.BlockSpec((LEN, width), lambda h: (seq, 0))
    out_specs = [by_rows]
    out_shape = [jax.ShapeDtypeStruct((rows, width), F32)]
    in_specs = [
        pl.BlockSpec((1, LEN, LEN), lambda h: (seq * heads + h, 0, 0)),
        pl.BlockSpec((HEAD, LEN), lambda h: (h, seq)),
        pl.BlockSpec((1, 1, LEN), lambda h: (seq * heads + h, 0, 0)),
        by_rows,
        whole((width, local)),
        whole((width, local)),
        whole((width, local)),
        by_rows,
    ]
    args = [e, do, dl, x, wq, wk, wv, gs]
    aliases = {7: 0}
    if own:
        out_specs.append(whole((width, 3 * local)))
        out_shape.append(jax.ShapeDtypeStruct((width, 3 * local), F32))
        if more:
            in_specs.append(whole((width, 3 * local)))
            args.append(before)
            aliases[8] = 1
    return pl.pallas_call(
        functools.partial(attention_backward_kernel, heads=heads, own=own, more=more),
        grid=(heads,),
        in_specs=in_specs,
        out_specs=out_specs,
        out_shape=out_shape,
        scratch_shapes=[
            pltpu.VMEM((heads, HEAD, LEN), BF),
            pltpu.VMEM((heads, HEAD, LEN), BF),
            pltpu.VMEM((heads, LEN, 256), BF),
            pltpu.VMEM((local, LEN), BF),
            pltpu.VMEM((heads, LEN, HEAD), BF),
            pltpu.VMEM((heads, LEN, HEAD), BF),
        ],
        compiler_params=params(),
        input_output_aliases=aliases,
        cost_estimate=pl.CostEstimate(
            flops=16 * 2 * heads * LEN * LEN * HEAD,
            bytes_accessed=2 * heads * LEN * LEN,
            transcendentals=0,
        ),
        name="attention_backward_own" if own else "attention_backward_other",
    )(*args)


def rows_at(index, size):
    return pl.ds(pl.multiple_of(index * size, size), size)


def local_kernel(fn, count, place, *refs):
    fn(place, refs[:count], refs[count:])


def local_call(name, fn, place, ins, outs):
    return pl.pallas_call(
        functools.partial(local_kernel, fn, len(ins)),
        in_specs=[pl.BlockSpec(memory_space=pltpu.SMEM)]
        + [pl.BlockSpec(memory_space=pltpu.VMEM)] * len(ins),
        out_specs=[pl.BlockSpec(memory_space=pltpu.VMEM)] * len(outs),
        out_shape=[jax.ShapeDtypeStruct(shape, kind) for shape, kind in outs],
        compiler_params=params(),
        name=name,
    )(place, *ins)


def flipped(size, bit):
    return [(i, i ^ bit) for i in range(size)]


CORE, Y, Z = 4, 5, 6


def pack(place, ins, outs):
    wq, wk, wv, wo, wi, wu = ins
    out_a, out_b, out_c = outs
    p = place[0]
    width, local = wq.shape
    quarter = width // 4

    def cut(ref, size):
        return ref[rows_at(p, size)].astype(F32)

    for n, ref in enumerate((wq, wk, wv)):
        out_a[:, n * local : (n + 1) * local] = cut(ref, quarter)
    inner = cut(wi, quarter)
    blocks = wi.shape[1] // width
    for n in range(blocks):
        out_b[n * quarter : (n + 1) * quarter] = inner[:, n * width : (n + 1) * width]
    out_b[blocks * quarter :] = cut(wo, wo.shape[0] // 4)
    out_c[...] = cut(wu, wu.shape[0] // 4)


def embed(place, ins, outs):
    state, timing = ins
    for s in range(state.shape[0] // LEN):
        rows = slice(s * LEN, (s + 1) * LEN)
        outs[0][rows] = (state[rows].astype(F32) + timing[...]).astype(BF)


def unpack_qkv(place, ins, outs):
    local = outs[0].shape[1]
    for p, ref in zip((0, 2, 1, 3), ins):
        rows = rows_at(place[p], ref.shape[0])
        for n, out in enumerate(outs):
            out[rows] = ref[:, n * local : (n + 1) * local].astype(BF)


def unpack_inner(place, ins, outs):
    wo, wi = outs
    width = wi.shape[0]
    quarter, blocks = width // 4, wi.shape[1] // width
    for p, ref in zip((0, 2, 1, 3), ins):
        rows = rows_at(place[p], quarter)
        for n in range(blocks):
            wi[rows, n * width : (n + 1) * width] = ref[
                n * quarter : (n + 1) * quarter
            ].astype(BF)
        wo[rows_at(place[p], wo.shape[0] // 4)] = ref[blocks * quarter :].astype(BF)


def unpack_outer(place, ins, outs):
    for p, ref in zip((0, 2, 1, 3), ins):
        outs[0][rows_at(place[p], ref.shape[0])] = ref[...].astype(BF)


def pair_cut(place, bit, value, keep, send):
    half = value.shape[0] // 2
    keep[...] = value[rows_at(place[bit], half)]
    send[...] = value[rows_at(1 - place[bit], half)]


def quad_cut(place, value, outs):
    size = value.shape[0] // 4
    for d, out in enumerate(outs):
        out[...] = value[rows_at(jnp.bitwise_xor(place[Z], d), size)]


def pair_join(place, bit, mine, theirs, out):
    half = mine.shape[0]
    out[rows_at(place[bit], half)] = mine[...]
    out[rows_at(1 - place[bit], half)] = theirs[...]


def quad_join(place, parts, out):
    size = parts[0].shape[0]
    for d, part in enumerate(parts):
        out[rows_at(jnp.bitwise_xor(place[Z], d), size)] = part[...]


def total(refs):
    out = refs[0][...]
    for ref in refs[1:]:
        out = out + ref[...]
    return out


def f32s(*shapes):
    return [(shape, F32) for shape in shapes]


def shards(
    dp, state, lengths, halt_mask, wq, wk, wv, wo, gain1, bias1, wi, wu, gain2, bias2,
    halt_weight, cotangent
):
    rows, width = state.shape
    local, ff = wq.shape[1], wi.shape[1]
    timing = jnp.asarray(timing_rows(width))
    me = lax.axis_index("dp").astype(jnp.int32)
    shift = np.array([0, 0, 0, 0, 0, 1, 2], np.int32)
    mask = np.array([3, 3, 3, 3, 1, 1, 3], np.int32)
    flip = np.array([0, 1, 2, 3, 0, 0, 0], np.int32)
    place = jnp.bitwise_xor(jnp.bitwise_and(jnp.right_shift(me, shift), mask), flip)
    bits = dp.bit_length() - 1

    def across(v):
        return lax.ppermute(v, "mp", [(0, 1), (1, 0)])

    def core(v):
        return lax.ppermute(v, "dp", flipped(dp, 1))

    def along_y(v):
        return lax.ppermute(v, "dp", flipped(dp, 2))

    def along_z(values):
        return [lax.ppermute(v, "dp", flipped(dp, 4 * d)) for d, v in zip((1, 2, 3), values)]

    def beyond(v):
        for bit in range(4, bits):
            v = v + lax.ppermute(v, "dp", flipped(dp, 1 << bit))
        return v

    tie = lax.optimization_barrier
    call = functools.partial(local_call, place=place)

    quarter = width // 4
    chunk_a, chunk_b, chunk_c = call(
        "pack", pack, ins=(wq, wk, wv, wo, wi, wu),
        outs=f32s((quarter, 3 * local), (ff // 4 + local // 4, width), (ff // 4, width)),
    )
    qkv0 = across(chunk_a)
    (x,) = call("embed", embed, ins=(state, timing), outs=[((rows, width), BF)])
    fwd = attention_forward(0, lengths, x, wq, wk, wv)
    qkv0, chunk_b, fwd = tie((qkv0, chunk_b, fwd))
    qkv1 = along_y(qkv0)
    in0 = across(chunk_b)
    fwd = attention_forward(1, lengths, x, wq, wk, wv, fwd)
    qkv1, fwd = tie((qkv1, fwd))
    qkv2, qkv3 = core(qkv0), core(qkv1)
    wq2, wk2, wv2 = call(
        "unpack_qkv", unpack_qkv, ins=(qkv0, qkv1, qkv2, qkv3),
        outs=[((width, local), BF)] * 3,
    )
    in0, chunk_c, wq2, wk2, wv2 = tie((in0, chunk_c, wq2, wk2, wv2))
    in1 = along_y(in0)
    out0 = across(chunk_c)
    fwd2 = attention_forward(0, lengths, x, wq2, wk2, wv2)
    fwd2 = attention_forward(1, lengths, x, wq2, wk2, wv2, fwd2)
    in1, out0, fwd2 = tie((in1, out0, fwd2))
    in2, in3 = core(in0), core(in1)
    out1 = along_y(out0)
    wo2, wi2 = call(
        "unpack_inner", unpack_inner, ins=(in0, in1, in2, in3),
        outs=[((local, width), BF), ((width, ff), BF)],
    )
    out2, out3 = core(out0), core(out1)
    (wu2,) = call(
        "unpack_outer", unpack_outer, ins=(out0, out1, out2, out3), outs=[((ff, width), BF)]
    )
    e_a, mix_a, r_a = fwd
    e_b, mix_b, r_b = fwd2
    vectors = jnp.stack([gain1, bias1, gain2, bias2, halt_weight] + [gain1] * 3)
    new_state, gs, do_a, do_b, dl_a, dl_b, grads = middle(
        state, timing, cotangent, halt_mask[:, None], mix_a, mix_b, r_a, r_b, wo, wo2, wi,
        wi2, wu, wu2, vectors
    )

    long = grads.shape[1]
    na, nb = 768, long - 768
    send = lax.dynamic_index_in_dim(grads, 1 - place[CORE], 0, False)
    got = core(send)

    def first(place, ins, outs):
        full, got = ins
        value = full[place[CORE]] + got[...]
        pair_cut_value(place, Y, value, outs[0], outs[1], outs[6])
        quad_cut_value(place, value[na:], outs[2:6], outs[7])

    def pair_cut_value(place, bit, value, keep, send, hold):
        hold[...] = value[:na]
        pair_cut(place, bit, hold, keep, send)

    def quad_cut_value(place, value, outs, hold):
        hold[...] = value
        quad_cut(place, hold, outs)

    a_keep, a_send, *b_parts = call(
        "sum_core", first, ins=(grads, got),
        outs=f32s(*[(na // 2, width)] * 2, *[(nb // 4, width)] * 4, (na, width), (nb, width)),
    )[:6]
    a_got = along_y(a_send)
    b_got = along_z(b_parts[1:])
    back = functools.partial(attention_backward, x=x)
    own = dict(e=e_a, do=do_a, dl=dl_a, wq=wq, wk=wk, wv=wv, own=True)
    other = dict(e=e_b, do=do_b, dl=dl_b, wq=wq2, wk=wk2, wv=wv2, own=False)
    gs, g0 = back(0, gs=gs, **own)
    a_got, b_got, gs, g0 = tie((a_got, b_got, gs, g0))

    def second(place, ins, outs):
        a = ins[:2]
        b = ins[2:]
        outs[6][...] = total(a)
        quad_cut(place, outs[6], outs[:4])
        outs[7][...] = total(b)
        pair_cut(place, Y, outs[7], outs[4], outs[5])

    *a_parts, b_keep, b_send = call(
        "sum_first", second, ins=(a_keep, a_got, b_parts[0], *b_got),
        outs=f32s(*[(na // 8, width)] * 4, *[(nb // 8, width)] * 2, (na // 2, width),
                  (nb // 4, width)),
    )[:6]
    a_got = along_z(a_parts[1:])
    b_got = along_y(b_send)
    gs, g1 = back(1, gs=gs, before=g0, **own)
    a_got, b_got, gs, g1 = tie((a_got, b_got, gs, g1))

    def third(place, ins, outs):
        outs[0][...] = total(ins[:4])
        outs[1][...] = total(ins[4:6])
        pair_cut(place, CORE, ins[6], outs[2], outs[3])

    a_sum, b_sum, q_keep, q_send = call(
        "sum_second", third, ins=(a_parts[0], *a_got, b_keep, b_got, g1),
        outs=f32s((na // 8, width), (nb // 8, width), *[(width // 2, 3 * local)] * 2),
    )
    a_sum, b_sum = beyond(a_sum), beyond(b_sum)
    q_got = core(q_send)
    a_got = along_z([a_sum] * 3)
    b_got = along_y(b_sum)

    def q_first(place, ins, outs):
        outs[2][...] = total(ins)
        pair_cut(place, Y, outs[2], outs[0], outs[1])

    q_keep, q_send = call(
        "sum_core_qkv", q_first, ins=(q_keep, q_got),
        outs=f32s(*[(width // 4, 3 * local)] * 2, (width // 2, 3 * local)),
    )[:2]
    q_got = along_y(q_send)
    (gs,) = back(0, gs=gs, **other)
    a_got, b_got, q_got, gs = tie((a_got, b_got, q_got, gs))

    def fourth(place, ins, outs):
        quad_join(place, ins[:4], outs[0])
        pair_join(place, Y, ins[4], ins[5], outs[1])
        outs[6][...] = total(ins[6:])
        quad_cut(place, outs[6], outs[2:6])

    a_half, b_half, *q_parts = call(
        "join_first", fourth, ins=(a_sum, *a_got, b_sum, b_got, q_keep, q_got),
        outs=f32s((na // 2, width), (nb // 4, width), *[(width // 16, 3 * local)] * 4,
                  (width // 4, 3 * local)),
    )[:6]
    a_got = along_y(a_half)
    b_got = along_z([b_half] * 3)
    q_got = along_z(q_parts[1:])
    (gs,) = back(1, gs=gs, **other)
    a_got, b_got, q_got, gs = tie((a_got, b_got, q_got, gs))

    def fifth(place, ins, outs):
        pair_join(place, Y, ins[0], ins[1], outs[0])
        quad_join(place, ins[2:6], outs[1])
        outs[2][...] = total(ins[6:])

    a_full, b_full, q_sum = call(
        "join_second", fifth, ins=(a_half, a_got, b_half, *b_got, q_parts[0], *q_got),
        outs=f32s((na, width), (nb, width), (width // 16, 3 * local)),
    )
    q_sum = beyond(q_sum)
    q_got = along_z([q_sum] * 3)
    a_got, b_got = core(a_full), core(b_full)

    def finish_ff(place, ins, outs):
        gu, gi, go, vec = outs
        half, small, few = ff // 2, width // 2, local // 2
        for flip, (a, b) in ((0, ins[:2]), (1, ins[2:])):
            c = jnp.bitwise_xor(place[CORE], flip)
            gu[rows_at(c, half)] = a[:half]
            gi[rows_at(c, small), :width] = a[half:]
            gi[rows_at(c, small), width:] = b[:small]
            go[rows_at(c, few)] = b[small : small + few]

            @pl.when(c == 0)
            def _():
                vec[...] = b[small + few : small + few + 8]

    gu, gi, go, vec = call(
        "finish_ff", finish_ff, ins=(a_full, b_full, a_got, b_got),
        outs=f32s((ff, width), (width, ff), (local, width), (8, width)),
    )

    def q_join(place, ins, outs):
        quad_join(place, ins, outs[0])

    (q_half,) = call(
        "join_z_qkv", q_join, ins=(q_sum, *q_got), outs=f32s((width // 4, 3 * local))
    )
    q_got = along_y(q_half)

    def q_join2(place, ins, outs):
        pair_join(place, Y, ins[0], ins[1], outs[0])

    (q_full,) = call(
        "join_y_qkv", q_join2, ins=(q_half, q_got), outs=f32s((width // 2, 3 * local))
    )
    q_got = core(q_full)

    def finish_qkv(place, ins, outs):
        for flip, ref in enumerate(ins):
            rows = rows_at(jnp.bitwise_xor(place[CORE], flip), width // 2)
            for n, out in enumerate(outs):
                out[rows] = ref[:, n * local : (n + 1) * local]

    gq, gk, gv = call(
        "finish_qkv", finish_qkv, ins=(q_full, q_got), outs=f32s(*[(width, local)] * 3)
    )
    return (
        new_state, gs, gq, gk, gv, go, vec[0], vec[1], gi, gu, vec[2], vec[3], vec[4]
    )


def solution(mesh):
    rows, columns, parts = P("dp", None), P(None, "mp"), P("mp", None)
    return jax.shard_map(
        functools.partial(shards, mesh.shape["dp"]),
        mesh=mesh,
        in_specs=(
            rows, P("dp"), P("dp"), columns, columns, columns, parts, P(), P(), columns,
            parts, P(), P(), P(), rows
        ),
        out_specs=(
            rows, rows, columns, columns, columns, parts, P(), P(), columns, parts, P(), P(),
            P()
        ),
        check_vma=False,
    )
```

```python
import functools
import math

import jax
import jax.numpy as jnp
import numpy as np
from jax import lax
from jax.experimental import pallas as pl
from jax.experimental.pallas import tpu as pltpu
from jax.sharding import PartitionSpec as P

HEAD = 64
LEN = 1024
STEP = 2
LOG2E = 1.4426950408889634
BF = jnp.bfloat16
F32 = jnp.float32
NN = (((1,), (0,)), ((), ()))
NT = (((1,), (1,)), ((), ()))
TN = (((0,), (0,)), ((), ()))
TT = (((0,), (1,)), ((), ()))
VMEM_LIMIT = 60 << 20
CHUNK = 256


def mm(a, b, dims=NN):
    return lax.dot_general(a, b, dims, preferred_element_type=F32)


def params():
    return pltpu.CompilerParams(vmem_limit_bytes=VMEM_LIMIT)


def whole(shape):
    zeros = (0,) * len(shape)
    return pl.BlockSpec(shape, lambda *_: zeros)


def timing_rows(width):
    half = width // 2
    rates = np.exp(-math.log(10000.0) * np.arange(half, dtype=np.float64) / (half - 1))

    def rows(positions):
        angles = positions[:, None] * rates[None, :]
        return np.concatenate([np.sin(angles), np.cos(angles)], axis=1)

    return (rows(np.arange(LEN, dtype=np.float64)) + rows(np.array([float(STEP)]))).astype(
        np.float32
    )


def split_low(value):
    high = value.astype(BF)
    return high, (value - high.astype(F32)).astype(BF)


def rolled(pair):
    return jnp.concatenate([pair[:, HEAD:], pair[:, :HEAD]], axis=1)


def lane_index(shape):
    return lax.broadcasted_iota(jnp.int32, shape, 1)


def row_index(shape):
    return lax.broadcasted_iota(jnp.int32, shape, 0)


def attention_forward_kernel(seq, lengths, x_in, wq, wk, wv, *rest, heads):
    e_out, mixed_out, r_out, kaug, qaug, vaug, sa, sb, ma, mb = rest[-10:]
    j = pl.program_id(0)
    last = heads // 2 - 1
    pieces = LEN // CHUNK

    def score_piece(i, c, target):
        rows = slice(c * CHUNK, (c + 1) * CHUNK)
        s = mm(kaug[i, rows], qaug[i])
        target[rows] = s
        return jnp.max(s.reshape(CHUNK // 8, 8, LEN), axis=0)

    @pl.when(j == 0)
    def _():
        x = x_in[...]
        query = mm(wq[...], x, TT).astype(BF).astype(F32) * (LOG2E / math.sqrt(HEAD))
        high, rest = split_low(query)
        key = mm(x, wk[...]).astype(BF)
        value = mm(wv[...], x, TT).astype(BF)
        shape = (LEN, 2 * HEAD)
        lane = lane_index(shape)
        padded = row_index(shape) >= lengths[seq]
        mask = jnp.where(padded & ((lane == 0) | (lane == HEAD)), -1e30, 0.0).astype(BF)
        first = row_index((HEAD, LEN)) == 0
        ones = jnp.where(first, 1.0, 0.0).astype(BF)
        zeros = jnp.zeros((HEAD, LEN), BF)
        for i in range(heads):
            pair = key[:, (i // 2) * 128 : (i // 2) * 128 + 128]
            turned = rolled(pair)
            mine = slice(i * HEAD, (i + 1) * HEAD)
            kaug[i, :, 0:128] = pair
            if i % 2 == 0:
                kaug[i, :, 128:256] = jnp.where(lane < HEAD, mask, turned)
                parts = (high[mine], zeros, ones, rest[mine])
            else:
                kaug[i, :, 128:256] = jnp.where(lane < HEAD, turned, mask)
                parts = (zeros, high[mine], rest[mine], ones)
            for n, part in enumerate(parts):
                qaug[i, n * HEAD : (n + 1) * HEAD] = part
            vaug[i, 0:HEAD] = value[mine]
            vaug[i, HEAD : HEAD + 16] = jnp.ones((16, LEN), BF)
        top = None
        for c in range(pieces):
            m = score_piece(0, c, sa)
            top = m if top is None else jnp.maximum(top, m)
        ma[...] = jnp.max(top, axis=0, keepdims=True)

    def step(slot, cur, cur_m, nxt, nxt_m, ahead=True):
        i = 2 * j + slot
        shift = cur_m[...]
        top = None
        out = None
        for c in range(pieces):
            rows = slice(c * CHUNK, (c + 1) * CHUNK)
            if ahead:
                m = score_piece(i + 1, c, nxt)
                top = m if top is None else jnp.maximum(top, m)
            e = jnp.exp2(cur[rows] - shift).astype(BF)
            e_out[slot, rows] = e
            o = mm(vaug[i, :, rows], e)
            out = o if out is None else out + o
        if ahead:
            nxt_m[...] = jnp.max(top, axis=0, keepdims=True)
        r = 1.0 / out[HEAD : HEAD + 1]
        mixed_out[slot * HEAD : (slot + 1) * HEAD] = (out[:HEAD] * r).astype(BF)
        r_out[slot] = r

    step(0, sa, ma, sb, mb)

    @pl.when(j < last)
    def _():
        step(1, sb, mb, sa, ma)

    @pl.when(j == last)
    def _():
        step(1, sb, mb, sa, ma, ahead=False)


def attention_forward(seq, lengths, x, wq, wk, wv, earlier=()):
    rows, width = x.shape
    local = wq.shape[1]
    heads = local // HEAD
    steps, total = heads // 2, rows // LEN * heads
    return pl.pallas_call(
        functools.partial(attention_forward_kernel, seq, heads=heads),
        grid=(steps,),
        in_specs=[
            pl.BlockSpec(memory_space=pltpu.SMEM),
            pl.BlockSpec((LEN, width), lambda j: (seq, 0)),
            whole((width, local)),
            whole((width, local)),
            whole((width, local)),
        ]
        + [pl.BlockSpec(memory_space=pl.ANY)] * len(earlier),
        out_specs=[
            pl.BlockSpec((2, LEN, LEN), lambda j: (seq * steps + j, 0, 0)),
            pl.BlockSpec((2 * HEAD, LEN), lambda j: (j, seq)),
            pl.BlockSpec((2, 1, LEN), lambda j: (seq * steps + j, 0, 0)),
        ],
        out_shape=[
            jax.ShapeDtypeStruct((total, LEN, LEN), BF),
            jax.ShapeDtypeStruct((local, rows), BF),
            jax.ShapeDtypeStruct((total, 1, LEN), F32),
        ],
        scratch_shapes=[
            pltpu.VMEM((heads, LEN, 256), BF),
            pltpu.VMEM((heads, 256, LEN), BF),
            pltpu.VMEM((heads, HEAD + 16, LEN), BF),
            pltpu.VMEM((LEN, LEN), F32),
            pltpu.VMEM((LEN, LEN), F32),
            pltpu.VMEM((1, LEN), F32),
            pltpu.VMEM((1, LEN), F32),
        ],
        compiler_params=params(),
        input_output_aliases={5 + n: n for n in range(len(earlier))},
        cost_estimate=pl.CostEstimate(
            flops=8 * 2 * heads * LEN * LEN * HEAD,
            bytes_accessed=2 * heads * LEN * LEN,
            transcendentals=heads * LEN * LEN,
        ),
        name="attention_forward",
    )(lengths, x, wq, wk, wv, *earlier)


def row_mean(v):
    return jnp.mean(v, axis=-1, keepdims=True)


def norm_rows(v):
    centre = v - row_mean(v)
    deviation = lax.rsqrt(row_mean(centre * centre) + 1e-05)
    return centre * deviation, deviation


def norm_back(e, xhat, deviation):
    return deviation * (e - row_mean(e) - xhat * row_mean(e * xhat))


def fold_rows(v):
    return jnp.sum(v.reshape(v.shape[0] // 8, 8, v.shape[1]), axis=0)


def middle_kernel(
    state, timing, cot, run, mix_a, mix_b, r_a, r_b, wo_a, wo_b, wi_a, wi_b, wu_a, wu_b,
    vectors, new_state, gs, do_a, do_b, dl_a, dl_b, grads, act, slope, fold, *, heads
):
    t = pl.program_id(0)
    last = pl.num_programs(0) - 1
    ff = wi_a.shape[1]
    local = wo_a.shape[0]
    width = state.shape[1]
    gain1, bias1, gain2, bias2, halt_w = (vectors[n : n + 1] for n in range(5))

    @pl.when(t == 0)
    def _():
        grads[...] = jnp.zeros(grads.shape, F32)
        fold[...] = jnp.zeros(fold.shape, F32)

    old = state[...].astype(F32)
    embedded = old + timing[...]
    attended = mm(mix_a[...], wo_a[...], TN) + mm(mix_b[...], wo_b[...], TN)
    xhat1, dev1 = norm_rows(embedded + attended)
    normed1 = xhat1 * gain1 + bias1
    low1 = normed1.astype(BF)
    c0 = math.sqrt(2.0 / math.pi)
    outer = None
    for n, (wi, wu) in enumerate(((wi_a, wu_a), (wi_b, wu_b))):
        v = mm(low1, wi[...])
        square = v * v
        h = 0.5 + 0.5 * jnp.tanh(v * (c0 + (c0 * 0.044715) * square))
        g = v * h
        act[n] = g.astype(BF)
        slope[n] = (
            h + g * (1.0 - h) * (2.0 * c0 + (6.0 * c0 * 0.044715) * square)
        ).astype(slope.dtype)
        o = mm(act[n], wu[...])
        outer = o if outer is None else outer + o
    xhat2, dev2 = norm_rows(normed1 + outer)
    block = xhat2 * gain2 + bias2
    halt = jax.nn.sigmoid(jnp.sum(block * halt_w, axis=-1, keepdims=True))
    running = run[...].astype(F32)
    gate = running * halt
    new_state[...] = old + gate * (block - old)
    g_in = cot[...].astype(F32)
    d_prob = running * jnp.sum(g_in * (block - old), axis=-1, keepdims=True)
    d_logit = d_prob * halt * (1.0 - halt)
    d_block = gate * g_in + d_logit * halt_w
    fold[4] += fold_rows(d_logit * block)
    fold[2] += fold_rows(d_block * xhat2)
    fold[3] += fold_rows(d_block)
    d_hidden2 = norm_back(d_block * gain2, xhat2, dev2)
    d_outer = d_hidden2.astype(BF)
    d_normed1 = d_hidden2
    for n, (wi, wu) in enumerate(((wi_a, wu_a), (wi_b, wu_b))):
        d_act = mm(d_outer, wu[...], NT)
        d_inner = (d_act * slope[n].astype(F32)).astype(BF)
        d_normed1 = d_normed1 + mm(d_inner, wi[...], NT)
        if n == 0:
            grads[:ff] += mm(act[0], d_outer, TN)
            gi = mm(low1, d_inner, TN)
            for p in range(ff // width):
                columns = slice(p * width, (p + 1) * width)
                grads[ff + p * width : ff + (p + 1) * width] += gi[:, columns]
    fold[0] += fold_rows(d_normed1 * xhat1)
    fold[1] += fold_rows(d_normed1)
    d_hidden1 = norm_back(d_normed1 * gain1, xhat1, dev1)
    d_att = d_hidden1.astype(BF)
    gs[...] = g_in * (1.0 - gate) + d_hidden1
    grads[2 * ff : 2 * ff + local] += mm(mix_a[...], d_att)
    for mix, r, wo, do, dl in (
        (mix_a, r_a, wo_a, do_a, dl_a),
        (mix_b, r_b, wo_b, do_b, dl_b),
    ):
        d_mixed = mm(wo[...], d_att, NT).astype(BF).astype(F32)
        for h in range(heads):
            mine = slice(h * HEAD, (h + 1) * HEAD)
            part = d_mixed[mine]
            scale = r[h]
            do[mine] = part * scale
            total = jnp.sum(part * mix[mine].astype(F32), axis=0, keepdims=True)
            dl[h] = total * scale

    @pl.when(t == last)
    def _():
        base = 2 * ff + local
        for n in range(8):
            grads[base + n : base + n + 1] = jnp.sum(fold[n], axis=0, keepdims=True)


def middle(state, timing, cot, run, mix_a, mix_b, r_a, r_b, wo_a, wo_b, wi_a, wi_b, wu_a,
           wu_b, vectors):
    rows, width = state.shape
    local, ff = wo_a.shape[0], wi_a.shape[1]
    heads = local // HEAD
    tile = 512
    per = LEN // tile
    by_rows = pl.BlockSpec((tile, width), lambda t: (t, 0))
    by_columns = pl.BlockSpec((local, tile), lambda t: (0, t))
    per_head = pl.BlockSpec((heads, 1, tile), lambda t: (t // per, 0, t % per))
    return pl.pallas_call(
        functools.partial(middle_kernel, heads=heads),
        grid=(rows // tile,),
        in_specs=[
            by_rows,
            pl.BlockSpec((tile, width), lambda t: (t % per, 0)),
            by_rows,
            pl.BlockSpec((tile, 1), lambda t: (t, 0)),
            by_columns,
            by_columns,
            per_head,
            per_head,
            whole((local, width)),
            whole((local, width)),
            whole((width, ff)),
            whole((width, ff)),
            whole((ff, width)),
            whole((ff, width)),
            whole((8, width)),
        ],
        out_specs=[
            by_rows,
            by_rows,
            by_columns,
            by_columns,
            per_head,
            per_head,
            whole((2 * ff + local + 8, width)),
        ],
        out_shape=[
            jax.ShapeDtypeStruct((rows, width), F32),
            jax.ShapeDtypeStruct((rows, width), F32),
            jax.ShapeDtypeStruct((local, rows), F32),
            jax.ShapeDtypeStruct((local, rows), F32),
            jax.ShapeDtypeStruct((rows // LEN * heads, 1, LEN), F32),
            jax.ShapeDtypeStruct((rows // LEN * heads, 1, LEN), F32),
            jax.ShapeDtypeStruct((2 * ff + local + 8, width), F32),
        ],
        scratch_shapes=[
            pltpu.VMEM((2, tile, ff), BF),
            pltpu.VMEM((2, tile, ff), F32),
            pltpu.VMEM((8, 8, width), F32),
        ],
        compiler_params=params(),
        cost_estimate=pl.CostEstimate(
            flops=2 * rows * width * ff * 10 + 2 * rows * width * local * 6,
            bytes_accessed=rows * width * 20,
            transcendentals=2 * rows * ff,
        ),
        name="middle",
    )(state, timing, cot, run, mix_a, mix_b, r_a, r_b, wo_a, wo_b, wi_a, wi_b, wu_a, wu_b,
      vectors)


def attention_backward_kernel(
    e_in, do_in, dl_in, x_in, wq, wk, wv, gs_in, *rest, heads, own, more
):
    if own:
        before, gs_out, gqkv, qt, kt, vaug, dq, dk, dv = rest if more else (None, *rest)
    else:
        gs_out, qt, kt, vaug, dq, dk, dv = rest
    h = pl.program_id(0)
    factor = 1.0 / math.sqrt(HEAD)
    pieces = LEN // CHUNK
    local = wq.shape[1]

    @pl.when(h == 0)
    def _():
        x = x_in[...]
        query = mm(wq[...], x, TT).astype(BF)
        key = mm(wk[...], x, TT).astype(BF)
        value = mm(x, wv[...]).astype(BF)
        lane = lane_index((LEN, 2 * HEAD))
        ones = jnp.where((lane % HEAD) < 3, 1.0, 0.0).astype(BF)
        for n in range(heads):
            mine = slice(n * HEAD, (n + 1) * HEAD)
            qt[n] = query[mine]
            kt[n] = key[mine]
            pair = value[:, (n // 2) * 128 : (n // 2) * 128 + 128]
            turned = rolled(pair)
            if n % 2 == 0:
                vaug[n, :, 0:128] = jnp.where(lane < HEAD, pair, turned)
            else:
                vaug[n, :, 0:128] = jnp.where(lane < HEAD, turned, pair)
            vaug[n, :, 128:256] = ones

    high, low = split_low(do_in[...])
    delta = -dl_in[0]
    d1 = delta.astype(BF)
    left = delta - d1.astype(F32)
    d2 = left.astype(BF)
    d3 = (left - d2.astype(F32)).astype(BF)
    index = row_index((2 * HEAD, LEN))
    tail = jnp.where(
        index == 0,
        d1.astype(F32),
        jnp.where(index == 1, d2.astype(F32), jnp.where(index == 2, d3.astype(F32), 0.0)),
    ).astype(BF)
    right = jnp.concatenate([high, low, tail], axis=0)
    query = qt[h]
    out = None
    for c in range(pieces):
        rows = slice(c * CHUNK, (c + 1) * CHUNK)
        d_probs = mm(vaug[h, rows], right)
        e = e_in[0, rows]
        d_scores = (e.astype(F32) * d_probs).astype(BF)
        dv[h, rows] = mm(e, high, NT).astype(BF)
        dk[h, rows] = (mm(d_scores, query, NT) * factor).astype(BF)
        o = mm(kt[h, :, rows], d_scores)
        out = o if out is None else out + o
    dq[pl.ds(pl.multiple_of(h * HEAD, HEAD), HEAD)] = (out * factor).astype(BF)

    @pl.when(h == heads - 1)
    def _():
        d_query = dq[...]
        d_key = jnp.concatenate([dk[n] for n in range(heads)], axis=1)
        d_value = jnp.concatenate([dv[n] for n in range(heads)], axis=1)
        total = mm(d_query, wq[...], TT)
        total = total + mm(d_key, wk[...], NT)
        total = total + mm(d_value, wv[...], NT)
        gs_out[...] = gs_in[...] + total
        if own:
            x = x_in[...]
            g1 = mm(d_query, x).T
            g2 = mm(x, jnp.concatenate([d_key, d_value], axis=1), TN)
            if more:
                g1 = g1 + before[:, :local]
                g2 = g2 + before[:, local:]
            gqkv[:, :local] = g1
            gqkv[:, local:] = g2


def attention_backward(seq, e, do, dl, x, wq, wk, wv, gs, own, before=None):
    rows, width = x.shape
    local = wq.shape[1]
    heads = local // HEAD
    more = before is not None
    by_rows = pl.BlockSpec((LEN, width), lambda h: (seq, 0))
    out_specs = [by_rows]
    out_shape = [jax.ShapeDtypeStruct((rows, width), F32)]
    in_specs = [
        pl.BlockSpec((1, LEN, LEN), lambda h: (seq * heads + h, 0, 0)),
        pl.BlockSpec((HEAD, LEN), lambda h: (h, seq)),
        pl.BlockSpec((1, 1, LEN), lambda h: (seq * heads + h, 0, 0)),
        by_rows,
        whole((width, local)),
        whole((width, local)),
        whole((width, local)),
        by_rows,
    ]
    args = [e, do, dl, x, wq, wk, wv, gs]
    aliases = {7: 0}
    if own:
        out_specs.append(whole((width, 3 * local)))
        out_shape.append(jax.ShapeDtypeStruct((width, 3 * local), F32))
        if more:
            in_specs.append(whole((width, 3 * local)))
            args.append(before)
            aliases[8] = 1
    return pl.pallas_call(
        functools.partial(attention_backward_kernel, heads=heads, own=own, more=more),
        grid=(heads,),
        in_specs=in_specs,
        out_specs=out_specs,
        out_shape=out_shape,
        scratch_shapes=[
            pltpu.VMEM((heads, HEAD, LEN), BF),
            pltpu.VMEM((heads, HEAD, LEN), BF),
            pltpu.VMEM((heads, LEN, 256), BF),
            pltpu.VMEM((local, LEN), BF),
            pltpu.VMEM((heads, LEN, HEAD), BF),
            pltpu.VMEM((heads, LEN, HEAD), BF),
        ],
        compiler_params=params(),
        input_output_aliases=aliases,
        cost_estimate=pl.CostEstimate(
            flops=32 * 2 * heads * LEN * LEN * HEAD, bytes_accessed=1000, transcendentals=0
        ),
        name="attention_backward_own" if own else "attention_backward_other",
    )(*args)


def rows_at(index, size):
    return pl.ds(pl.multiple_of(index * size, size), size)


def local_kernel(fn, count, place, *refs):
    fn(place, refs[:count], refs[count:])


def local_call(name, fn, place, ins, outs):
    return pl.pallas_call(
        functools.partial(local_kernel, fn, len(ins)),
        in_specs=[pl.BlockSpec(memory_space=pltpu.SMEM)]
        + [pl.BlockSpec(memory_space=pltpu.VMEM)] * len(ins),
        out_specs=[pl.BlockSpec(memory_space=pltpu.VMEM)] * len(outs),
        out_shape=[jax.ShapeDtypeStruct(shape, kind) for shape, kind in outs],
        compiler_params=params(),
        name=name,
    )(place, *ins)


def cut_call(name, fn, place, ins, outs):
    return pl.pallas_call(
        functools.partial(local_kernel, fn, len(ins)),
        grid_spec=pltpu.PrefetchScalarGridSpec(
            num_scalar_prefetch=1,
            grid=(1,),
            in_specs=[
                pl.BlockSpec((v.shape[0] // 4, v.shape[1]), lambda _, p: (p[0], 0)) for v in ins
            ],
            out_specs=[pl.BlockSpec(shape, lambda _, p: (0, 0)) for shape in outs],
        ),
        out_shape=[jax.ShapeDtypeStruct(shape, F32) for shape in outs],
        compiler_params=params(),
        name=name,
    )(place, *ins)


def pack_qkv(place, ins, outs):
    local = ins[0].shape[1]
    for n, ref in enumerate(ins):
        outs[0][:, n * local : (n + 1) * local] = ref[...].astype(F32)


def pack_ff(place, ins, outs):
    wo, wi, wu = ins
    quarter, width = wi.shape[0], wo.shape[1]
    blocks = wi.shape[1] // width
    for n in range(blocks):
        outs[0][n * quarter : (n + 1) * quarter] = wi[:, n * width : (n + 1) * width].astype(F32)
    outs[0][blocks * quarter :] = wo[...].astype(F32)
    outs[1][...] = wu[...].astype(F32)


def embed_kernel(state, timing, out):
    out[...] = (state[...].astype(F32) + timing[...]).astype(BF)


def embed(state, timing):
    rows, width = state.shape
    tile = 512
    per = LEN // tile
    by_rows = pl.BlockSpec((tile, width), lambda p, s: (s * per + p, 0))
    return pl.pallas_call(
        embed_kernel,
        grid=(per, rows // LEN),
        in_specs=[by_rows, pl.BlockSpec((tile, width), lambda p, s: (p, 0))],
        out_specs=by_rows,
        out_shape=jax.ShapeDtypeStruct((rows, width), BF),
        compiler_params=params(),
        name="embed",
    )(state, timing)


def unpack_qkv(place, ins, outs):
    local = outs[0].shape[1]
    for p, ref in zip((0, 2, 1, 3), ins):
        rows = rows_at(place[p], ref.shape[0])
        for n, out in enumerate(outs):
            out[rows] = ref[:, n * local : (n + 1) * local].astype(BF)


def unpack_inner(place, ins, outs):
    wo, wi = outs
    width = wi.shape[0]
    quarter, blocks = width // 4, wi.shape[1] // width
    for p, ref in zip((0, 2, 1, 3), ins):
        rows = rows_at(place[p], quarter)
        for n in range(blocks):
            wi[rows, n * width : (n + 1) * width] = ref[
                n * quarter : (n + 1) * quarter
            ].astype(BF)
        wo[rows_at(place[p], wo.shape[0] // 4)] = ref[blocks * quarter :].astype(BF)


def unpack_outer(place, ins, outs):
    for p, ref in zip((0, 2, 1, 3), ins):
        outs[0][rows_at(place[p], ref.shape[0])] = ref[...].astype(BF)


def finish_qkv(place, ins, outs):
    local = outs[0].shape[1]
    for flip, ref in enumerate(ins):
        rows = rows_at(jnp.bitwise_xor(place[4], flip), ref.shape[0])
        for n, out in enumerate(outs):
            out[rows] = ref[:, n * local : (n + 1) * local]


def flipped(size, even, odd):
    return [(i, i ^ (odd if i & 1 else even)) for i in range(size)]


def shards(
    dp, state, lengths, halt_mask, wq, wk, wv, wo, gain1, bias1, wi, wu, gain2, bias2,
    halt_weight, cotangent
):
    rows, width = state.shape
    local, ff = wq.shape[1], wi.shape[1]
    timing = jnp.asarray(timing_rows(width))
    me = lax.axis_index("dp").astype(jnp.int32)
    mask = np.array([3, 3, 3, 3, 1], np.int32)
    flip = np.array([0, 1, 2, 3, 0], np.int32)
    place = jnp.bitwise_xor(jnp.bitwise_and(me, mask), flip)
    bits = dp.bit_length() - 1
    tie = lax.optimization_barrier
    call = functools.partial(local_call, place=place)

    def across(v):
        return lax.ppermute(v, "mp", [(0, 1), (1, 0)])

    def along(v, even, odd=None):
        return lax.ppermute(v, "dp", flipped(dp, even, odd or even))

    quarter = width // 4
    (chunk_a,) = cut_call("pack_qkv", pack_qkv, place, (wq, wk, wv), [(quarter, 3 * local)])
    qkv0 = across(chunk_a)
    chunk_b, chunk_c = cut_call(
        "pack_ff", pack_ff, place, (wo, wi, wu),
        [(ff // 4 + local // 4, width), (ff // 4, width)],
    )
    x = embed(state, timing)
    run = halt_mask[:, None]
    vectors = jnp.stack([gain1, bias1, gain2, bias2, halt_weight] + [gain1] * 3)
    fwd = attention_forward(0, lengths, x, wq, wk, wv)
    qkv0, chunk_b, chunk_c, run, vectors, fwd = tie((qkv0, chunk_b, chunk_c, run, vectors, fwd))
    qkv1 = along(qkv0, 2)
    in0 = across(chunk_b)
    fwd = attention_forward(1, lengths, x, wq, wk, wv, fwd)
    qkv1, fwd = tie((qkv1, fwd))
    qkv2, qkv3 = along(qkv0, 1), along(qkv1, 1)
    wq2, wk2, wv2 = call(
        "unpack_qkv", unpack_qkv, ins=(qkv0, qkv1, qkv2, qkv3),
        outs=[((width, local), BF)] * 3,
    )
    in0, chunk_c, wq2, wk2, wv2 = tie((in0, chunk_c, wq2, wk2, wv2))
    in1 = along(in0, 2)
    out0 = across(chunk_c)
    fwd2 = attention_forward(0, lengths, x, wq2, wk2, wv2)
    fwd2 = attention_forward(1, lengths, x, wq2, wk2, wv2, fwd2)
    in1, out0, fwd2 = tie((in1, out0, fwd2))
    in2, in3 = along(in0, 1), along(in1, 1)
    out1 = along(out0, 2)
    out2 = along(out0, 1)
    wo2, wi2 = call(
        "unpack_inner", unpack_inner, ins=(in0, in1, in2, in3),
        outs=[((local, width), BF), ((width, ff), BF)],
    )
    out1, out2, wo2, wi2 = tie((out1, out2, wo2, wi2))
    out3 = along(out1, 1)
    (wu2,) = call(
        "unpack_outer", unpack_outer, ins=(out0, out1, out2, out3), outs=[((ff, width), BF)]
    )
    e_a, mix_a, r_a = fwd
    e_b, mix_b, r_b = fwd2
    new_state, gs, do_a, do_b, dl_a, dl_b, grads = middle(
        state, timing, cotangent, run, mix_a, mix_b, r_a, r_b, wo, wo2, wi, wi2, wu, wu2,
        vectors
    )

    grads = lax.psum(grads, "dp")
    own = dict(e=e_a, do=do_a, dl=dl_a, x=x, wq=wq, wk=wk, wv=wv)
    other = dict(e=e_b, do=do_b, dl=dl_b, x=x, wq=wq2, wk=wk2, wv=wv2)
    half = width // 2
    core = lax.rem(me, 2)

    def attention_and_sums(carry):
        step, gs, *_ = carry
        back = attention_backward
        gs, g = back(0, gs=gs, own=True, **own)
        gs, g = back(1, gs=gs, own=True, before=g, **own)
        got = along(lax.dynamic_slice_in_dim(g, (1 - core) * half, half), 1)
        g = lax.dynamic_slice_in_dim(g, core * half, half) + got
        g, gs = tie((g, gs))
        got = along(g, 2, 4)
        (gs,) = back(0, gs=gs, own=False, **other)
        got, gs = tie((got, gs))
        g = g + got
        g, gs = tie((g, gs))
        got = along(g, 4, 8)
        (gs,) = back(1, gs=gs, own=False, **other)
        got, gs = tie((got, gs))
        g = g + got
        g = g + along(g, 8, 2)
        for bit in range(4, bits):
            g = g + along(g, 1 << bit)
        parts = call(
            "finish_qkv", finish_qkv, ins=(g, along(g, 1)), outs=[((width, local), F32)] * 3
        )
        return (step + 1, gs, *parts)

    once = jnp.minimum(lengths[0], 1)
    empty = jnp.zeros((width, local), F32)
    _, gs, gq, gk, gv = lax.cond(
        once > 0, attention_and_sums, lambda c: c,
        (jnp.zeros_like(once), gs, empty, empty, empty),
    )
    grads, gs, gq = tie((grads, gs, gq))
    base = 2 * ff + local
    gi = jnp.concatenate([grads[n : n + width] for n in range(ff, 2 * ff, width)], axis=1)
    vec = grads[base:]
    return (
        new_state, gs, gq, gk, gv, grads[2 * ff : base], vec[0], vec[1], gi, grads[:ff],
        vec[2], vec[3], vec[4]
    )


def solution(mesh):
    rows, columns, parts = P("dp", None), P(None, "mp"), P("mp", None)
    return jax.shard_map(
        functools.partial(shards, mesh.shape["dp"]),
        mesh=mesh,
        in_specs=(
            rows, P("dp"), P("dp"), columns, columns, columns, parts, P(), P(), columns,
            parts, P(), P(), P(), rows
        ),
        out_specs=(
            rows, rows, columns, columns, columns, parts, P(), P(), columns, parts, P(), P(),
            P()
        ),
        check_vma=False,
    )
```

```python
import functools
import math

import jax
import jax.numpy as jnp
import numpy as np
from jax import lax
from jax.experimental import pallas as pl
from jax.experimental.pallas import tpu as pltpu
from jax.sharding import PartitionSpec as P

HEAD = 64
LEN = 1024
STEP = 2
LOG2E = 1.4426950408889634
BF = jnp.bfloat16
F32 = jnp.float32
NN = (((1,), (0,)), ((), ()))
NT = (((1,), (1,)), ((), ()))
TN = (((0,), (0,)), ((), ()))
TT = (((0,), (1,)), ((), ()))
VMEM_LIMIT = 60 << 20
CHUNK = 256
SUBS = 2


def mm(a, b, dims=NN):
    return lax.dot_general(a, b, dims, preferred_element_type=F32)


def params():
    return pltpu.CompilerParams(vmem_limit_bytes=VMEM_LIMIT)


def whole(shape):
    zeros = (0,) * len(shape)
    return pl.BlockSpec(shape, lambda *_: zeros)


def timing_rows(width):
    half = width // 2
    rates = np.exp(-math.log(10000.0) * np.arange(half, dtype=np.float64) / (half - 1))

    def rows(positions):
        angles = positions[:, None] * rates[None, :]
        return np.concatenate([np.sin(angles), np.cos(angles)], axis=1)

    return (rows(np.arange(LEN, dtype=np.float64)) + rows(np.array([float(STEP)]))).astype(
        np.float32
    )


def split_low(value):
    high = value.astype(BF)
    return high, (value - high.astype(F32)).astype(BF)


def rolled(pair):
    return jnp.concatenate([pair[:, HEAD:], pair[:, :HEAD]], axis=1)


def lane_index(shape):
    return lax.broadcasted_iota(jnp.int32, shape, 1)


def row_index(shape):
    return lax.broadcasted_iota(jnp.int32, shape, 0)


def attention_forward_kernel(seq, lengths, x_in, wq, wk, wv, *rest, heads):
    e_out, mixed_out, r_out, kaug, qaug, vaug, sa, sb, ma, mb = rest[-10:]
    j = pl.program_id(0)
    last = heads // 2 - 1
    pieces = LEN // CHUNK

    def score_piece(i, c, target):
        rows = slice(c * CHUNK, (c + 1) * CHUNK)
        s = mm(kaug[i, rows], qaug[i])
        target[rows] = s
        return jnp.max(s.reshape(CHUNK // 8, 8, LEN), axis=0)

    @pl.when(j == 0)
    def _():
        x = x_in[...]
        query = mm(wq[...], x, TT).astype(BF).astype(F32) * (LOG2E / math.sqrt(HEAD))
        high, rest = split_low(query)
        key = mm(x, wk[...]).astype(BF)
        value = mm(wv[...], x, TT).astype(BF)
        shape = (LEN, 2 * HEAD)
        lane = lane_index(shape)
        padded = row_index(shape) >= lengths[seq]
        mask = jnp.where(padded & ((lane == 0) | (lane == HEAD)), -1e30, 0.0).astype(BF)
        first = row_index((HEAD, LEN)) == 0
        ones = jnp.where(first, 1.0, 0.0).astype(BF)
        zeros = jnp.zeros((HEAD, LEN), BF)
        for i in range(heads):
            pair = key[:, (i // 2) * 128 : (i // 2) * 128 + 128]
            turned = rolled(pair)
            mine = slice(i * HEAD, (i + 1) * HEAD)
            kaug[i, :, 0:128] = pair
            if i % 2 == 0:
                kaug[i, :, 128:256] = jnp.where(lane < HEAD, mask, turned)
                parts = (high[mine], zeros, ones, rest[mine])
            else:
                kaug[i, :, 128:256] = jnp.where(lane < HEAD, turned, mask)
                parts = (zeros, high[mine], rest[mine], ones)
            for n, part in enumerate(parts):
                qaug[i, n * HEAD : (n + 1) * HEAD] = part
            vaug[i, 0:HEAD] = value[mine]
            vaug[i, HEAD : HEAD + 16] = jnp.ones((16, LEN), BF)
        top = None
        for c in range(pieces):
            m = score_piece(0, c, sa)
            top = m if top is None else jnp.maximum(top, m)
        ma[...] = jnp.max(top, axis=0, keepdims=True)

    def step(slot, cur, cur_m, nxt, nxt_m, ahead=True):
        i = 2 * j + slot
        shift = cur_m[...]
        top = None
        out = None
        for c in range(pieces):
            rows = slice(c * CHUNK, (c + 1) * CHUNK)
            if ahead:
                m = score_piece(i + 1, c, nxt)
                top = m if top is None else jnp.maximum(top, m)
            e = jnp.exp2(cur[rows] - shift).astype(BF)
            e_out[slot, rows] = e
            o = mm(vaug[i, :, rows], e)
            out = o if out is None else out + o
        if ahead:
            nxt_m[...] = jnp.max(top, axis=0, keepdims=True)
        r = 1.0 / out[HEAD : HEAD + 1]
        mixed_out[slot * HEAD : (slot + 1) * HEAD] = (out[:HEAD] * r).astype(BF)
        r_out[slot] = r

    step(0, sa, ma, sb, mb)

    @pl.when(j < last)
    def _():
        step(1, sb, mb, sa, ma)

    @pl.when(j == last)
    def _():
        step(1, sb, mb, sa, ma, ahead=False)


def attention_forward(seq, lengths, x, wq, wk, wv, earlier=()):
    rows, width = x.shape
    local = wq.shape[1]
    heads = local // HEAD
    steps, total = heads // 2, rows // LEN * heads
    return pl.pallas_call(
        functools.partial(attention_forward_kernel, seq, heads=heads),
        grid=(steps,),
        in_specs=[
            pl.BlockSpec(memory_space=pltpu.SMEM),
            pl.BlockSpec((LEN, width), lambda j: (seq, 0)),
            whole((width, local)),
            whole((width, local)),
            whole((width, local)),
        ]
        + [pl.BlockSpec(memory_space=pl.ANY)] * len(earlier),
        out_specs=[
            pl.BlockSpec((2, LEN, LEN), lambda j: (seq * steps + j, 0, 0)),
            pl.BlockSpec((2 * HEAD, LEN), lambda j: (j, seq)),
            pl.BlockSpec((2, 1, LEN), lambda j: (seq * steps + j, 0, 0)),
        ],
        out_shape=[
            jax.ShapeDtypeStruct((total, LEN, LEN), BF),
            jax.ShapeDtypeStruct((local, rows), BF),
            jax.ShapeDtypeStruct((total, 1, LEN), F32),
        ],
        scratch_shapes=[
            pltpu.VMEM((heads, LEN, 256), BF),
            pltpu.VMEM((heads, 256, LEN), BF),
            pltpu.VMEM((heads, HEAD + 16, LEN), BF),
            pltpu.VMEM((LEN, LEN), F32),
            pltpu.VMEM((LEN, LEN), F32),
            pltpu.VMEM((1, LEN), F32),
            pltpu.VMEM((1, LEN), F32),
        ],
        compiler_params=params(),
        input_output_aliases={5 + n: n for n in range(len(earlier))},
        cost_estimate=pl.CostEstimate(
            flops=8 * 2 * heads * LEN * LEN * HEAD,
            bytes_accessed=2 * heads * LEN * LEN,
            transcendentals=heads * LEN * LEN,
        ),
        name="attention_forward",
    )(lengths, x, wq, wk, wv, *earlier)


def row_mean(v):
    return jnp.mean(v, axis=-1, keepdims=True)


def norm_rows(v):
    centre = v - row_mean(v)
    deviation = lax.rsqrt(row_mean(centre * centre) + 1e-05)
    return centre * deviation, deviation


def norm_back(e, xhat, deviation):
    return deviation * (e - row_mean(e) - xhat * row_mean(e * xhat))


def fold_rows(v):
    return jnp.sum(v.reshape(v.shape[0] // 8, 8, v.shape[1]), axis=0)


def middle_kernel(
    state, timing, cot, run, mix_a, mix_b, r_a, r_b, wo_a, wo_b, wi_a, wi_b, wu_a, wu_b,
    vectors, new_state, gs, do_a, do_b, dl_a, dl_b, gu, gi, go, act, slope, inner_low, low1,
    out_low, att_low, fold, *, heads
):
    t = pl.program_id(0)
    last = pl.num_programs(0) - 1
    tile = state.shape[0]
    size = tile // SUBS
    local = wo_a.shape[0]
    gain1, bias1, gain2, bias2, halt_w = (vectors[n : n + 1] for n in range(5))
    c0 = math.sqrt(2.0 / math.pi)
    halves = ((wi_a, wu_a), (wi_b, wu_b))

    @pl.when(t == 0)
    def _():
        for ref in (gu, gi, go, fold):
            ref[...] = jnp.zeros(ref.shape, F32)

    def first_norm(k):
        rows = slice(k * size, (k + 1) * size)
        embedded = state[rows].astype(F32) + timing[rows]
        attended = mm(mix_a[:, rows], wo_a[...], TN) + mm(mix_b[:, rows], wo_b[...], TN)
        xhat1, dev1 = norm_rows(embedded + attended)
        normed1 = xhat1 * gain1 + bias1
        low1[rows] = normed1.astype(BF)
        return xhat1, dev1, normed1

    def forward(k, normed1):
        rows = slice(k * size, (k + 1) * size)
        total = normed1
        for n, (wi, wu) in enumerate(halves):
            v = mm(low1[rows], wi[...])
            square = v * v
            h = 0.5 + 0.5 * jnp.tanh(v * (c0 + (c0 * 0.044715) * square))
            g = v * h
            act[n, rows] = g.astype(BF)
            slope[n, rows] = h + g * (1.0 - h) * (2.0 * c0 + (6.0 * c0 * 0.044715) * square)
            total = total + mm(act[n, rows], wu[...])
        return total

    def second_norm(k, hidden2):
        rows = slice(k * size, (k + 1) * size)
        old = state[rows].astype(F32)
        xhat2, dev2 = norm_rows(hidden2)
        block = xhat2 * gain2 + bias2
        halt = jax.nn.sigmoid(jnp.sum(block * halt_w, axis=-1, keepdims=True))
        running = run[rows].astype(F32)
        gate = running * halt
        change = block - old
        new_state[rows] = old + gate * change
        g_in = cot[rows].astype(F32)
        d_prob = running * jnp.sum(g_in * change, axis=-1, keepdims=True)
        d_logit = d_prob * halt * (1.0 - halt)
        d_block = gate * g_in + d_logit * halt_w
        fold[4] += fold_rows(d_logit * block)
        fold[2] += fold_rows(d_block * xhat2)
        fold[3] += fold_rows(d_block)
        gs[rows] = g_in * (1.0 - gate)
        d_hidden2 = norm_back(d_block * gain2, xhat2, dev2)
        out_low[rows] = d_hidden2.astype(BF)
        return d_hidden2

    def backward(k, d_hidden2):
        rows = slice(k * size, (k + 1) * size)
        total = d_hidden2
        for n, (wi, wu) in enumerate(halves):
            d_act = mm(out_low[rows], wu[...], NT)
            inner_low[n, rows] = (d_act * slope[n, rows]).astype(BF)
            total = total + mm(inner_low[n, rows], wi[...], NT)
        return total

    def first_back(k, d_normed1, xhat1, dev1):
        rows = slice(k * size, (k + 1) * size)
        fold[0] += fold_rows(d_normed1 * xhat1)
        fold[1] += fold_rows(d_normed1)
        d_hidden1 = norm_back(d_normed1 * gain1, xhat1, dev1)
        att_low[rows] = d_hidden1.astype(BF)
        gs[rows] += d_hidden1

    def mixed_back():
        for mix, r, wo, do, dl in (
            (mix_a, r_a, wo_a, do_a, dl_a),
            (mix_b, r_b, wo_b, do_b, dl_b),
        ):
            d_mixed = mm(wo[...], att_low[...], NT).astype(BF).astype(F32)
            for h in range(heads):
                mine = slice(h * HEAD, (h + 1) * HEAD)
                part = d_mixed[mine]
                scale = r[h]
                do[mine] = part * scale
                total = jnp.sum(part * mix[mine].astype(F32), axis=0, keepdims=True)
                dl[h] = total * scale

    ks = range(SUBS)
    firsts = [first_norm(k) for k in ks]
    hidden2 = {0: forward(0, firsts[0][2])}
    d_hidden2, d_normed1 = {}, {}
    for k in ks:
        d_hidden2[k] = second_norm(k, hidden2[k])
        if k + 1 < SUBS:
            hidden2[k + 1] = forward(k + 1, firsts[k + 1][2])
    d_normed1[0] = backward(0, d_hidden2[0])
    for k in ks:
        first_back(k, d_normed1[k], *firsts[k][:2])
        if k + 1 < SUBS:
            d_normed1[k + 1] = backward(k + 1, d_hidden2[k + 1])
    gu[...] += mm(act[0], out_low[...], TN)
    gi[...] += mm(low1[...], inner_low[0], TN)
    go[:local] += mm(mix_a[...], att_low[...])
    mixed_back()

    @pl.when(t == last)
    def _():
        for n in range(8):
            go[local + n : local + n + 1] = jnp.sum(fold[n], axis=0, keepdims=True)


def middle(state, timing, cot, run, mix_a, mix_b, r_a, r_b, wo_a, wo_b, wi_a, wi_b, wu_a,
           wu_b, vectors):
    rows, width = state.shape
    local, ff = wo_a.shape[0], wi_a.shape[1]
    heads = local // HEAD
    tile = 512
    per = LEN // tile
    by_rows = pl.BlockSpec((tile, width), lambda t: (t, 0))
    by_columns = pl.BlockSpec((local, tile), lambda t: (0, t))
    per_head = pl.BlockSpec((heads, 1, tile), lambda t: (t // per, 0, t % per))
    return pl.pallas_call(
        functools.partial(middle_kernel, heads=heads),
        grid=(rows // tile,),
        in_specs=[
            by_rows,
            pl.BlockSpec((tile, width), lambda t: (t % per, 0)),
            by_rows,
            pl.BlockSpec((tile, 1), lambda t: (t, 0)),
            by_columns,
            by_columns,
            per_head,
            per_head,
            whole((local, width)),
            whole((local, width)),
            whole((width, ff)),
            whole((width, ff)),
            whole((ff, width)),
            whole((ff, width)),
            whole((8, width)),
        ],
        out_specs=[
            by_rows,
            by_rows,
            by_columns,
            by_columns,
            per_head,
            per_head,
            whole((ff, width)),
            whole((width, ff)),
            whole((local + 8, width)),
        ],
        out_shape=[
            jax.ShapeDtypeStruct((rows, width), F32),
            jax.ShapeDtypeStruct((rows, width), F32),
            jax.ShapeDtypeStruct((local, rows), F32),
            jax.ShapeDtypeStruct((local, rows), F32),
            jax.ShapeDtypeStruct((rows // LEN * heads, 1, LEN), F32),
            jax.ShapeDtypeStruct((rows // LEN * heads, 1, LEN), F32),
            jax.ShapeDtypeStruct((ff, width), F32),
            jax.ShapeDtypeStruct((width, ff), F32),
            jax.ShapeDtypeStruct((local + 8, width), F32),
        ],
        scratch_shapes=[
            pltpu.VMEM((2, tile, ff), BF),
            pltpu.VMEM((2, tile, ff), F32),
            pltpu.VMEM((2, tile, ff), BF),
            pltpu.VMEM((tile, width), BF),
            pltpu.VMEM((tile, width), BF),
            pltpu.VMEM((tile, width), BF),
            pltpu.VMEM((8, 8, width), F32),
        ],
        compiler_params=params(),
        cost_estimate=pl.CostEstimate(
            flops=2 * rows * width * ff * 10 + 2 * rows * width * local * 6,
            bytes_accessed=rows * width * 20,
            transcendentals=2 * rows * ff,
        ),
        name="middle",
    )(state, timing, cot, run, mix_a, mix_b, r_a, r_b, wo_a, wo_b, wi_a, wi_b, wu_a, wu_b,
      vectors)


def attention_backward_kernel(
    e_in, do_in, dl_in, x_in, wq, wk, wv, gs_in, *rest, heads, own, more
):
    if own:
        before, gs_out, gqkv, qt, kt, vaug, dq, dk, dv = rest if more else (None, *rest)
    else:
        gs_out, qt, kt, vaug, dq, dk, dv = rest
    h = pl.program_id(0)
    factor = 1.0 / math.sqrt(HEAD)
    pieces = LEN // CHUNK
    local = wq.shape[1]

    @pl.when(h == 0)
    def _():
        x = x_in[...]
        query = mm(wq[...], x, TT).astype(BF)
        key = mm(wk[...], x, TT).astype(BF)
        value = mm(x, wv[...]).astype(BF)
        lane = lane_index((LEN, 2 * HEAD))
        ones = jnp.where((lane % HEAD) < 3, 1.0, 0.0).astype(BF)
        for n in range(heads):
            mine = slice(n * HEAD, (n + 1) * HEAD)
            qt[n] = query[mine]
            kt[n] = key[mine]
            pair = value[:, (n // 2) * 128 : (n // 2) * 128 + 128]
            turned = rolled(pair)
            if n % 2 == 0:
                vaug[n, :, 0:128] = jnp.where(lane < HEAD, pair, turned)
            else:
                vaug[n, :, 0:128] = jnp.where(lane < HEAD, turned, pair)
            vaug[n, :, 128:256] = ones

    high, low = split_low(do_in[...])
    delta = -dl_in[0]
    d1 = delta.astype(BF)
    left = delta - d1.astype(F32)
    d2 = left.astype(BF)
    d3 = (left - d2.astype(F32)).astype(BF)
    index = row_index((2 * HEAD, LEN))
    tail = jnp.where(
        index == 0,
        d1.astype(F32),
        jnp.where(index == 1, d2.astype(F32), jnp.where(index == 2, d3.astype(F32), 0.0)),
    ).astype(BF)
    right = jnp.concatenate([high, low, tail], axis=0)
    query = qt[h]
    out = None
    for c in range(pieces):
        rows = slice(c * CHUNK, (c + 1) * CHUNK)
        d_probs = mm(vaug[h, rows], right)
        e = e_in[0, rows]
        d_scores = (e.astype(F32) * d_probs).astype(BF)
        dv[h, rows] = mm(e, high, NT).astype(BF)
        dk[h, rows] = (mm(d_scores, query, NT) * factor).astype(BF)
        o = mm(kt[h, :, rows], d_scores)
        out = o if out is None else out + o
    dq[pl.ds(pl.multiple_of(h * HEAD, HEAD), HEAD)] = (out * factor).astype(BF)

    @pl.when(h == heads - 1)
    def _():
        d_query = dq[...]
        d_key = jnp.concatenate([dk[n] for n in range(heads)], axis=1)
        d_value = jnp.concatenate([dv[n] for n in range(heads)], axis=1)
        total = mm(d_query, wq[...], TT)
        total = total + mm(d_key, wk[...], NT)
        total = total + mm(d_value, wv[...], NT)
        gs_out[...] = gs_in[...] + total
        if own:
            x = x_in[...]
            g1 = mm(d_query, x).T
            g2 = mm(x, jnp.concatenate([d_key, d_value], axis=1), TN)
            if more:
                g1 = g1 + before[:, :local]
                g2 = g2 + before[:, local:]
            gqkv[:, :local] = g1
            gqkv[:, local:] = g2


def attention_backward(seq, e, do, dl, x, wq, wk, wv, gs, own, before=None):
    rows, width = x.shape
    local = wq.shape[1]
    heads = local // HEAD
    more = before is not None
    by_rows = pl.BlockSpec((LEN, width), lambda h: (seq, 0))
    out_specs = [by_rows]
    out_shape = [jax.ShapeDtypeStruct((rows, width), F32)]
    in_specs = [
        pl.BlockSpec((1, LEN, LEN), lambda h: (seq * heads + h, 0, 0)),
        pl.BlockSpec((HEAD, LEN), lambda h: (h, seq)),
        pl.BlockSpec((1, 1, LEN), lambda h: (seq * heads + h, 0, 0)),
        by_rows,
        whole((width, local)),
        whole((width, local)),
        whole((width, local)),
        by_rows,
    ]
    args = [e, do, dl, x, wq, wk, wv, gs]
    aliases = {7: 0}
    if own:
        out_specs.append(whole((width, 3 * local)))
        out_shape.append(jax.ShapeDtypeStruct((width, 3 * local), F32))
        if more:
            in_specs.append(whole((width, 3 * local)))
            args.append(before)
            aliases[8] = 1
    return pl.pallas_call(
        functools.partial(attention_backward_kernel, heads=heads, own=own, more=more),
        grid=(heads,),
        in_specs=in_specs,
        out_specs=out_specs,
        out_shape=out_shape,
        scratch_shapes=[
            pltpu.VMEM((heads, HEAD, LEN), BF),
            pltpu.VMEM((heads, HEAD, LEN), BF),
            pltpu.VMEM((heads, LEN, 256), BF),
            pltpu.VMEM((local, LEN), BF),
            pltpu.VMEM((heads, LEN, HEAD), BF),
            pltpu.VMEM((heads, LEN, HEAD), BF),
        ],
        compiler_params=params(),
        input_output_aliases=aliases,
        cost_estimate=pl.CostEstimate(
            flops=32 * 2 * heads * LEN * LEN * HEAD, bytes_accessed=1000, transcendentals=0
        ),
        name="attention_backward_own" if own else "attention_backward_other",
    )(*args)


def rows_at(index, size):
    return pl.ds(pl.multiple_of(index * size, size), size)


def local_kernel(fn, count, place, *refs):
    fn(place, refs[:count], refs[count:])


def local_call(name, fn, place, ins, outs):
    return pl.pallas_call(
        functools.partial(local_kernel, fn, len(ins)),
        in_specs=[pl.BlockSpec(memory_space=pltpu.SMEM)]
        + [pl.BlockSpec(memory_space=pltpu.VMEM)] * len(ins),
        out_specs=[pl.BlockSpec(memory_space=pltpu.VMEM)] * len(outs),
        out_shape=[jax.ShapeDtypeStruct(shape, kind) for shape, kind in outs],
        compiler_params=params(),
        name=name,
    )(place, *ins)


def cut_call(name, fn, place, ins, outs):
    return pl.pallas_call(
        functools.partial(local_kernel, fn, len(ins)),
        grid_spec=pltpu.PrefetchScalarGridSpec(
            num_scalar_prefetch=1,
            grid=(1,),
            in_specs=[
                pl.BlockSpec((v.shape[0] // 4, v.shape[1]), lambda _, p: (p[0], 0)) for v in ins
            ],
            out_specs=[pl.BlockSpec(shape, lambda _, p: (0, 0)) for shape in outs],
        ),
        out_shape=[jax.ShapeDtypeStruct(shape, F32) for shape in outs],
        compiler_params=params(),
        name=name,
    )(place, *ins)


def pack_qkv(place, ins, outs):
    local = ins[0].shape[1]
    for n, ref in enumerate(ins):
        outs[0][:, n * local : (n + 1) * local] = ref[...].astype(F32)


def pack_ff(place, ins, outs):
    wo, wi, wu = ins
    quarter, width = wi.shape[0], wo.shape[1]
    blocks = wi.shape[1] // width
    for n in range(blocks):
        outs[0][n * quarter : (n + 1) * quarter] = wi[:, n * width : (n + 1) * width].astype(F32)
    outs[0][blocks * quarter :] = wo[...].astype(F32)
    outs[1][...] = wu[...].astype(F32)


def embed_kernel(state, timing, out):
    out[...] = (state[...].astype(F32) + timing[...]).astype(BF)


def embed(state, timing):
    rows, width = state.shape
    tile = 512
    per = LEN // tile
    by_rows = pl.BlockSpec((tile, width), lambda p, s: (s * per + p, 0))
    return pl.pallas_call(
        embed_kernel,
        grid=(per, rows // LEN),
        in_specs=[by_rows, pl.BlockSpec((tile, width), lambda p, s: (p, 0))],
        out_specs=by_rows,
        out_shape=jax.ShapeDtypeStruct((rows, width), BF),
        compiler_params=params(),
        name="embed",
    )(state, timing)


def unpack_qkv(place, ins, outs):
    local = outs[0].shape[1]
    for p, ref in zip((0, 2, 1, 3), ins):
        rows = rows_at(place[p], ref.shape[0])
        for n, out in enumerate(outs):
            out[rows] = ref[:, n * local : (n + 1) * local].astype(BF)


def unpack_inner(place, ins, outs):
    wo, wi = outs
    width = wi.shape[0]
    quarter, blocks = width // 4, wi.shape[1] // width
    for p, ref in zip((0, 2, 1, 3), ins):
        rows = rows_at(place[p], quarter)
        for n in range(blocks):
            wi[rows, n * width : (n + 1) * width] = ref[
                n * quarter : (n + 1) * quarter
            ].astype(BF)
        wo[rows_at(place[p], wo.shape[0] // 4)] = ref[blocks * quarter :].astype(BF)


def unpack_outer(place, ins, outs):
    for p, ref in zip((0, 2, 1, 3), ins):
        outs[0][rows_at(place[p], ref.shape[0])] = ref[...].astype(BF)


def finish_qkv(place, ins, outs):
    local = outs[0].shape[1]
    for flip, ref in enumerate(ins):
        rows = rows_at(jnp.bitwise_xor(place[4], flip), ref.shape[0])
        for n, out in enumerate(outs):
            out[rows] = ref[:, n * local : (n + 1) * local]


def flipped(size, even, odd):
    return [(i, i ^ (odd if i & 1 else even)) for i in range(size)]


def shards(
    dp, state, lengths, halt_mask, wq, wk, wv, wo, gain1, bias1, wi, wu, gain2, bias2,
    halt_weight, cotangent
):
    rows, width = state.shape
    local, ff = wq.shape[1], wi.shape[1]
    timing = jnp.asarray(timing_rows(width))
    me = lax.axis_index("dp").astype(jnp.int32)
    mask = np.array([3, 3, 3, 3, 1], np.int32)
    flip = np.array([0, 1, 2, 3, 0], np.int32)
    place = jnp.bitwise_xor(jnp.bitwise_and(me, mask), flip)
    bits = dp.bit_length() - 1
    tie = lax.optimization_barrier
    call = functools.partial(local_call, place=place)

    def across(v):
        return lax.ppermute(v, "mp", [(0, 1), (1, 0)])

    def along(v, even, odd=None):
        return lax.ppermute(v, "dp", flipped(dp, even, odd or even))

    quarter = width // 4
    (chunk_a,) = cut_call("pack_qkv", pack_qkv, place, (wq, wk, wv), [(quarter, 3 * local)])
    qkv0 = across(chunk_a)
    chunk_b, chunk_c = cut_call(
        "pack_ff", pack_ff, place, (wo, wi, wu),
        [(ff // 4 + local // 4, width), (ff // 4, width)],
    )
    x = embed(state, timing)
    chunk_b, x = tie((chunk_b, x))
    in0 = across(chunk_b)
    run = halt_mask[:, None]
    vectors = jnp.stack([gain1, bias1, gain2, bias2, halt_weight] + [gain1] * 3)
    fwd = attention_forward(0, lengths, x, wq, wk, wv)
    qkv0, chunk_c, run, vectors, fwd = tie((qkv0, chunk_c, run, vectors, fwd))
    qkv1 = along(qkv0, 2)
    out0 = across(chunk_c)
    fwd = attention_forward(1, lengths, x, wq, wk, wv, fwd)
    qkv1, in0, fwd = tie((qkv1, in0, fwd))
    qkv2, qkv3 = along(qkv0, 1), along(qkv1, 1)
    in1 = along(in0, 2)
    wq2, wk2, wv2 = call(
        "unpack_qkv", unpack_qkv, ins=(qkv0, qkv1, qkv2, qkv3),
        outs=[((width, local), BF)] * 3,
    )
    fwd2 = attention_forward(0, lengths, x, wq2, wk2, wv2)
    in1, out0, fwd2 = tie((in1, out0, fwd2))
    in2, in3 = along(in0, 1), along(in1, 1)
    out1 = along(out0, 2)
    out2 = along(out0, 1)
    fwd2 = attention_forward(1, lengths, x, wq2, wk2, wv2, fwd2)
    in2, in3, out2, fwd2 = tie((in2, in3, out2, fwd2))
    wo2, wi2 = call(
        "unpack_inner", unpack_inner, ins=(in0, in1, in2, in3),
        outs=[((local, width), BF), ((width, ff), BF)],
    )
    out1, wo2, wi2 = tie((out1, wo2, wi2))
    out3 = along(out1, 1)
    (wu2,) = call(
        "unpack_outer", unpack_outer, ins=(out0, out1, out2, out3), outs=[((ff, width), BF)]
    )
    e_a, mix_a, r_a = fwd
    e_b, mix_b, r_b = fwd2
    new_state, gs, do_a, do_b, dl_a, dl_b, *grads = middle(
        state, timing, cotangent, run, mix_a, mix_b, r_a, r_b, wo, wo2, wi, wi2, wu, wu2,
        vectors
    )

    grads = lax.psum(tuple(grads), "dp")
    own = dict(e=e_a, do=do_a, dl=dl_a, x=x, wq=wq, wk=wk, wv=wv)
    other = dict(e=e_b, do=do_b, dl=dl_b, x=x, wq=wq2, wk=wk2, wv=wv2)
    half = width // 2
    core = lax.rem(me, 2)

    def attention_and_sums(carry):
        step, gs, *_ = carry
        back = attention_backward
        gs, g = back(0, gs=gs, own=True, **own)
        gs, g = back(1, gs=gs, own=True, before=g, **own)
        got = along(lax.dynamic_slice_in_dim(g, (1 - core) * half, half), 1)
        g = lax.dynamic_slice_in_dim(g, core * half, half) + got
        g, gs = tie((g, gs))
        got = along(g, 2, 4)
        (gs,) = back(0, gs=gs, own=False, **other)
        got, gs = tie((got, gs))
        g = g + got
        g, gs = tie((g, gs))
        got = along(g, 4, 8)
        (gs,) = back(1, gs=gs, own=False, **other)
        got, gs = tie((got, gs))
        g = g + got
        g = g + along(g, 8, 2)
        for bit in range(4, bits):
            g = g + along(g, 1 << bit)
        parts = call(
            "finish_qkv", finish_qkv, ins=(g, along(g, 1)), outs=[((width, local), F32)] * 3
        )
        return (step + 1, gs, *parts)

    once = jnp.minimum(lengths[0], 1)
    empty = jnp.zeros((width, local), F32)
    _, gs, gq, gk, gv = lax.cond(
        once > 0, attention_and_sums, lambda c: c,
        (jnp.zeros_like(once), gs, empty, empty, empty),
    )
    grads, gs, gq = tie((grads, gs, gq))
    gu, gi, go = grads
    vec = go[local:]
    return (
        new_state, gs, gq, gk, gv, go[:local], vec[0], vec[1], gi, gu, vec[2], vec[3], vec[4]
    )


def solution(mesh):
    rows, columns, parts = P("dp", None), P(None, "mp"), P("mp", None)
    return jax.shard_map(
        functools.partial(shards, mesh.shape["dp"]),
        mesh=mesh,
        in_specs=(
            rows, P("dp"), P("dp"), columns, columns, columns, parts, P(), P(), columns,
            parts, P(), P(), P(), rows
        ),
        out_specs=(
            rows, rows, columns, columns, columns, parts, P(), P(), columns, parts, P(), P(),
            P()
        ),
        check_vma=False,
    )
```

```python
import functools
import math

import jax
import jax.numpy as jnp
import numpy as np
from jax import lax
from jax.experimental import pallas as pl
from jax.experimental.pallas import tpu as pltpu
from jax.sharding import PartitionSpec as P

HEAD = 64
LEN = 1024
STEP = 2
LOG2E = 1.4426950408889634
BF = jnp.bfloat16
F32 = jnp.float32
NN = (((1,), (0,)), ((), ()))
NT = (((1,), (1,)), ((), ()))
TN = (((0,), (0,)), ((), ()))
TT = (((0,), (1,)), ((), ()))
VMEM_LIMIT = 60 << 20
CHUNK = 256
SUBS = 2


def mm(a, b, dims=NN):
    return lax.dot_general(a, b, dims, preferred_element_type=F32)


def params():
    return pltpu.CompilerParams(vmem_limit_bytes=VMEM_LIMIT)


def whole(shape):
    zeros = (0,) * len(shape)
    return pl.BlockSpec(shape, lambda *_: zeros)


def timing_rows(width):
    half = width // 2
    rates = np.exp(-math.log(10000.0) * np.arange(half, dtype=np.float64) / (half - 1))

    def rows(positions):
        angles = positions[:, None] * rates[None, :]
        return np.concatenate([np.sin(angles), np.cos(angles)], axis=1)

    return (rows(np.arange(LEN, dtype=np.float64)) + rows(np.array([float(STEP)]))).astype(
        np.float32
    )


def split_low(value):
    high = value.astype(BF)
    return high, (value - high.astype(F32)).astype(BF)


def rolled(pair):
    return jnp.concatenate([pair[:, HEAD:], pair[:, :HEAD]], axis=1)


def lane_index(shape):
    return lax.broadcasted_iota(jnp.int32, shape, 1)


def row_index(shape):
    return lax.broadcasted_iota(jnp.int32, shape, 0)


def attention_forward_kernel(seq, lengths, x_in, wq, wk, wv, *rest, heads):
    e_out, mixed_out, r_out, kaug, qaug, vaug, sa, sb, ma, mb = rest[-10:]
    j = pl.program_id(0)
    last = heads // 2 - 1
    pieces = LEN // CHUNK

    def score_piece(i, c, target):
        rows = slice(c * CHUNK, (c + 1) * CHUNK)
        s = mm(kaug[i, rows], qaug[i])
        target[rows] = s
        return jnp.max(s.reshape(CHUNK // 8, 8, LEN), axis=0)

    @pl.when(j == 0)
    def _():
        x = x_in[...]
        query = mm(wq[...], x, TT).astype(BF).astype(F32) * (LOG2E / math.sqrt(HEAD))
        high, rest = split_low(query)
        key = mm(x, wk[...]).astype(BF)
        value = mm(wv[...], x, TT).astype(BF)
        shape = (LEN, 2 * HEAD)
        lane = lane_index(shape)
        padded = row_index(shape) >= lengths[seq]
        mask = jnp.where(padded & ((lane == 0) | (lane == HEAD)), -1e30, 0.0).astype(BF)
        first = row_index((HEAD, LEN)) == 0
        ones = jnp.where(first, 1.0, 0.0).astype(BF)
        zeros = jnp.zeros((HEAD, LEN), BF)
        for i in range(heads):
            pair = key[:, (i // 2) * 128 : (i // 2) * 128 + 128]
            turned = rolled(pair)
            mine = slice(i * HEAD, (i + 1) * HEAD)
            kaug[i, :, 0:128] = pair
            if i % 2 == 0:
                kaug[i, :, 128:256] = jnp.where(lane < HEAD, mask, turned)
                parts = (high[mine], zeros, ones, rest[mine])
            else:
                kaug[i, :, 128:256] = jnp.where(lane < HEAD, turned, mask)
                parts = (zeros, high[mine], rest[mine], ones)
            for n, part in enumerate(parts):
                qaug[i, n * HEAD : (n + 1) * HEAD] = part
            vaug[i, 0:HEAD] = value[mine]
            vaug[i, HEAD : HEAD + 16] = jnp.ones((16, LEN), BF)
        top = None
        for c in range(pieces):
            m = score_piece(0, c, sa)
            top = m if top is None else jnp.maximum(top, m)
        ma[...] = jnp.max(top, axis=0, keepdims=True)

    def step(slot, cur, cur_m, nxt, nxt_m, ahead=True):
        i = 2 * j + slot
        shift = cur_m[...]
        top = None
        out = None
        for c in range(pieces):
            rows = slice(c * CHUNK, (c + 1) * CHUNK)
            if ahead:
                m = score_piece(i + 1, c, nxt)
                top = m if top is None else jnp.maximum(top, m)
            e = jnp.exp2(cur[rows] - shift).astype(BF)
            e_out[slot, rows] = e
            o = mm(vaug[i, :, rows], e)
            out = o if out is None else out + o
        if ahead:
            nxt_m[...] = jnp.max(top, axis=0, keepdims=True)
        r = 1.0 / out[HEAD : HEAD + 1]
        mixed_out[slot * HEAD : (slot + 1) * HEAD] = (out[:HEAD] * r).astype(BF)
        r_out[slot] = r

    step(0, sa, ma, sb, mb)

    @pl.when(j < last)
    def _():
        step(1, sb, mb, sa, ma)

    @pl.when(j == last)
    def _():
        step(1, sb, mb, sa, ma, ahead=False)


def attention_forward(seq, lengths, x, wq, wk, wv, earlier=()):
    rows, width = x.shape
    local = wq.shape[1]
    heads = local // HEAD
    steps, total = heads // 2, rows // LEN * heads
    return pl.pallas_call(
        functools.partial(attention_forward_kernel, seq, heads=heads),
        grid=(steps,),
        in_specs=[
            pl.BlockSpec(memory_space=pltpu.SMEM),
            pl.BlockSpec((LEN, width), lambda j: (seq, 0)),
            whole((width, local)),
            whole((width, local)),
            whole((width, local)),
        ]
        + [pl.BlockSpec(memory_space=pl.ANY)] * len(earlier),
        out_specs=[
            pl.BlockSpec((2, LEN, LEN), lambda j: (seq * steps + j, 0, 0)),
            pl.BlockSpec((2 * HEAD, LEN), lambda j: (j, seq)),
            pl.BlockSpec((2, 1, LEN), lambda j: (seq * steps + j, 0, 0)),
        ],
        out_shape=[
            jax.ShapeDtypeStruct((total, LEN, LEN), BF),
            jax.ShapeDtypeStruct((local, rows), BF),
            jax.ShapeDtypeStruct((total, 1, LEN), F32),
        ],
        scratch_shapes=[
            pltpu.VMEM((heads, LEN, 256), BF),
            pltpu.VMEM((heads, 256, LEN), BF),
            pltpu.VMEM((heads, HEAD + 16, LEN), BF),
            pltpu.VMEM((LEN, LEN), F32),
            pltpu.VMEM((LEN, LEN), F32),
            pltpu.VMEM((1, LEN), F32),
            pltpu.VMEM((1, LEN), F32),
        ],
        compiler_params=params(),
        input_output_aliases={5 + n: n for n in range(len(earlier))},
        cost_estimate=pl.CostEstimate(
            flops=8 * 2 * heads * LEN * LEN * HEAD,
            bytes_accessed=2 * heads * LEN * LEN,
            transcendentals=heads * LEN * LEN,
        ),
        name="attention_forward",
    )(lengths, x, wq, wk, wv, *earlier)


def row_mean(v):
    return jnp.mean(v, axis=-1, keepdims=True)


def norm_rows(v):
    centre = v - row_mean(v)
    deviation = lax.rsqrt(row_mean(centre * centre) + 1e-05)
    return centre * deviation, deviation


def norm_back(e, xhat, deviation):
    return deviation * (e - row_mean(e) - xhat * row_mean(e * xhat))


def fold_rows(v):
    return jnp.sum(v.reshape(v.shape[0] // 8, 8, v.shape[1]), axis=0)


def middle_kernel(
    state, timing, cot, run, mix_a, mix_b, r_a, r_b, wo_a, wo_b, wi_a, wi_b, wu_a, wu_b,
    vectors, new_state, gs, do_a, do_b, dl_a, dl_b, gu, gi, go, act, slope, inner_low, low1,
    out_low, att_low, fold, *, heads
):
    t = pl.program_id(0)
    last = pl.num_programs(0) - 1
    tile = state.shape[0]
    size = tile // SUBS
    local = wo_a.shape[0]
    gain1, bias1, gain2, bias2, halt_w = (vectors[n : n + 1] for n in range(5))
    c0 = math.sqrt(2.0 / math.pi)
    halves = ((wi_a, wu_a), (wi_b, wu_b))
    running_column = jnp.broadcast_to(run[0].astype(F32), (8, tile)).T[:, 0:1]

    @pl.when(t == 0)
    def _():
        for ref in (gu, gi, go, fold):
            ref[...] = jnp.zeros(ref.shape, F32)

    def first_norm(k):
        rows = slice(k * size, (k + 1) * size)
        embedded = state[rows].astype(F32) + timing[rows]
        attended = mm(mix_a[:, rows], wo_a[...], TN) + mm(mix_b[:, rows], wo_b[...], TN)
        xhat1, dev1 = norm_rows(embedded + attended)
        normed1 = xhat1 * gain1 + bias1
        low1[rows] = normed1.astype(BF)
        return xhat1, dev1, normed1

    def forward(k, normed1):
        rows = slice(k * size, (k + 1) * size)
        total = normed1
        for n, (wi, wu) in enumerate(halves):
            v = mm(low1[rows], wi[...])
            square = v * v
            h = 0.5 + 0.5 * jnp.tanh(v * (c0 + (c0 * 0.044715) * square))
            g = v * h
            act[n, rows] = g.astype(BF)
            slope[n, rows] = h + g * (1.0 - h) * (2.0 * c0 + (6.0 * c0 * 0.044715) * square)
            total = total + mm(act[n, rows], wu[...])
        return total

    def second_norm(k, hidden2):
        rows = slice(k * size, (k + 1) * size)
        old = state[rows].astype(F32)
        xhat2, dev2 = norm_rows(hidden2)
        block = xhat2 * gain2 + bias2
        halt = jax.nn.sigmoid(jnp.sum(block * halt_w, axis=-1, keepdims=True))
        running = running_column[rows]
        gate = running * halt
        change = block - old
        new_state[rows] = old + gate * change
        g_in = cot[rows].astype(F32)
        d_prob = running * jnp.sum(g_in * change, axis=-1, keepdims=True)
        d_logit = d_prob * halt * (1.0 - halt)
        d_block = gate * g_in + d_logit * halt_w
        fold[4] += fold_rows(d_logit * block)
        fold[2] += fold_rows(d_block * xhat2)
        fold[3] += fold_rows(d_block)
        gs[rows] = g_in * (1.0 - gate)
        d_hidden2 = norm_back(d_block * gain2, xhat2, dev2)
        out_low[rows] = d_hidden2.astype(BF)
        return d_hidden2

    def backward(k, d_hidden2):
        rows = slice(k * size, (k + 1) * size)
        total = d_hidden2
        for n, (wi, wu) in enumerate(halves):
            d_act = mm(out_low[rows], wu[...], NT)
            inner_low[n, rows] = (d_act * slope[n, rows]).astype(BF)
            total = total + mm(inner_low[n, rows], wi[...], NT)
        return total

    def first_back(k, d_normed1, xhat1, dev1):
        rows = slice(k * size, (k + 1) * size)
        fold[0] += fold_rows(d_normed1 * xhat1)
        fold[1] += fold_rows(d_normed1)
        d_hidden1 = norm_back(d_normed1 * gain1, xhat1, dev1)
        att_low[rows] = d_hidden1.astype(BF)
        gs[rows] += d_hidden1

    def mixed_back():
        for mix, r, wo, do, dl in (
            (mix_a, r_a, wo_a, do_a, dl_a),
            (mix_b, r_b, wo_b, do_b, dl_b),
        ):
            d_mixed = mm(wo[...], att_low[...], NT).astype(BF).astype(F32)
            for h in range(heads):
                mine = slice(h * HEAD, (h + 1) * HEAD)
                part = d_mixed[mine]
                scale = r[h]
                do[mine] = part * scale
                total = jnp.sum(part * mix[mine].astype(F32), axis=0, keepdims=True)
                dl[h] = total * scale

    ks = range(SUBS)
    firsts = [first_norm(k) for k in ks]
    hidden2 = {0: forward(0, firsts[0][2])}
    d_hidden2, d_normed1 = {}, {}
    for k in ks:
        d_hidden2[k] = second_norm(k, hidden2[k])
        if k + 1 < SUBS:
            hidden2[k + 1] = forward(k + 1, firsts[k + 1][2])
    d_normed1[0] = backward(0, d_hidden2[0])
    for k in ks:
        first_back(k, d_normed1[k], *firsts[k][:2])
        if k + 1 < SUBS:
            d_normed1[k + 1] = backward(k + 1, d_hidden2[k + 1])
    gu[...] += mm(act[0], out_low[...], TN)
    gi[...] += mm(low1[...], inner_low[0], TN)
    go[:local] += mm(mix_a[...], att_low[...])
    mixed_back()

    @pl.when(t == last)
    def _():
        for n in range(8):
            go[local + n : local + n + 1] = jnp.sum(fold[n], axis=0, keepdims=True)


def middle(state, timing, cot, run, mix_a, mix_b, r_a, r_b, wo_a, wo_b, wi_a, wi_b, wu_a,
           wu_b, vectors):
    rows, width = state.shape
    local, ff = wo_a.shape[0], wi_a.shape[1]
    heads = local // HEAD
    tile = 512
    per = LEN // tile
    by_rows = pl.BlockSpec((tile, width), lambda t: (t, 0))
    by_columns = pl.BlockSpec((local, tile), lambda t: (0, t))
    per_head = pl.BlockSpec((heads, 1, tile), lambda t: (t // per, 0, t % per))
    return pl.pallas_call(
        functools.partial(middle_kernel, heads=heads),
        grid=(rows // tile,),
        in_specs=[
            by_rows,
            pl.BlockSpec((tile, width), lambda t: (t % per, 0)),
            by_rows,
            pl.BlockSpec((1, 1, tile), lambda t: (t, 0, 0)),
            by_columns,
            by_columns,
            per_head,
            per_head,
            whole((local, width)),
            whole((local, width)),
            whole((width, ff)),
            whole((width, ff)),
            whole((ff, width)),
            whole((ff, width)),
            whole((8, width)),
        ],
        out_specs=[
            by_rows,
            by_rows,
            by_columns,
            by_columns,
            per_head,
            per_head,
            whole((ff, width)),
            whole((width, ff)),
            whole((local + 8, width)),
        ],
        out_shape=[
            jax.ShapeDtypeStruct((rows, width), F32),
            jax.ShapeDtypeStruct((rows, width), F32),
            jax.ShapeDtypeStruct((local, rows), F32),
            jax.ShapeDtypeStruct((local, rows), F32),
            jax.ShapeDtypeStruct((rows // LEN * heads, 1, LEN), F32),
            jax.ShapeDtypeStruct((rows // LEN * heads, 1, LEN), F32),
            jax.ShapeDtypeStruct((ff, width), F32),
            jax.ShapeDtypeStruct((width, ff), F32),
            jax.ShapeDtypeStruct((local + 8, width), F32),
        ],
        scratch_shapes=[
            pltpu.VMEM((2, tile, ff), BF),
            pltpu.VMEM((2, tile, ff), F32),
            pltpu.VMEM((2, tile, ff), BF),
            pltpu.VMEM((tile, width), BF),
            pltpu.VMEM((tile, width), BF),
            pltpu.VMEM((tile, width), BF),
            pltpu.VMEM((8, 8, width), F32),
        ],
        compiler_params=params(),
        cost_estimate=pl.CostEstimate(
            flops=2 * rows * width * ff * 10 + 2 * rows * width * local * 6,
            bytes_accessed=rows * width * 20,
            transcendentals=2 * rows * ff,
        ),
        name="middle",
    )(state, timing, cot, run.reshape(rows // tile, 1, tile), mix_a, mix_b, r_a, r_b, wo_a, wo_b, wi_a, wi_b, wu_a, wu_b,
      vectors)


def attention_backward_kernel(
    core, e_in, do_in, dl_in, x_in, wq, wk, wv, gs_in, gs_out, *rest, heads, own
):
    if own:
        keep, send, gqkv, qt, kt, vaug, dq, dk, dv = rest
    else:
        qt, kt, vaug, dq, dk, dv = rest
    s, h = pl.program_id(0), pl.program_id(1)
    factor = 1.0 / math.sqrt(HEAD)
    pieces = LEN // CHUNK
    local = wq.shape[1]

    @pl.when(h == 0)
    def _():
        x = x_in[...]
        query = mm(wq[...], x, TT).astype(BF)
        key = mm(wk[...], x, TT).astype(BF)
        value = mm(x, wv[...]).astype(BF)
        lane = lane_index((LEN, 2 * HEAD))
        ones = jnp.where((lane % HEAD) < 3, 1.0, 0.0).astype(BF)
        for n in range(heads):
            mine = slice(n * HEAD, (n + 1) * HEAD)
            qt[n] = query[mine]
            kt[n] = key[mine]
            pair = value[:, (n // 2) * 128 : (n // 2) * 128 + 128]
            turned = rolled(pair)
            if n % 2 == 0:
                vaug[n, :, 0:128] = jnp.where(lane < HEAD, pair, turned)
            else:
                vaug[n, :, 0:128] = jnp.where(lane < HEAD, turned, pair)
            vaug[n, :, 128:256] = ones

    high, low = split_low(do_in[...])
    delta = -dl_in[0]
    d1 = delta.astype(BF)
    left = delta - d1.astype(F32)
    d2 = left.astype(BF)
    d3 = (left - d2.astype(F32)).astype(BF)
    index = row_index((2 * HEAD, LEN))
    tail = jnp.where(
        index == 0,
        d1.astype(F32),
        jnp.where(index == 1, d2.astype(F32), jnp.where(index == 2, d3.astype(F32), 0.0)),
    ).astype(BF)
    right = jnp.concatenate([high, low, tail], axis=0)
    query = qt[h]
    out = None
    for c in range(pieces):
        rows = slice(c * CHUNK, (c + 1) * CHUNK)
        d_probs = mm(vaug[h, rows], right)
        e = e_in[0, rows]
        d_scores = (e.astype(F32) * d_probs).astype(BF)
        dv[h, rows] = mm(e, high, NT).astype(BF)
        dk[h, rows] = (mm(d_scores, query, NT) * factor).astype(BF)
        o = mm(kt[h, :, rows], d_scores)
        out = o if out is None else out + o
    dq[pl.ds(pl.multiple_of(h * HEAD, HEAD), HEAD)] = (out * factor).astype(BF)

    @pl.when(h == heads - 1)
    def _():
        d_query = dq[...]
        d_key = jnp.concatenate([dk[n] for n in range(heads)], axis=1)
        d_value = jnp.concatenate([dv[n] for n in range(heads)], axis=1)
        total = mm(d_query, wq[...], TT)
        total = total + mm(d_key, wk[...], NT)
        total = total + mm(d_value, wv[...], NT)
        gs_out[...] = gs_in[...] + total
        if own:
            x = x_in[...]
            g1 = mm(d_query, x).T
            g2 = mm(x, jnp.concatenate([d_key, d_value], axis=1), TN)

            @pl.when(s == 0)
            def _():
                gqkv[:, :local] = g1
                gqkv[:, local:] = g2

            @pl.when(s > 0)
            def _():
                gqkv[:, :local] += g1
                gqkv[:, local:] += g2

            @pl.when(s == pl.num_programs(0) - 1)
            def _():
                half = keep.shape[0]
                keep[...] = gqkv[rows_at(core[0], half)]
                send[...] = gqkv[rows_at(1 - core[0], half)]


def attention_backward(first, seqs, core, e, do, dl, x, wq, wk, wv, gs, own):
    rows, width = x.shape
    local = wq.shape[1]
    heads = local // HEAD
    by_rows = pl.BlockSpec((LEN, width), lambda s, h: (first + s, 0))
    out_specs = [by_rows]
    out_shape = [jax.ShapeDtypeStruct((rows, width), F32)]
    scratch = []
    if own:
        out_specs += [whole((width // 2, 3 * local))] * 2
        out_shape += [jax.ShapeDtypeStruct((width // 2, 3 * local), F32)] * 2
        scratch = [pltpu.VMEM((width, 3 * local), F32)]
    return pl.pallas_call(
        functools.partial(attention_backward_kernel, heads=heads, own=own),
        grid=(seqs, heads),
        in_specs=[
            pl.BlockSpec(memory_space=pltpu.SMEM),
            pl.BlockSpec((1, LEN, LEN), lambda s, h: ((first + s) * heads + h, 0, 0)),
            pl.BlockSpec((HEAD, LEN), lambda s, h: (h, first + s)),
            pl.BlockSpec((1, 1, LEN), lambda s, h: ((first + s) * heads + h, 0, 0)),
            by_rows,
            whole((width, local)),
            whole((width, local)),
            whole((width, local)),
            by_rows,
        ],
        out_specs=out_specs,
        out_shape=out_shape,
        scratch_shapes=scratch
        + [
            pltpu.VMEM((heads, HEAD, LEN), BF),
            pltpu.VMEM((heads, HEAD, LEN), BF),
            pltpu.VMEM((heads, LEN, 256), BF),
            pltpu.VMEM((local, LEN), BF),
            pltpu.VMEM((heads, LEN, HEAD), BF),
            pltpu.VMEM((heads, LEN, HEAD), BF),
        ],
        compiler_params=params(),
        input_output_aliases={8: 0},
        cost_estimate=pl.CostEstimate(
            flops=32 * 2 * seqs * heads * LEN * LEN * HEAD, bytes_accessed=1000,
            transcendentals=0,
        ),
        name="attention_backward_own" if own else "attention_backward_other",
    )(core, e, do, dl, x, wq, wk, wv, gs)


def rows_at(index, size):
    return pl.ds(pl.multiple_of(index * size, size), size)


def local_kernel(fn, count, place, *refs):
    fn(place, refs[:count], refs[count:])


def local_call(name, fn, place, ins, outs):
    return pl.pallas_call(
        functools.partial(local_kernel, fn, len(ins)),
        in_specs=[pl.BlockSpec(memory_space=pltpu.SMEM)]
        + [pl.BlockSpec(memory_space=pltpu.VMEM)] * len(ins),
        out_specs=[pl.BlockSpec(memory_space=pltpu.VMEM)] * len(outs),
        out_shape=[jax.ShapeDtypeStruct(shape, kind) for shape, kind in outs],
        compiler_params=params(),
        name=name,
    )(place, *ins)


def cut_call(name, fn, place, ins, outs):
    return pl.pallas_call(
        functools.partial(local_kernel, fn, len(ins)),
        grid_spec=pltpu.PrefetchScalarGridSpec(
            num_scalar_prefetch=1,
            grid=(1,),
            in_specs=[
                pl.BlockSpec((v.shape[0] // 4, v.shape[1]), lambda _, p: (p[0], 0)) for v in ins
            ],
            out_specs=[pl.BlockSpec(shape, lambda _, p: (0, 0)) for shape in outs],
        ),
        out_shape=[jax.ShapeDtypeStruct(shape, F32) for shape in outs],
        compiler_params=params(),
        name=name,
    )(place, *ins)


def pack_qkv(place, ins, outs):
    local = ins[0].shape[1]
    for n, ref in enumerate(ins):
        outs[0][:, n * local : (n + 1) * local] = ref[...].astype(F32)


def pack_ff(place, ins, outs):
    wo, wi, wu = ins
    quarter, width = wi.shape[0], wo.shape[1]
    blocks = wi.shape[1] // width
    for n in range(blocks):
        outs[0][n * quarter : (n + 1) * quarter] = wi[:, n * width : (n + 1) * width].astype(F32)
    outs[0][blocks * quarter :] = wo[...].astype(F32)
    outs[1][...] = wu[...].astype(F32)


def embed_kernel(state, timing, out):
    out[...] = (state[...].astype(F32) + timing[...]).astype(BF)


def embed(state, timing):
    rows, width = state.shape
    tile = 512
    per = LEN // tile
    by_rows = pl.BlockSpec((tile, width), lambda p, s: (s * per + p, 0))
    return pl.pallas_call(
        embed_kernel,
        grid=(per, rows // LEN),
        in_specs=[by_rows, pl.BlockSpec((tile, width), lambda p, s: (p, 0))],
        out_specs=by_rows,
        out_shape=jax.ShapeDtypeStruct((rows, width), BF),
        compiler_params=params(),
        name="embed",
    )(state, timing)


def unpack_qkv(place, ins, outs):
    local = outs[0].shape[1]
    for p, ref in zip((0, 2, 1, 3), ins):
        rows = rows_at(place[p], ref.shape[0])
        for n, out in enumerate(outs):
            out[rows] = ref[:, n * local : (n + 1) * local].astype(BF)


def unpack_inner(place, ins, outs):
    wo, wi = outs
    width = wi.shape[0]
    quarter, blocks = width // 4, wi.shape[1] // width
    for p, ref in zip((0, 2, 1, 3), ins):
        rows = rows_at(place[p], quarter)
        for n in range(blocks):
            wi[rows, n * width : (n + 1) * width] = ref[
                n * quarter : (n + 1) * quarter
            ].astype(BF)
        wo[rows_at(place[p], wo.shape[0] // 4)] = ref[blocks * quarter :].astype(BF)


def unpack_outer(place, ins, outs):
    for p, ref in zip((0, 2, 1, 3), ins):
        outs[0][rows_at(place[p], ref.shape[0])] = ref[...].astype(BF)


def finish_qkv(place, ins, outs):
    local = outs[0].shape[1]
    for flip, ref in enumerate(ins):
        rows = rows_at(jnp.bitwise_xor(place[4], flip), ref.shape[0])
        for n, out in enumerate(outs):
            out[rows] = ref[:, n * local : (n + 1) * local]


def finish_ff_kernel(gu_in, gi_in, go_in, gu, gi, go, *vec):
    gu[...] = gu_in[...]
    gi[...] = gi_in[...]

    @pl.when(pl.program_id(0) == 0)
    def _():
        local = go.shape[0]
        go[...] = go_in[:local]
        for n, out in enumerate(vec):
            out[...] = go_in[local + n]


def finish_ff(gu, gi, go):
    ff, width = gu.shape
    local = go.shape[0] - 8
    steps = 4
    upper = pl.BlockSpec((ff // steps, width), lambda i: (i, 0))
    inner = pl.BlockSpec((width // steps, ff), lambda i: (i, 0))
    return pl.pallas_call(
        finish_ff_kernel,
        grid=(steps,),
        in_specs=[upper, inner, whole(go.shape)],
        out_specs=[upper, inner, whole((local, width))] + [whole((width,))] * 5,
        out_shape=[
            jax.ShapeDtypeStruct(shape, F32)
            for shape in [gu.shape, gi.shape, (local, width)] + [(width,)] * 5
        ],
        compiler_params=params(),
        name="finish_ff",
    )(gu, gi, go)


def flipped(size, even, odd):
    return [(i, i ^ (odd if i & 1 else even)) for i in range(size)]


def shards(
    dp, state, lengths, halt_mask, wq, wk, wv, wo, gain1, bias1, wi, wu, gain2, bias2,
    halt_weight, cotangent
):
    rows, width = state.shape
    local, ff = wq.shape[1], wi.shape[1]
    timing = jnp.asarray(timing_rows(width))
    me = lax.axis_index("dp").astype(jnp.int32)
    mask = np.array([3, 3, 3, 3, 1], np.int32)
    flip = np.array([0, 1, 2, 3, 0], np.int32)
    place = jnp.bitwise_xor(jnp.bitwise_and(me, mask), flip)
    bits = dp.bit_length() - 1
    tie = lax.optimization_barrier
    call = functools.partial(local_call, place=place)

    def across(v):
        return lax.ppermute(v, "mp", [(0, 1), (1, 0)])

    def along(v, even, odd=None):
        return lax.ppermute(v, "dp", flipped(dp, even, odd or even))

    quarter = width // 4
    (chunk_a,) = cut_call("pack_qkv", pack_qkv, place, (wq, wk, wv), [(quarter, 3 * local)])
    qkv0 = across(chunk_a)
    chunk_b, chunk_c = cut_call(
        "pack_ff", pack_ff, place, (wo, wi, wu),
        [(ff // 4 + local // 4, width), (ff // 4, width)],
    )
    x = embed(state, timing)
    chunk_b, x = tie((chunk_b, x))
    in0 = across(chunk_b)
    vectors = jnp.stack([gain1, bias1, gain2, bias2, halt_weight] + [gain1] * 3)
    fwd = attention_forward(0, lengths, x, wq, wk, wv)
    qkv0, chunk_c, vectors, fwd = tie((qkv0, chunk_c, vectors, fwd))
    qkv1 = along(qkv0, 2)
    out0 = across(chunk_c)
    fwd = attention_forward(1, lengths, x, wq, wk, wv, fwd)
    qkv1, in0, fwd = tie((qkv1, in0, fwd))
    qkv2, qkv3 = along(qkv0, 1), along(qkv1, 1)
    in1 = along(in0, 2)
    wq2, wk2, wv2 = call(
        "unpack_qkv", unpack_qkv, ins=(qkv0, qkv1, qkv2, qkv3),
        outs=[((width, local), BF)] * 3,
    )
    fwd2 = attention_forward(0, lengths, x, wq2, wk2, wv2)
    in1, out0, fwd2 = tie((in1, out0, fwd2))
    in2, in3 = along(in0, 1), along(in1, 1)
    out1 = along(out0, 2)
    out2 = along(out0, 1)
    fwd2 = attention_forward(1, lengths, x, wq2, wk2, wv2, fwd2)
    in2, in3, out2, fwd2 = tie((in2, in3, out2, fwd2))
    wo2, wi2 = call(
        "unpack_inner", unpack_inner, ins=(in0, in1, in2, in3),
        outs=[((local, width), BF), ((width, ff), BF)],
    )
    out1, wo2, wi2 = tie((out1, wo2, wi2))
    out3 = along(out1, 1)
    (wu2,) = call(
        "unpack_outer", unpack_outer, ins=(out0, out1, out2, out3), outs=[((ff, width), BF)]
    )
    e_a, mix_a, r_a = fwd
    e_b, mix_b, r_b = fwd2
    new_state, gs, do_a, do_b, dl_a, dl_b, *grads = middle(
        state, timing, cotangent, halt_mask, mix_a, mix_b, r_a, r_b, wo, wo2, wi, wi2, wu, wu2,
        vectors
    )

    grads = lax.psum(tuple(grads), "dp")
    own = dict(core=place[4:], e=e_a, do=do_a, dl=dl_a, x=x, wq=wq, wk=wk, wv=wv)
    other = dict(core=place[4:], e=e_b, do=do_b, dl=dl_b, x=x, wq=wq2, wk=wk2, wv=wv2)

    def attention_and_sums(carry):
        step, gs, *_ = carry
        back = attention_backward
        gs, keep, send = back(0, rows // LEN, gs=gs, own=True, **own)
        g = keep + along(send, 1)
        g, gs = tie((g, gs))
        got = along(g, 2, 4)
        (gs,) = back(0, 1, gs=gs, own=False, **other)
        got, gs = tie((got, gs))
        g = g + got
        g, gs = tie((g, gs))
        got = along(g, 4, 8)
        (gs,) = back(1, rows // LEN - 1, gs=gs, own=False, **other)
        got, gs = tie((got, gs))
        g = g + got
        g = g + along(g, 8, 2)
        for bit in range(4, bits):
            g = g + along(g, 1 << bit)
        parts = call(
            "finish_qkv", finish_qkv, ins=(g, along(g, 1)), outs=[((width, local), F32)] * 3
        )
        return (step + 1, gs, *parts)

    once = jnp.minimum(lengths[0], 1)
    empty = jnp.zeros((width, local), F32)
    _, gs, gq, gk, gv = lax.cond(
        once > 0, attention_and_sums, lambda c: c,
        (jnp.zeros_like(once), gs, empty, empty, empty),
    )
    grads, gs, gq = tie((grads, gs, gq))
    gu, gi, go, *vec = finish_ff(*grads)
    return (
        new_state, gs, gq, gk, gv, go, vec[0], vec[1], gi, gu, vec[2], vec[3], vec[4]
    )


def solution(mesh):
    rows, columns, parts = P("dp", None), P(None, "mp"), P("mp", None)
    return jax.shard_map(
        functools.partial(shards, mesh.shape["dp"]),
        mesh=mesh,
        in_specs=(
            rows, P("dp"), P("dp"), columns, columns, columns, parts, P(), P(), columns,
            parts, P(), P(), P(), rows
        ),
        out_specs=(
            rows, rows, columns, columns, columns, parts, P(), P(), columns, parts, P(), P(),
            P()
        ),
        check_vma=False,
    )
```

```python
import functools
import math

import jax
import jax.numpy as jnp
import numpy as np
from jax import lax
from jax.experimental import pallas as pl
from jax.experimental.pallas import tpu as pltpu
from jax.sharding import PartitionSpec as P

HEAD = 64
LEN = 1024
STEP = 2
LOG2E = 1.4426950408889634
BF = jnp.bfloat16
F32 = jnp.float32
NN = (((1,), (0,)), ((), ()))
NT = (((1,), (1,)), ((), ()))
TN = (((0,), (0,)), ((), ()))
TT = (((0,), (1,)), ((), ()))
VMEM_LIMIT = 60 << 20
CHUNK = 256
SUBS = 2


def mm(a, b, dims=NN):
    return lax.dot_general(a, b, dims, preferred_element_type=F32)


def params():
    return pltpu.CompilerParams(vmem_limit_bytes=VMEM_LIMIT)


def whole(shape):
    zeros = (0,) * len(shape)
    return pl.BlockSpec(shape, lambda *_: zeros)


def timing_rows(width):
    half = width // 2
    rates = np.exp(-math.log(10000.0) * np.arange(half, dtype=np.float64) / (half - 1))

    def rows(positions):
        angles = positions[:, None] * rates[None, :]
        return np.concatenate([np.sin(angles), np.cos(angles)], axis=1)

    return (rows(np.arange(LEN, dtype=np.float64)) + rows(np.array([float(STEP)]))).astype(
        np.float32
    )


def split_low(value):
    high = value.astype(BF)
    return high, (value - high.astype(F32)).astype(BF)


def rolled(pair):
    return jnp.concatenate([pair[:, HEAD:], pair[:, :HEAD]], axis=1)


def lane_index(shape):
    return lax.broadcasted_iota(jnp.int32, shape, 1)


def row_index(shape):
    return lax.broadcasted_iota(jnp.int32, shape, 0)


def attention_forward_kernel(seq, lengths, x_in, wq, wk, wv, *rest, heads):
    e_out, mixed_out, r_out, kaug, qaug, vaug, sa, sb, ma, mb = rest[-10:]
    j = pl.program_id(0)
    last = heads // 2 - 1
    pieces = LEN // CHUNK

    def score_piece(i, c, target):
        rows = slice(c * CHUNK, (c + 1) * CHUNK)
        s = mm(kaug[i, rows], qaug[i])
        target[rows] = s
        return jnp.max(s.reshape(CHUNK // 8, 8, LEN), axis=0)

    @pl.when(j == 0)
    def _():
        x = x_in[...]
        query = mm(wq[...], x, TT).astype(BF).astype(F32) * (LOG2E / math.sqrt(HEAD))
        high, rest = split_low(query)
        key = mm(x, wk[...]).astype(BF)
        value = mm(wv[...], x, TT).astype(BF)
        shape = (LEN, 2 * HEAD)
        lane = lane_index(shape)
        padded = row_index(shape) >= lengths[seq]
        mask = jnp.where(padded & ((lane == 0) | (lane == HEAD)), -1e30, 0.0).astype(BF)
        first = row_index((HEAD, LEN)) == 0
        ones = jnp.where(first, 1.0, 0.0).astype(BF)
        zeros = jnp.zeros((HEAD, LEN), BF)
        for i in range(heads):
            pair = key[:, (i // 2) * 128 : (i // 2) * 128 + 128]
            turned = rolled(pair)
            mine = slice(i * HEAD, (i + 1) * HEAD)
            kaug[i, :, 0:128] = pair
            if i % 2 == 0:
                kaug[i, :, 128:256] = jnp.where(lane < HEAD, mask, turned)
                parts = (high[mine], zeros, ones, rest[mine])
            else:
                kaug[i, :, 128:256] = jnp.where(lane < HEAD, turned, mask)
                parts = (zeros, high[mine], rest[mine], ones)
            for n, part in enumerate(parts):
                qaug[i, n * HEAD : (n + 1) * HEAD] = part
            vaug[i, 0:HEAD] = value[mine]
            vaug[i, HEAD : HEAD + 16] = jnp.ones((16, LEN), BF)
        top = None
        for c in range(pieces):
            m = score_piece(0, c, sa)
            top = m if top is None else jnp.maximum(top, m)
        ma[...] = jnp.max(top, axis=0, keepdims=True)

    def step(slot, cur, cur_m, nxt, nxt_m, ahead=True):
        i = 2 * j + slot
        shift = cur_m[...]
        top = None
        out = None
        for c in range(pieces):
            rows = slice(c * CHUNK, (c + 1) * CHUNK)
            if ahead:
                m = score_piece(i + 1, c, nxt)
                top = m if top is None else jnp.maximum(top, m)
            e = jnp.exp2(cur[rows] - shift).astype(BF)
            e_out[slot, rows] = e
            o = mm(vaug[i, :, rows], e)
            out = o if out is None else out + o
        if ahead:
            nxt_m[...] = jnp.max(top, axis=0, keepdims=True)
        r = 1.0 / out[HEAD : HEAD + 1]
        mixed_out[slot * HEAD : (slot + 1) * HEAD] = (out[:HEAD] * r).astype(BF)
        r_out[slot] = r

    step(0, sa, ma, sb, mb)

    @pl.when(j < last)
    def _():
        step(1, sb, mb, sa, ma)

    @pl.when(j == last)
    def _():
        step(1, sb, mb, sa, ma, ahead=False)


def attention_forward(seq, lengths, x, wq, wk, wv, earlier=()):
    rows, width = x.shape
    local = wq.shape[1]
    heads = local // HEAD
    steps, total = heads // 2, rows // LEN * heads
    return pl.pallas_call(
        functools.partial(attention_forward_kernel, seq, heads=heads),
        grid=(steps,),
        in_specs=[
            pl.BlockSpec(memory_space=pltpu.SMEM),
            pl.BlockSpec((LEN, width), lambda j: (seq, 0)),
            whole((width, local)),
            whole((width, local)),
            whole((width, local)),
        ]
        + [pl.BlockSpec(memory_space=pl.ANY)] * len(earlier),
        out_specs=[
            pl.BlockSpec((2, LEN, LEN), lambda j: (seq * steps + j, 0, 0)),
            pl.BlockSpec((2 * HEAD, LEN), lambda j: (j, seq)),
            pl.BlockSpec((2, 1, LEN), lambda j: (seq * steps + j, 0, 0)),
        ],
        out_shape=[
            jax.ShapeDtypeStruct((total, LEN, LEN), BF),
            jax.ShapeDtypeStruct((local, rows), BF),
            jax.ShapeDtypeStruct((total, 1, LEN), F32),
        ],
        scratch_shapes=[
            pltpu.VMEM((heads, LEN, 256), BF),
            pltpu.VMEM((heads, 256, LEN), BF),
            pltpu.VMEM((heads, HEAD + 16, LEN), BF),
            pltpu.VMEM((LEN, LEN), F32),
            pltpu.VMEM((LEN, LEN), F32),
            pltpu.VMEM((1, LEN), F32),
            pltpu.VMEM((1, LEN), F32),
        ],
        compiler_params=params(),
        input_output_aliases={5 + n: n for n in range(len(earlier))},
        cost_estimate=pl.CostEstimate(
            flops=8 * 2 * heads * LEN * LEN * HEAD,
            bytes_accessed=2 * heads * LEN * LEN,
            transcendentals=heads * LEN * LEN,
        ),
        name="attention_forward",
    )(lengths, x, wq, wk, wv, *earlier)


def row_mean(v):
    return jnp.mean(v, axis=-1, keepdims=True)


def norm_rows(v):
    centre = v - row_mean(v)
    deviation = lax.rsqrt(row_mean(centre * centre) + 1e-05)
    return centre * deviation, deviation


def norm_back(e, xhat, deviation):
    return deviation * (e - row_mean(e) - xhat * row_mean(e * xhat))


def fold_rows(v):
    return jnp.sum(v.reshape(v.shape[0] // 8, 8, v.shape[1]), axis=0)


def tile_rows(k, size):
    return slice(k * size, (k + 1) * size)


def middle_kernel(
    state, timing, cot, run, mix_a, mix_b, wo_a, wo_b, wi_a, wi_b, wu_a, wu_b, vectors,
    new_state, gs, hidden, out_low, inner_low, slope_b, xhat_out, dev_out, gu, gi,
    act, slope, low1, fold
):
    t = pl.program_id(0)
    last = pl.num_programs(0) - 1
    tile = state.shape[0]
    size = tile // SUBS
    ff = wi_a.shape[1]
    gain1, bias1, gain2, bias2, halt_w = (vectors[n : n + 1] for n in range(5))
    c0 = math.sqrt(2.0 / math.pi)
    halves = ((wi_a, wu_a), (wi_b, wu_b))
    running_column = jnp.broadcast_to(run[0].astype(F32), (8, tile)).T[:, 0:1]

    @pl.when(t == 0)
    def _():
        for ref in (gu, gi, fold):
            ref[...] = jnp.zeros(ref.shape, F32)

    def first_norm(k):
        rows = tile_rows(k, size)
        embedded = state[rows].astype(F32) + timing[rows]
        attended = mm(mix_a[:, rows], wo_a[...], TN) + mm(mix_b[:, rows], wo_b[...], TN)
        xhat1, dev1 = norm_rows(embedded + attended)
        normed1 = xhat1 * gain1 + bias1
        low1[rows] = normed1.astype(BF)
        xhat_out[rows] = xhat1
        dev_out[rows] = jnp.broadcast_to(dev1, (size, 128))
        return normed1

    def forward(k, normed1):
        rows = tile_rows(k, size)
        total = normed1
        for n, (wi, wu) in enumerate(halves):
            v = mm(low1[rows], wi[...])
            square = v * v
            h = 0.5 + 0.5 * jnp.tanh(v * (c0 + (c0 * 0.044715) * square))
            g = v * h
            low = g.astype(BF)
            d = h + g * (1.0 - h) * (2.0 * c0 + (6.0 * c0 * 0.044715) * square)
            if n == 0:
                act[rows] = low
                slope[rows] = d
            else:
                slope_b[rows] = d.astype(BF)
            total = total + mm(low, wu[...])
        return total

    def second_norm(k, hidden2):
        rows = tile_rows(k, size)
        old = state[rows].astype(F32)
        xhat2, dev2 = norm_rows(hidden2)
        block = xhat2 * gain2 + bias2
        halt = jax.nn.sigmoid(jnp.sum(block * halt_w, axis=-1, keepdims=True))
        running = running_column[rows]
        gate = running * halt
        change = block - old
        new_state[rows] = old + gate * change
        g_in = cot[rows].astype(F32)
        d_prob = running * jnp.sum(g_in * change, axis=-1, keepdims=True)
        d_logit = d_prob * halt * (1.0 - halt)
        d_block = gate * g_in + d_logit * halt_w
        fold[2] += fold_rows(d_logit * block)
        fold[0] += fold_rows(d_block * xhat2)
        fold[1] += fold_rows(d_block)
        gs[rows] = g_in * (1.0 - gate)
        d_hidden2 = norm_back(d_block * gain2, xhat2, dev2)
        out_low[rows] = d_hidden2.astype(BF)
        hidden[rows] = d_hidden2

    def backward(k):
        rows = tile_rows(k, size)
        inner_low[rows] = (mm(out_low[rows], wu_a[...], NT) * slope[rows]).astype(BF)

    normed1 = [first_norm(k) for k in range(SUBS)]
    hidden2 = {0: forward(0, normed1[0])}
    for k in range(SUBS):
        second_norm(k, hidden2[k])
        if k + 1 < SUBS:
            hidden2[k + 1] = forward(k + 1, normed1[k + 1])
    for k in range(SUBS):
        backward(k)
    gu[:ff] += mm(act[...], out_low[...], TN)
    gi[...] += mm(low1[...], inner_low[...], TN)

    @pl.when(t == last)
    def _():
        for n in range(8):
            gu[ff + n : ff + n + 1] = jnp.sum(fold[n], axis=0, keepdims=True)


def middle_back_kernel(
    hidden, out_low, inner_low, slope_b, xhat_in, dev_in, gs_in, mix_a, mix_b, r_a, r_b,
    wo_a, wo_b, wi_a, wi_b, wu_b, vectors, gs, do_a, do_b, dl_a, dl_b, go,
    inner_b, att_low, fold, *, heads
):
    t = pl.program_id(0)
    last = pl.num_programs(0) - 1
    tile = hidden.shape[0]
    size = tile // SUBS
    local = wo_a.shape[0]
    gain1 = vectors[0:1]

    @pl.when(t == 0)
    def _():
        for ref in (go, fold):
            ref[...] = jnp.zeros(ref.shape, F32)

    def backward(k):
        rows = tile_rows(k, size)
        d_act = mm(out_low[rows], wu_b[...], NT)
        inner_b[rows] = (d_act * slope_b[rows].astype(F32)).astype(BF)
        total = hidden[rows] + mm(inner_low[rows], wi_a[...], NT)
        return total + mm(inner_b[rows], wi_b[...], NT)

    def first_back(k, d_normed1):
        rows = tile_rows(k, size)
        xhat1 = xhat_in[rows]
        fold[0] += fold_rows(d_normed1 * xhat1)
        fold[1] += fold_rows(d_normed1)
        d_hidden1 = norm_back(d_normed1 * gain1, xhat1, dev_in[rows, 0:1])
        att_low[rows] = d_hidden1.astype(BF)
        gs[rows] = gs_in[rows] + d_hidden1

    d_normed1 = {0: backward(0)}
    for k in range(SUBS):
        first_back(k, d_normed1[k])
        if k + 1 < SUBS:
            d_normed1[k + 1] = backward(k + 1)
    go[:local] += mm(mix_a[...], att_low[...])
    for mix, r, wo, do, dl in (
        (mix_a, r_a, wo_a, do_a, dl_a),
        (mix_b, r_b, wo_b, do_b, dl_b),
    ):
        d_mixed = mm(wo[...], att_low[...], NT).astype(BF).astype(F32)
        for h in range(heads):
            mine = slice(h * HEAD, (h + 1) * HEAD)
            part = d_mixed[mine]
            scale = r[h]
            do[mine] = part * scale
            total = jnp.sum(part * mix[mine].astype(F32), axis=0, keepdims=True)
            dl[h] = total * scale

    @pl.when(t == last)
    def _():
        for n in range(8):
            go[local + n : local + n + 1] = jnp.sum(fold[n], axis=0, keepdims=True)


TILE = 512


def middle_specs(width, local, ff):
    per = LEN // TILE
    return (
        pl.BlockSpec((TILE, width), lambda t: (t, 0)),
        pl.BlockSpec((TILE, ff), lambda t: (t, 0)),
        pl.BlockSpec((TILE, 128), lambda t: (t, 0)),
        pl.BlockSpec((local, TILE), lambda t: (0, t)),
        pl.BlockSpec((local // HEAD, 1, TILE), lambda t: (t // per, 0, t % per)),
    )


def middle(state, timing, cot, run, mix_a, mix_b, wo_a, wo_b, wi_a, wi_b, wu_a, wu_b, vectors):
    rows, width = state.shape
    local, ff = wo_a.shape[0], wi_a.shape[1]
    per = LEN // TILE
    by_rows, by_units, by_lanes, by_columns, _ = middle_specs(width, local, ff)
    outs = [
        (by_rows, (rows, width), F32),
        (by_rows, (rows, width), F32),
        (by_rows, (rows, width), F32),
        (by_rows, (rows, width), BF),
        (by_units, (rows, ff), BF),
        (by_units, (rows, ff), BF),
        (by_rows, (rows, width), F32),
        (by_lanes, (rows, 128), F32),
        (whole((ff + 8, width)), (ff + 8, width), F32),
        (whole((width, ff)), (width, ff), F32),
    ]
    return pl.pallas_call(
        middle_kernel,
        grid=(rows // TILE,),
        in_specs=[
            by_rows,
            pl.BlockSpec((TILE, width), lambda t: (t % per, 0)),
            by_rows,
            pl.BlockSpec((1, 1, TILE), lambda t: (t, 0, 0)),
            by_columns,
            by_columns,
            whole((local, width)),
            whole((local, width)),
            whole((width, ff)),
            whole((width, ff)),
            whole((ff, width)),
            whole((ff, width)),
            whole((8, width)),
        ],
        out_specs=[spec for spec, _, _ in outs],
        out_shape=[jax.ShapeDtypeStruct(shape, kind) for _, shape, kind in outs],
        scratch_shapes=[
            pltpu.VMEM((TILE, ff), BF),
            pltpu.VMEM((TILE, ff), F32),
            pltpu.VMEM((TILE, width), BF),
            pltpu.VMEM((8, 8, width), F32),
        ],
        compiler_params=params(),
        cost_estimate=pl.CostEstimate(
            flops=2 * rows * width * ff * 7 + 2 * rows * width * local * 2,
            bytes_accessed=rows * width * 30,
            transcendentals=2 * rows * ff,
        ),
        name="middle",
    )(state, timing, cot, run.reshape(rows // TILE, 1, TILE), mix_a, mix_b, wo_a, wo_b, wi_a,
      wi_b, wu_a, wu_b, vectors)


def middle_back(hidden, out_low, inner_low, slope_b, xhat, dev, gs, mix_a, mix_b, r_a, r_b,
                wo_a, wo_b, wi_a, wi_b, wu_b, vectors):
    rows, width = hidden.shape
    local, ff = wo_a.shape[0], wi_a.shape[1]
    heads = local // HEAD
    by_rows, by_units, by_lanes, by_columns, per_head = middle_specs(width, local, ff)
    outs = [
        (by_rows, (rows, width)),
        (by_columns, (local, rows)),
        (by_columns, (local, rows)),
        (per_head, (rows // LEN * heads, 1, LEN)),
        (per_head, (rows // LEN * heads, 1, LEN)),
        (whole((local + 8, width)), (local + 8, width)),
    ]
    return pl.pallas_call(
        functools.partial(middle_back_kernel, heads=heads),
        grid=(rows // TILE,),
        in_specs=[
            by_rows,
            by_rows,
            by_units,
            by_units,
            by_rows,
            by_lanes,
            by_rows,
            by_columns,
            by_columns,
            per_head,
            per_head,
            whole((local, width)),
            whole((local, width)),
            whole((width, ff)),
            whole((width, ff)),
            whole((ff, width)),
            whole((8, width)),
        ],
        out_specs=[spec for spec, _ in outs],
        out_shape=[jax.ShapeDtypeStruct(shape, F32) for _, shape in outs],
        scratch_shapes=[
            pltpu.VMEM((TILE, ff), BF),
            pltpu.VMEM((TILE, width), BF),
            pltpu.VMEM((8, 8, width), F32),
        ],
        compiler_params=params(),
        input_output_aliases={6: 0},
        cost_estimate=pl.CostEstimate(
            flops=2 * rows * width * ff * 3 + 2 * rows * width * local * 3,
            bytes_accessed=rows * width * 30,
            transcendentals=0,
        ),
        name="middle_back",
    )(hidden, out_low, inner_low, slope_b, xhat, dev, gs, mix_a, mix_b, r_a, r_b, wo_a, wo_b,
      wi_a, wi_b, wu_b, vectors)


def attention_backward_kernel(
    core, e_in, do_in, dl_in, x_in, wq, wk, wv, gs_in, *rest, heads, own
):
    if own:
        go, gs_out, keep, send, gqkv, qt, kt, vaug, dq, dk, dv = rest
    else:
        gs_out, qt, kt, vaug, dq, dk, dv = rest
    s, h = pl.program_id(0), pl.program_id(1)
    factor = 1.0 / math.sqrt(HEAD)
    pieces = LEN // CHUNK
    local = wq.shape[1]

    @pl.when(h == 0)
    def _():
        x = x_in[...]
        query = mm(wq[...], x, TT).astype(BF)
        key = mm(wk[...], x, TT).astype(BF)
        value = mm(x, wv[...]).astype(BF)
        lane = lane_index((LEN, 2 * HEAD))
        ones = jnp.where((lane % HEAD) < 3, 1.0, 0.0).astype(BF)
        for n in range(heads):
            mine = slice(n * HEAD, (n + 1) * HEAD)
            qt[n] = query[mine]
            kt[n] = key[mine]
            pair = value[:, (n // 2) * 128 : (n // 2) * 128 + 128]
            turned = rolled(pair)
            if n % 2 == 0:
                vaug[n, :, 0:128] = jnp.where(lane < HEAD, pair, turned)
            else:
                vaug[n, :, 0:128] = jnp.where(lane < HEAD, turned, pair)
            vaug[n, :, 128:256] = ones

    high, low = split_low(do_in[...])
    delta = -dl_in[0]
    d1 = delta.astype(BF)
    left = delta - d1.astype(F32)
    d2 = left.astype(BF)
    d3 = (left - d2.astype(F32)).astype(BF)
    index = row_index((2 * HEAD, LEN))
    tail = jnp.where(
        index == 0,
        d1.astype(F32),
        jnp.where(index == 1, d2.astype(F32), jnp.where(index == 2, d3.astype(F32), 0.0)),
    ).astype(BF)
    right = jnp.concatenate([high, low, tail], axis=0)
    query = qt[h]
    out = None
    for c in range(pieces):
        rows = slice(c * CHUNK, (c + 1) * CHUNK)
        d_probs = mm(vaug[h, rows], right)
        e = e_in[0, rows]
        d_scores = (e.astype(F32) * d_probs).astype(BF)
        dv[h, rows] = mm(e, high, NT).astype(BF)
        dk[h, rows] = (mm(d_scores, query, NT) * factor).astype(BF)
        o = mm(kt[h, :, rows], d_scores)
        out = o if out is None else out + o
    dq[pl.ds(pl.multiple_of(h * HEAD, HEAD), HEAD)] = (out * factor).astype(BF)

    @pl.when(h == heads - 1)
    def _():
        d_query = dq[...]
        d_key = jnp.concatenate([dk[n] for n in range(heads)], axis=1)
        d_value = jnp.concatenate([dv[n] for n in range(heads)], axis=1)
        total = mm(d_query, wq[...], TT)
        total = total + mm(d_key, wk[...], NT)
        total = total + mm(d_value, wv[...], NT)
        gs_out[...] = gs_in[...] + total
        if own:
            x = x_in[...]
            g1 = mm(d_query, x).T
            g2 = mm(x, jnp.concatenate([d_key, d_value], axis=1), TN)

            @pl.when(s == 0)
            def _():
                gqkv[:, :local] = g1
                gqkv[:, local:] = g2

            @pl.when(s > 0)
            def _():
                gqkv[:, :local] += g1
                gqkv[:, local:] += g2

            @pl.when(s == pl.num_programs(0) - 1)
            def _():
                half, quarter = gqkv.shape[0] // 2, local // 2
                wide, width = gqkv.shape[1], go.shape[1]
                for place, out in ((core[0], keep), (1 - core[0], send)):
                    out[:half, :wide] = gqkv[rows_at(place, half)]
                    few = go[rows_at(place, quarter)]
                    out[:quarter, wide:] = few[:, : width // 2]
                    out[quarter:half, wide:] = few[:, width // 2 :]
                    out[half:, :width] = go[local:]
                    out[half:, width:] = jnp.zeros((8, out.shape[1] - width), F32)


def attention_backward(first, seqs, core, e, do, dl, x, wq, wk, wv, gs, go=None):
    own = go is not None
    rows, width = x.shape
    local = wq.shape[1]
    heads = local // HEAD
    by_rows = pl.BlockSpec((LEN, width), lambda s, h: (first + s, 0))
    out_specs = [by_rows]
    out_shape = [jax.ShapeDtypeStruct((rows, width), F32)]
    scratch = []
    if own:
        both = (width // 2 + 8, 3 * local + width // 2)
        out_specs += [whole(both)] * 2
        out_shape += [jax.ShapeDtypeStruct(both, F32)] * 2
        scratch = [pltpu.VMEM((width, 3 * local), F32)]
    return pl.pallas_call(
        functools.partial(attention_backward_kernel, heads=heads, own=own),
        grid=(seqs, heads),
        in_specs=[
            pl.BlockSpec(memory_space=pltpu.SMEM),
            pl.BlockSpec((1, LEN, LEN), lambda s, h: ((first + s) * heads + h, 0, 0)),
            pl.BlockSpec((HEAD, LEN), lambda s, h: (h, first + s)),
            pl.BlockSpec((1, 1, LEN), lambda s, h: ((first + s) * heads + h, 0, 0)),
            by_rows,
            whole((width, local)),
            whole((width, local)),
            whole((width, local)),
            by_rows,
        ]
        + ([whole(go.shape)] if own else []),
        out_specs=out_specs,
        out_shape=out_shape,
        scratch_shapes=scratch
        + [
            pltpu.VMEM((heads, HEAD, LEN), BF),
            pltpu.VMEM((heads, HEAD, LEN), BF),
            pltpu.VMEM((heads, LEN, 256), BF),
            pltpu.VMEM((local, LEN), BF),
            pltpu.VMEM((heads, LEN, HEAD), BF),
            pltpu.VMEM((heads, LEN, HEAD), BF),
        ],
        compiler_params=params(),
        input_output_aliases={8: 0},
        cost_estimate=pl.CostEstimate(
            flops=32 * 2 * seqs * heads * LEN * LEN * HEAD, bytes_accessed=1000,
            transcendentals=0,
        ),
        name="attention_backward_own" if own else "attention_backward_other",
    )(core, e, do, dl, x, wq, wk, wv, gs, *([go] if own else []))


def rows_at(index, size):
    return pl.ds(pl.multiple_of(index * size, size), size)


def local_kernel(fn, count, place, *refs):
    fn(place, refs[:count], refs[count:])


def local_call(name, fn, place, ins, outs):
    return pl.pallas_call(
        functools.partial(local_kernel, fn, len(ins)),
        in_specs=[pl.BlockSpec(memory_space=pltpu.SMEM)]
        + [pl.BlockSpec(memory_space=pltpu.VMEM)] * len(ins),
        out_specs=[pl.BlockSpec(memory_space=pltpu.VMEM)] * len(outs),
        out_shape=[jax.ShapeDtypeStruct(shape, kind) for shape, kind in outs],
        compiler_params=params(),
        name=name,
    )(place, *ins)


def cut_call(name, fn, place, ins, outs):
    return pl.pallas_call(
        functools.partial(local_kernel, fn, len(ins)),
        grid_spec=pltpu.PrefetchScalarGridSpec(
            num_scalar_prefetch=1,
            grid=(1,),
            in_specs=[
                pl.BlockSpec((v.shape[0] // 4, v.shape[1]), lambda _, p: (p[0], 0)) for v in ins
            ],
            out_specs=[pl.BlockSpec(shape, lambda _, p: (0, 0)) for shape in outs],
        ),
        out_shape=[jax.ShapeDtypeStruct(shape, F32) for shape in outs],
        compiler_params=params(),
        name=name,
    )(place, *ins)


def pack_qkv(place, ins, outs):
    local = ins[0].shape[1]
    for n, ref in enumerate(ins):
        outs[0][:, n * local : (n + 1) * local] = ref[...].astype(F32)


def pack_ff(place, ins, outs):
    wo, wi, wu = ins
    quarter, width = wi.shape[0], wo.shape[1]
    blocks = wi.shape[1] // width
    for n in range(blocks):
        outs[0][n * quarter : (n + 1) * quarter] = wi[:, n * width : (n + 1) * width].astype(F32)
    outs[0][blocks * quarter :] = wo[...].astype(F32)
    outs[1][...] = wu[...].astype(F32)


def embed_kernel(state, timing, out):
    out[...] = (state[...].astype(F32) + timing[...]).astype(BF)


def embed(state, timing):
    rows, width = state.shape
    tile = 512
    per = LEN // tile
    by_rows = pl.BlockSpec((tile, width), lambda p, s: (s * per + p, 0))
    return pl.pallas_call(
        embed_kernel,
        grid=(per, rows // LEN),
        in_specs=[by_rows, pl.BlockSpec((tile, width), lambda p, s: (p, 0))],
        out_specs=by_rows,
        out_shape=jax.ShapeDtypeStruct((rows, width), BF),
        compiler_params=params(),
        name="embed",
    )(state, timing)


def unpack_qkv(place, ins, outs):
    local = outs[0].shape[1]
    for p, ref in zip((0, 2, 1, 3), ins):
        rows = rows_at(place[p], ref.shape[0])
        for n, out in enumerate(outs):
            out[rows] = ref[:, n * local : (n + 1) * local].astype(BF)


def unpack_inner(place, ins, outs):
    wo, wi = outs
    width = wi.shape[0]
    quarter, blocks = width // 4, wi.shape[1] // width
    for p, ref in zip((0, 2, 1, 3), ins):
        rows = rows_at(place[p], quarter)
        for n in range(blocks):
            wi[rows, n * width : (n + 1) * width] = ref[
                n * quarter : (n + 1) * quarter
            ].astype(BF)
        wo[rows_at(place[p], wo.shape[0] // 4)] = ref[blocks * quarter :].astype(BF)


def unpack_outer(place, ins, outs):
    for p, ref in zip((0, 2, 1, 3), ins):
        outs[0][rows_at(place[p], ref.shape[0])] = ref[...].astype(BF)


def finish_qkv(place, ins, outs):
    gq, gk, gv, go, *vec = outs
    width, local = gq.shape
    half, few, wide = width // 2, local // 2, 3 * local
    for flip, ref in enumerate(ins):
        core = jnp.bitwise_xor(place[4], flip)
        for n, out in enumerate((gq, gk, gv)):
            out[rows_at(core, half)] = ref[:half, n * local : (n + 1) * local]
        go[rows_at(core, few), : width // 2] = ref[:few, wide:]
        go[rows_at(core, few), width // 2 :] = ref[few:half, wide:]
    for n, out in enumerate(vec):
        out[...] = ins[0][half + n, :width]


def finish_ff_kernel(gu_in, vec_in, gi_in, gu, gi, *vec):
    gu[...] = gu_in[...]
    gi[...] = gi_in[...]

    @pl.when(pl.program_id(0) == 0)
    def _():
        for n, out in enumerate(vec):
            out[...] = vec_in[n]


def finish_ff(gu, gi):
    width, ff = gi.shape
    steps = 4
    upper = pl.BlockSpec((ff // steps, width), lambda i: (i, 0))
    inner = pl.BlockSpec((width // steps, ff), lambda i: (i, 0))
    return pl.pallas_call(
        finish_ff_kernel,
        grid=(steps,),
        in_specs=[upper, pl.BlockSpec((8, width), lambda i: (ff // 8, 0)), inner],
        out_specs=[upper, inner] + [whole((width,))] * 3,
        out_shape=[
            jax.ShapeDtypeStruct(shape, F32)
            for shape in [(ff, width), (width, ff)] + [(width,)] * 3
        ],
        compiler_params=params(),
        name="finish_ff",
    )(gu, gu, gi)


def flipped(size, even, odd):
    return [(i, i ^ (odd if i & 1 else even)) for i in range(size)]


def shards(
    dp, state, lengths, halt_mask, wq, wk, wv, wo, gain1, bias1, wi, wu, gain2, bias2,
    halt_weight, cotangent
):
    rows, width = state.shape
    local, ff = wq.shape[1], wi.shape[1]
    timing = jnp.asarray(timing_rows(width))
    me = lax.axis_index("dp").astype(jnp.int32)
    mask = np.array([3, 3, 3, 3, 1], np.int32)
    flip = np.array([0, 1, 2, 3, 0], np.int32)
    place = jnp.bitwise_xor(jnp.bitwise_and(me, mask), flip)
    bits = dp.bit_length() - 1
    tie = lax.optimization_barrier
    call = functools.partial(local_call, place=place)

    def across(v):
        return lax.ppermute(v, "mp", [(0, 1), (1, 0)])

    def along(v, even, odd=None):
        return lax.ppermute(v, "dp", flipped(dp, even, odd or even))

    quarter = width // 4
    (chunk_a,) = cut_call("pack_qkv", pack_qkv, place, (wq, wk, wv), [(quarter, 3 * local)])
    qkv0 = across(chunk_a)
    chunk_b, chunk_c = cut_call(
        "pack_ff", pack_ff, place, (wo, wi, wu),
        [(ff // 4 + local // 4, width), (ff // 4, width)],
    )
    x = embed(state, timing)
    chunk_b, x = tie((chunk_b, x))
    in0 = across(chunk_b)
    vectors = jnp.stack([gain1, bias1, gain2, bias2, halt_weight] + [gain1] * 3)
    fwd = attention_forward(0, lengths, x, wq, wk, wv)
    qkv0, chunk_c, vectors, fwd = tie((qkv0, chunk_c, vectors, fwd))
    qkv1 = along(qkv0, 2)
    out0 = across(chunk_c)
    fwd = attention_forward(1, lengths, x, wq, wk, wv, fwd)
    qkv1, in0, fwd = tie((qkv1, in0, fwd))
    qkv2, qkv3 = along(qkv0, 1), along(qkv1, 1)
    in1 = along(in0, 2)
    wq2, wk2, wv2 = call(
        "unpack_qkv", unpack_qkv, ins=(qkv0, qkv1, qkv2, qkv3),
        outs=[((width, local), BF)] * 3,
    )
    fwd2 = attention_forward(0, lengths, x, wq2, wk2, wv2)
    in1, out0, fwd2 = tie((in1, out0, fwd2))
    in2, in3 = along(in0, 1), along(in1, 1)
    out1 = along(out0, 2)
    out2 = along(out0, 1)
    fwd2 = attention_forward(1, lengths, x, wq2, wk2, wv2, fwd2)
    in2, in3, out2, fwd2 = tie((in2, in3, out2, fwd2))
    wo2, wi2 = call(
        "unpack_inner", unpack_inner, ins=(in0, in1, in2, in3),
        outs=[((local, width), BF), ((width, ff), BF)],
    )
    out1, wo2, wi2 = tie((out1, wo2, wi2))
    out3 = along(out1, 1)
    (wu2,) = call(
        "unpack_outer", unpack_outer, ins=(out0, out1, out2, out3), outs=[((ff, width), BF)]
    )
    e_a, mix_a, r_a = fwd
    e_b, mix_b, r_b = fwd2
    new_state, gs, hidden, out_low, inner_low, slope_b, xhat, dev, *grads = middle(
        state, timing, cotangent, halt_mask, mix_a, mix_b, wo, wo2, wi, wi2, wu, wu2, vectors
    )

    grads = lax.psum(tuple(grads), "dp")

    def rest(carry):
        step, gs, *_ = carry
        gs, do_a, do_b, dl_a, dl_b, go = middle_back(
            hidden, out_low, inner_low, slope_b, xhat, dev, gs, mix_a, mix_b, r_a, r_b, wo,
            wo2, wi, wi2, wu2, vectors
        )
        place_core = place[4:]
        other = dict(core=place_core, e=e_b, do=do_b, dl=dl_b, x=x, wq=wq2, wk=wk2, wv=wv2)
        gs, keep, send = attention_backward(
            0, rows // LEN, place_core, e_a, do_a, dl_a, x, wq, wk, wv, gs, go
        )
        g = keep + along(send, 1)
        g, gs = tie((g, gs))
        got = along(g, 8, 2)
        (gs,) = attention_backward(0, 1, gs=gs, **other)
        got, gs = tie((got, gs))
        g = g + got
        g, gs = tie((g, gs))
        got = along(g, 4, 8)
        (gs,) = attention_backward(1, rows // LEN - 1, gs=gs, **other)
        got, gs = tie((got, gs))
        g = g + got
        g = g + along(g, 2, 4)
        for bit in range(4, bits):
            g = g + along(g, 1 << bit)
        parts = call("finish_qkv", finish_qkv, ins=(g, along(g, 1)), outs=finals)
        return (step + 1, gs, *parts)

    finals = [((width, local), F32)] * 3 + [((local, width), F32)] + [((width,), F32)] * 2
    once = jnp.minimum(lengths[0], 1)
    _, gs, gq, gk, gv, go, gain1_sum, bias1_sum = lax.cond(
        once > 0, rest, lambda c: c,
        (jnp.zeros_like(once), gs, *[jnp.zeros(shape, F32) for shape, _ in finals]),
    )
    grads, gs, gq = tie((grads, gs, gq))
    gu, gi, gain2_sum, bias2_sum, halt_sum = finish_ff(*grads)
    return (
        new_state, gs, gq, gk, gv, go, gain1_sum, bias1_sum, gi, gu, gain2_sum, bias2_sum,
        halt_sum
    )


def solution(mesh):
    rows, columns, parts = P("dp", None), P(None, "mp"), P("mp", None)
    return jax.shard_map(
        functools.partial(shards, mesh.shape["dp"]),
        mesh=mesh,
        in_specs=(
            rows, P("dp"), P("dp"), columns, columns, columns, parts, P(), P(), columns,
            parts, P(), P(), P(), rows
        ),
        out_specs=(
            rows, rows, columns, columns, columns, parts, P(), P(), columns, parts, P(), P(),
            P()
        ),
        check_vma=False,
    )
```

```python
import functools
import math

import jax
import jax.numpy as jnp
import numpy as np
from jax import lax
from jax.experimental import pallas as pl
from jax.experimental.pallas import tpu as pltpu
from jax.sharding import PartitionSpec as P

HEAD = 64
LEN = 1024
STEP = 2
LOG2E = 1.4426950408889634
BF = jnp.bfloat16
F32 = jnp.float32
NN = (((1,), (0,)), ((), ()))
NT = (((1,), (1,)), ((), ()))
TN = (((0,), (0,)), ((), ()))
TT = (((0,), (1,)), ((), ()))
VMEM_LIMIT = 60 << 20
CHUNK = 256
SUBS = 2


def mm(a, b, dims=NN):
    return lax.dot_general(a, b, dims, preferred_element_type=F32)


def params():
    return pltpu.CompilerParams(vmem_limit_bytes=VMEM_LIMIT)


def whole(shape):
    zeros = (0,) * len(shape)
    return pl.BlockSpec(shape, lambda *_: zeros)


def timing_rows(width):
    half = width // 2
    rates = np.exp(-math.log(10000.0) * np.arange(half, dtype=np.float64) / (half - 1))

    def rows(positions):
        angles = positions[:, None] * rates[None, :]
        return np.concatenate([np.sin(angles), np.cos(angles)], axis=1)

    return (rows(np.arange(LEN, dtype=np.float64)) + rows(np.array([float(STEP)]))).astype(
        np.float32
    )


def split_low(value):
    high = value.astype(BF)
    return high, (value - high.astype(F32)).astype(BF)


def rolled(pair):
    return jnp.concatenate([pair[:, HEAD:], pair[:, :HEAD]], axis=1)


def lane_index(shape):
    return lax.broadcasted_iota(jnp.int32, shape, 1)


def row_index(shape):
    return lax.broadcasted_iota(jnp.int32, shape, 0)


def attention_forward_kernel(seq, lengths, x_in, wq, wk, wv, *rest, heads):
    e_out, mixed_out, r_out, kaug, qaug, vaug, sa, sb, ma, mb = rest[-10:]
    j = pl.program_id(0)
    last = heads // 2 - 1
    pieces = LEN // CHUNK

    def score_piece(i, c, target):
        rows = slice(c * CHUNK, (c + 1) * CHUNK)
        s = mm(kaug[i, rows], qaug[i])
        target[rows] = s
        return jnp.max(s.reshape(CHUNK // 8, 8, LEN), axis=0)

    @pl.when(j == 0)
    def _():
        x = x_in[...]
        query = mm(wq[...], x, TT).astype(BF).astype(F32) * (LOG2E / math.sqrt(HEAD))
        high, rest = split_low(query)
        key = mm(x, wk[...]).astype(BF)
        value = mm(wv[...], x, TT).astype(BF)
        shape = (LEN, 2 * HEAD)
        lane = lane_index(shape)
        padded = row_index(shape) >= lengths[seq]
        mask = jnp.where(padded & ((lane == 0) | (lane == HEAD)), -1e30, 0.0).astype(BF)
        first = row_index((HEAD, LEN)) == 0
        ones = jnp.where(first, 1.0, 0.0).astype(BF)
        zeros = jnp.zeros((HEAD, LEN), BF)
        for i in range(heads):
            pair = key[:, (i // 2) * 128 : (i // 2) * 128 + 128]
            turned = rolled(pair)
            mine = slice(i * HEAD, (i + 1) * HEAD)
            kaug[i, :, 0:128] = pair
            if i % 2 == 0:
                kaug[i, :, 128:256] = jnp.where(lane < HEAD, mask, turned)
                parts = (high[mine], zeros, ones, rest[mine])
            else:
                kaug[i, :, 128:256] = jnp.where(lane < HEAD, turned, mask)
                parts = (zeros, high[mine], rest[mine], ones)
            for n, part in enumerate(parts):
                qaug[i, n * HEAD : (n + 1) * HEAD] = part
            vaug[i, 0:HEAD] = value[mine]
            vaug[i, HEAD : HEAD + 16] = jnp.ones((16, LEN), BF)
        top = None
        for c in range(pieces):
            m = score_piece(0, c, sa)
            top = m if top is None else jnp.maximum(top, m)
        ma[...] = jnp.max(top, axis=0, keepdims=True)

    def step(slot, cur, cur_m, nxt, nxt_m, ahead=True):
        i = 2 * j + slot
        shift = cur_m[...]
        top = None
        out = None
        for c in range(pieces):
            rows = slice(c * CHUNK, (c + 1) * CHUNK)
            if ahead:
                m = score_piece(i + 1, c, nxt)
                top = m if top is None else jnp.maximum(top, m)
            e = jnp.exp2(cur[rows] - shift).astype(BF)
            e_out[slot, rows] = e
            o = mm(vaug[i, :, rows], e)
            out = o if out is None else out + o
        if ahead:
            nxt_m[...] = jnp.max(top, axis=0, keepdims=True)
        r = 1.0 / out[HEAD : HEAD + 1]
        mixed_out[slot * HEAD : (slot + 1) * HEAD] = (out[:HEAD] * r).astype(BF)
        r_out[slot] = r

    step(0, sa, ma, sb, mb)

    @pl.when(j < last)
    def _():
        step(1, sb, mb, sa, ma)

    @pl.when(j == last)
    def _():
        step(1, sb, mb, sa, ma, ahead=False)


def attention_forward(seq, lengths, x, wq, wk, wv, earlier=()):
    rows, width = x.shape
    local = wq.shape[1]
    heads = local // HEAD
    steps, total = heads // 2, rows // LEN * heads
    return pl.pallas_call(
        functools.partial(attention_forward_kernel, seq, heads=heads),
        grid=(steps,),
        in_specs=[
            pl.BlockSpec(memory_space=pltpu.SMEM),
            pl.BlockSpec((LEN, width), lambda j: (seq, 0)),
            whole((width, local)),
            whole((width, local)),
            whole((width, local)),
        ]
        + [pl.BlockSpec(memory_space=pl.ANY)] * len(earlier),
        out_specs=[
            pl.BlockSpec((2, LEN, LEN), lambda j: (seq * steps + j, 0, 0)),
            pl.BlockSpec((2 * HEAD, LEN), lambda j: (j, seq)),
            pl.BlockSpec((2, 1, LEN), lambda j: (seq * steps + j, 0, 0)),
        ],
        out_shape=[
            jax.ShapeDtypeStruct((total, LEN, LEN), BF),
            jax.ShapeDtypeStruct((local, rows), BF),
            jax.ShapeDtypeStruct((total, 1, LEN), F32),
        ],
        scratch_shapes=[
            pltpu.VMEM((heads, LEN, 256), BF),
            pltpu.VMEM((heads, 256, LEN), BF),
            pltpu.VMEM((heads, HEAD + 16, LEN), BF),
            pltpu.VMEM((LEN, LEN), F32),
            pltpu.VMEM((LEN, LEN), F32),
            pltpu.VMEM((1, LEN), F32),
            pltpu.VMEM((1, LEN), F32),
        ],
        compiler_params=params(),
        input_output_aliases={5 + n: n for n in range(len(earlier))},
        cost_estimate=pl.CostEstimate(
            flops=8 * 2 * heads * LEN * LEN * HEAD,
            bytes_accessed=2 * heads * LEN * LEN,
            transcendentals=heads * LEN * LEN,
        ),
        name="attention_forward",
    )(lengths, x, wq, wk, wv, *earlier)


def row_mean(v):
    return jnp.mean(v, axis=-1, keepdims=True)


def norm_rows(v):
    centre = v - row_mean(v)
    deviation = lax.rsqrt(row_mean(centre * centre) + 1e-05)
    return centre * deviation, deviation


def norm_back(e, xhat, deviation):
    return deviation * (e - row_mean(e) - xhat * row_mean(e * xhat))


def fold_rows(v):
    return jnp.sum(v.reshape(v.shape[0] // 8, 8, v.shape[1]), axis=0)


def unpack(place, inner, outer, wo, wi, wu):
    width = wi.shape[0]
    quarter, blocks = width // 4, wi.shape[1] // width
    for p, ref, more in zip((0, 2, 1, 3), inner, outer):
        rows = rows_at(place[p], quarter)
        for n in range(blocks):
            columns = slice(n * width, (n + 1) * width)
            wi[rows, columns] = ref[n * quarter : (n + 1) * quarter].astype(BF)
        wo[rows_at(place[p], wo.shape[0] // 4)] = ref[blocks * quarter :].astype(BF)
        wu[rows_at(place[p], more.shape[0])] = more[...].astype(BF)


def middle_kernel(
    place, state, timing, cot, run, mix_a, mix_b, r_a, r_b, wo_a, wi_a, wu_a, v0, v1, v2, v3,
    v4, i0, i1, i2, i3, o0, o1, o2, o3, new_state, gs, do_a, do_b, dl_a, dl_b, gu, gi, go, act,
    slope, inner_low, low1, out_low, att_low, fold, wo_b, wi_b, wu_b, *, heads
):
    t = pl.program_id(0)
    last = pl.num_programs(0) - 1
    tile = state.shape[0]
    size = tile // SUBS
    local = wo_a.shape[0]
    gain1, bias1, gain2, bias2, halt_w = (v[...].reshape(1, -1) for v in (v0, v1, v2, v3, v4))
    c0 = math.sqrt(2.0 / math.pi)
    halves = ((wi_a, wu_a), (wi_b, wu_b))
    running_column = jnp.broadcast_to(run[0].astype(F32), (8, tile)).T[:, 0:1]

    @pl.when(t == 0)
    def _():
        for ref in (gu, gi, go, fold):
            ref[...] = jnp.zeros(ref.shape, F32)
        unpack(place, (i0, i1, i2, i3), (o0, o1, o2, o3), wo_b, wi_b, wu_b)

    def first_norm(k):
        rows = slice(k * size, (k + 1) * size)
        embedded = state[rows].astype(F32) + timing[rows]
        attended = mm(mix_a[:, rows], wo_a[...], TN) + mm(mix_b[:, rows], wo_b[...], TN)
        xhat1, dev1 = norm_rows(embedded + attended)
        normed1 = xhat1 * gain1 + bias1
        low1[rows] = normed1.astype(BF)
        return xhat1, dev1, normed1

    def forward(k, normed1):
        rows = slice(k * size, (k + 1) * size)
        total = normed1
        for n, (wi, wu) in enumerate(halves):
            v = mm(low1[rows], wi[...])
            square = v * v
            h = 0.5 + 0.5 * jnp.tanh(v * (c0 + (c0 * 0.044715) * square))
            g = v * h
            act[n, rows] = g.astype(BF)
            slope[n, rows] = h + g * (1.0 - h) * (2.0 * c0 + (6.0 * c0 * 0.044715) * square)
            total = total + mm(act[n, rows], wu[...])
        return total

    def second_norm(k, hidden2):
        rows = slice(k * size, (k + 1) * size)
        old = state[rows].astype(F32)
        xhat2, dev2 = norm_rows(hidden2)
        block = xhat2 * gain2 + bias2
        halt = jax.nn.sigmoid(jnp.sum(block * halt_w, axis=-1, keepdims=True))
        running = running_column[rows]
        gate = running * halt
        change = block - old
        new_state[rows] = old + gate * change
        g_in = cot[rows].astype(F32)
        d_prob = running * jnp.sum(g_in * change, axis=-1, keepdims=True)
        d_logit = d_prob * halt * (1.0 - halt)
        d_block = gate * g_in + d_logit * halt_w
        fold[4] += fold_rows(d_logit * block)
        fold[2] += fold_rows(d_block * xhat2)
        fold[3] += fold_rows(d_block)
        gs[rows] = g_in * (1.0 - gate)
        d_hidden2 = norm_back(d_block * gain2, xhat2, dev2)
        out_low[rows] = d_hidden2.astype(BF)
        return d_hidden2

    def backward(k, d_hidden2):
        rows = slice(k * size, (k + 1) * size)
        total = d_hidden2
        for n, (wi, wu) in enumerate(halves):
            d_act = mm(out_low[rows], wu[...], NT)
            inner_low[n, rows] = (d_act * slope[n, rows]).astype(BF)
            total = total + mm(inner_low[n, rows], wi[...], NT)
        return total

    def first_back(k, d_normed1, xhat1, dev1):
        rows = slice(k * size, (k + 1) * size)
        fold[0] += fold_rows(d_normed1 * xhat1)
        fold[1] += fold_rows(d_normed1)
        d_hidden1 = norm_back(d_normed1 * gain1, xhat1, dev1)
        att_low[rows] = d_hidden1.astype(BF)
        gs[rows] += d_hidden1

    def mixed_back():
        for mix, r, wo, do, dl in (
            (mix_a, r_a, wo_a, do_a, dl_a),
            (mix_b, r_b, wo_b, do_b, dl_b),
        ):
            d_mixed = mm(wo[...], att_low[...], NT).astype(BF).astype(F32)
            for h in range(heads):
                mine = slice(h * HEAD, (h + 1) * HEAD)
                part = d_mixed[mine]
                scale = r[h]
                do[mine] = part * scale
                total = jnp.sum(part * mix[mine].astype(F32), axis=0, keepdims=True)
                dl[h] = total * scale

    ks = range(SUBS)
    firsts = [first_norm(k) for k in ks]
    hidden2 = {0: forward(0, firsts[0][2])}
    d_hidden2, d_normed1 = {}, {}
    for k in ks:
        d_hidden2[k] = second_norm(k, hidden2[k])
        if k + 1 < SUBS:
            hidden2[k + 1] = forward(k + 1, firsts[k + 1][2])
    d_normed1[0] = backward(0, d_hidden2[0])
    for k in ks:
        first_back(k, d_normed1[k], *firsts[k][:2])
        if k + 1 < SUBS:
            d_normed1[k + 1] = backward(k + 1, d_hidden2[k + 1])
    gu[...] += mm(act[0], out_low[...], TN)
    gi[...] += mm(low1[...], inner_low[0], TN)
    go[:local] += mm(mix_a[...], att_low[...])
    mixed_back()

    @pl.when(t == last)
    def _():
        for n in range(8):
            go[local + n : local + n + 1] = jnp.sum(fold[n], axis=0, keepdims=True)


def middle(place, state, timing, cot, run, mix_a, mix_b, r_a, r_b, wo_a, wi_a, wu_a, vectors,
           inner, outer):
    rows, width = state.shape
    local, ff = wo_a.shape[0], wi_a.shape[1]
    heads = local // HEAD
    tile = 512
    per = LEN // tile
    by_rows = pl.BlockSpec((tile, width), lambda t: (t, 0))
    by_columns = pl.BlockSpec((local, tile), lambda t: (0, t))
    per_head = pl.BlockSpec((heads, 1, tile), lambda t: (t // per, 0, t % per))
    return pl.pallas_call(
        functools.partial(middle_kernel, heads=heads),
        grid=(rows // tile,),
        in_specs=[
            pl.BlockSpec(memory_space=pltpu.SMEM),
            by_rows,
            pl.BlockSpec((tile, width), lambda t: (t % per, 0)),
            by_rows,
            pl.BlockSpec((1, 1, tile), lambda t: (t, 0, 0)),
            by_columns,
            by_columns,
            per_head,
            per_head,
            whole((local, width)),
            whole((width, ff)),
            whole((ff, width)),
        ]
        + [whole((width,))] * 5
        + [whole(v.shape) for v in (*inner, *outer)],
        out_specs=[
            by_rows,
            by_rows,
            by_columns,
            by_columns,
            per_head,
            per_head,
            whole((ff, width)),
            whole((width, ff)),
            whole((local + 8, width)),
        ],
        out_shape=[
            jax.ShapeDtypeStruct((rows, width), F32),
            jax.ShapeDtypeStruct((rows, width), F32),
            jax.ShapeDtypeStruct((local, rows), F32),
            jax.ShapeDtypeStruct((local, rows), F32),
            jax.ShapeDtypeStruct((rows // LEN * heads, 1, LEN), F32),
            jax.ShapeDtypeStruct((rows // LEN * heads, 1, LEN), F32),
            jax.ShapeDtypeStruct((ff, width), F32),
            jax.ShapeDtypeStruct((width, ff), F32),
            jax.ShapeDtypeStruct((local + 8, width), F32),
        ],
        scratch_shapes=[
            pltpu.VMEM((2, tile, ff), BF),
            pltpu.VMEM((2, tile, ff), F32),
            pltpu.VMEM((2, tile, ff), BF),
            pltpu.VMEM((tile, width), BF),
            pltpu.VMEM((tile, width), BF),
            pltpu.VMEM((tile, width), BF),
            pltpu.VMEM((8, 8, width), F32),
            pltpu.VMEM((local, width), BF),
            pltpu.VMEM((width, ff), BF),
            pltpu.VMEM((ff, width), BF),
        ],
        compiler_params=params(),
        cost_estimate=pl.CostEstimate(
            flops=2 * rows * width * ff * 10 + 2 * rows * width * local * 6,
            bytes_accessed=rows * width * 20,
            transcendentals=2 * rows * ff,
        ),
        name="middle",
    )(place, state, timing, cot, run.reshape(rows // tile, 1, tile), mix_a, mix_b, r_a, r_b,
      wo_a, wi_a, wu_a, *vectors, *inner, *outer)


def attention_backward_kernel(
    core, e_in, do_in, dl_in, x_in, wq, wk, wv, gs_in, gs_out, *rest, heads, own
):
    if own:
        keep, send, gqkv, qt, kt, vaug, dq, dk, dv = rest
    else:
        qt, kt, vaug, dq, dk, dv = rest
    s, h = pl.program_id(0), pl.program_id(1)
    factor = 1.0 / math.sqrt(HEAD)
    pieces = LEN // CHUNK
    local = wq.shape[1]

    @pl.when(h == 0)
    def _():
        x = x_in[...]
        query = mm(wq[...], x, TT).astype(BF)
        key = mm(wk[...], x, TT).astype(BF)
        value = mm(x, wv[...]).astype(BF)
        lane = lane_index((LEN, 2 * HEAD))
        ones = jnp.where((lane % HEAD) < 3, 1.0, 0.0).astype(BF)
        for n in range(heads):
            mine = slice(n * HEAD, (n + 1) * HEAD)
            qt[n] = query[mine]
            kt[n] = key[mine]
            pair = value[:, (n // 2) * 128 : (n // 2) * 128 + 128]
            turned = rolled(pair)
            if n % 2 == 0:
                vaug[n, :, 0:128] = jnp.where(lane < HEAD, pair, turned)
            else:
                vaug[n, :, 0:128] = jnp.where(lane < HEAD, turned, pair)
            vaug[n, :, 128:256] = ones

    high, low = split_low(do_in[...])
    delta = -dl_in[0]
    d1 = delta.astype(BF)
    left = delta - d1.astype(F32)
    d2 = left.astype(BF)
    d3 = (left - d2.astype(F32)).astype(BF)
    index = row_index((2 * HEAD, LEN))
    tail = jnp.where(
        index == 0,
        d1.astype(F32),
        jnp.where(index == 1, d2.astype(F32), jnp.where(index == 2, d3.astype(F32), 0.0)),
    ).astype(BF)
    right = jnp.concatenate([high, low, tail], axis=0)
    query = qt[h]
    out = None
    for c in range(pieces):
        rows = slice(c * CHUNK, (c + 1) * CHUNK)
        d_probs = mm(vaug[h, rows], right)
        e = e_in[0, rows]
        d_scores = (e.astype(F32) * d_probs).astype(BF)
        dv[h, rows] = mm(e, high, NT).astype(BF)
        dk[h, rows] = (mm(d_scores, query, NT) * factor).astype(BF)
        o = mm(kt[h, :, rows], d_scores)
        out = o if out is None else out + o
    dq[pl.ds(pl.multiple_of(h * HEAD, HEAD), HEAD)] = (out * factor).astype(BF)

    @pl.when(h == heads - 1)
    def _():
        d_query = dq[...]
        d_key = jnp.concatenate([dk[n] for n in range(heads)], axis=1)
        d_value = jnp.concatenate([dv[n] for n in range(heads)], axis=1)
        total = mm(d_query, wq[...], TT)
        total = total + mm(d_key, wk[...], NT)
        total = total + mm(d_value, wv[...], NT)
        gs_out[...] = gs_in[...] + total
        if own:
            x = x_in[...]
            g1 = mm(d_query, x).T
            g2 = mm(x, jnp.concatenate([d_key, d_value], axis=1), TN)

            @pl.when(s == 0)
            def _():
                gqkv[:, :local] = g1
                gqkv[:, local:] = g2

            @pl.when(s > 0)
            def _():
                gqkv[:, :local] += g1
                gqkv[:, local:] += g2

            @pl.when(s == pl.num_programs(0) - 1)
            def _():
                half = keep.shape[0]
                keep[...] = gqkv[rows_at(core[0], half)]
                send[...] = gqkv[rows_at(1 - core[0], half)]


def attention_backward(first, seqs, core, e, do, dl, x, wq, wk, wv, gs, own):
    rows, width = x.shape
    local = wq.shape[1]
    heads = local // HEAD
    by_rows = pl.BlockSpec((LEN, width), lambda s, h: (first + s, 0))
    out_specs = [by_rows]
    out_shape = [jax.ShapeDtypeStruct((rows, width), F32)]
    scratch = []
    if own:
        out_specs += [whole((width // 2, 3 * local))] * 2
        out_shape += [jax.ShapeDtypeStruct((width // 2, 3 * local), F32)] * 2
        scratch = [pltpu.VMEM((width, 3 * local), F32)]
    return pl.pallas_call(
        functools.partial(attention_backward_kernel, heads=heads, own=own),
        grid=(seqs, heads),
        in_specs=[
            pl.BlockSpec(memory_space=pltpu.SMEM),
            pl.BlockSpec((1, LEN, LEN), lambda s, h: ((first + s) * heads + h, 0, 0)),
            pl.BlockSpec((HEAD, LEN), lambda s, h: (h, first + s)),
            pl.BlockSpec((1, 1, LEN), lambda s, h: ((first + s) * heads + h, 0, 0)),
            by_rows,
            whole((width, local)),
            whole((width, local)),
            whole((width, local)),
            by_rows,
        ],
        out_specs=out_specs,
        out_shape=out_shape,
        scratch_shapes=scratch
        + [
            pltpu.VMEM((heads, HEAD, LEN), BF),
            pltpu.VMEM((heads, HEAD, LEN), BF),
            pltpu.VMEM((heads, LEN, 256), BF),
            pltpu.VMEM((local, LEN), BF),
            pltpu.VMEM((heads, LEN, HEAD), BF),
            pltpu.VMEM((heads, LEN, HEAD), BF),
        ],
        compiler_params=params(),
        input_output_aliases={8: 0},
        cost_estimate=pl.CostEstimate(
            flops=32 * 2 * seqs * heads * LEN * LEN * HEAD, bytes_accessed=1000,
            transcendentals=0,
        ),
        name="attention_backward_own" if own else "attention_backward_other",
    )(core, e, do, dl, x, wq, wk, wv, gs)


def rows_at(index, size):
    return pl.ds(pl.multiple_of(index * size, size), size)


def local_kernel(fn, count, place, *refs):
    fn(place, refs[:count], refs[count:])


def local_call(name, fn, place, ins, outs):
    return pl.pallas_call(
        functools.partial(local_kernel, fn, len(ins)),
        in_specs=[pl.BlockSpec(memory_space=pltpu.SMEM)]
        + [pl.BlockSpec(memory_space=pltpu.VMEM)] * len(ins),
        out_specs=[pl.BlockSpec(memory_space=pltpu.VMEM)] * len(outs),
        out_shape=[jax.ShapeDtypeStruct(shape, kind) for shape, kind in outs],
        compiler_params=params(),
        name=name,
    )(place, *ins)


def cut_call(name, fn, place, ins, outs):
    return pl.pallas_call(
        functools.partial(local_kernel, fn, len(ins)),
        grid_spec=pltpu.PrefetchScalarGridSpec(
            num_scalar_prefetch=1,
            grid=(1,),
            in_specs=[
                pl.BlockSpec((v.shape[0] // 4, v.shape[1]), lambda _, p: (p[0], 0)) for v in ins
            ],
            out_specs=[pl.BlockSpec(shape, lambda _, p: (0, 0)) for shape in outs],
        ),
        out_shape=[jax.ShapeDtypeStruct(shape, F32) for shape in outs],
        compiler_params=params(),
        name=name,
    )(place, *ins)


def pack(place, ins, outs):
    wq, wk, wv, wo, wi, wu = ins
    local = wq.shape[1]
    for n, ref in enumerate((wq, wk, wv)):
        outs[0][:, n * local : (n + 1) * local] = ref[...].astype(F32)
    quarter, width = wi.shape[0], wo.shape[1]
    blocks = wi.shape[1] // width
    for n in range(blocks):
        outs[1][n * quarter : (n + 1) * quarter] = wi[:, n * width : (n + 1) * width].astype(F32)
    outs[1][blocks * quarter :] = wo[...].astype(F32)
    outs[2][...] = wu[...].astype(F32)


def embed_kernel(state, timing, out):
    out[...] = (state[...].astype(F32) + timing[...]).astype(BF)


def embed(state, timing):
    rows, width = state.shape
    tile = 512
    per = LEN // tile
    by_rows = pl.BlockSpec((tile, width), lambda p, s: (s * per + p, 0))
    return pl.pallas_call(
        embed_kernel,
        grid=(per, rows // LEN),
        in_specs=[by_rows, pl.BlockSpec((tile, width), lambda p, s: (p, 0))],
        out_specs=by_rows,
        out_shape=jax.ShapeDtypeStruct((rows, width), BF),
        compiler_params=params(),
        name="embed",
    )(state, timing)


def unpack_qkv(place, ins, outs):
    local = outs[0].shape[1]
    for p, ref in zip((0, 2, 1, 3), ins):
        rows = rows_at(place[p], ref.shape[0])
        for n, out in enumerate(outs):
            out[rows] = ref[:, n * local : (n + 1) * local].astype(BF)


def finish_qkv(place, ins, outs):
    few, local = ins[0].shape[0], outs[0].shape[1]
    for n, ref in enumerate(ins):
        core, y = jnp.bitwise_xor(place[4], n // 2), jnp.bitwise_xor(place[5], n % 2)
        rows = rows_at(2 * core + y, few)
        for n, out in enumerate(outs):
            out[rows] = ref[:, n * local : (n + 1) * local]


def finish_ff_kernel(gu_in, gi_in, go_in, gu, gi, go, *vec):
    gu[...] = gu_in[...]
    gi[...] = gi_in[...]

    @pl.when(pl.program_id(0) == 0)
    def _():
        local = go.shape[0]
        go[...] = go_in[:local]
        for n, out in enumerate(vec):
            out[...] = go_in[local + n]


def finish_ff(gu, gi, go):
    ff, width = gu.shape
    local = go.shape[0] - 8
    steps = 4
    upper = pl.BlockSpec((ff // steps, width), lambda i: (i, 0))
    inner = pl.BlockSpec((width // steps, ff), lambda i: (i, 0))
    return pl.pallas_call(
        finish_ff_kernel,
        grid=(steps,),
        in_specs=[upper, inner, whole(go.shape)],
        out_specs=[upper, inner, whole((local, width))] + [whole((width,))] * 5,
        out_shape=[
            jax.ShapeDtypeStruct(shape, F32)
            for shape in [gu.shape, gi.shape, (local, width)] + [(width,)] * 5
        ],
        compiler_params=params(),
        name="finish_ff",
    )(gu, gi, go)


def flipped(size, even, odd):
    return [(i, i ^ (odd if i & 1 else even)) for i in range(size)]


def shards(
    dp, state, lengths, halt_mask, wq, wk, wv, wo, gain1, bias1, wi, wu, gain2, bias2,
    halt_weight, cotangent
):
    rows, width = state.shape
    local, ff = wq.shape[1], wi.shape[1]
    timing = jnp.asarray(timing_rows(width))
    me = lax.axis_index("dp").astype(jnp.int32)
    shift = np.array([0, 0, 0, 0, 0, 1], np.int32)
    mask = np.array([3, 3, 3, 3, 1, 1], np.int32)
    flip = np.array([0, 1, 2, 3, 0, 0], np.int32)
    place = jnp.bitwise_xor(jnp.bitwise_and(jnp.right_shift(me, shift), mask), flip)
    bits = dp.bit_length() - 1
    tie = lax.optimization_barrier
    call = functools.partial(local_call, place=place)

    def across(v):
        return lax.ppermute(v, "mp", [(0, 1), (1, 0)])

    def along(v, even, odd=None):
        return lax.ppermute(v, "dp", flipped(dp, even, odd or even))

    quarter = width // 4
    chunk_a, chunk_b, chunk_c = cut_call(
        "pack", pack, place, (wq, wk, wv, wo, wi, wu),
        [(quarter, 3 * local), (ff // 4 + local // 4, width), (ff // 4, width)],
    )
    qkv0 = across(chunk_a)
    x = embed(state, timing)
    chunk_b, x = tie((chunk_b, x))
    in0 = across(chunk_b)
    fwd = attention_forward(0, lengths, x, wq, wk, wv)
    qkv0, chunk_c, fwd = tie((qkv0, chunk_c, fwd))
    qkv1 = along(qkv0, 2)
    out0 = across(chunk_c)
    fwd = attention_forward(1, lengths, x, wq, wk, wv, fwd)
    qkv1, in0, fwd = tie((qkv1, in0, fwd))
    qkv2, qkv3 = along(qkv0, 1), along(qkv1, 1)
    in1 = along(in0, 2)
    wq2, wk2, wv2 = call(
        "unpack_qkv", unpack_qkv, ins=(qkv0, qkv1, qkv2, qkv3),
        outs=[((width, local), BF)] * 3,
    )
    fwd2 = attention_forward(0, lengths, x, wq2, wk2, wv2)
    in1, out0, fwd2 = tie((in1, out0, fwd2))
    in2, in3 = along(in0, 1), along(in1, 1)
    out1 = along(out0, 2)
    out2 = along(out0, 1)
    fwd2 = attention_forward(1, lengths, x, wq2, wk2, wv2, fwd2)
    in2, in3, out1, out2, fwd2 = tie((in2, in3, out1, out2, fwd2))
    out3 = along(out1, 1)
    e_a, mix_a, r_a = fwd
    e_b, mix_b, r_b = fwd2
    new_state, gs, do_a, do_b, dl_a, dl_b, *grads = middle(
        place, state, timing, cotangent, halt_mask, mix_a, mix_b, r_a, r_b, wo, wi, wu,
        (gain1, bias1, gain2, bias2, halt_weight), (in0, in1, in2, in3), (out0, out1, out2, out3)
    )

    grads = lax.psum(tuple(grads), "dp")
    own = dict(core=place[4:5], e=e_a, do=do_a, dl=dl_a, x=x, wq=wq, wk=wk, wv=wv)
    other = dict(core=place[4:5], e=e_b, do=do_b, dl=dl_b, x=x, wq=wq2, wk=wk2, wv=wv2)

    def attention_and_sums(carry):
        step, gs, *_ = carry
        back = attention_backward
        gs, keep, send = back(0, rows // LEN, gs=gs, own=True, **own)
        g = keep + along(send, 1)
        g, gs = tie((g, gs))
        few = g.shape[0] // 2
        y = place[5]
        got = along(lax.dynamic_slice_in_dim(g, (1 - y) * few, few), 2)
        (gs,) = back(0, 1, gs=gs, own=False, **other)
        got, gs = tie((got, gs))
        g = lax.dynamic_slice_in_dim(g, y * few, few) + got
        g, gs = tie((g, gs))
        got = along(g, 4, 8)
        (gs,) = back(1, rows // LEN - 1, gs=gs, own=False, **other)
        got, gs = tie((got, gs))
        g = g + got
        g = g + along(g, 8, 4)
        for bit in range(4, bits):
            g = g + along(g, 1 << bit)
        got = along(g, 2)
        parts = call(
            "finish_qkv", finish_qkv, ins=(g, got, along(g, 1), along(got, 1)),
            outs=[((width, local), F32)] * 3,
        )
        return (step + 1, gs, *parts)

    once = jnp.minimum(lengths[0], 1)
    empty = jnp.zeros((width, local), F32)
    _, gs, gq, gk, gv = lax.cond(
        once > 0, attention_and_sums, lambda c: c,
        (jnp.zeros_like(once), gs, empty, empty, empty),
    )
    grads, gs, gq = tie((grads, gs, gq))
    gu, gi, go, *vec = finish_ff(*grads)
    return (
        new_state, gs, gq, gk, gv, go, vec[0], vec[1], gi, gu, vec[2], vec[3], vec[4]
    )


def solution(mesh):
    rows, columns, parts = P("dp", None), P(None, "mp"), P("mp", None)
    return jax.shard_map(
        functools.partial(shards, mesh.shape["dp"]),
        mesh=mesh,
        in_specs=(
            rows, P("dp"), P("dp"), columns, columns, columns, parts, P(), P(), columns,
            parts, P(), P(), P(), rows
        ),
        out_specs=(
            rows, rows, columns, columns, columns, parts, P(), P(), columns, parts, P(), P(),
            P()
        ),
        check_vma=False,
    )
```

```python
import functools
import math

import jax
import jax.numpy as jnp
import numpy as np
from jax import lax
from jax.experimental import pallas as pl
from jax.experimental.pallas import tpu as pltpu
from jax.sharding import PartitionSpec as P

HEAD = 64
LEN = 1024
STEP = 2
LOG2E = 1.4426950408889634
BF = jnp.bfloat16
F32 = jnp.float32
NN = (((1,), (0,)), ((), ()))
NT = (((1,), (1,)), ((), ()))
TN = (((0,), (0,)), ((), ()))
TT = (((0,), (1,)), ((), ()))
VMEM_LIMIT = 60 << 20
CHUNK = 256
SUBS = 2


def mm(a, b, dims=NN):
    return lax.dot_general(a, b, dims, preferred_element_type=F32)


def params():
    return pltpu.CompilerParams(vmem_limit_bytes=VMEM_LIMIT)


def whole(shape):
    zeros = (0,) * len(shape)
    return pl.BlockSpec(shape, lambda *_: zeros)


def timing_rows(width):
    half = width // 2
    rates = np.exp(-math.log(10000.0) * np.arange(half, dtype=np.float64) / (half - 1))

    def rows(positions):
        angles = positions[:, None] * rates[None, :]
        return np.concatenate([np.sin(angles), np.cos(angles)], axis=1)

    return (rows(np.arange(LEN, dtype=np.float64)) + rows(np.array([float(STEP)]))).astype(
        np.float32
    )


def split_low(value):
    high = value.astype(BF)
    return high, (value - high.astype(F32)).astype(BF)


def rolled(pair):
    return jnp.concatenate([pair[:, HEAD:], pair[:, :HEAD]], axis=1)


def lane_index(shape):
    return lax.broadcasted_iota(jnp.int32, shape, 1)


def row_index(shape):
    return lax.broadcasted_iota(jnp.int32, shape, 0)


def attention_forward_kernel(seq, lengths, x_in, wq, wk, wv, *rest, heads):
    e_out, mixed_out, r_out, kaug, qaug, vaug, sa, sb, ma, mb = rest[-10:]
    j = pl.program_id(0)
    last = heads // 2 - 1
    pieces = LEN // CHUNK

    def score_piece(i, c, target):
        rows = slice(c * CHUNK, (c + 1) * CHUNK)
        s = mm(kaug[i, rows], qaug[i])
        target[rows] = s
        return jnp.max(s.reshape(CHUNK // 8, 8, LEN), axis=0)

    @pl.when(j == 0)
    def _():
        x = x_in[...]
        query = mm(wq[...], x, TT).astype(BF).astype(F32) * (LOG2E / math.sqrt(HEAD))
        high, rest = split_low(query)
        key = mm(x, wk[...]).astype(BF)
        value = mm(wv[...], x, TT).astype(BF)
        shape = (LEN, 2 * HEAD)
        lane = lane_index(shape)
        padded = row_index(shape) >= lengths[seq]
        mask = jnp.where(padded & ((lane == 0) | (lane == HEAD)), -1e30, 0.0).astype(BF)
        first = row_index((HEAD, LEN)) == 0
        ones = jnp.where(first, 1.0, 0.0).astype(BF)
        zeros = jnp.zeros((HEAD, LEN), BF)
        for i in range(heads):
            pair = key[:, (i // 2) * 128 : (i // 2) * 128 + 128]
            turned = rolled(pair)
            mine = slice(i * HEAD, (i + 1) * HEAD)
            kaug[i, :, 0:128] = pair
            if i % 2 == 0:
                kaug[i, :, 128:256] = jnp.where(lane < HEAD, mask, turned)
                parts = (high[mine], zeros, ones, rest[mine])
            else:
                kaug[i, :, 128:256] = jnp.where(lane < HEAD, turned, mask)
                parts = (zeros, high[mine], rest[mine], ones)
            for n, part in enumerate(parts):
                qaug[i, n * HEAD : (n + 1) * HEAD] = part
            vaug[i, 0:HEAD] = value[mine]
            vaug[i, HEAD : HEAD + 16] = jnp.ones((16, LEN), BF)
        top = None
        for c in range(pieces):
            m = score_piece(0, c, sa)
            top = m if top is None else jnp.maximum(top, m)
        ma[...] = jnp.max(top, axis=0, keepdims=True)

    def step(slot, cur, cur_m, nxt, nxt_m, ahead=True):
        i = 2 * j + slot
        shift = cur_m[...]
        top = None
        out = None
        for c in range(pieces):
            rows = slice(c * CHUNK, (c + 1) * CHUNK)
            if ahead:
                m = score_piece(i + 1, c, nxt)
                top = m if top is None else jnp.maximum(top, m)
            e = jnp.exp2(cur[rows] - shift).astype(BF)
            e_out[slot, rows] = e
            o = mm(vaug[i, :, rows], e)
            out = o if out is None else out + o
        if ahead:
            nxt_m[...] = jnp.max(top, axis=0, keepdims=True)
        r = 1.0 / out[HEAD : HEAD + 1]
        mixed_out[slot * HEAD : (slot + 1) * HEAD] = (out[:HEAD] * r).astype(BF)
        r_out[slot] = r

    step(0, sa, ma, sb, mb)

    @pl.when(j < last)
    def _():
        step(1, sb, mb, sa, ma)

    @pl.when(j == last)
    def _():
        step(1, sb, mb, sa, ma, ahead=False)


def attention_forward(seq, lengths, x, wq, wk, wv, earlier=()):
    rows, width = x.shape
    local = wq.shape[1]
    heads = local // HEAD
    steps, total = heads // 2, rows // LEN * heads
    return pl.pallas_call(
        functools.partial(attention_forward_kernel, seq, heads=heads),
        grid=(steps,),
        in_specs=[
            pl.BlockSpec(memory_space=pltpu.SMEM),
            pl.BlockSpec((LEN, width), lambda j: (seq, 0)),
            whole((width, local)),
            whole((width, local)),
            whole((width, local)),
        ]
        + [pl.BlockSpec(memory_space=pl.ANY)] * len(earlier),
        out_specs=[
            pl.BlockSpec((2, LEN, LEN), lambda j: (seq * steps + j, 0, 0)),
            pl.BlockSpec((2 * HEAD, LEN), lambda j: (j, seq)),
            pl.BlockSpec((2, 1, LEN), lambda j: (seq * steps + j, 0, 0)),
        ],
        out_shape=[
            jax.ShapeDtypeStruct((total, LEN, LEN), BF),
            jax.ShapeDtypeStruct((local, rows), BF),
            jax.ShapeDtypeStruct((total, 1, LEN), F32),
        ],
        scratch_shapes=[
            pltpu.VMEM((heads, LEN, 256), BF),
            pltpu.VMEM((heads, 256, LEN), BF),
            pltpu.VMEM((heads, HEAD + 16, LEN), BF),
            pltpu.VMEM((LEN, LEN), F32),
            pltpu.VMEM((LEN, LEN), F32),
            pltpu.VMEM((1, LEN), F32),
            pltpu.VMEM((1, LEN), F32),
        ],
        compiler_params=params(),
        input_output_aliases={5 + n: n for n in range(len(earlier))},
        cost_estimate=pl.CostEstimate(
            flops=8 * 2 * heads * LEN * LEN * HEAD,
            bytes_accessed=2 * heads * LEN * LEN,
            transcendentals=heads * LEN * LEN,
        ),
        name="attention_forward",
    )(lengths, x, wq, wk, wv, *earlier)


def row_mean(v):
    return jnp.mean(v, axis=-1, keepdims=True)


def norm_rows(v):
    centre = v - row_mean(v)
    deviation = lax.rsqrt(row_mean(centre * centre) + 1e-05)
    return centre * deviation, deviation


def norm_back(e, xhat, deviation):
    return deviation * (e - row_mean(e) - xhat * row_mean(e * xhat))


def fold_rows(v):
    return jnp.sum(v.reshape(v.shape[0] // 8, 8, v.shape[1]), axis=0)


def unpack(place, inner, outer, wo, wi, wu):
    width = wi.shape[0]
    quarter, blocks = width // 4, wi.shape[1] // width
    for p, ref, more in zip((0, 2, 1, 3), inner, outer):
        rows = rows_at(place[p], quarter)
        for n in range(blocks):
            columns = slice(n * width, (n + 1) * width)
            wi[rows, columns] = ref[n * quarter : (n + 1) * quarter].astype(BF)
        wo[rows_at(place[p], wo.shape[0] // 4)] = ref[blocks * quarter :].astype(BF)
        wu[rows_at(place[p], more.shape[0])] = more[...].astype(BF)


def middle_kernel(
    place, state, timing, cot, run, mix_a, mix_b, wo_a, wi_a, wu_a, v0, v1, v2, v3, v4, i0, i1,
    i2, i3, o0, o1, o2, o3, new_state, gs, att_low, wo_b, gu, gi, act, slope, inner_low, low1,
    out_low, fold, wi_b, wu_b
):
    t = pl.program_id(0)
    last = pl.num_programs(0) - 1
    tile = state.shape[0]
    size = tile // SUBS
    ff = wi_a.shape[1]
    gain1, bias1, gain2, bias2, halt_w = (v[...].reshape(1, -1) for v in (v0, v1, v2, v3, v4))
    c0 = math.sqrt(2.0 / math.pi)
    halves = ((wi_a, wu_a), (wi_b, wu_b))
    running_column = jnp.broadcast_to(run[0].astype(F32), (8, tile)).T[:, 0:1]

    @pl.when(t == 0)
    def _():
        for ref in (gu, gi, fold):
            ref[...] = jnp.zeros(ref.shape, F32)
        unpack(place, (i0, i1, i2, i3), (o0, o1, o2, o3), wo_b, wi_b, wu_b)

    def first_norm(k):
        rows = slice(k * size, (k + 1) * size)
        embedded = state[rows].astype(F32) + timing[rows]
        attended = mm(mix_a[:, rows], wo_a[...], TN) + mm(mix_b[:, rows], wo_b[...], TN)
        xhat1, dev1 = norm_rows(embedded + attended)
        normed1 = xhat1 * gain1 + bias1
        low1[rows] = normed1.astype(BF)
        return xhat1, dev1, normed1

    def forward(k, normed1):
        rows = slice(k * size, (k + 1) * size)
        total = normed1
        for n, (wi, wu) in enumerate(halves):
            v = mm(low1[rows], wi[...])
            square = v * v
            h = 0.5 + 0.5 * jnp.tanh(v * (c0 + (c0 * 0.044715) * square))
            g = v * h
            act[n, rows] = g.astype(BF)
            slope[n, rows] = h + g * (1.0 - h) * (2.0 * c0 + (6.0 * c0 * 0.044715) * square)
            total = total + mm(act[n, rows], wu[...])
        return total

    def second_norm(k, hidden2):
        rows = slice(k * size, (k + 1) * size)
        old = state[rows].astype(F32)
        xhat2, dev2 = norm_rows(hidden2)
        block = xhat2 * gain2 + bias2
        halt = jax.nn.sigmoid(jnp.sum(block * halt_w, axis=-1, keepdims=True))
        running = running_column[rows]
        gate = running * halt
        change = block - old
        new_state[rows] = old + gate * change
        g_in = cot[rows].astype(F32)
        d_prob = running * jnp.sum(g_in * change, axis=-1, keepdims=True)
        d_logit = d_prob * halt * (1.0 - halt)
        d_block = gate * g_in + d_logit * halt_w
        fold[4] += fold_rows(d_logit * block)
        fold[2] += fold_rows(d_block * xhat2)
        fold[3] += fold_rows(d_block)
        gs[rows] = g_in * (1.0 - gate)
        d_hidden2 = norm_back(d_block * gain2, xhat2, dev2)
        out_low[rows] = d_hidden2.astype(BF)
        return d_hidden2

    def backward(k, d_hidden2):
        rows = slice(k * size, (k + 1) * size)
        total = d_hidden2
        for n, (wi, wu) in enumerate(halves):
            d_act = mm(out_low[rows], wu[...], NT)
            inner_low[n, rows] = (d_act * slope[n, rows]).astype(BF)
            total = total + mm(inner_low[n, rows], wi[...], NT)
        return total

    def first_back(k, d_normed1, xhat1, dev1):
        rows = slice(k * size, (k + 1) * size)
        fold[0] += fold_rows(d_normed1 * xhat1)
        fold[1] += fold_rows(d_normed1)
        d_hidden1 = norm_back(d_normed1 * gain1, xhat1, dev1)
        att_low[rows] = d_hidden1.astype(BF)
        gs[rows] += d_hidden1

    ks = range(SUBS)
    firsts = [first_norm(k) for k in ks]
    hidden2 = {0: forward(0, firsts[0][2])}
    d_hidden2, d_normed1 = {}, {}
    for k in ks:
        d_hidden2[k] = second_norm(k, hidden2[k])
        if k + 1 < SUBS:
            hidden2[k + 1] = forward(k + 1, firsts[k + 1][2])
    d_normed1[0] = backward(0, d_hidden2[0])
    for k in ks:
        first_back(k, d_normed1[k], *firsts[k][:2])
        if k + 1 < SUBS:
            d_normed1[k + 1] = backward(k + 1, d_hidden2[k + 1])
    gu[:ff] += mm(act[0], out_low[...], TN)
    gi[...] += mm(low1[...], inner_low[0], TN)

    @pl.when(t == last)
    def _():
        for n in range(8):
            gu[ff + n : ff + n + 1] = jnp.sum(fold[n], axis=0, keepdims=True)


def middle(place, state, timing, cot, run, mix_a, mix_b, wo_a, wi_a, wu_a, vectors, inner, outer):
    rows, width = state.shape
    local, ff = wo_a.shape[0], wi_a.shape[1]
    tile = 512
    per = LEN // tile
    by_rows = pl.BlockSpec((tile, width), lambda t: (t, 0))
    by_columns = pl.BlockSpec((local, tile), lambda t: (0, t))
    return pl.pallas_call(
        middle_kernel,
        grid=(rows // tile,),
        in_specs=[
            pl.BlockSpec(memory_space=pltpu.SMEM),
            by_rows,
            pl.BlockSpec((tile, width), lambda t: (t % per, 0)),
            by_rows,
            pl.BlockSpec((1, 1, tile), lambda t: (t, 0, 0)),
            by_columns,
            by_columns,
            whole((local, width)),
            whole((width, ff)),
            whole((ff, width)),
        ]
        + [whole((width,))] * 5
        + [whole(v.shape) for v in (*inner, *outer)],
        out_specs=[
            by_rows,
            by_rows,
            by_rows,
            whole((local, width)),
            whole((ff + 8, width)),
            whole((width, ff)),
        ],
        out_shape=[
            jax.ShapeDtypeStruct((rows, width), F32),
            jax.ShapeDtypeStruct((rows, width), F32),
            jax.ShapeDtypeStruct((rows, width), BF),
            jax.ShapeDtypeStruct((local, width), BF),
            jax.ShapeDtypeStruct((ff + 8, width), F32),
            jax.ShapeDtypeStruct((width, ff), F32),
        ],
        scratch_shapes=[
            pltpu.VMEM((2, tile, ff), BF),
            pltpu.VMEM((2, tile, ff), F32),
            pltpu.VMEM((2, tile, ff), BF),
            pltpu.VMEM((tile, width), BF),
            pltpu.VMEM((tile, width), BF),
            pltpu.VMEM((8, 8, width), F32),
            pltpu.VMEM((width, ff), BF),
            pltpu.VMEM((ff, width), BF),
        ],
        compiler_params=params(),
        cost_estimate=pl.CostEstimate(
            flops=2 * rows * width * ff * 10 + 2 * rows * width * local * 2,
            bytes_accessed=rows * width * 20,
            transcendentals=2 * rows * ff,
        ),
        name="middle",
    )(place, state, timing, cot, run.reshape(rows // tile, 1, tile), mix_a, mix_b, wo_a, wi_a,
      wu_a, *vectors, *inner, *outer)


def attention_backward_kernel(
    core, e_in, att_in, mix_in, r_in, x_in, wq, wk, wv, wo, gs_in, gs_out, *rest, heads, own
):
    if own:
        keep, send, gqkv, go, qt, kt, vaug, right, dq, dk, dv = rest
    else:
        qt, kt, vaug, right, dq, dk, dv = rest
    s, h = pl.program_id(0), pl.program_id(1)
    factor = 1.0 / math.sqrt(HEAD)
    pieces = LEN // CHUNK
    local = wq.shape[1]

    @pl.when(h == 0)
    def _():
        x = x_in[...]
        query = mm(wq[...], x, TT).astype(BF)
        key = mm(wk[...], x, TT).astype(BF)
        value = mm(x, wv[...]).astype(BF)
        lane = lane_index((LEN, 2 * HEAD))
        ones = jnp.where((lane % HEAD) < 3, 1.0, 0.0).astype(BF)
        for n in range(heads):
            mine = slice(n * HEAD, (n + 1) * HEAD)
            qt[n] = query[mine]
            kt[n] = key[mine]
            pair = value[:, (n // 2) * 128 : (n // 2) * 128 + 128]
            turned = rolled(pair)
            if n % 2 == 0:
                vaug[n, :, 0:128] = jnp.where(lane < HEAD, pair, turned)
            else:
                vaug[n, :, 0:128] = jnp.where(lane < HEAD, turned, pair)
            vaug[n, :, 128:256] = ones
        d_att = att_in[...]
        d_mixed = mm(wo[...], d_att, NT).astype(BF).astype(F32)
        index = row_index((2 * HEAD, LEN))
        for n in range(heads):
            mine = slice(n * HEAD, (n + 1) * HEAD)
            part = d_mixed[mine]
            scale = r_in[n]
            high, low = split_low(part * scale)
            right[n, 0:HEAD] = high
            right[n, HEAD : 2 * HEAD] = low
            delta = -scale * jnp.sum(part * mix_in[mine].astype(F32), axis=0, keepdims=True)
            d1 = delta.astype(BF).astype(F32)
            d2 = (delta - d1).astype(BF).astype(F32)
            d3 = delta - d1 - d2
            right[n, 2 * HEAD :] = jnp.where(
                index == 0, d1, jnp.where(index == 1, d2, jnp.where(index == 2, d3, 0.0))
            ).astype(BF)
        if own:
            g_out = mm(mix_in[...], d_att)

            @pl.when(s == 0)
            def _():
                go[...] = g_out

            @pl.when(s > 0)
            def _():
                go[...] += g_out

    high = right[h, 0:HEAD]
    query = qt[h]
    out = None
    for c in range(pieces):
        rows = slice(c * CHUNK, (c + 1) * CHUNK)
        d_probs = mm(vaug[h, rows], right[h])
        e = e_in[0, rows]
        d_scores = (e.astype(F32) * d_probs).astype(BF)
        dv[h, rows] = mm(e, high, NT).astype(BF)
        dk[h, rows] = (mm(d_scores, query, NT) * factor).astype(BF)
        o = mm(kt[h, :, rows], d_scores)
        out = o if out is None else out + o
    dq[pl.ds(pl.multiple_of(h * HEAD, HEAD), HEAD)] = (out * factor).astype(BF)

    @pl.when(h == heads - 1)
    def _():
        d_query = dq[...]
        d_key = jnp.concatenate([dk[n] for n in range(heads)], axis=1)
        d_value = jnp.concatenate([dv[n] for n in range(heads)], axis=1)
        total = mm(d_query, wq[...], TT)
        total = total + mm(d_key, wk[...], NT)
        total = total + mm(d_value, wv[...], NT)
        gs_out[...] = gs_in[...] + total
        if own:
            x = x_in[...]
            g1 = mm(d_query, x).T
            g2 = mm(x, jnp.concatenate([d_key, d_value], axis=1), TN)

            @pl.when(s == 0)
            def _():
                gqkv[:, :local] = g1
                gqkv[:, local:] = g2

            @pl.when(s > 0)
            def _():
                gqkv[:, :local] += g1
                gqkv[:, local:] += g2

            @pl.when(s == pl.num_programs(0) - 1)
            def _():
                half, few = keep.shape[0], local // 2
                wide, width = gqkv.shape[1], go.shape[1]
                for place, out in ((core[0], keep), (1 - core[0], send)):
                    out[:, :wide] = gqkv[rows_at(place, half)]
                    piece = go[rows_at(place, few)]
                    out[:few, wide:] = piece[:, : width // 2]
                    out[few:, wide:] = piece[:, width // 2 :]


def attention_backward(first, seqs, core, e, att, mix, r, x, wq, wk, wv, wo, gs, own):
    rows, width = x.shape
    local = wq.shape[1]
    heads = local // HEAD
    by_rows = pl.BlockSpec((LEN, width), lambda s, h: (first + s, 0))
    out_specs = [by_rows]
    out_shape = [jax.ShapeDtypeStruct((rows, width), F32)]
    scratch = []
    if own:
        both = (width // 2, 3 * local + width // 2)
        out_specs += [whole(both)] * 2
        out_shape += [jax.ShapeDtypeStruct(both, F32)] * 2
        scratch = [pltpu.VMEM((width, 3 * local), F32), pltpu.VMEM((local, width), F32)]
    return pl.pallas_call(
        functools.partial(attention_backward_kernel, heads=heads, own=own),
        grid=(seqs, heads),
        in_specs=[
            pl.BlockSpec(memory_space=pltpu.SMEM),
            pl.BlockSpec((1, LEN, LEN), lambda s, h: ((first + s) * heads + h, 0, 0)),
            by_rows,
            pl.BlockSpec((local, LEN), lambda s, h: (0, first + s)),
            pl.BlockSpec((heads, 1, LEN), lambda s, h: (first + s, 0, 0)),
            by_rows,
            whole((width, local)),
            whole((width, local)),
            whole((width, local)),
            whole((local, width)),
            by_rows,
        ],
        out_specs=out_specs,
        out_shape=out_shape,
        scratch_shapes=scratch
        + [
            pltpu.VMEM((heads, HEAD, LEN), BF),
            pltpu.VMEM((heads, HEAD, LEN), BF),
            pltpu.VMEM((heads, LEN, 256), BF),
            pltpu.VMEM((heads, 256, LEN), BF),
            pltpu.VMEM((local, LEN), BF),
            pltpu.VMEM((heads, LEN, HEAD), BF),
            pltpu.VMEM((heads, LEN, HEAD), BF),
        ],
        compiler_params=params(),
        input_output_aliases={10: 0},
        cost_estimate=pl.CostEstimate(
            flops=32 * 2 * seqs * heads * LEN * LEN * HEAD, bytes_accessed=1000,
            transcendentals=0,
        ),
        name="attention_backward_own" if own else "attention_backward_other",
    )(core, e, att, mix, r, x, wq, wk, wv, wo, gs)


def rows_at(index, size):
    return pl.ds(pl.multiple_of(index * size, size), size)


def local_kernel(fn, count, place, *refs):
    fn(place, refs[:count], refs[count:])


def local_call(name, fn, place, ins, outs):
    return pl.pallas_call(
        functools.partial(local_kernel, fn, len(ins)),
        in_specs=[pl.BlockSpec(memory_space=pltpu.SMEM)]
        + [pl.BlockSpec(memory_space=pltpu.VMEM)] * len(ins),
        out_specs=[pl.BlockSpec(memory_space=pltpu.VMEM)] * len(outs),
        out_shape=[jax.ShapeDtypeStruct(shape, kind) for shape, kind in outs],
        compiler_params=params(),
        name=name,
    )(place, *ins)


def cut_call(name, fn, place, ins, outs):
    return pl.pallas_call(
        functools.partial(local_kernel, fn, len(ins)),
        grid_spec=pltpu.PrefetchScalarGridSpec(
            num_scalar_prefetch=1,
            grid=(1,),
            in_specs=[
                pl.BlockSpec((v.shape[0] // 4, v.shape[1]), lambda _, p: (p[0], 0)) for v in ins
            ],
            out_specs=[pl.BlockSpec(shape, lambda _, p: (0, 0)) for shape in outs],
        ),
        out_shape=[jax.ShapeDtypeStruct(shape, F32) for shape in outs],
        compiler_params=params(),
        name=name,
    )(place, *ins)


def pack(place, ins, outs):
    wq, wk, wv, wo, wi, wu = ins
    local = wq.shape[1]
    for n, ref in enumerate((wq, wk, wv)):
        outs[0][:, n * local : (n + 1) * local] = ref[...].astype(F32)
    quarter, width = wi.shape[0], wo.shape[1]
    blocks = wi.shape[1] // width
    for n in range(blocks):
        outs[1][n * quarter : (n + 1) * quarter] = wi[:, n * width : (n + 1) * width].astype(F32)
    outs[1][blocks * quarter :] = wo[...].astype(F32)
    outs[2][...] = wu[...].astype(F32)


def embed_kernel(state, timing, out):
    out[...] = (state[...].astype(F32) + timing[...]).astype(BF)


def embed(state, timing):
    rows, width = state.shape
    tile = 512
    per = LEN // tile
    by_rows = pl.BlockSpec((tile, width), lambda p, s: (s * per + p, 0))
    return pl.pallas_call(
        embed_kernel,
        grid=(per, rows // LEN),
        in_specs=[by_rows, pl.BlockSpec((tile, width), lambda p, s: (p, 0))],
        out_specs=by_rows,
        out_shape=jax.ShapeDtypeStruct((rows, width), BF),
        compiler_params=params(),
        name="embed",
    )(state, timing)


def unpack_qkv(place, ins, outs):
    local = outs[0].shape[1]
    for p, ref in zip((0, 2, 1, 3), ins):
        rows = rows_at(place[p], ref.shape[0])
        for n, out in enumerate(outs):
            out[rows] = ref[:, n * local : (n + 1) * local].astype(BF)


def finish_qkv(place, ins, outs):
    gq, gk, gv, go = outs
    width, local = gq.shape
    few, wide, half = ins[0].shape[0], 3 * local, width // 2
    for n, ref in enumerate(ins):
        core, y = jnp.bitwise_xor(place[4], n // 2), jnp.bitwise_xor(place[5], n % 2)
        rows = rows_at(2 * core + y, few)
        for k, out in enumerate((gq, gk, gv)):
            out[rows] = ref[:, k * local : (k + 1) * local]
        for k in range(2):

            @pl.when(y == k)
            def _():
                go[rows_at(core, few), k * half : (k + 1) * half] = ref[:, wide:]


def finish_ff_kernel(gu_in, vec_in, gi_in, gu, gi, *vec):
    gu[...] = gu_in[...]
    gi[...] = gi_in[...]

    @pl.when(pl.program_id(0) == 0)
    def _():
        for n, out in enumerate(vec):
            out[...] = vec_in[n]


def finish_ff(gu, gi):
    width, ff = gi.shape
    steps = 4
    upper = pl.BlockSpec((ff // steps, width), lambda i: (i, 0))
    inner = pl.BlockSpec((width // steps, ff), lambda i: (i, 0))
    return pl.pallas_call(
        finish_ff_kernel,
        grid=(steps,),
        in_specs=[upper, pl.BlockSpec((8, width), lambda i: (ff // 8, 0)), inner],
        out_specs=[upper, inner] + [whole((width,))] * 5,
        out_shape=[
            jax.ShapeDtypeStruct(shape, F32)
            for shape in [(ff, width), (width, ff)] + [(width,)] * 5
        ],
        compiler_params=params(),
        name="finish_ff",
    )(gu, gu, gi)


def flipped(size, even, odd):
    return [(i, i ^ (odd if i & 1 else even)) for i in range(size)]


def shards(
    dp, state, lengths, halt_mask, wq, wk, wv, wo, gain1, bias1, wi, wu, gain2, bias2,
    halt_weight, cotangent
):
    rows, width = state.shape
    local, ff = wq.shape[1], wi.shape[1]
    timing = jnp.asarray(timing_rows(width))
    me = lax.axis_index("dp").astype(jnp.int32)
    shift = np.array([0, 0, 0, 0, 0, 1], np.int32)
    mask = np.array([3, 3, 3, 3, 1, 1], np.int32)
    flip = np.array([0, 1, 2, 3, 0, 0], np.int32)
    place = jnp.bitwise_xor(jnp.bitwise_and(jnp.right_shift(me, shift), mask), flip)
    bits = dp.bit_length() - 1
    tie = lax.optimization_barrier
    call = functools.partial(local_call, place=place)

    def across(v):
        return lax.ppermute(v, "mp", [(0, 1), (1, 0)])

    def along(v, even, odd=None):
        return lax.ppermute(v, "dp", flipped(dp, even, odd or even))

    quarter = width // 4
    chunk_a, chunk_b, chunk_c = cut_call(
        "pack", pack, place, (wq, wk, wv, wo, wi, wu),
        [(quarter, 3 * local), (ff // 4 + local // 4, width), (ff // 4, width)],
    )
    qkv0 = across(chunk_a)
    x = embed(state, timing)
    chunk_b, x = tie((chunk_b, x))
    in0 = across(chunk_b)
    fwd = attention_forward(0, lengths, x, wq, wk, wv)
    qkv0, chunk_c, fwd = tie((qkv0, chunk_c, fwd))
    qkv1 = along(qkv0, 2)
    out0 = across(chunk_c)
    fwd = attention_forward(1, lengths, x, wq, wk, wv, fwd)
    qkv1, in0, fwd = tie((qkv1, in0, fwd))
    qkv2, qkv3 = along(qkv0, 1), along(qkv1, 1)
    in1 = along(in0, 2)
    wq2, wk2, wv2 = call(
        "unpack_qkv", unpack_qkv, ins=(qkv0, qkv1, qkv2, qkv3),
        outs=[((width, local), BF)] * 3,
    )
    fwd2 = attention_forward(0, lengths, x, wq2, wk2, wv2)
    in1, out0, fwd2 = tie((in1, out0, fwd2))
    in2, in3 = along(in0, 1), along(in1, 1)
    out1 = along(out0, 2)
    out2 = along(out0, 1)
    fwd2 = attention_forward(1, lengths, x, wq2, wk2, wv2, fwd2)
    in2, in3, out1, out2, fwd2 = tie((in2, in3, out1, out2, fwd2))
    out3 = along(out1, 1)
    e_a, mix_a, r_a = fwd
    e_b, mix_b, r_b = fwd2
    new_state, gs, att, wo2, *grads = middle(
        place, state, timing, cotangent, halt_mask, mix_a, mix_b, wo, wi, wu,
        (gain1, bias1, gain2, bias2, halt_weight), (in0, in1, in2, in3), (out0, out1, out2, out3)
    )

    grads = lax.psum(tuple(grads), "dp")
    own = dict(core=place[4:5], e=e_a, att=att, mix=mix_a, r=r_a, x=x, wq=wq, wk=wk, wv=wv, wo=wo)
    other = dict(
        core=place[4:5], e=e_b, att=att, mix=mix_b, r=r_b, x=x, wq=wq2, wk=wk2, wv=wv2, wo=wo2
    )

    def attention_and_sums(carry):
        step, gs, *_ = carry
        back = attention_backward
        gs, keep, send = back(0, rows // LEN, gs=gs, own=True, **own)
        g = keep + along(send, 1)
        g, gs = tie((g, gs))
        few = g.shape[0] // 2
        y = place[5]
        got = along(lax.dynamic_slice_in_dim(g, (1 - y) * few, few), 2)
        (gs,) = back(0, 1, gs=gs, own=False, **other)
        got, gs = tie((got, gs))
        g = lax.dynamic_slice_in_dim(g, y * few, few) + got
        g, gs = tie((g, gs))
        got = along(g, 4, 8)
        (gs,) = back(1, rows // LEN - 1, gs=gs, own=False, **other)
        got, gs = tie((got, gs))
        g = g + got
        g = g + along(g, 8, 4)
        for bit in range(4, bits):
            g = g + along(g, 1 << bit)
        got = along(g, 2)
        parts = call(
            "finish_qkv", finish_qkv, ins=(g, got, along(g, 1), along(got, 1)),
            outs=[((width, local), F32)] * 3 + [((local, width), F32)],
        )
        return (step + 1, gs, *parts)

    once = jnp.minimum(lengths[0], 1)
    empty = [jnp.zeros(shape, F32) for shape in [(width, local)] * 3 + [(local, width)]]
    _, gs, gq, gk, gv, go = lax.cond(
        once > 0, attention_and_sums, lambda c: c,
        (jnp.zeros_like(once), gs, *empty),
    )
    grads, gs, gq = tie((grads, gs, gq))
    gu, gi, *vec = finish_ff(*grads)
    return (
        new_state, gs, gq, gk, gv, go, vec[0], vec[1], gi, gu, vec[2], vec[3], vec[4]
    )


def solution(mesh):
    rows, columns, parts = P("dp", None), P(None, "mp"), P("mp", None)
    return jax.shard_map(
        functools.partial(shards, mesh.shape["dp"]),
        mesh=mesh,
        in_specs=(
            rows, P("dp"), P("dp"), columns, columns, columns, parts, P(), P(), columns,
            parts, P(), P(), P(), rows
        ),
        out_specs=(
            rows, rows, columns, columns, columns, parts, P(), P(), columns, parts, P(), P(),
            P()
        ),
        check_vma=False,
    )
```

```python
import functools
import math

import jax
import jax.numpy as jnp
import numpy as np
from jax import lax
from jax.experimental import pallas as pl
from jax.experimental.pallas import tpu as pltpu
from jax.sharding import PartitionSpec as P

HEAD = 64
LEN = 1024
STEP = 2
LOG2E = 1.4426950408889634
BF = jnp.bfloat16
F32 = jnp.float32
NN = (((1,), (0,)), ((), ()))
NT = (((1,), (1,)), ((), ()))
TN = (((0,), (0,)), ((), ()))
TT = (((0,), (1,)), ((), ()))
VMEM_LIMIT = 60 << 20
CHUNK = 256
SUBS = 2


def mm(a, b, dims=NN):
    return lax.dot_general(a, b, dims, preferred_element_type=F32)


def params():
    return pltpu.CompilerParams(vmem_limit_bytes=VMEM_LIMIT)


def whole(shape):
    zeros = (0,) * len(shape)
    return pl.BlockSpec(shape, lambda *_: zeros)


def timing_rows(width):
    half = width // 2
    rates = np.exp(-math.log(10000.0) * np.arange(half, dtype=np.float64) / (half - 1))

    def rows(positions):
        angles = positions[:, None] * rates[None, :]
        return np.concatenate([np.sin(angles), np.cos(angles)], axis=1)

    return (rows(np.arange(LEN, dtype=np.float64)) + rows(np.array([float(STEP)]))).astype(
        np.float32
    )


def split_low(value):
    high = value.astype(BF)
    return high, (value - high.astype(F32)).astype(BF)


def rolled(pair):
    return jnp.concatenate([pair[:, HEAD:], pair[:, :HEAD]], axis=1)


def lane_index(shape):
    return lax.broadcasted_iota(jnp.int32, shape, 1)


def row_index(shape):
    return lax.broadcasted_iota(jnp.int32, shape, 0)


def attention_forward_kernel(seq, lengths, x_in, wq, wk, wv, *rest, heads):
    e_out, mixed_out, r_out, kaug, qaug, vaug, sa, sb, ma, mb = rest[-10:]
    j = pl.program_id(0)
    last = heads // 2 - 1
    pieces = LEN // CHUNK

    def score_piece(i, c, target):
        rows = slice(c * CHUNK, (c + 1) * CHUNK)
        s = mm(kaug[i, rows], qaug[i])
        target[rows] = s
        return jnp.max(s.reshape(CHUNK // 8, 8, LEN), axis=0)

    @pl.when(j == 0)
    def _():
        x = x_in[...]
        query = mm(wq[...], x, TT).astype(BF).astype(F32) * (LOG2E / math.sqrt(HEAD))
        high, rest = split_low(query)
        key = mm(x, wk[...]).astype(BF)
        value = mm(wv[...], x, TT).astype(BF)
        shape = (LEN, 2 * HEAD)
        lane = lane_index(shape)
        padded = row_index(shape) >= lengths[seq]
        mask = jnp.where(padded & ((lane == 0) | (lane == HEAD)), -1e30, 0.0).astype(BF)
        first = row_index((HEAD, LEN)) == 0
        ones = jnp.where(first, 1.0, 0.0).astype(BF)
        zeros = jnp.zeros((HEAD, LEN), BF)
        for i in range(heads):
            pair = key[:, (i // 2) * 128 : (i // 2) * 128 + 128]
            turned = rolled(pair)
            mine = slice(i * HEAD, (i + 1) * HEAD)
            kaug[i, :, 0:128] = pair
            if i % 2 == 0:
                kaug[i, :, 128:256] = jnp.where(lane < HEAD, mask, turned)
                parts = (high[mine], zeros, ones, rest[mine])
            else:
                kaug[i, :, 128:256] = jnp.where(lane < HEAD, turned, mask)
                parts = (zeros, high[mine], rest[mine], ones)
            for n, part in enumerate(parts):
                qaug[i, n * HEAD : (n + 1) * HEAD] = part
            vaug[i, 0:HEAD] = value[mine]
            vaug[i, HEAD : HEAD + 16] = jnp.ones((16, LEN), BF)
        top = None
        for c in range(pieces):
            m = score_piece(0, c, sa)
            top = m if top is None else jnp.maximum(top, m)
        ma[...] = jnp.max(top, axis=0, keepdims=True)

    def step(slot, cur, cur_m, nxt, nxt_m, ahead=True):
        i = 2 * j + slot
        shift = cur_m[...]
        top = None
        out = None
        for c in range(pieces):
            rows = slice(c * CHUNK, (c + 1) * CHUNK)
            if ahead:
                m = score_piece(i + 1, c, nxt)
                top = m if top is None else jnp.maximum(top, m)
            e = jnp.exp2(cur[rows] - shift).astype(BF)
            e_out[slot, rows] = e
            o = mm(vaug[i, :, rows], e)
            out = o if out is None else out + o
        if ahead:
            nxt_m[...] = jnp.max(top, axis=0, keepdims=True)
        r = 1.0 / out[HEAD : HEAD + 1]
        mixed_out[slot * HEAD : (slot + 1) * HEAD] = (out[:HEAD] * r).astype(BF)
        r_out[slot] = r

    step(0, sa, ma, sb, mb)

    @pl.when(j < last)
    def _():
        step(1, sb, mb, sa, ma)

    @pl.when(j == last)
    def _():
        step(1, sb, mb, sa, ma, ahead=False)


def attention_forward(seq, lengths, x, wq, wk, wv, earlier=()):
    rows, width = x.shape
    local = wq.shape[1]
    heads = local // HEAD
    steps, total = heads // 2, rows // LEN * heads
    return pl.pallas_call(
        functools.partial(attention_forward_kernel, seq, heads=heads),
        grid=(steps,),
        in_specs=[
            pl.BlockSpec(memory_space=pltpu.SMEM),
            pl.BlockSpec((LEN, width), lambda j: (seq, 0)),
            whole((width, local)),
            whole((width, local)),
            whole((width, local)),
        ]
        + [pl.BlockSpec(memory_space=pl.ANY)] * len(earlier),
        out_specs=[
            pl.BlockSpec((2, LEN, LEN), lambda j: (seq * steps + j, 0, 0)),
            pl.BlockSpec((2 * HEAD, LEN), lambda j: (j, seq)),
            pl.BlockSpec((2, 1, LEN), lambda j: (seq * steps + j, 0, 0)),
        ],
        out_shape=[
            jax.ShapeDtypeStruct((total, LEN, LEN), BF),
            jax.ShapeDtypeStruct((local, rows), BF),
            jax.ShapeDtypeStruct((total, 1, LEN), F32),
        ],
        scratch_shapes=[
            pltpu.VMEM((heads, LEN, 256), BF),
            pltpu.VMEM((heads, 256, LEN), BF),
            pltpu.VMEM((heads, HEAD + 16, LEN), BF),
            pltpu.VMEM((LEN, LEN), F32),
            pltpu.VMEM((LEN, LEN), F32),
            pltpu.VMEM((1, LEN), F32),
            pltpu.VMEM((1, LEN), F32),
        ],
        compiler_params=params(),
        input_output_aliases={5 + n: n for n in range(len(earlier))},
        cost_estimate=pl.CostEstimate(
            flops=8 * 2 * heads * LEN * LEN * HEAD,
            bytes_accessed=2 * heads * LEN * LEN,
            transcendentals=heads * LEN * LEN,
        ),
        name="attention_forward",
    )(lengths, x, wq, wk, wv, *earlier)


def row_mean(v):
    return jnp.mean(v, axis=-1, keepdims=True)


def norm_rows(v):
    centre = v - row_mean(v)
    deviation = lax.rsqrt(row_mean(centre * centre) + 1e-05)
    return centre * deviation, deviation


def norm_back(e, xhat, deviation):
    return deviation * (e - row_mean(e) - xhat * row_mean(e * xhat))


def fold_rows(v):
    return jnp.sum(v.reshape(v.shape[0] // 8, 8, v.shape[1]), axis=0)


def unpack(place, inner, outer, wo, wi, wu):
    width = wi.shape[0]
    quarter, blocks = width // 4, wi.shape[1] // width
    for p, ref, more in zip((0, 2, 1, 3), inner, outer):
        rows = rows_at(place[p], quarter)
        for n in range(blocks):
            columns = slice(n * width, (n + 1) * width)
            wi[rows, columns] = ref[n * quarter : (n + 1) * quarter].astype(BF)
        wo[rows_at(place[p], wo.shape[0] // 4)] = ref[blocks * quarter :].astype(BF)
        wu[rows_at(place[p], more.shape[0])] = more[...].astype(BF)


def middle_kernel(
    place, state, timing, cot, run, mix_a, mix_b, wo_a, wi_a, wu_a, v0, v1, v2, v3, v4, i0, i1,
    i2, i3, o0, o1, o2, o3, new_state, gs, att_low, wo_b, gu, gi, act, slope, inner_low, low1,
    out_low, fold, wi_b, wu_b
):
    t = pl.program_id(0)
    last = pl.num_programs(0) - 1
    tile = state.shape[0]
    size = tile // SUBS
    ff = wi_a.shape[1]
    gain1, bias1, gain2, bias2, halt_w = (v[...].reshape(1, -1) for v in (v0, v1, v2, v3, v4))
    c0 = math.sqrt(2.0 / math.pi)
    halves = ((wi_a, wu_a), (wi_b, wu_b))
    running_column = jnp.broadcast_to(run[0].astype(F32), (8, tile)).T[:, 0:1]

    @pl.when(t == 0)
    def _():
        for ref in (gu, gi, fold):
            ref[...] = jnp.zeros(ref.shape, F32)
        unpack(place, (i0, i1, i2, i3), (o0, o1, o2, o3), wo_b, wi_b, wu_b)

    def first_norm(k):
        rows = slice(k * size, (k + 1) * size)
        embedded = state[rows].astype(F32) + timing[rows]
        attended = mm(mix_a[:, rows], wo_a[...], TN) + mm(mix_b[:, rows], wo_b[...], TN)
        xhat1, dev1 = norm_rows(embedded + attended)
        normed1 = xhat1 * gain1 + bias1
        low1[rows] = normed1.astype(BF)
        return xhat1, dev1, normed1

    def forward(k, normed1):
        rows = slice(k * size, (k + 1) * size)
        total = normed1
        for n, (wi, wu) in enumerate(halves):
            v = mm(low1[rows], wi[...])
            square = v * v
            h = 0.5 + 0.5 * jnp.tanh(v * (c0 + (c0 * 0.044715) * square))
            g = v * h
            act[n, rows] = g.astype(BF)
            slope[n, rows] = h + g * (1.0 - h) * (2.0 * c0 + (6.0 * c0 * 0.044715) * square)
            total = total + mm(act[n, rows], wu[...])
        return total

    def second_norm(k, hidden2):
        rows = slice(k * size, (k + 1) * size)
        old = state[rows].astype(F32)
        xhat2, dev2 = norm_rows(hidden2)
        block = xhat2 * gain2 + bias2
        halt = jax.nn.sigmoid(jnp.sum(block * halt_w, axis=-1, keepdims=True))
        running = running_column[rows]
        gate = running * halt
        change = block - old
        new_state[rows] = old + gate * change
        g_in = cot[rows].astype(F32)
        d_prob = running * jnp.sum(g_in * change, axis=-1, keepdims=True)
        d_logit = d_prob * halt * (1.0 - halt)
        d_block = gate * g_in + d_logit * halt_w
        fold[4] += fold_rows(d_logit * block)
        fold[2] += fold_rows(d_block * xhat2)
        fold[3] += fold_rows(d_block)
        gs[rows] = g_in * (1.0 - gate)
        d_hidden2 = norm_back(d_block * gain2, xhat2, dev2)
        out_low[rows] = d_hidden2.astype(BF)
        return d_hidden2

    def backward(k, d_hidden2):
        rows = slice(k * size, (k + 1) * size)
        total = d_hidden2
        for n, (wi, wu) in enumerate(halves):
            d_act = mm(out_low[rows], wu[...], NT)
            inner_low[n, rows] = (d_act * slope[n, rows]).astype(BF)
            total = total + mm(inner_low[n, rows], wi[...], NT)
        return total

    def first_back(k, d_normed1, xhat1, dev1):
        rows = slice(k * size, (k + 1) * size)
        fold[0] += fold_rows(d_normed1 * xhat1)
        fold[1] += fold_rows(d_normed1)
        d_hidden1 = norm_back(d_normed1 * gain1, xhat1, dev1)
        att_low[rows] = d_hidden1.astype(BF)
        gs[rows] += d_hidden1

    n0 = first_norm(0)
    n1 = first_norm(1)
    f0 = forward(0, n0[2])
    s0 = second_norm(0, f0)
    f1 = forward(1, n1[2])
    b0 = backward(0, s0)
    s1 = second_norm(1, f1)
    first_back(0, b0, *n0[:2])
    b1 = backward(1, s1)
    gi[...] += mm(low1[...], inner_low[0], TN)
    gu[:ff] += mm(act[0], out_low[...], TN)
    first_back(1, b1, *n1[:2])

    @pl.when(t == last)
    def _():
        for n in range(8):
            gu[ff + n : ff + n + 1] = jnp.sum(fold[n], axis=0, keepdims=True)


def middle(place, state, timing, cot, run, mix_a, mix_b, wo_a, wi_a, wu_a, vectors, inner, outer):
    rows, width = state.shape
    local, ff = wo_a.shape[0], wi_a.shape[1]
    tile = 512
    per = LEN // tile
    by_rows = pl.BlockSpec((tile, width), lambda t: (t, 0))
    by_columns = pl.BlockSpec((local, tile), lambda t: (0, t))
    return pl.pallas_call(
        middle_kernel,
        grid=(rows // tile,),
        in_specs=[
            pl.BlockSpec(memory_space=pltpu.SMEM),
            by_rows,
            pl.BlockSpec((tile, width), lambda t: (t % per, 0)),
            by_rows,
            pl.BlockSpec((1, 1, tile), lambda t: (t, 0, 0)),
            by_columns,
            by_columns,
            whole((local, width)),
            whole((width, ff)),
            whole((ff, width)),
        ]
        + [whole((width,))] * 5
        + [whole(v.shape) for v in (*inner, *outer)],
        out_specs=[
            by_rows,
            by_rows,
            by_rows,
            whole((local, width)),
            whole((ff + 8, width)),
            whole((width, ff)),
        ],
        out_shape=[
            jax.ShapeDtypeStruct((rows, width), F32),
            jax.ShapeDtypeStruct((rows, width), F32),
            jax.ShapeDtypeStruct((rows, width), BF),
            jax.ShapeDtypeStruct((local, width), BF),
            jax.ShapeDtypeStruct((ff + 8, width), F32),
            jax.ShapeDtypeStruct((width, ff), F32),
        ],
        scratch_shapes=[
            pltpu.VMEM((2, tile, ff), BF),
            pltpu.VMEM((2, tile, ff), F32),
            pltpu.VMEM((2, tile, ff), BF),
            pltpu.VMEM((tile, width), BF),
            pltpu.VMEM((tile, width), BF),
            pltpu.VMEM((8, 8, width), F32),
            pltpu.VMEM((width, ff), BF),
            pltpu.VMEM((ff, width), BF),
        ],
        compiler_params=params(),
        cost_estimate=pl.CostEstimate(
            flops=2 * rows * width * ff * 10 + 2 * rows * width * local * 2,
            bytes_accessed=rows * width * 20,
            transcendentals=2 * rows * ff,
        ),
        name="middle",
    )(place, state, timing, cot, run.reshape(rows // tile, 1, tile), mix_a, mix_b, wo_a, wi_a,
      wu_a, *vectors, *inner, *outer)


def attention_backward_kernel(
    core, e_in, att_in, mix_in, r_in, x_in, wq, wk, wv, wo, gs_in, gs_out, *rest, heads, own
):
    if own:
        keep, send, gqkv, go, qt, kt, vaug, right, dq, dk, dv = rest
    else:
        qt, kt, vaug, right, dq, dk, dv = rest
    s, h = pl.program_id(0), pl.program_id(1)
    factor = 1.0 / math.sqrt(HEAD)
    pieces = LEN // CHUNK
    local = wq.shape[1]

    @pl.when(h == 0)
    def _():
        x = x_in[...]
        query = mm(wq[...], x, TT).astype(BF)
        key = mm(wk[...], x, TT).astype(BF)
        value = mm(x, wv[...]).astype(BF)
        lane = lane_index((LEN, 2 * HEAD))
        ones = jnp.where((lane % HEAD) < 3, 1.0, 0.0).astype(BF)
        for n in range(heads):
            mine = slice(n * HEAD, (n + 1) * HEAD)
            qt[n] = query[mine]
            kt[n] = key[mine]
            pair = value[:, (n // 2) * 128 : (n // 2) * 128 + 128]
            turned = rolled(pair)
            if n % 2 == 0:
                vaug[n, :, 0:128] = jnp.where(lane < HEAD, pair, turned)
            else:
                vaug[n, :, 0:128] = jnp.where(lane < HEAD, turned, pair)
            vaug[n, :, 128:256] = ones
        d_att = att_in[...]
        d_mixed = mm(wo[...], d_att, NT).astype(BF).astype(F32)
        index = row_index((2 * HEAD, LEN))
        for n in range(heads):
            mine = slice(n * HEAD, (n + 1) * HEAD)
            part = d_mixed[mine]
            scale = r_in[n]
            high, low = split_low(part * scale)
            right[n, 0:HEAD] = high
            right[n, HEAD : 2 * HEAD] = low
            delta = -scale * jnp.sum(part * mix_in[mine].astype(F32), axis=0, keepdims=True)
            d1 = delta.astype(BF).astype(F32)
            d2 = (delta - d1).astype(BF).astype(F32)
            d3 = delta - d1 - d2
            right[n, 2 * HEAD :] = jnp.where(
                index == 0, d1, jnp.where(index == 1, d2, jnp.where(index == 2, d3, 0.0))
            ).astype(BF)
        if own:
            g_out = mm(mix_in[...], d_att)

            @pl.when(s == 0)
            def _():
                go[...] = g_out

            @pl.when(s > 0)
            def _():
                go[...] += g_out

    high = right[h, 0:HEAD]
    query = qt[h]
    out = None
    for c in range(pieces):
        rows = slice(c * CHUNK, (c + 1) * CHUNK)
        d_probs = mm(vaug[h, rows], right[h])
        e = e_in[0, rows]
        d_scores = (e.astype(F32) * d_probs).astype(BF)
        dv[h, rows] = mm(e, high, NT).astype(BF)
        dk[h, rows] = (mm(d_scores, query, NT) * factor).astype(BF)
        o = mm(kt[h, :, rows], d_scores)
        out = o if out is None else out + o
    dq[pl.ds(pl.multiple_of(h * HEAD, HEAD), HEAD)] = (out * factor).astype(BF)

    @pl.when(h == heads - 1)
    def _():
        d_query = dq[...]
        d_key = jnp.concatenate([dk[n] for n in range(heads)], axis=1)
        d_value = jnp.concatenate([dv[n] for n in range(heads)], axis=1)
        total = mm(d_query, wq[...], TT)
        total = total + mm(d_key, wk[...], NT)
        total = total + mm(d_value, wv[...], NT)
        gs_out[...] = gs_in[...] + total
        if own:
            x = x_in[...]
            g1 = mm(d_query, x).T
            g2 = mm(x, jnp.concatenate([d_key, d_value], axis=1), TN)

            @pl.when(s == 0)
            def _():
                gqkv[:, :local] = g1
                gqkv[:, local:] = g2

            @pl.when(s > 0)
            def _():
                gqkv[:, :local] += g1
                gqkv[:, local:] += g2

            @pl.when(s == pl.num_programs(0) - 1)
            def _():
                half, few = keep.shape[0], local // 2
                wide, width = gqkv.shape[1], go.shape[1]
                for place, out in ((core[0], keep), (1 - core[0], send)):
                    out[:, :wide] = gqkv[rows_at(place, half)]
                    piece = go[rows_at(place, few)]
                    out[:few, wide:] = piece[:, : width // 2]
                    out[few:, wide:] = piece[:, width // 2 :]


def attention_backward(first, seqs, core, e, att, mix, r, x, wq, wk, wv, wo, gs, own):
    rows, width = x.shape
    local = wq.shape[1]
    heads = local // HEAD
    by_rows = pl.BlockSpec((LEN, width), lambda s, h: (first + s, 0))
    out_specs = [by_rows]
    out_shape = [jax.ShapeDtypeStruct((rows, width), F32)]
    scratch = []
    if own:
        both = (width // 2, 3 * local + width // 2)
        out_specs += [whole(both)] * 2
        out_shape += [jax.ShapeDtypeStruct(both, F32)] * 2
        scratch = [pltpu.VMEM((width, 3 * local), F32), pltpu.VMEM((local, width), F32)]
    return pl.pallas_call(
        functools.partial(attention_backward_kernel, heads=heads, own=own),
        grid=(seqs, heads),
        in_specs=[
            pl.BlockSpec(memory_space=pltpu.SMEM),
            pl.BlockSpec((1, LEN, LEN), lambda s, h: ((first + s) * heads + h, 0, 0)),
            by_rows,
            pl.BlockSpec((local, LEN), lambda s, h: (0, first + s)),
            pl.BlockSpec((heads, 1, LEN), lambda s, h: (first + s, 0, 0)),
            by_rows,
            whole((width, local)),
            whole((width, local)),
            whole((width, local)),
            whole((local, width)),
            by_rows,
        ],
        out_specs=out_specs,
        out_shape=out_shape,
        scratch_shapes=scratch
        + [
            pltpu.VMEM((heads, HEAD, LEN), BF),
            pltpu.VMEM((heads, HEAD, LEN), BF),
            pltpu.VMEM((heads, LEN, 256), BF),
            pltpu.VMEM((heads, 256, LEN), BF),
            pltpu.VMEM((local, LEN), BF),
            pltpu.VMEM((heads, LEN, HEAD), BF),
            pltpu.VMEM((heads, LEN, HEAD), BF),
        ],
        compiler_params=params(),
        input_output_aliases={10: 0},
        cost_estimate=pl.CostEstimate(
            flops=32 * 2 * seqs * heads * LEN * LEN * HEAD, bytes_accessed=1000,
            transcendentals=0,
        ),
        name="attention_backward_own" if own else "attention_backward_other",
    )(core, e, att, mix, r, x, wq, wk, wv, wo, gs)


def rows_at(index, size):
    return pl.ds(pl.multiple_of(index * size, size), size)


def local_kernel(fn, count, place, *refs):
    fn(place, refs[:count], refs[count:])


def local_call(name, fn, place, ins, outs):
    return pl.pallas_call(
        functools.partial(local_kernel, fn, len(ins)),
        in_specs=[pl.BlockSpec(memory_space=pltpu.SMEM)]
        + [pl.BlockSpec(memory_space=pltpu.VMEM)] * len(ins),
        out_specs=[pl.BlockSpec(memory_space=pltpu.VMEM)] * len(outs),
        out_shape=[jax.ShapeDtypeStruct(shape, kind) for shape, kind in outs],
        compiler_params=params(),
        name=name,
    )(place, *ins)


def cut_call(name, fn, place, ins, outs):
    return pl.pallas_call(
        functools.partial(local_kernel, fn, len(ins)),
        grid_spec=pltpu.PrefetchScalarGridSpec(
            num_scalar_prefetch=1,
            grid=(1,),
            in_specs=[
                pl.BlockSpec((v.shape[0] // 4, v.shape[1]), lambda _, p: (p[0], 0)) for v in ins
            ],
            out_specs=[pl.BlockSpec(shape, lambda _, p: (0, 0)) for shape in outs],
        ),
        out_shape=[jax.ShapeDtypeStruct(shape, F32) for shape in outs],
        compiler_params=params(),
        name=name,
    )(place, *ins)


def pack(place, ins, outs):
    wq, wk, wv, wo, wi, wu = ins
    local = wq.shape[1]
    for n, ref in enumerate((wq, wk, wv)):
        outs[0][:, n * local : (n + 1) * local] = ref[...].astype(F32)
    quarter, width = wi.shape[0], wo.shape[1]
    blocks = wi.shape[1] // width
    for n in range(blocks):
        outs[1][n * quarter : (n + 1) * quarter] = wi[:, n * width : (n + 1) * width].astype(F32)
    outs[1][blocks * quarter :] = wo[...].astype(F32)
    outs[2][...] = wu[...].astype(F32)


def embed_kernel(state, timing, out):
    out[...] = (state[...].astype(F32) + timing[...]).astype(BF)


def embed(state, timing):
    rows, width = state.shape
    tile = 512
    per = LEN // tile
    by_rows = pl.BlockSpec((tile, width), lambda p, s: (s * per + p, 0))
    return pl.pallas_call(
        embed_kernel,
        grid=(per, rows // LEN),
        in_specs=[by_rows, pl.BlockSpec((tile, width), lambda p, s: (p, 0))],
        out_specs=by_rows,
        out_shape=jax.ShapeDtypeStruct((rows, width), BF),
        compiler_params=params(),
        name="embed",
    )(state, timing)


def unpack_qkv(place, ins, outs):
    local = outs[0].shape[1]
    for p, ref in zip((0, 2, 1, 3), ins):
        rows = rows_at(place[p], ref.shape[0])
        for n, out in enumerate(outs):
            out[rows] = ref[:, n * local : (n + 1) * local].astype(BF)


def finish_kernel(
    place, g0, g1, g2, g3, gu_in, gi_in, gq, gk, gv, go, gu, gi, v0, v1, v2, v3, v4, upper,
    inner, came, left
):
    width, local = gq.shape
    ff = gu.shape[0]
    few, wide, half = g0.shape[0], 3 * local, width // 2
    pieces = [
        (gu_in, upper, gu, pl.ds(0, ff // 2)),
        (gi_in, inner, gi, pl.ds(0, width // 2)),
        (gu_in, upper, gu, pl.ds(ff // 2, ff // 2)),
        (gi_in, inner, gi, pl.ds(width // 2, width // 2)),
    ]
    into = [
        pltpu.make_async_copy(source.at[rows], held.at[rows], came.at[n])
        for n, (source, held, _, rows) in enumerate(pieces)
    ]
    tail = pl.ds(ff, 8)
    last = pltpu.make_async_copy(gu_in.at[tail], upper.at[tail], came.at[4])
    for copy in into:
        copy.start()
    last.start()
    for n, ref in enumerate((g0, g1, g2, g3)):
        core, y = jnp.bitwise_xor(place[4], n // 2), jnp.bitwise_xor(place[5], n % 2)
        rows = rows_at(2 * core + y, few)
        for k, out in enumerate((gq, gk, gv)):
            out[rows] = ref[:, k * local : (k + 1) * local]
        for k in range(2):

            @pl.when(y == k)
            def _():
                go[rows_at(core, few), k * half : (k + 1) * half] = ref[:, wide:]

    out_of = []
    for n, (_, held, target, rows) in enumerate(pieces):
        into[n].wait()
        copy = pltpu.make_async_copy(held.at[rows], target.at[rows], left.at[n])
        copy.start()
        out_of.append(copy)
    last.wait()
    for n, out in enumerate((v0, v1, v2, v3, v4)):
        out[...] = upper[ff + n]
    for copy in out_of:
        copy.wait()


def finish(place, parts, gu, gi, local):
    width, ff = gi.shape
    shapes = [(width, local)] * 3 + [(local, width), (ff, width), (width, ff)] + [(width,)] * 5
    held = pl.BlockSpec(memory_space=pltpu.VMEM)
    free = pl.BlockSpec(memory_space=pl.ANY)
    return pl.pallas_call(
        finish_kernel,
        in_specs=[pl.BlockSpec(memory_space=pltpu.SMEM)] + [held] * 4 + [free] * 2,
        out_specs=[held] * 4 + [free] * 2 + [held] * 5,
        out_shape=[jax.ShapeDtypeStruct(shape, F32) for shape in shapes],
        scratch_shapes=[
            pltpu.VMEM((ff + 8, width), F32),
            pltpu.VMEM((width, ff), F32),
            pltpu.SemaphoreType.DMA((5,)),
            pltpu.SemaphoreType.DMA((4,)),
        ],
        compiler_params=params(),
        name="finish",
    )(place, *parts, gu, gi)


def flipped(size, even, odd):
    return [(i, i ^ (odd if i & 1 else even)) for i in range(size)]


def shards(
    dp, state, lengths, halt_mask, wq, wk, wv, wo, gain1, bias1, wi, wu, gain2, bias2,
    halt_weight, cotangent
):
    rows, width = state.shape
    local, ff = wq.shape[1], wi.shape[1]
    timing = jnp.asarray(timing_rows(width))
    me = lax.axis_index("dp").astype(jnp.int32)
    shift = np.array([0, 0, 0, 0, 0, 1], np.int32)
    mask = np.array([3, 3, 3, 3, 1, 1], np.int32)
    flip = np.array([0, 1, 2, 3, 0, 0], np.int32)
    place = jnp.bitwise_xor(jnp.bitwise_and(jnp.right_shift(me, shift), mask), flip)
    bits = dp.bit_length() - 1
    tie = lax.optimization_barrier
    call = functools.partial(local_call, place=place)

    def across(v):
        return lax.ppermute(v, "mp", [(0, 1), (1, 0)])

    def along(v, even, odd=None):
        return lax.ppermute(v, "dp", flipped(dp, even, odd or even))

    quarter = width // 4
    chunk_a, chunk_b, chunk_c = cut_call(
        "pack", pack, place, (wq, wk, wv, wo, wi, wu),
        [(quarter, 3 * local), (ff // 4 + local // 4, width), (ff // 4, width)],
    )
    qkv0 = across(chunk_a)
    x = embed(state, timing)
    chunk_b, x = tie((chunk_b, x))
    in0 = across(chunk_b)
    fwd = attention_forward(0, lengths, x, wq, wk, wv)
    qkv0, chunk_c, fwd = tie((qkv0, chunk_c, fwd))
    qkv1 = along(qkv0, 2)
    out0 = across(chunk_c)
    fwd = attention_forward(1, lengths, x, wq, wk, wv, fwd)
    qkv1, in0, fwd = tie((qkv1, in0, fwd))
    qkv2, qkv3 = along(qkv0, 1), along(qkv1, 1)
    in1 = along(in0, 2)
    wq2, wk2, wv2 = call(
        "unpack_qkv", unpack_qkv, ins=(qkv0, qkv1, qkv2, qkv3),
        outs=[((width, local), BF)] * 3,
    )
    fwd2 = attention_forward(0, lengths, x, wq2, wk2, wv2)
    in1, out0, fwd2 = tie((in1, out0, fwd2))
    in2, in3 = along(in0, 1), along(in1, 1)
    out1 = along(out0, 2)
    out2 = along(out0, 1)
    fwd2 = attention_forward(1, lengths, x, wq2, wk2, wv2, fwd2)
    in2, in3, out1, out2, fwd2 = tie((in2, in3, out1, out2, fwd2))
    out3 = along(out1, 1)
    e_a, mix_a, r_a = fwd
    e_b, mix_b, r_b = fwd2
    new_state, gs, att, wo2, *grads = middle(
        place, state, timing, cotangent, halt_mask, mix_a, mix_b, wo, wi, wu,
        (gain1, bias1, gain2, bias2, halt_weight), (in0, in1, in2, in3), (out0, out1, out2, out3)
    )

    grads = lax.psum(tuple(grads), "dp")
    own = dict(core=place[4:5], e=e_a, att=att, mix=mix_a, r=r_a, x=x, wq=wq, wk=wk, wv=wv, wo=wo)
    other = dict(
        core=place[4:5], e=e_b, att=att, mix=mix_b, r=r_b, x=x, wq=wq2, wk=wk2, wv=wv2, wo=wo2
    )

    def attention_and_sums(carry):
        step, gs, *_ = carry
        back = attention_backward
        gs, keep, send = back(0, rows // LEN, gs=gs, own=True, **own)
        g = keep + along(send, 1)
        g, gs = tie((g, gs))
        few = g.shape[0] // 2
        y = place[5]
        got = along(lax.dynamic_slice_in_dim(g, (1 - y) * few, few), 2)
        (gs,) = back(0, 1, gs=gs, own=False, **other)
        got, gs = tie((got, gs))
        g = lax.dynamic_slice_in_dim(g, y * few, few) + got
        g, gs = tie((g, gs))
        got = along(g, 4, 8)
        (gs,) = back(1, rows // LEN - 1, gs=gs, own=False, **other)
        got, gs = tie((got, gs))
        g = g + got
        g = g + along(g, 8, 4)
        for bit in range(4, bits):
            g = g + along(g, 1 << bit)
        got = along(g, 2)
        parts = (g, got, along(g, 1), along(got, 1))
        return (step + 1, gs, *parts)

    once = jnp.minimum(lengths[0], 1)
    empty = [jnp.zeros((width // 4, 3 * local + width // 2), F32)] * 4
    _, gs, *parts = lax.cond(
        once > 0, attention_and_sums, lambda c: c,
        (jnp.zeros_like(once), gs, *empty),
    )
    grads, gs, parts = tie((grads, gs, parts))
    gq, gk, gv, go, gu, gi, *vec = finish(place, parts, *grads, local)
    return (
        new_state, gs, gq, gk, gv, go, vec[0], vec[1], gi, gu, vec[2], vec[3], vec[4]
    )


def solution(mesh):
    rows, columns, parts = P("dp", None), P(None, "mp"), P("mp", None)
    return jax.shard_map(
        functools.partial(shards, mesh.shape["dp"]),
        mesh=mesh,
        in_specs=(
            rows, P("dp"), P("dp"), columns, columns, columns, parts, P(), P(), columns,
            parts, P(), P(), P(), rows
        ),
        out_specs=(
            rows, rows, columns, columns, columns, parts, P(), P(), columns, parts, P(), P(),
            P()
        ),
        check_vma=False,
    )
```

```python
import functools
import math

import jax
import jax.numpy as jnp
import numpy as np
from jax import lax
from jax.experimental import pallas as pl
from jax.experimental.pallas import tpu as pltpu
from jax.sharding import PartitionSpec as P

HEAD = 64
LEN = 1024
STEP = 2
LOG2E = 1.4426950408889634
BF = jnp.bfloat16
F32 = jnp.float32
NN = (((1,), (0,)), ((), ()))
NT = (((1,), (1,)), ((), ()))
TN = (((0,), (0,)), ((), ()))
TT = (((0,), (1,)), ((), ()))
VMEM_LIMIT = 60 << 20
CHUNK = 256
SUBS = 2


def mm(a, b, dims=NN):
    return lax.dot_general(a, b, dims, preferred_element_type=F32)


def params():
    return pltpu.CompilerParams(vmem_limit_bytes=VMEM_LIMIT)


def whole(shape):
    zeros = (0,) * len(shape)
    return pl.BlockSpec(shape, lambda *_: zeros)


def timing_rows(width):
    half = width // 2
    rates = np.exp(-math.log(10000.0) * np.arange(half, dtype=np.float64) / (half - 1))

    def rows(positions):
        angles = positions[:, None] * rates[None, :]
        return np.concatenate([np.sin(angles), np.cos(angles)], axis=1)

    return (rows(np.arange(LEN, dtype=np.float64)) + rows(np.array([float(STEP)]))).astype(
        np.float32
    )


def split_low(value):
    high = value.astype(BF)
    return high, (value - high.astype(F32)).astype(BF)


def rolled(pair):
    return jnp.concatenate([pair[:, HEAD:], pair[:, :HEAD]], axis=1)


def lane_index(shape):
    return lax.broadcasted_iota(jnp.int32, shape, 1)


def row_index(shape):
    return lax.broadcasted_iota(jnp.int32, shape, 0)


def attention_forward_kernel(seq, lengths, x_in, wq, wk, wv, *rest, heads):
    e_out, mixed_out, r_out, kaug, qaug, vaug, sa, sb, ma, mb = rest[-10:]
    j = pl.program_id(0)
    last = heads // 2 - 1
    pieces = LEN // CHUNK

    def score_piece(i, c, target):
        rows = slice(c * CHUNK, (c + 1) * CHUNK)
        s = mm(kaug[i, rows], qaug[i])
        target[rows] = s
        return jnp.max(s.reshape(CHUNK // 8, 8, LEN), axis=0)

    @pl.when(j == 0)
    def _():
        x = x_in[...]
        query = mm(wq[...], x, TT).astype(BF).astype(F32) * (LOG2E / math.sqrt(HEAD))
        high, rest = split_low(query)
        key = mm(x, wk[...]).astype(BF)
        value = mm(wv[...], x, TT).astype(BF)
        shape = (LEN, 2 * HEAD)
        lane = lane_index(shape)
        padded = row_index(shape) >= lengths[seq]
        mask = jnp.where(padded & ((lane == 0) | (lane == HEAD)), -1e30, 0.0).astype(BF)
        first = row_index((HEAD, LEN)) == 0
        ones = jnp.where(first, 1.0, 0.0).astype(BF)
        zeros = jnp.zeros((HEAD, LEN), BF)
        for i in range(heads):
            pair = key[:, (i // 2) * 128 : (i // 2) * 128 + 128]
            turned = rolled(pair)
            mine = slice(i * HEAD, (i + 1) * HEAD)
            kaug[i, :, 0:128] = pair
            if i % 2 == 0:
                kaug[i, :, 128:256] = jnp.where(lane < HEAD, mask, turned)
                parts = (high[mine], zeros, ones, rest[mine])
            else:
                kaug[i, :, 128:256] = jnp.where(lane < HEAD, turned, mask)
                parts = (zeros, high[mine], rest[mine], ones)
            for n, part in enumerate(parts):
                qaug[i, n * HEAD : (n + 1) * HEAD] = part
            vaug[i, 0:HEAD] = value[mine]
            vaug[i, HEAD : HEAD + 16] = jnp.ones((16, LEN), BF)
        top = None
        for c in range(pieces):
            m = score_piece(0, c, sa)
            top = m if top is None else jnp.maximum(top, m)
        ma[...] = jnp.max(top, axis=0, keepdims=True)

    def step(slot, cur, cur_m, nxt, nxt_m, ahead=True):
        i = 2 * j + slot
        shift = cur_m[...]
        top = None
        out = None
        for c in range(pieces):
            rows = slice(c * CHUNK, (c + 1) * CHUNK)
            if ahead:
                m = score_piece(i + 1, c, nxt)
                top = m if top is None else jnp.maximum(top, m)
            e = jnp.exp2(cur[rows] - shift).astype(BF)
            e_out[slot, rows] = e
            o = mm(vaug[i, :, rows], e)
            out = o if out is None else out + o
        if ahead:
            nxt_m[...] = jnp.max(top, axis=0, keepdims=True)
        r = 1.0 / out[HEAD : HEAD + 1]
        mixed_out[slot * HEAD : (slot + 1) * HEAD] = (out[:HEAD] * r).astype(BF)
        r_out[slot] = r

    step(0, sa, ma, sb, mb)

    @pl.when(j < last)
    def _():
        step(1, sb, mb, sa, ma)

    @pl.when(j == last)
    def _():
        step(1, sb, mb, sa, ma, ahead=False)


def attention_forward(seq, lengths, x, wq, wk, wv, earlier=()):
    rows, width = x.shape
    local = wq.shape[1]
    heads = local // HEAD
    steps, total = heads // 2, rows // LEN * heads
    return pl.pallas_call(
        functools.partial(attention_forward_kernel, seq, heads=heads),
        grid=(steps,),
        in_specs=[
            pl.BlockSpec(memory_space=pltpu.SMEM),
            pl.BlockSpec((LEN, width), lambda j: (seq, 0)),
            whole((width, local)),
            whole((width, local)),
            whole((width, local)),
        ]
        + [pl.BlockSpec(memory_space=pl.ANY)] * len(earlier),
        out_specs=[
            pl.BlockSpec((2, LEN, LEN), lambda j: (seq * steps + j, 0, 0)),
            pl.BlockSpec((2 * HEAD, LEN), lambda j: (j, seq)),
            pl.BlockSpec((2, 1, LEN), lambda j: (seq * steps + j, 0, 0)),
        ],
        out_shape=[
            jax.ShapeDtypeStruct((total, LEN, LEN), BF),
            jax.ShapeDtypeStruct((local, rows), BF),
            jax.ShapeDtypeStruct((total, 1, LEN), F32),
        ],
        scratch_shapes=[
            pltpu.VMEM((heads, LEN, 256), BF),
            pltpu.VMEM((heads, 256, LEN), BF),
            pltpu.VMEM((heads, HEAD + 16, LEN), BF),
            pltpu.VMEM((LEN, LEN), F32),
            pltpu.VMEM((LEN, LEN), F32),
            pltpu.VMEM((1, LEN), F32),
            pltpu.VMEM((1, LEN), F32),
        ],
        compiler_params=params(),
        input_output_aliases={5 + n: n for n in range(len(earlier))},
        cost_estimate=pl.CostEstimate(
            flops=8 * 2 * heads * LEN * LEN * HEAD,
            bytes_accessed=2 * heads * LEN * LEN,
            transcendentals=heads * LEN * LEN,
        ),
        name="attention_forward",
    )(lengths, x, wq, wk, wv, *earlier)


def row_mean(v):
    return jnp.mean(v, axis=-1, keepdims=True)


def norm_rows(v):
    centre = v - row_mean(v)
    deviation = lax.rsqrt(row_mean(centre * centre) + 1e-05)
    return centre * deviation, deviation


def norm_back(e, xhat, deviation):
    return deviation * (e - row_mean(e) - xhat * row_mean(e * xhat))


def fold_rows(v):
    return jnp.sum(v.reshape(v.shape[0] // 8, 8, v.shape[1]), axis=0)


def middle_kernel(
    place, state, timing, cot, run, mix_a, mix_b, wo_a, wo_b, wi_a, wi_b, wu_a, v0, v1, v2, v3,
    v4, o0, o1, o2, o3, new_state, gs, att_low, gu, gi, act, slope, inner_low, low1, out_low,
    fold, wu_b
):
    t = pl.program_id(0)
    last = pl.num_programs(0) - 1
    tile = state.shape[0]
    size = tile // SUBS
    ff = wi_a.shape[1]
    gain1, bias1, gain2, bias2, halt_w = (v[...].reshape(1, -1) for v in (v0, v1, v2, v3, v4))
    c0 = math.sqrt(2.0 / math.pi)
    halves = ((wi_a, wu_a), (wi_b, wu_b))
    running_column = jnp.broadcast_to(run[0].astype(F32), (8, tile)).T[:, 0:1]

    @pl.when(t == 0)
    def _():
        for ref in (gu, gi, fold):
            ref[...] = jnp.zeros(ref.shape, F32)
        for p, ref in zip((0, 2, 1, 3), (o0, o1, o2, o3)):
            wu_b[rows_at(place[p], ref.shape[0])] = ref[...].astype(BF)

    def first_norm(k):
        rows = slice(k * size, (k + 1) * size)
        embedded = state[rows].astype(F32) + timing[rows]
        attended = mm(mix_a[:, rows], wo_a[...], TN) + mm(mix_b[:, rows], wo_b[...], TN)
        xhat1, dev1 = norm_rows(embedded + attended)
        normed1 = xhat1 * gain1 + bias1
        low1[rows] = normed1.astype(BF)
        return xhat1, dev1, normed1

    def forward(k, normed1):
        rows = slice(k * size, (k + 1) * size)
        total = normed1
        for n, (wi, wu) in enumerate(halves):
            v = mm(low1[rows], wi[...])
            square = v * v
            h = 0.5 + 0.5 * jnp.tanh(v * (c0 + (c0 * 0.044715) * square))
            g = v * h
            act[n, rows] = g.astype(BF)
            slope[n, rows] = h + g * (1.0 - h) * (2.0 * c0 + (6.0 * c0 * 0.044715) * square)
            total = total + mm(act[n, rows], wu[...])
        return total

    def second_norm(k, hidden2):
        rows = slice(k * size, (k + 1) * size)
        old = state[rows].astype(F32)
        xhat2, dev2 = norm_rows(hidden2)
        block = xhat2 * gain2 + bias2
        halt = jax.nn.sigmoid(jnp.sum(block * halt_w, axis=-1, keepdims=True))
        running = running_column[rows]
        gate = running * halt
        change = block - old
        new_state[rows] = old + gate * change
        g_in = cot[rows].astype(F32)
        d_prob = running * jnp.sum(g_in * change, axis=-1, keepdims=True)
        d_logit = d_prob * halt * (1.0 - halt)
        d_block = gate * g_in + d_logit * halt_w
        fold[4] += fold_rows(d_logit * block)
        fold[2] += fold_rows(d_block * xhat2)
        fold[3] += fold_rows(d_block)
        gs[rows] = g_in * (1.0 - gate)
        d_hidden2 = norm_back(d_block * gain2, xhat2, dev2)
        out_low[rows] = d_hidden2.astype(BF)
        return d_hidden2

    def backward(k, d_hidden2):
        rows = slice(k * size, (k + 1) * size)
        total = d_hidden2
        for n, (wi, wu) in enumerate(halves):
            d_act = mm(out_low[rows], wu[...], NT)
            inner_low[n, rows] = (d_act * slope[n, rows]).astype(BF)
            total = total + mm(inner_low[n, rows], wi[...], NT)
        return total

    def first_back(k, d_normed1, xhat1, dev1):
        rows = slice(k * size, (k + 1) * size)
        fold[0] += fold_rows(d_normed1 * xhat1)
        fold[1] += fold_rows(d_normed1)
        d_hidden1 = norm_back(d_normed1 * gain1, xhat1, dev1)
        att_low[rows] = d_hidden1.astype(BF)
        gs[rows] += d_hidden1

    n0 = first_norm(0)
    n1 = first_norm(1)
    f0 = forward(0, n0[2])
    s0 = second_norm(0, f0)
    f1 = forward(1, n1[2])
    b0 = backward(0, s0)
    s1 = second_norm(1, f1)
    first_back(0, b0, *n0[:2])
    b1 = backward(1, s1)
    gi[...] += mm(low1[...], inner_low[0], TN)
    gu[:ff] += mm(act[0], out_low[...], TN)
    first_back(1, b1, *n1[:2])

    @pl.when(t == last)
    def _():
        for n in range(8):
            gu[ff + n : ff + n + 1] = jnp.sum(fold[n], axis=0, keepdims=True)


def middle(place, state, timing, cot, run, mix_a, mix_b, wo_a, wo_b, wi_a, wi_b, wu_a, vectors,
           outer):
    rows, width = state.shape
    local, ff = wo_a.shape[0], wi_a.shape[1]
    tile = 512
    per = LEN // tile
    by_rows = pl.BlockSpec((tile, width), lambda t: (t, 0))
    by_columns = pl.BlockSpec((local, tile), lambda t: (0, t))
    return pl.pallas_call(
        middle_kernel,
        grid=(rows // tile,),
        in_specs=[
            pl.BlockSpec(memory_space=pltpu.SMEM),
            by_rows,
            pl.BlockSpec((tile, width), lambda t: (t % per, 0)),
            by_rows,
            pl.BlockSpec((1, 1, tile), lambda t: (t, 0, 0)),
            by_columns,
            by_columns,
            whole((local, width)),
            whole((local, width)),
            whole((width, ff)),
            whole((width, ff)),
            whole((ff, width)),
        ]
        + [whole((width,))] * 5
        + [whole(v.shape) for v in outer],
        out_specs=[
            by_rows,
            by_rows,
            by_rows,
            whole((ff + 8, width)),
            whole((width, ff)),
        ],
        out_shape=[
            jax.ShapeDtypeStruct((rows, width), F32),
            jax.ShapeDtypeStruct((rows, width), F32),
            jax.ShapeDtypeStruct((rows, width), BF),
            jax.ShapeDtypeStruct((ff + 8, width), F32),
            jax.ShapeDtypeStruct((width, ff), F32),
        ],
        scratch_shapes=[
            pltpu.VMEM((2, tile, ff), BF),
            pltpu.VMEM((2, tile, ff), F32),
            pltpu.VMEM((2, tile, ff), BF),
            pltpu.VMEM((tile, width), BF),
            pltpu.VMEM((tile, width), BF),
            pltpu.VMEM((8, 8, width), F32),
            pltpu.VMEM((ff, width), BF),
        ],
        compiler_params=params(),
        cost_estimate=pl.CostEstimate(
            flops=2 * rows * width * ff * 10 + 2 * rows * width * local * 2,
            bytes_accessed=rows * width * 20,
            transcendentals=2 * rows * ff,
        ),
        name="middle",
    )(place, state, timing, cot, run.reshape(rows // tile, 1, tile), mix_a, mix_b, wo_a, wo_b,
      wi_a, wi_b, wu_a, *vectors, *outer)


def attention_backward_kernel(
    core, e_in, att_in, mix_in, r_in, x_in, wq, wk, wv, wo, gs_in, gs_out, *rest, heads, own
):
    if own:
        keep, send, gqkv, go, qt, kt, vaug, right, dq, dk, dv = rest
    else:
        qt, kt, vaug, right, dq, dk, dv = rest
    s, h = pl.program_id(0), pl.program_id(1)
    factor = 1.0 / math.sqrt(HEAD)
    pieces = LEN // CHUNK
    local = wq.shape[1]

    @pl.when(h == 0)
    def _():
        x = x_in[...]
        query = mm(wq[...], x, TT).astype(BF)
        key = mm(wk[...], x, TT).astype(BF)
        value = mm(x, wv[...]).astype(BF)
        lane = lane_index((LEN, 2 * HEAD))
        ones = jnp.where((lane % HEAD) < 3, 1.0, 0.0).astype(BF)
        for n in range(heads):
            mine = slice(n * HEAD, (n + 1) * HEAD)
            qt[n] = query[mine]
            kt[n] = key[mine]
            pair = value[:, (n // 2) * 128 : (n // 2) * 128 + 128]
            turned = rolled(pair)
            if n % 2 == 0:
                vaug[n, :, 0:128] = jnp.where(lane < HEAD, pair, turned)
            else:
                vaug[n, :, 0:128] = jnp.where(lane < HEAD, turned, pair)
            vaug[n, :, 128:256] = ones
        d_att = att_in[...]
        d_mixed = mm(wo[...], d_att, NT).astype(BF).astype(F32)
        index = row_index((2 * HEAD, LEN))
        for n in range(heads):
            mine = slice(n * HEAD, (n + 1) * HEAD)
            part = d_mixed[mine]
            scale = r_in[n]
            high, low = split_low(part * scale)
            right[n, 0:HEAD] = high
            right[n, HEAD : 2 * HEAD] = low
            delta = -scale * jnp.sum(part * mix_in[mine].astype(F32), axis=0, keepdims=True)
            d1 = delta.astype(BF).astype(F32)
            d2 = (delta - d1).astype(BF).astype(F32)
            d3 = delta - d1 - d2
            right[n, 2 * HEAD :] = jnp.where(
                index == 0, d1, jnp.where(index == 1, d2, jnp.where(index == 2, d3, 0.0))
            ).astype(BF)
        if own:
            g_out = mm(mix_in[...], d_att)

            @pl.when(s == 0)
            def _():
                go[...] = g_out

            @pl.when(s > 0)
            def _():
                go[...] += g_out

    high = right[h, 0:HEAD]
    query = qt[h]
    out = None
    for c in range(pieces):
        rows = slice(c * CHUNK, (c + 1) * CHUNK)
        d_probs = mm(vaug[h, rows], right[h])
        e = e_in[0, rows]
        d_scores = (e.astype(F32) * d_probs).astype(BF)
        dv[h, rows] = mm(e, high, NT).astype(BF)
        dk[h, rows] = (mm(d_scores, query, NT) * factor).astype(BF)
        o = mm(kt[h, :, rows], d_scores)
        out = o if out is None else out + o
    dq[pl.ds(pl.multiple_of(h * HEAD, HEAD), HEAD)] = (out * factor).astype(BF)

    @pl.when(h == heads - 1)
    def _():
        d_query = dq[...]
        d_key = jnp.concatenate([dk[n] for n in range(heads)], axis=1)
        d_value = jnp.concatenate([dv[n] for n in range(heads)], axis=1)
        total = mm(d_query, wq[...], TT)
        total = total + mm(d_key, wk[...], NT)
        total = total + mm(d_value, wv[...], NT)
        gs_out[...] = gs_in[...] + total
        if own:
            x = x_in[...]
            g1 = mm(d_query, x).T
            g2 = mm(x, jnp.concatenate([d_key, d_value], axis=1), TN)

            @pl.when(s == 0)
            def _():
                gqkv[:, :local] = g1
                gqkv[:, local:] = g2

            @pl.when(s > 0)
            def _():
                gqkv[:, :local] += g1
                gqkv[:, local:] += g2

            @pl.when(s == pl.num_programs(0) - 1)
            def _():
                half, few = keep.shape[0], local // 2
                wide, width = gqkv.shape[1], go.shape[1]
                for place, out in ((core[0], keep), (1 - core[0], send)):
                    out[:, :wide] = gqkv[rows_at(place, half)]
                    piece = go[rows_at(place, few)]
                    out[:few, wide:] = piece[:, : width // 2]
                    out[few:, wide:] = piece[:, width // 2 :]


def attention_backward(first, seqs, core, e, att, mix, r, x, wq, wk, wv, wo, gs, own):
    rows, width = x.shape
    local = wq.shape[1]
    heads = local // HEAD
    by_rows = pl.BlockSpec((LEN, width), lambda s, h: (first + s, 0))
    out_specs = [by_rows]
    out_shape = [jax.ShapeDtypeStruct((rows, width), F32)]
    scratch = []
    if own:
        both = (width // 2, 3 * local + width // 2)
        out_specs += [whole(both)] * 2
        out_shape += [jax.ShapeDtypeStruct(both, F32)] * 2
        scratch = [pltpu.VMEM((width, 3 * local), F32), pltpu.VMEM((local, width), F32)]
    return pl.pallas_call(
        functools.partial(attention_backward_kernel, heads=heads, own=own),
        grid=(seqs, heads),
        in_specs=[
            pl.BlockSpec(memory_space=pltpu.SMEM),
            pl.BlockSpec((1, LEN, LEN), lambda s, h: ((first + s) * heads + h, 0, 0)),
            by_rows,
            pl.BlockSpec((local, LEN), lambda s, h: (0, first + s)),
            pl.BlockSpec((heads, 1, LEN), lambda s, h: (first + s, 0, 0)),
            by_rows,
            whole((width, local)),
            whole((width, local)),
            whole((width, local)),
            whole((local, width)),
            by_rows,
        ],
        out_specs=out_specs,
        out_shape=out_shape,
        scratch_shapes=scratch
        + [
            pltpu.VMEM((heads, HEAD, LEN), BF),
            pltpu.VMEM((heads, HEAD, LEN), BF),
            pltpu.VMEM((heads, LEN, 256), BF),
            pltpu.VMEM((heads, 256, LEN), BF),
            pltpu.VMEM((local, LEN), BF),
            pltpu.VMEM((heads, LEN, HEAD), BF),
            pltpu.VMEM((heads, LEN, HEAD), BF),
        ],
        compiler_params=params(),
        input_output_aliases={10: 0},
        cost_estimate=pl.CostEstimate(
            flops=32 * 2 * seqs * heads * LEN * LEN * HEAD, bytes_accessed=1000,
            transcendentals=0,
        ),
        name="attention_backward_own" if own else "attention_backward_other",
    )(core, e, att, mix, r, x, wq, wk, wv, wo, gs)


def rows_at(index, size):
    return pl.ds(pl.multiple_of(index * size, size), size)


def local_kernel(fn, count, place, *refs):
    fn(place, refs[:count], refs[count:])


def local_call(name, fn, place, ins, outs):
    return pl.pallas_call(
        functools.partial(local_kernel, fn, len(ins)),
        in_specs=[pl.BlockSpec(memory_space=pltpu.SMEM)]
        + [pl.BlockSpec(memory_space=pltpu.VMEM)] * len(ins),
        out_specs=[pl.BlockSpec(memory_space=pltpu.VMEM)] * len(outs),
        out_shape=[jax.ShapeDtypeStruct(shape, kind) for shape, kind in outs],
        compiler_params=params(),
        name=name,
    )(place, *ins)


def cut_call(name, fn, place, ins, outs):
    return pl.pallas_call(
        functools.partial(local_kernel, fn, len(ins)),
        grid_spec=pltpu.PrefetchScalarGridSpec(
            num_scalar_prefetch=1,
            grid=(1,),
            in_specs=[
                pl.BlockSpec((v.shape[0] // 4, v.shape[1]), lambda _, p: (p[0], 0)) for v in ins
            ],
            out_specs=[pl.BlockSpec(shape, lambda _, p: (0, 0)) for shape in outs],
        ),
        out_shape=[jax.ShapeDtypeStruct(shape, F32) for shape in outs],
        compiler_params=params(),
        name=name,
    )(place, *ins)


def pack(place, ins, outs):
    wq, wk, wv, wo, wi, wu = ins
    local = wq.shape[1]
    for n, ref in enumerate((wq, wk, wv)):
        outs[0][:, n * local : (n + 1) * local] = ref[...].astype(F32)
    quarter, width = wi.shape[0], wo.shape[1]
    blocks = wi.shape[1] // width
    for n in range(blocks):
        outs[1][n * quarter : (n + 1) * quarter] = wi[:, n * width : (n + 1) * width].astype(F32)
    outs[1][blocks * quarter :] = wo[...].astype(F32)
    outs[2][...] = wu[...].astype(F32)


def embed_kernel(state, timing, out):
    out[...] = (state[...].astype(F32) + timing[...]).astype(BF)


def embed(state, timing):
    rows, width = state.shape
    tile = 512
    per = LEN // tile
    by_rows = pl.BlockSpec((tile, width), lambda p, s: (s * per + p, 0))
    return pl.pallas_call(
        embed_kernel,
        grid=(per, rows // LEN),
        in_specs=[by_rows, pl.BlockSpec((tile, width), lambda p, s: (p, 0))],
        out_specs=by_rows,
        out_shape=jax.ShapeDtypeStruct((rows, width), BF),
        compiler_params=params(),
        name="embed",
    )(state, timing)


def unpack_qkv(place, ins, outs):
    local = outs[0].shape[1]
    for p, ref in zip((0, 2, 1, 3), ins):
        rows = rows_at(place[p], ref.shape[0])
        for n, out in enumerate(outs):
            out[rows] = ref[:, n * local : (n + 1) * local].astype(BF)


def unpack_inner(place, ins, outs):
    wo, wi = outs
    width = wi.shape[0]
    quarter, blocks = width // 4, wi.shape[1] // width
    for p, ref in zip((0, 2, 1, 3), ins):
        rows = rows_at(place[p], quarter)
        for n in range(blocks):
            columns = slice(n * width, (n + 1) * width)
            wi[rows, columns] = ref[n * quarter : (n + 1) * quarter].astype(BF)
        wo[rows_at(place[p], wo.shape[0] // 4)] = ref[blocks * quarter :].astype(BF)


def finish_qkv(place, ins, outs):
    gq, gk, gv, go = outs
    width, local = gq.shape
    few, wide, half = ins[0].shape[0], 3 * local, width // 2
    for n, ref in enumerate(ins):
        core, y = jnp.bitwise_xor(place[4], n // 2), jnp.bitwise_xor(place[5], n % 2)
        rows = rows_at(2 * core + y, few)
        for k, out in enumerate((gq, gk, gv)):
            out[rows] = ref[:, k * local : (k + 1) * local]
        for k in range(2):

            @pl.when(y == k)
            def _():
                go[rows_at(core, few), k * half : (k + 1) * half] = ref[:, wide:]


def finish_ff_kernel(gu_in, vec_in, gi_in, gu, gi, *vec):
    gu[...] = gu_in[...]
    gi[...] = gi_in[...]

    @pl.when(pl.program_id(0) == 0)
    def _():
        for n, out in enumerate(vec):
            out[...] = vec_in[n]


def finish_ff(gu, gi):
    width, ff = gi.shape
    steps = 2
    upper = pl.BlockSpec((ff // steps, width), lambda i: (i, 0))
    inner = pl.BlockSpec((width // steps, ff), lambda i: (i, 0))
    return pl.pallas_call(
        finish_ff_kernel,
        grid=(steps,),
        in_specs=[upper, pl.BlockSpec((8, width), lambda i: (ff // 8, 0)), inner],
        out_specs=[upper, inner] + [whole((width,))] * 5,
        out_shape=[
            jax.ShapeDtypeStruct(shape, F32)
            for shape in [(ff, width), (width, ff)] + [(width,)] * 5
        ],
        compiler_params=params(),
        name="finish_ff",
    )(gu, gu, gi)


def flipped(size, even, odd):
    return [(i, i ^ (odd if i & 1 else even)) for i in range(size)]


def shards(
    dp, state, lengths, halt_mask, wq, wk, wv, wo, gain1, bias1, wi, wu, gain2, bias2,
    halt_weight, cotangent
):
    rows, width = state.shape
    local, ff = wq.shape[1], wi.shape[1]
    timing = jnp.asarray(timing_rows(width))
    me = lax.axis_index("dp").astype(jnp.int32)
    shift = np.array([0, 0, 0, 0, 0, 1], np.int32)
    mask = np.array([3, 3, 3, 3, 1, 1], np.int32)
    flip = np.array([0, 1, 2, 3, 0, 0], np.int32)
    place = jnp.bitwise_xor(jnp.bitwise_and(jnp.right_shift(me, shift), mask), flip)
    bits = dp.bit_length() - 1
    tie = lax.optimization_barrier
    call = functools.partial(local_call, place=place)

    def across(v):
        return lax.ppermute(v, "mp", [(0, 1), (1, 0)])

    def along(v, even, odd=None):
        return lax.ppermute(v, "dp", flipped(dp, even, odd or even))

    quarter = width // 4
    chunk_a, chunk_b, chunk_c = cut_call(
        "pack", pack, place, (wq, wk, wv, wo, wi, wu),
        [(quarter, 3 * local), (ff // 4 + local // 4, width), (ff // 4, width)],
    )
    qkv0 = across(chunk_a)
    x = embed(state, timing)
    chunk_b, x = tie((chunk_b, x))
    in0 = across(chunk_b)
    fwd = attention_forward(0, lengths, x, wq, wk, wv)
    qkv0, chunk_c, fwd = tie((qkv0, chunk_c, fwd))
    qkv1 = along(qkv0, 2)
    out0 = across(chunk_c)
    fwd = attention_forward(1, lengths, x, wq, wk, wv, fwd)
    qkv1, in0, fwd = tie((qkv1, in0, fwd))
    qkv2, qkv3 = along(qkv0, 1), along(qkv1, 1)
    in1 = along(in0, 2)
    wq2, wk2, wv2 = call(
        "unpack_qkv", unpack_qkv, ins=(qkv0, qkv1, qkv2, qkv3),
        outs=[((width, local), BF)] * 3,
    )
    fwd2 = attention_forward(0, lengths, x, wq2, wk2, wv2)
    in1, out0, fwd2 = tie((in1, out0, fwd2))
    in2, in3 = along(in0, 1), along(in1, 1)
    out1 = along(out0, 2)
    out2 = along(out0, 1)
    fwd2 = attention_forward(1, lengths, x, wq2, wk2, wv2, fwd2)
    in2, in3, fwd2 = tie((in2, in3, fwd2))
    wo2, wi2 = call(
        "unpack_inner", unpack_inner, ins=(in0, in1, in2, in3),
        outs=[((local, width), BF), ((width, ff), BF)],
    )
    out1, out2, wo2, wi2 = tie((out1, out2, wo2, wi2))
    out3 = along(out1, 1)
    e_a, mix_a, r_a = fwd
    e_b, mix_b, r_b = fwd2
    new_state, gs, att, *grads = middle(
        place, state, timing, cotangent, halt_mask, mix_a, mix_b, wo, wo2, wi, wi2, wu,
        (gain1, bias1, gain2, bias2, halt_weight), (out0, out1, out2, out3)
    )

    grads = lax.psum(tuple(grads), "dp")
    own = dict(core=place[4:5], e=e_a, att=att, mix=mix_a, r=r_a, x=x, wq=wq, wk=wk, wv=wv, wo=wo)
    other = dict(
        core=place[4:5], e=e_b, att=att, mix=mix_b, r=r_b, x=x, wq=wq2, wk=wk2, wv=wv2, wo=wo2
    )

    def attention_and_sums(carry):
        step, gs, *_ = carry
        back = attention_backward
        gs, keep, send = back(0, rows // LEN, gs=gs, own=True, **own)
        g = keep + along(send, 1)
        g, gs = tie((g, gs))
        few = g.shape[0] // 2
        y = place[5]
        got = along(lax.dynamic_slice_in_dim(g, (1 - y) * few, few), 2)
        (gs,) = back(0, 1, gs=gs, own=False, **other)
        got, gs = tie((got, gs))
        g = lax.dynamic_slice_in_dim(g, y * few, few) + got
        g, gs = tie((g, gs))
        got = along(g, 4, 8)
        (gs,) = back(1, rows // LEN - 1, gs=gs, own=False, **other)
        got, gs = tie((got, gs))
        g = g + got
        g = g + along(g, 8, 4)
        for bit in range(4, bits):
            g = g + along(g, 1 << bit)
        got = along(g, 2)
        parts = call(
            "finish_qkv", finish_qkv, ins=(g, got, along(g, 1), along(got, 1)),
            outs=[((width, local), F32)] * 3 + [((local, width), F32)],
        )
        return (step + 1, gs, *parts)

    once = jnp.minimum(lengths[0], 1)
    empty = [jnp.zeros(shape, F32) for shape in [(width, local)] * 3 + [(local, width)]]
    _, gs, gq, gk, gv, go = lax.cond(
        once > 0, attention_and_sums, lambda c: c,
        (jnp.zeros_like(once), gs, *empty),
    )
    grads, gs, gq = tie((grads, gs, gq))
    gu, gi, *vec = finish_ff(*grads)
    return (
        new_state, gs, gq, gk, gv, go, vec[0], vec[1], gi, gu, vec[2], vec[3], vec[4]
    )


def solution(mesh):
    rows, columns, parts = P("dp", None), P(None, "mp"), P("mp", None)
    return jax.shard_map(
        functools.partial(shards, mesh.shape["dp"]),
        mesh=mesh,
        in_specs=(
            rows, P("dp"), P("dp"), columns, columns, columns, parts, P(), P(), columns,
            parts, P(), P(), P(), rows
        ),
        out_specs=(
            rows, rows, columns, columns, columns, parts, P(), P(), columns, parts, P(), P(),
            P()
        ),
        check_vma=False,
    )
```

```python
import functools
import math

import jax
import jax.numpy as jnp
import numpy as np
from jax import lax
from jax.experimental import pallas as pl
from jax.experimental.pallas import tpu as pltpu
from jax.sharding import PartitionSpec as P

HEAD = 64
LEN = 1024
STEP = 2
LOG2E = 1.4426950408889634
BF = jnp.bfloat16
F32 = jnp.float32
NN = (((1,), (0,)), ((), ()))
NT = (((1,), (1,)), ((), ()))
TN = (((0,), (0,)), ((), ()))
TT = (((0,), (1,)), ((), ()))
VMEM_LIMIT = 60 << 20
CHUNK = 256
SUBS = 2


def mm(a, b, dims=NN):
    return lax.dot_general(a, b, dims, preferred_element_type=F32)


def params():
    return pltpu.CompilerParams(vmem_limit_bytes=VMEM_LIMIT)


def whole(shape):
    zeros = (0,) * len(shape)
    return pl.BlockSpec(shape, lambda *_: zeros)


def timing_rows(width):
    half = width // 2
    rates = np.exp(-math.log(10000.0) * np.arange(half, dtype=np.float64) / (half - 1))

    def rows(positions):
        angles = positions[:, None] * rates[None, :]
        return np.concatenate([np.sin(angles), np.cos(angles)], axis=1)

    return (rows(np.arange(LEN, dtype=np.float64)) + rows(np.array([float(STEP)]))).astype(
        np.float32
    )


def split_low(value):
    high = value.astype(BF)
    return high, (value - high.astype(F32)).astype(BF)


def rolled(pair):
    return jnp.concatenate([pair[:, HEAD:], pair[:, :HEAD]], axis=1)


def lane_index(shape):
    return lax.broadcasted_iota(jnp.int32, shape, 1)


def row_index(shape):
    return lax.broadcasted_iota(jnp.int32, shape, 0)


def attention_forward_kernel(seq, lengths, x_in, wq, wk, wv, *rest, heads):
    e_out, mixed_out, r_out, kaug, qaug, vaug, sa, sb, ma, mb = rest[-10:]
    j = pl.program_id(0)
    last = heads // 2 - 1
    pieces = LEN // CHUNK

    def score_piece(i, c, target):
        rows = slice(c * CHUNK, (c + 1) * CHUNK)
        s = mm(kaug[i, rows], qaug[i])
        target[rows] = s
        return jnp.max(s.reshape(CHUNK // 8, 8, LEN), axis=0)

    @pl.when(j == 0)
    def _():
        x = x_in[...]
        query = mm(wq[...], x, TT).astype(BF).astype(F32) * (LOG2E / math.sqrt(HEAD))
        high, rest = split_low(query)
        key = mm(x, wk[...]).astype(BF)
        value = mm(wv[...], x, TT).astype(BF)
        shape = (LEN, 2 * HEAD)
        lane = lane_index(shape)
        padded = row_index(shape) >= lengths[seq]
        mask = jnp.where(padded & ((lane == 0) | (lane == HEAD)), -1e30, 0.0).astype(BF)
        first = row_index((HEAD, LEN)) == 0
        ones = jnp.where(first, 1.0, 0.0).astype(BF)
        zeros = jnp.zeros((HEAD, LEN), BF)
        for i in range(heads):
            pair = key[:, (i // 2) * 128 : (i // 2) * 128 + 128]
            turned = rolled(pair)
            mine = slice(i * HEAD, (i + 1) * HEAD)
            kaug[i, :, 0:128] = pair
            if i % 2 == 0:
                kaug[i, :, 128:256] = jnp.where(lane < HEAD, mask, turned)
                parts = (high[mine], zeros, ones, rest[mine])
            else:
                kaug[i, :, 128:256] = jnp.where(lane < HEAD, turned, mask)
                parts = (zeros, high[mine], rest[mine], ones)
            for n, part in enumerate(parts):
                qaug[i, n * HEAD : (n + 1) * HEAD] = part
            vaug[i, 0:HEAD] = value[mine]
            vaug[i, HEAD : HEAD + 16] = jnp.ones((16, LEN), BF)
        top = None
        for c in range(pieces):
            m = score_piece(0, c, sa)
            top = m if top is None else jnp.maximum(top, m)
        ma[...] = jnp.max(top, axis=0, keepdims=True)

    def step(slot, cur, cur_m, nxt, nxt_m, ahead=True):
        i = 2 * j + slot
        shift = cur_m[...]
        top = None
        out = None
        for c in range(pieces):
            rows = slice(c * CHUNK, (c + 1) * CHUNK)
            if ahead:
                m = score_piece(i + 1, c, nxt)
                top = m if top is None else jnp.maximum(top, m)
            e = jnp.exp2(cur[rows] - shift).astype(BF)
            e_out[slot, rows] = e
            o = mm(vaug[i, :, rows], e)
            out = o if out is None else out + o
        if ahead:
            nxt_m[...] = jnp.max(top, axis=0, keepdims=True)
        r = 1.0 / out[HEAD : HEAD + 1]
        mixed_out[slot * HEAD : (slot + 1) * HEAD] = (out[:HEAD] * r).astype(BF)
        r_out[slot] = r

    step(0, sa, ma, sb, mb)

    @pl.when(j < last)
    def _():
        step(1, sb, mb, sa, ma)

    @pl.when(j == last)
    def _():
        step(1, sb, mb, sa, ma, ahead=False)


def attention_forward(seq, lengths, x, wq, wk, wv, earlier=()):
    rows, width = x.shape
    local = wq.shape[1]
    heads = local // HEAD
    steps, total = heads // 2, rows // LEN * heads
    return pl.pallas_call(
        functools.partial(attention_forward_kernel, seq, heads=heads),
        grid=(steps,),
        in_specs=[
            pl.BlockSpec(memory_space=pltpu.SMEM),
            pl.BlockSpec((LEN, width), lambda j: (seq, 0)),
            whole((width, local)),
            whole((width, local)),
            whole((width, local)),
        ]
        + [pl.BlockSpec(memory_space=pl.ANY)] * len(earlier),
        out_specs=[
            pl.BlockSpec((2, LEN, LEN), lambda j: (seq * steps + j, 0, 0)),
            pl.BlockSpec((2 * HEAD, LEN), lambda j: (j, seq)),
            pl.BlockSpec((2, 1, LEN), lambda j: (seq * steps + j, 0, 0)),
        ],
        out_shape=[
            jax.ShapeDtypeStruct((total, LEN, LEN), BF),
            jax.ShapeDtypeStruct((local, rows), BF),
            jax.ShapeDtypeStruct((total, 1, LEN), F32),
        ],
        scratch_shapes=[
            pltpu.VMEM((heads, LEN, 256), BF),
            pltpu.VMEM((heads, 256, LEN), BF),
            pltpu.VMEM((heads, HEAD + 16, LEN), BF),
            pltpu.VMEM((LEN, LEN), F32),
            pltpu.VMEM((LEN, LEN), F32),
            pltpu.VMEM((1, LEN), F32),
            pltpu.VMEM((1, LEN), F32),
        ],
        compiler_params=params(),
        input_output_aliases={5 + n: n for n in range(len(earlier))},
        cost_estimate=pl.CostEstimate(
            flops=8 * 2 * heads * LEN * LEN * HEAD,
            bytes_accessed=2 * heads * LEN * LEN,
            transcendentals=heads * LEN * LEN,
        ),
        name="attention_forward",
    )(lengths, x, wq, wk, wv, *earlier)


def row_mean(v):
    return jnp.mean(v, axis=-1, keepdims=True)


def norm_rows(v):
    centre = v - row_mean(v)
    deviation = lax.rsqrt(row_mean(centre * centre) + 1e-05)
    return centre * deviation, deviation


def norm_back(e, xhat, deviation):
    return deviation * (e - row_mean(e) - xhat * row_mean(e * xhat))


def fold_rows(v):
    return jnp.sum(v.reshape(v.shape[0] // 8, 8, v.shape[1]), axis=0)


def middle_kernel(
    place, state, timing, cot, run, mix_a, mix_b, wo_a, wo_b, wi_a, wi_b, wu_a, v0, v1, v2, v3,
    v4, o0, o1, o2, o3, new_state, gs, att_low, gu, gi, act, slope, inner_low, low1, out_low,
    fold, wu_b
):
    t = pl.program_id(0)
    last = pl.num_programs(0) - 1
    tile = state.shape[0]
    size = tile // SUBS
    ff = wi_a.shape[1]
    gain1, bias1, gain2, bias2, halt_w = (v[...].reshape(1, -1) for v in (v0, v1, v2, v3, v4))
    c0 = math.sqrt(2.0 / math.pi)
    halves = ((wi_a, wu_a), (wi_b, wu_b))
    running_column = jnp.broadcast_to(run[0].astype(F32), (8, tile)).T[:, 0:1]

    @pl.when(t == 0)
    def _():
        for ref in (gu, gi, fold):
            ref[...] = jnp.zeros(ref.shape, F32)
        for p, ref in zip((0, 2, 1, 3), (o0, o1, o2, o3)):
            wu_b[rows_at(place[p], ref.shape[0])] = ref[...].astype(BF)

    def first_norm(k):
        rows = slice(k * size, (k + 1) * size)
        embedded = state[rows].astype(F32) + timing[rows]
        attended = mm(mix_a[:, rows], wo_a[...], TN) + mm(mix_b[:, rows], wo_b[...], TN)
        xhat1, dev1 = norm_rows(embedded + attended)
        normed1 = xhat1 * gain1 + bias1
        low1[rows] = normed1.astype(BF)
        return xhat1, dev1, normed1

    def forward(k, normed1):
        rows = slice(k * size, (k + 1) * size)
        total = normed1
        for n, (wi, wu) in enumerate(halves):
            v = mm(low1[rows], wi[...])
            square = v * v
            h = 0.5 + 0.5 * jnp.tanh(v * (c0 + (c0 * 0.044715) * square))
            g = v * h
            act[n, rows] = g.astype(BF)
            slope[n, rows] = h + g * (1.0 - h) * (2.0 * c0 + (6.0 * c0 * 0.044715) * square)
            total = total + mm(act[n, rows], wu[...])
        return total

    def second_norm(k, hidden2):
        rows = slice(k * size, (k + 1) * size)
        old = state[rows].astype(F32)
        xhat2, dev2 = norm_rows(hidden2)
        block = xhat2 * gain2 + bias2
        halt = jax.nn.sigmoid(jnp.sum(block * halt_w, axis=-1, keepdims=True))
        running = running_column[rows]
        gate = running * halt
        change = block - old
        new_state[rows] = old + gate * change
        g_in = cot[rows].astype(F32)
        d_prob = running * jnp.sum(g_in * change, axis=-1, keepdims=True)
        d_logit = d_prob * halt * (1.0 - halt)
        d_block = gate * g_in + d_logit * halt_w
        fold[4] += fold_rows(d_logit * block)
        fold[2] += fold_rows(d_block * xhat2)
        fold[3] += fold_rows(d_block)
        gs[rows] = g_in * (1.0 - gate)
        d_hidden2 = norm_back(d_block * gain2, xhat2, dev2)
        out_low[rows] = d_hidden2.astype(BF)
        return d_hidden2

    def backward(k, d_hidden2):
        rows = slice(k * size, (k + 1) * size)
        total = d_hidden2
        for n, (wi, wu) in enumerate(halves):
            d_act = mm(out_low[rows], wu[...], NT)
            inner_low[n, rows] = (d_act * slope[n, rows]).astype(BF)
            total = total + mm(inner_low[n, rows], wi[...], NT)
        return total

    def first_back(k, d_normed1, xhat1, dev1):
        rows = slice(k * size, (k + 1) * size)
        fold[0] += fold_rows(d_normed1 * xhat1)
        fold[1] += fold_rows(d_normed1)
        d_hidden1 = norm_back(d_normed1 * gain1, xhat1, dev1)
        att_low[rows] = d_hidden1.astype(BF)
        gs[rows] += d_hidden1

    n0 = first_norm(0)
    n1 = first_norm(1)
    f0 = forward(0, n0[2])
    s0 = second_norm(0, f0)
    f1 = forward(1, n1[2])
    b0 = backward(0, s0)
    s1 = second_norm(1, f1)
    first_back(0, b0, *n0[:2])
    b1 = backward(1, s1)
    gi[...] += mm(low1[...], inner_low[0], TN)
    gu[:ff] += mm(act[0], out_low[...], TN)
    first_back(1, b1, *n1[:2])

    @pl.when(t == last)
    def _():
        for n in range(8):
            gu[ff + n : ff + n + 1] = jnp.sum(fold[n], axis=0, keepdims=True)


def middle(place, state, timing, cot, run, mix_a, mix_b, wo_a, wo_b, wi_a, wi_b, wu_a, vectors,
           outer):
    rows, width = state.shape
    local, ff = wo_a.shape[0], wi_a.shape[1]
    tile = 512
    per = LEN // tile
    by_rows = pl.BlockSpec((tile, width), lambda t: (t, 0))
    by_columns = pl.BlockSpec((local, tile), lambda t: (0, t))
    return pl.pallas_call(
        middle_kernel,
        grid=(rows // tile,),
        in_specs=[
            pl.BlockSpec(memory_space=pltpu.SMEM),
            by_rows,
            pl.BlockSpec((tile, width), lambda t: (t % per, 0)),
            by_rows,
            pl.BlockSpec((1, 1, tile), lambda t: (t, 0, 0)),
            by_columns,
            by_columns,
            whole((local, width)),
            whole((local, width)),
            whole((width, ff)),
            whole((width, ff)),
            whole((ff, width)),
        ]
        + [whole((width,))] * 5
        + [whole(v.shape) for v in outer],
        out_specs=[
            by_rows,
            by_rows,
            by_rows,
            whole((ff + 8, width)),
            whole((width, ff)),
        ],
        out_shape=[
            jax.ShapeDtypeStruct((rows, width), F32),
            jax.ShapeDtypeStruct((rows, width), F32),
            jax.ShapeDtypeStruct((rows, width), BF),
            jax.ShapeDtypeStruct((ff + 8, width), F32),
            jax.ShapeDtypeStruct((width, ff), F32),
        ],
        scratch_shapes=[
            pltpu.VMEM((2, tile, ff), BF),
            pltpu.VMEM((2, tile, ff), F32),
            pltpu.VMEM((2, tile, ff), BF),
            pltpu.VMEM((tile, width), BF),
            pltpu.VMEM((tile, width), BF),
            pltpu.VMEM((8, 8, width), F32),
            pltpu.VMEM((ff, width), BF),
        ],
        compiler_params=params(),
        cost_estimate=pl.CostEstimate(
            flops=2 * rows * width * ff * 10 + 2 * rows * width * local * 2,
            bytes_accessed=rows * width * 20,
            transcendentals=2 * rows * ff,
        ),
        name="middle",
    )(place, state, timing, cot, run.reshape(rows // tile, 1, tile), mix_a, mix_b, wo_a, wo_b,
      wi_a, wi_b, wu_a, *vectors, *outer)


def attention_backward_kernel(
    core, e_in, att_in, mix_in, r_in, x_in, wq, wk, wv, wo, gs_in, gs_out, *rest, heads, own
):
    if own:
        keep, send, gqkv, go, qt, kt, vaug, right, dq, dk, dv = rest
    else:
        qt, kt, vaug, right, dq, dk, dv = rest
    s, h = pl.program_id(0), pl.program_id(1)
    factor = 1.0 / math.sqrt(HEAD)
    pieces = LEN // CHUNK
    local = wq.shape[1]

    @pl.when(h == 0)
    def _():
        x = x_in[...]
        query = mm(wq[...], x, TT).astype(BF)
        key = mm(wk[...], x, TT).astype(BF)
        value = mm(x, wv[...]).astype(BF)
        lane = lane_index((LEN, 2 * HEAD))
        ones = jnp.where((lane % HEAD) < 3, 1.0, 0.0).astype(BF)
        for n in range(heads):
            mine = slice(n * HEAD, (n + 1) * HEAD)
            qt[n] = query[mine]
            kt[n] = key[mine]
            pair = value[:, (n // 2) * 128 : (n // 2) * 128 + 128]
            turned = rolled(pair)
            if n % 2 == 0:
                vaug[n, :, 0:128] = jnp.where(lane < HEAD, pair, turned)
            else:
                vaug[n, :, 0:128] = jnp.where(lane < HEAD, turned, pair)
            vaug[n, :, 128:256] = ones
        d_att = att_in[...]
        d_mixed = mm(wo[...], d_att, NT).astype(BF).astype(F32)
        index = row_index((2 * HEAD, LEN))
        for n in range(heads):
            mine = slice(n * HEAD, (n + 1) * HEAD)
            part = d_mixed[mine]
            scale = r_in[n]
            high, low = split_low(part * scale)
            right[n, 0:HEAD] = high
            right[n, HEAD : 2 * HEAD] = low
            delta = -scale * jnp.sum(part * mix_in[mine].astype(F32), axis=0, keepdims=True)
            d1 = delta.astype(BF).astype(F32)
            d2 = (delta - d1).astype(BF).astype(F32)
            d3 = delta - d1 - d2
            right[n, 2 * HEAD :] = jnp.where(
                index == 0, d1, jnp.where(index == 1, d2, jnp.where(index == 2, d3, 0.0))
            ).astype(BF)
        if own:
            g_out = mm(mix_in[...], d_att)

            @pl.when(s == 0)
            def _():
                go[...] = g_out

            @pl.when(s > 0)
            def _():
                go[...] += g_out

    high = right[h, 0:HEAD]
    query = qt[h]
    out = None
    for c in range(pieces):
        rows = slice(c * CHUNK, (c + 1) * CHUNK)
        d_probs = mm(vaug[h, rows], right[h])
        e = e_in[0, rows]
        d_scores = (e.astype(F32) * d_probs).astype(BF)
        dv[h, rows] = mm(e, high, NT).astype(BF)
        dk[h, rows] = (mm(d_scores, query, NT) * factor).astype(BF)
        o = mm(kt[h, :, rows], d_scores)
        out = o if out is None else out + o
    dq[pl.ds(pl.multiple_of(h * HEAD, HEAD), HEAD)] = (out * factor).astype(BF)

    @pl.when(h == heads - 1)
    def _():
        d_query = dq[...]
        d_key = jnp.concatenate([dk[n] for n in range(heads)], axis=1)
        d_value = jnp.concatenate([dv[n] for n in range(heads)], axis=1)
        total = mm(d_query, wq[...], TT)
        total = total + mm(d_key, wk[...], NT)
        total = total + mm(d_value, wv[...], NT)
        gs_out[...] = gs_in[...] + total
        if own:
            x = x_in[...]
            g1 = mm(d_query, x).T
            g2 = mm(x, jnp.concatenate([d_key, d_value], axis=1), TN)

            @pl.when(s == 0)
            def _():
                gqkv[:, :local] = g1
                gqkv[:, local:] = g2

            @pl.when(s > 0)
            def _():
                gqkv[:, :local] += g1
                gqkv[:, local:] += g2

            @pl.when(s == pl.num_programs(0) - 1)
            def _():
                half, few = keep.shape[0], local // 2
                wide, width = gqkv.shape[1], go.shape[1]
                for place, out in ((core[0], keep), (1 - core[0], send)):
                    out[:, :wide] = gqkv[rows_at(place, half)]
                    piece = go[rows_at(place, few)]
                    out[:few, wide:] = piece[:, : width // 2]
                    out[few:, wide:] = piece[:, width // 2 :]


def attention_backward(first, seqs, core, e, att, mix, r, x, wq, wk, wv, wo, gs, own):
    rows, width = x.shape
    local = wq.shape[1]
    heads = local // HEAD
    by_rows = pl.BlockSpec((LEN, width), lambda s, h: (first + s, 0))
    out_specs = [by_rows]
    out_shape = [jax.ShapeDtypeStruct((rows, width), F32)]
    scratch = []
    if own:
        both = (width // 2, 3 * local + width // 2)
        out_specs += [whole(both)] * 2
        out_shape += [jax.ShapeDtypeStruct(both, F32)] * 2
        scratch = [pltpu.VMEM((width, 3 * local), F32), pltpu.VMEM((local, width), F32)]
    return pl.pallas_call(
        functools.partial(attention_backward_kernel, heads=heads, own=own),
        grid=(seqs, heads),
        in_specs=[
            pl.BlockSpec(memory_space=pltpu.SMEM),
            pl.BlockSpec((1, LEN, LEN), lambda s, h: ((first + s) * heads + h, 0, 0)),
            by_rows,
            pl.BlockSpec((local, LEN), lambda s, h: (0, first + s)),
            pl.BlockSpec((heads, 1, LEN), lambda s, h: (first + s, 0, 0)),
            by_rows,
            whole((width, local)),
            whole((width, local)),
            whole((width, local)),
            whole((local, width)),
            by_rows,
        ],
        out_specs=out_specs,
        out_shape=out_shape,
        scratch_shapes=scratch
        + [
            pltpu.VMEM((heads, HEAD, LEN), BF),
            pltpu.VMEM((heads, HEAD, LEN), BF),
            pltpu.VMEM((heads, LEN, 256), BF),
            pltpu.VMEM((heads, 256, LEN), BF),
            pltpu.VMEM((local, LEN), BF),
            pltpu.VMEM((heads, LEN, HEAD), BF),
            pltpu.VMEM((heads, LEN, HEAD), BF),
        ],
        compiler_params=params(),
        input_output_aliases={10: 0},
        cost_estimate=pl.CostEstimate(
            flops=32 * 2 * seqs * heads * LEN * LEN * HEAD, bytes_accessed=1000,
            transcendentals=0,
        ),
        name="attention_backward_own" if own else "attention_backward_other",
    )(core, e, att, mix, r, x, wq, wk, wv, wo, gs)


def rows_at(index, size):
    return pl.ds(pl.multiple_of(index * size, size), size)


def local_kernel(fn, count, place, *refs):
    fn(place, refs[:count], refs[count:])


def local_call(name, fn, place, ins, outs):
    return pl.pallas_call(
        functools.partial(local_kernel, fn, len(ins)),
        in_specs=[pl.BlockSpec(memory_space=pltpu.SMEM)]
        + [pl.BlockSpec(memory_space=pltpu.VMEM)] * len(ins),
        out_specs=[pl.BlockSpec(memory_space=pltpu.VMEM)] * len(outs),
        out_shape=[jax.ShapeDtypeStruct(shape, kind) for shape, kind in outs],
        compiler_params=params(),
        name=name,
    )(place, *ins)


def cut_call(name, fn, place, ins, outs):
    return pl.pallas_call(
        functools.partial(local_kernel, fn, len(ins)),
        grid_spec=pltpu.PrefetchScalarGridSpec(
            num_scalar_prefetch=1,
            grid=(1,),
            in_specs=[
                pl.BlockSpec((v.shape[0] // 4, v.shape[1]), lambda _, p: (p[0], 0)) for v in ins
            ],
            out_specs=[pl.BlockSpec(shape, lambda _, p: (0, 0)) for shape in outs],
        ),
        out_shape=[jax.ShapeDtypeStruct(shape, F32) for shape in outs],
        compiler_params=params(),
        name=name,
    )(place, *ins)


def pack(place, ins, outs):
    wq, wk, wv, wo, wi, wu = ins
    local = wq.shape[1]
    for n, ref in enumerate((wq, wk, wv)):
        outs[0][:, n * local : (n + 1) * local] = ref[...].astype(F32)
    quarter, width = wi.shape[0], wo.shape[1]
    blocks = wi.shape[1] // width
    for n in range(blocks):
        outs[1][n * quarter : (n + 1) * quarter] = wi[:, n * width : (n + 1) * width].astype(F32)
    outs[1][blocks * quarter :] = wo[...].astype(F32)
    outs[2][...] = wu[...].astype(F32)


def embed_kernel(state, timing, out):
    out[...] = (state[...].astype(F32) + timing[...]).astype(BF)


def embed(state, timing):
    rows, width = state.shape
    tile = 512
    per = LEN // tile
    by_rows = pl.BlockSpec((tile, width), lambda p, s: (s * per + p, 0))
    return pl.pallas_call(
        embed_kernel,
        grid=(per, rows // LEN),
        in_specs=[by_rows, pl.BlockSpec((tile, width), lambda p, s: (p, 0))],
        out_specs=by_rows,
        out_shape=jax.ShapeDtypeStruct((rows, width), BF),
        compiler_params=params(),
        name="embed",
    )(state, timing)


def unpack_qkv(place, ins, outs):
    local = outs[0].shape[1]
    for p, ref in zip((0, 2, 1, 3), ins):
        rows = rows_at(place[p], ref.shape[0])
        for n, out in enumerate(outs):
            out[rows] = ref[:, n * local : (n + 1) * local].astype(BF)


def unpack_inner(place, ins, outs):
    wo, wi = outs
    width = wi.shape[0]
    quarter, blocks = width // 4, wi.shape[1] // width
    for p, ref in zip((0, 2, 1, 3), ins):
        rows = rows_at(place[p], quarter)
        for n in range(blocks):
            columns = slice(n * width, (n + 1) * width)
            wi[rows, columns] = ref[n * quarter : (n + 1) * quarter].astype(BF)
        wo[rows_at(place[p], wo.shape[0] // 4)] = ref[blocks * quarter :].astype(BF)


def finish_qkv(place, ins, outs):
    gq, gk, gv, go = outs
    width, local = gq.shape
    few, wide, half = ins[0].shape[0], 3 * local, width // 2
    for n, ref in enumerate(ins):
        core, y = jnp.bitwise_xor(place[4], n // 2), jnp.bitwise_xor(place[5 + n // 2], n % 2)
        rows = rows_at(2 * core + y, few)
        for k, out in enumerate((gq, gk, gv)):
            out[rows] = ref[:, k * local : (k + 1) * local]
        for k in range(2):

            @pl.when(y == k)
            def _():
                go[rows_at(core, few), k * half : (k + 1) * half] = ref[:, wide:]


def finish_ff_kernel(gu_in, vec_in, gi_in, gu, gi, *vec):
    gu[...] = gu_in[...]
    gi[...] = gi_in[...]

    @pl.when(pl.program_id(0) == 0)
    def _():
        for n, out in enumerate(vec):
            out[...] = vec_in[n]


def finish_ff(gu, gi):
    width, ff = gi.shape
    steps = 2
    upper = pl.BlockSpec((ff // steps, width), lambda i: (i, 0))
    inner = pl.BlockSpec((width // steps, ff), lambda i: (i, 0))
    return pl.pallas_call(
        finish_ff_kernel,
        grid=(steps,),
        in_specs=[upper, pl.BlockSpec((8, width), lambda i: (ff // 8, 0)), inner],
        out_specs=[upper, inner] + [whole((width,))] * 5,
        out_shape=[
            jax.ShapeDtypeStruct(shape, F32)
            for shape in [(ff, width), (width, ff)] + [(width,)] * 5
        ],
        compiler_params=params(),
        name="finish_ff",
    )(gu, gu, gi)


def flipped(size, even, odd):
    return [(i, i ^ (odd if i & 1 else even)) for i in range(size)]


def shards(
    dp, state, lengths, halt_mask, wq, wk, wv, wo, gain1, bias1, wi, wu, gain2, bias2,
    halt_weight, cotangent
):
    rows, width = state.shape
    local, ff = wq.shape[1], wi.shape[1]
    timing = jnp.asarray(timing_rows(width))
    me = lax.axis_index("dp").astype(jnp.int32)
    even = np.array([0, 0, 0, 0, 0, 1, 2], np.int32)
    odd = np.array([0, 0, 0, 0, 0, 2, 1], np.int32)
    shift = jnp.where(lax.rem(me, 2) == 0, even, odd)
    mask = np.array([3, 3, 3, 3, 1, 1, 1], np.int32)
    flip = np.array([0, 1, 2, 3, 0, 0, 0], np.int32)
    place = jnp.bitwise_xor(jnp.bitwise_and(jnp.right_shift(me, shift), mask), flip)
    bits = dp.bit_length() - 1
    tie = lax.optimization_barrier
    call = functools.partial(local_call, place=place)

    def across(v):
        return lax.ppermute(v, "mp", [(0, 1), (1, 0)])

    def along(v, even, odd=None):
        return lax.ppermute(v, "dp", flipped(dp, even, odd or even))

    quarter = width // 4
    chunk_a, chunk_b, chunk_c = cut_call(
        "pack", pack, place, (wq, wk, wv, wo, wi, wu),
        [(quarter, 3 * local), (ff // 4 + local // 4, width), (ff // 4, width)],
    )
    qkv0 = across(chunk_a)
    x = embed(state, timing)
    chunk_b, x = tie((chunk_b, x))
    in0 = across(chunk_b)
    fwd = attention_forward(0, lengths, x, wq, wk, wv)
    qkv0, chunk_c, fwd = tie((qkv0, chunk_c, fwd))
    qkv1 = along(qkv0, 2)
    out0 = across(chunk_c)
    fwd = attention_forward(1, lengths, x, wq, wk, wv, fwd)
    qkv1, in0, fwd = tie((qkv1, in0, fwd))
    qkv2, qkv3 = along(qkv0, 1), along(qkv1, 1)
    in1 = along(in0, 2)
    wq2, wk2, wv2 = call(
        "unpack_qkv", unpack_qkv, ins=(qkv0, qkv1, qkv2, qkv3),
        outs=[((width, local), BF)] * 3,
    )
    fwd2 = attention_forward(0, lengths, x, wq2, wk2, wv2)
    in1, out0, fwd2 = tie((in1, out0, fwd2))
    in2, in3 = along(in0, 1), along(in1, 1)
    out1 = along(out0, 2)
    out2 = along(out0, 1)
    fwd2 = attention_forward(1, lengths, x, wq2, wk2, wv2, fwd2)
    in2, in3, fwd2 = tie((in2, in3, fwd2))
    wo2, wi2 = call(
        "unpack_inner", unpack_inner, ins=(in0, in1, in2, in3),
        outs=[((local, width), BF), ((width, ff), BF)],
    )
    out1, out2, wo2, wi2 = tie((out1, out2, wo2, wi2))
    out3 = along(out1, 1)
    e_a, mix_a, r_a = fwd
    e_b, mix_b, r_b = fwd2
    new_state, gs, att, *grads = middle(
        place, state, timing, cotangent, halt_mask, mix_a, mix_b, wo, wo2, wi, wi2, wu,
        (gain1, bias1, gain2, bias2, halt_weight), (out0, out1, out2, out3)
    )

    grads = lax.psum(tuple(grads), "dp")
    own = dict(core=place[4:5], e=e_a, att=att, mix=mix_a, r=r_a, x=x, wq=wq, wk=wk, wv=wv, wo=wo)
    other = dict(
        core=place[4:5], e=e_b, att=att, mix=mix_b, r=r_b, x=x, wq=wq2, wk=wk2, wv=wv2, wo=wo2
    )

    def attention_and_sums(carry):
        step, gs, *_ = carry
        back = attention_backward
        gs, keep, send = back(0, rows // LEN, gs=gs, own=True, **own)
        g = keep + along(send, 1)
        g, gs = tie((g, gs))
        few = g.shape[0] // 2
        y = place[5]
        got = along(lax.dynamic_slice_in_dim(g, (1 - y) * few, few), 2, 4)
        (gs,) = back(0, 1, gs=gs, own=False, **other)
        got, gs = tie((got, gs))
        g = lax.dynamic_slice_in_dim(g, y * few, few) + got
        g, gs = tie((g, gs))
        got = along(g, 4, 8)
        (gs,) = back(1, rows // LEN - 1, gs=gs, own=False, **other)
        got, gs = tie((got, gs))
        g = g + got
        g = g + along(g, 8, 2)
        for bit in range(4, bits):
            g = g + along(g, 1 << bit)
        got = along(g, 2, 4)
        parts = call(
            "finish_qkv", finish_qkv, ins=(g, got, along(g, 1), along(got, 1)),
            outs=[((width, local), F32)] * 3 + [((local, width), F32)],
        )
        return (step + 1, gs, *parts)

    once = jnp.minimum(lengths[0], 1)
    empty = [jnp.zeros(shape, F32) for shape in [(width, local)] * 3 + [(local, width)]]
    _, gs, gq, gk, gv, go = lax.cond(
        once > 0, attention_and_sums, lambda c: c,
        (jnp.zeros_like(once), gs, *empty),
    )
    grads, gs, gq = tie((grads, gs, gq))
    gu, gi, *vec = finish_ff(*grads)
    return (
        new_state, gs, gq, gk, gv, go, vec[0], vec[1], gi, gu, vec[2], vec[3], vec[4]
    )


def solution(mesh):
    rows, columns, parts = P("dp", None), P(None, "mp"), P("mp", None)
    return jax.shard_map(
        functools.partial(shards, mesh.shape["dp"]),
        mesh=mesh,
        in_specs=(
            rows, P("dp"), P("dp"), columns, columns, columns, parts, P(), P(), columns,
            parts, P(), P(), P(), rows
        ),
        out_specs=(
            rows, rows, columns, columns, columns, parts, P(), P(), columns, parts, P(), P(),
            P()
        ),
        check_vma=False,
    )
```

```python
import functools
import math

import jax
import jax.numpy as jnp
import numpy as np
from jax import lax
from jax.experimental import pallas as pl
from jax.experimental.pallas import tpu as pltpu
from jax.sharding import PartitionSpec as P

HEAD = 64
LEN = 1024
STEP = 2
LOG2E = 1.4426950408889634
BF = jnp.bfloat16
F32 = jnp.float32
NN = (((1,), (0,)), ((), ()))
NT = (((1,), (1,)), ((), ()))
TN = (((0,), (0,)), ((), ()))
TT = (((0,), (1,)), ((), ()))
VMEM_LIMIT = 60 << 20
CHUNK = 256
SUBS = 2


def mm(a, b, dims=NN):
    return lax.dot_general(a, b, dims, preferred_element_type=F32)


def params():
    return pltpu.CompilerParams(vmem_limit_bytes=VMEM_LIMIT)


def whole(shape):
    zeros = (0,) * len(shape)
    return pl.BlockSpec(shape, lambda *_: zeros)


def timing_rows(width):
    half = width // 2
    rates = np.exp(-math.log(10000.0) * np.arange(half, dtype=np.float64) / (half - 1))

    def rows(positions):
        angles = positions[:, None] * rates[None, :]
        return np.concatenate([np.sin(angles), np.cos(angles)], axis=1)

    return (rows(np.arange(LEN, dtype=np.float64)) + rows(np.array([float(STEP)]))).astype(
        np.float32
    )


def split_low(value):
    high = value.astype(BF)
    return high, (value - high.astype(F32)).astype(BF)


def rolled(pair):
    return jnp.concatenate([pair[:, HEAD:], pair[:, :HEAD]], axis=1)


def lane_index(shape):
    return lax.broadcasted_iota(jnp.int32, shape, 1)


def row_index(shape):
    return lax.broadcasted_iota(jnp.int32, shape, 0)


def attention_forward_kernel(seq, lengths, x_in, wq, wk, wv, *rest, heads):
    e_out, mixed_out, r_out, kaug, qaug, vaug, sa, sb, ma, mb = rest[-10:]
    j = pl.program_id(0)
    last = heads // 2 - 1
    pieces = LEN // CHUNK

    def score_piece(i, c, target):
        rows = slice(c * CHUNK, (c + 1) * CHUNK)
        s = mm(kaug[i, rows], qaug[i])
        target[rows] = s
        return jnp.max(s.reshape(CHUNK // 8, 8, LEN), axis=0)

    @pl.when(j == 0)
    def _():
        x = x_in[...]
        query = mm(wq[...], x, TT).astype(BF).astype(F32) * (LOG2E / math.sqrt(HEAD))
        high, rest = split_low(query)
        key = mm(x, wk[...]).astype(BF)
        value = mm(wv[...], x, TT).astype(BF)
        shape = (LEN, 2 * HEAD)
        lane = lane_index(shape)
        padded = row_index(shape) >= lengths[seq]
        mask = jnp.where(padded & ((lane == 0) | (lane == HEAD)), -1e30, 0.0).astype(BF)
        first = row_index((HEAD, LEN)) == 0
        ones = jnp.where(first, 1.0, 0.0).astype(BF)
        zeros = jnp.zeros((HEAD, LEN), BF)
        for i in range(heads):
            pair = key[:, (i // 2) * 128 : (i // 2) * 128 + 128]
            turned = rolled(pair)
            mine = slice(i * HEAD, (i + 1) * HEAD)
            kaug[i, :, 0:128] = pair
            if i % 2 == 0:
                kaug[i, :, 128:256] = jnp.where(lane < HEAD, mask, turned)
                parts = (high[mine], zeros, ones, rest[mine])
            else:
                kaug[i, :, 128:256] = jnp.where(lane < HEAD, turned, mask)
                parts = (zeros, high[mine], rest[mine], ones)
            for n, part in enumerate(parts):
                qaug[i, n * HEAD : (n + 1) * HEAD] = part
            vaug[i, 0:HEAD] = value[mine]
            vaug[i, HEAD : HEAD + 16] = jnp.ones((16, LEN), BF)
        top = None
        for c in range(pieces):
            m = score_piece(0, c, sa)
            top = m if top is None else jnp.maximum(top, m)
        ma[...] = jnp.max(top, axis=0, keepdims=True)

    def step(slot, cur, cur_m, nxt, nxt_m, ahead=True):
        i = 2 * j + slot
        shift = cur_m[...]
        top = None
        out = None
        for c in range(pieces):
            rows = slice(c * CHUNK, (c + 1) * CHUNK)
            if ahead:
                m = score_piece(i + 1, c, nxt)
                top = m if top is None else jnp.maximum(top, m)
            e = jnp.exp2(cur[rows] - shift).astype(BF)
            e_out[slot, rows] = e
            o = mm(vaug[i, :, rows], e)
            out = o if out is None else out + o
        if ahead:
            nxt_m[...] = jnp.max(top, axis=0, keepdims=True)
        r = 1.0 / out[HEAD : HEAD + 1]
        mixed_out[slot * HEAD : (slot + 1) * HEAD] = (out[:HEAD] * r).astype(BF)
        r_out[slot] = r

    step(0, sa, ma, sb, mb)

    @pl.when(j < last)
    def _():
        step(1, sb, mb, sa, ma)

    @pl.when(j == last)
    def _():
        step(1, sb, mb, sa, ma, ahead=False)


def attention_forward(seq, lengths, x, wq, wk, wv, earlier=()):
    rows, width = x.shape
    local = wq.shape[1]
    heads = local // HEAD
    steps, total = heads // 2, rows // LEN * heads
    return pl.pallas_call(
        functools.partial(attention_forward_kernel, seq, heads=heads),
        grid=(steps,),
        in_specs=[
            pl.BlockSpec(memory_space=pltpu.SMEM),
            pl.BlockSpec((LEN, width), lambda j: (seq, 0)),
            whole((width, local)),
            whole((width, local)),
            whole((width, local)),
        ]
        + [pl.BlockSpec(memory_space=pl.ANY)] * len(earlier),
        out_specs=[
            pl.BlockSpec((2, LEN, LEN), lambda j: (seq * steps + j, 0, 0)),
            pl.BlockSpec((2 * HEAD, LEN), lambda j: (j, seq)),
            pl.BlockSpec((2, 1, LEN), lambda j: (seq * steps + j, 0, 0)),
        ],
        out_shape=[
            jax.ShapeDtypeStruct((total, LEN, LEN), BF),
            jax.ShapeDtypeStruct((local, rows), BF),
            jax.ShapeDtypeStruct((total, 1, LEN), F32),
        ],
        scratch_shapes=[
            pltpu.VMEM((heads, LEN, 256), BF),
            pltpu.VMEM((heads, 256, LEN), BF),
            pltpu.VMEM((heads, HEAD + 16, LEN), BF),
            pltpu.VMEM((LEN, LEN), F32),
            pltpu.VMEM((LEN, LEN), F32),
            pltpu.VMEM((1, LEN), F32),
            pltpu.VMEM((1, LEN), F32),
        ],
        compiler_params=params(),
        input_output_aliases={5 + n: n for n in range(len(earlier))},
        cost_estimate=pl.CostEstimate(
            flops=8 * 2 * heads * LEN * LEN * HEAD,
            bytes_accessed=2 * heads * LEN * LEN,
            transcendentals=heads * LEN * LEN,
        ),
        name="attention_forward",
    )(lengths, x, wq, wk, wv, *earlier)


def row_mean(v):
    return jnp.mean(v, axis=-1, keepdims=True)


def norm_rows(v):
    centre = v - row_mean(v)
    deviation = lax.rsqrt(row_mean(centre * centre) + 1e-05)
    return centre * deviation, deviation


def norm_back(e, xhat, deviation):
    return deviation * (e - row_mean(e) - xhat * row_mean(e * xhat))


def fold_rows(v):
    return jnp.sum(v.reshape(v.shape[0] // 8, 8, v.shape[1]), axis=0)


def middle_kernel(
    place, state, timing, cot, run, mix_a, mix_b, wo_a, wo_b, wi_a, wi_b, wu_a, v0, v1, v2, v3,
    v4, o0, o1, o2, o3, new_state, gs, att_low, gu, gi, act, slope, inner_low, low1, out_low,
    fold, wu_b
):
    t = pl.program_id(0)
    last = pl.num_programs(0) - 1
    tile = state.shape[0]
    size = tile // SUBS
    ff = wi_a.shape[1]
    gain1, bias1, gain2, bias2, halt_w = (v[...].reshape(1, -1) for v in (v0, v1, v2, v3, v4))
    c0 = math.sqrt(2.0 / math.pi)
    halves = ((wi_a, wu_a), (wi_b, wu_b))
    running_column = jnp.broadcast_to(run[0].astype(F32), (8, tile)).T[:, 0:1]

    @pl.when(t == 0)
    def _():
        for ref in (gu, gi, fold):
            ref[...] = jnp.zeros(ref.shape, F32)
        for p, ref in zip((0, 2, 1, 3), (o0, o1, o2, o3)):
            wu_b[rows_at(place[p], ref.shape[0])] = ref[...].astype(BF)

    def first_norm(k):
        rows = slice(k * size, (k + 1) * size)
        embedded = state[rows].astype(F32) + timing[rows]
        attended = mm(mix_a[:, rows], wo_a[...], TN) + mm(mix_b[:, rows], wo_b[...], TN)
        xhat1, dev1 = norm_rows(embedded + attended)
        normed1 = xhat1 * gain1 + bias1
        low1[rows] = normed1.astype(BF)
        return xhat1, dev1, normed1

    def forward(k, normed1):
        rows = slice(k * size, (k + 1) * size)
        total = normed1
        for n, (wi, wu) in enumerate(halves):
            v = mm(low1[rows], wi[...])
            square = v * v
            h = 0.5 + 0.5 * jnp.tanh(v * (c0 + (c0 * 0.044715) * square))
            g = v * h
            act[n, rows] = g.astype(BF)
            slope[n, rows] = h + g * (1.0 - h) * (2.0 * c0 + (6.0 * c0 * 0.044715) * square)
            total = total + mm(act[n, rows], wu[...])
        return total

    def second_norm(k, hidden2):
        rows = slice(k * size, (k + 1) * size)
        old = state[rows].astype(F32)
        xhat2, dev2 = norm_rows(hidden2)
        block = xhat2 * gain2 + bias2
        halt = jax.nn.sigmoid(jnp.sum(block * halt_w, axis=-1, keepdims=True))
        running = running_column[rows]
        gate = running * halt
        change = block - old
        new_state[rows] = old + gate * change
        g_in = cot[rows].astype(F32)
        d_prob = running * jnp.sum(g_in * change, axis=-1, keepdims=True)
        d_logit = d_prob * halt * (1.0 - halt)
        d_block = gate * g_in + d_logit * halt_w
        fold[4] += fold_rows(d_logit * block)
        fold[2] += fold_rows(d_block * xhat2)
        fold[3] += fold_rows(d_block)
        gs[rows] = g_in * (1.0 - gate)
        d_hidden2 = norm_back(d_block * gain2, xhat2, dev2)
        out_low[rows] = d_hidden2.astype(BF)
        return d_hidden2

    def backward(k, d_hidden2):
        rows = slice(k * size, (k + 1) * size)
        total = d_hidden2
        for n, (wi, wu) in enumerate(halves):
            d_act = mm(out_low[rows], wu[...], NT)
            inner_low[n, rows] = (d_act * slope[n, rows]).astype(BF)
            total = total + mm(inner_low[n, rows], wi[...], NT)
        return total

    def first_back(k, d_normed1, xhat1, dev1):
        rows = slice(k * size, (k + 1) * size)
        fold[0] += fold_rows(d_normed1 * xhat1)
        fold[1] += fold_rows(d_normed1)
        d_hidden1 = norm_back(d_normed1 * gain1, xhat1, dev1)
        att_low[rows] = d_hidden1.astype(BF)
        gs[rows] += d_hidden1

    n0 = first_norm(0)
    n1 = first_norm(1)
    f0 = forward(0, n0[2])
    s0 = second_norm(0, f0)
    f1 = forward(1, n1[2])
    b0 = backward(0, s0)
    s1 = second_norm(1, f1)
    first_back(0, b0, *n0[:2])
    b1 = backward(1, s1)
    gi[...] += mm(low1[...], inner_low[0], TN)
    gu[:ff] += mm(act[0], out_low[...], TN)
    first_back(1, b1, *n1[:2])

    @pl.when(t == last)
    def _():
        for n in range(8):
            gu[ff + n : ff + n + 1] = jnp.sum(fold[n], axis=0, keepdims=True)


def middle(place, state, timing, cot, run, mix_a, mix_b, wo_a, wo_b, wi_a, wi_b, wu_a, vectors,
           outer):
    rows, width = state.shape
    local, ff = wo_a.shape[0], wi_a.shape[1]
    tile = 512
    per = LEN // tile
    by_rows = pl.BlockSpec((tile, width), lambda t: (t, 0))
    by_columns = pl.BlockSpec((local, tile), lambda t: (0, t))
    return pl.pallas_call(
        middle_kernel,
        grid=(rows // tile,),
        in_specs=[
            pl.BlockSpec(memory_space=pltpu.SMEM),
            by_rows,
            pl.BlockSpec((tile, width), lambda t: (t % per, 0)),
            by_rows,
            pl.BlockSpec((1, 1, tile), lambda t: (t, 0, 0)),
            by_columns,
            by_columns,
            whole((local, width)),
            whole((local, width)),
            whole((width, ff)),
            whole((width, ff)),
            whole((ff, width)),
        ]
        + [whole((width,))] * 5
        + [whole(v.shape) for v in outer],
        out_specs=[
            by_rows,
            by_rows,
            by_rows,
            whole((ff + 8, width)),
            whole((width, ff)),
        ],
        out_shape=[
            jax.ShapeDtypeStruct((rows, width), F32),
            jax.ShapeDtypeStruct((rows, width), F32),
            jax.ShapeDtypeStruct((rows, width), BF),
            jax.ShapeDtypeStruct((ff + 8, width), F32),
            jax.ShapeDtypeStruct((width, ff), F32),
        ],
        scratch_shapes=[
            pltpu.VMEM((2, tile, ff), BF),
            pltpu.VMEM((2, tile, ff), F32),
            pltpu.VMEM((2, tile, ff), BF),
            pltpu.VMEM((tile, width), BF),
            pltpu.VMEM((tile, width), BF),
            pltpu.VMEM((8, 8, width), F32),
            pltpu.VMEM((ff, width), BF),
        ],
        compiler_params=params(),
        cost_estimate=pl.CostEstimate(
            flops=2 * rows * width * ff * 10 + 2 * rows * width * local * 2,
            bytes_accessed=rows * width * 20,
            transcendentals=2 * rows * ff,
        ),
        name="middle",
    )(place, state, timing, cot, run.reshape(rows // tile, 1, tile), mix_a, mix_b, wo_a, wo_b,
      wi_a, wi_b, wu_a, *vectors, *outer)


def attention_backward_kernel(
    core, e_in, att_in, mix_in, r_in, x_in, wq, wk, wv, wo, gs_in, gs_out, *rest, heads, own
):
    if own:
        keep, send, gqkv, go, qt, kt, vaug, right, dq, dk, dv = rest
    else:
        qt, kt, vaug, right, dq, dk, dv = rest
    s, h = pl.program_id(0), pl.program_id(1)
    factor = 1.0 / math.sqrt(HEAD)
    pieces = LEN // CHUNK
    local = wq.shape[1]

    @pl.when(h == 0)
    def _():
        x = x_in[...]
        query = mm(wq[...], x, TT).astype(BF)
        key = mm(wk[...], x, TT).astype(BF)
        value = mm(x, wv[...]).astype(BF)
        lane = lane_index((LEN, 2 * HEAD))
        ones = jnp.where((lane % HEAD) < 3, 1.0, 0.0).astype(BF)
        for n in range(heads):
            mine = slice(n * HEAD, (n + 1) * HEAD)
            qt[n] = query[mine]
            kt[n] = key[mine]
            pair = value[:, (n // 2) * 128 : (n // 2) * 128 + 128]
            turned = rolled(pair)
            if n % 2 == 0:
                vaug[n, :, 0:128] = jnp.where(lane < HEAD, pair, turned)
            else:
                vaug[n, :, 0:128] = jnp.where(lane < HEAD, turned, pair)
            vaug[n, :, 128:256] = ones
        d_att = att_in[...]
        d_mixed = mm(wo[...], d_att, NT).astype(BF).astype(F32)
        index = row_index((2 * HEAD, LEN))
        for n in range(heads):
            mine = slice(n * HEAD, (n + 1) * HEAD)
            part = d_mixed[mine]
            scale = r_in[n]
            high, low = split_low(part * scale)
            right[n, 0:HEAD] = high
            right[n, HEAD : 2 * HEAD] = low
            delta = -scale * jnp.sum(part * mix_in[mine].astype(F32), axis=0, keepdims=True)
            d1 = delta.astype(BF).astype(F32)
            d2 = (delta - d1).astype(BF).astype(F32)
            d3 = delta - d1 - d2
            right[n, 2 * HEAD :] = jnp.where(
                index == 0, d1, jnp.where(index == 1, d2, jnp.where(index == 2, d3, 0.0))
            ).astype(BF)
        if own:
            g_out = mm(mix_in[...], d_att)

            @pl.when(s == 0)
            def _():
                go[...] = g_out

            @pl.when(s > 0)
            def _():
                go[...] += g_out

    high = right[h, 0:HEAD]
    query = qt[h]
    out = None
    for c in range(pieces):
        rows = slice(c * CHUNK, (c + 1) * CHUNK)
        d_probs = mm(vaug[h, rows], right[h])
        e = e_in[0, rows]
        d_scores = (e.astype(F32) * d_probs).astype(BF)
        dv[h, rows] = mm(e, high, NT).astype(BF)
        dk[h, rows] = (mm(d_scores, query, NT) * factor).astype(BF)
        o = mm(kt[h, :, rows], d_scores)
        out = o if out is None else out + o
    dq[pl.ds(pl.multiple_of(h * HEAD, HEAD), HEAD)] = (out * factor).astype(BF)

    @pl.when(h == heads - 1)
    def _():
        d_query = dq[...]
        d_key = jnp.concatenate([dk[n] for n in range(heads)], axis=1)
        d_value = jnp.concatenate([dv[n] for n in range(heads)], axis=1)
        total = mm(d_query, wq[...], TT)
        total = total + mm(d_key, wk[...], NT)
        total = total + mm(d_value, wv[...], NT)
        gs_out[...] = gs_in[...] + total
        if own:
            x = x_in[...]
            g1 = mm(d_query, x).T
            g2 = mm(x, jnp.concatenate([d_key, d_value], axis=1), TN)

            @pl.when(s == 0)
            def _():
                gqkv[:, :local] = g1
                gqkv[:, local:] = g2

            @pl.when(s > 0)
            def _():
                gqkv[:, :local] += g1
                gqkv[:, local:] += g2

            @pl.when(s == pl.num_programs(0) - 1)
            def _():
                half, few = keep.shape[0], local // 2
                wide, width = gqkv.shape[1], go.shape[1]
                for place, out in ((core[0], keep), (1 - core[0], send)):
                    out[:, :wide] = gqkv[rows_at(place, half)]
                    piece = go[rows_at(place, few)]
                    out[:few, wide:] = piece[:, : width // 2]
                    out[few:, wide:] = piece[:, width // 2 :]


def attention_backward(first, seqs, core, e, att, mix, r, x, wq, wk, wv, wo, gs, own):
    rows, width = x.shape
    local = wq.shape[1]
    heads = local // HEAD
    by_rows = pl.BlockSpec((LEN, width), lambda s, h: (first + s, 0))
    out_specs = [by_rows]
    out_shape = [jax.ShapeDtypeStruct((rows, width), F32)]
    scratch = []
    if own:
        both = (width // 2, 3 * local + width // 2)
        out_specs += [whole(both)] * 2
        out_shape += [jax.ShapeDtypeStruct(both, F32)] * 2
        scratch = [pltpu.VMEM((width, 3 * local), F32), pltpu.VMEM((local, width), F32)]
    return pl.pallas_call(
        functools.partial(attention_backward_kernel, heads=heads, own=own),
        grid=(seqs, heads),
        in_specs=[
            pl.BlockSpec(memory_space=pltpu.SMEM),
            pl.BlockSpec((1, LEN, LEN), lambda s, h: ((first + s) * heads + h, 0, 0)),
            by_rows,
            pl.BlockSpec((local, LEN), lambda s, h: (0, first + s)),
            pl.BlockSpec((heads, 1, LEN), lambda s, h: (first + s, 0, 0)),
            by_rows,
            whole((width, local)),
            whole((width, local)),
            whole((width, local)),
            whole((local, width)),
            by_rows,
        ],
        out_specs=out_specs,
        out_shape=out_shape,
        scratch_shapes=scratch
        + [
            pltpu.VMEM((heads, HEAD, LEN), BF),
            pltpu.VMEM((heads, HEAD, LEN), BF),
            pltpu.VMEM((heads, LEN, 256), BF),
            pltpu.VMEM((heads, 256, LEN), BF),
            pltpu.VMEM((local, LEN), BF),
            pltpu.VMEM((heads, LEN, HEAD), BF),
            pltpu.VMEM((heads, LEN, HEAD), BF),
        ],
        compiler_params=params(),
        input_output_aliases={10: 0},
        cost_estimate=pl.CostEstimate(
            flops=32 * 2 * seqs * heads * LEN * LEN * HEAD, bytes_accessed=1000,
            transcendentals=0,
        ),
        name="attention_backward_own" if own else "attention_backward_other",
    )(core, e, att, mix, r, x, wq, wk, wv, wo, gs)


def rows_at(index, size):
    return pl.ds(pl.multiple_of(index * size, size), size)


def local_kernel(fn, count, place, *refs):
    fn(place, refs[:count], refs[count:])


def local_call(name, fn, place, ins, outs):
    return pl.pallas_call(
        functools.partial(local_kernel, fn, len(ins)),
        in_specs=[pl.BlockSpec(memory_space=pltpu.SMEM)]
        + [pl.BlockSpec(memory_space=pltpu.VMEM)] * len(ins),
        out_specs=[pl.BlockSpec(memory_space=pltpu.VMEM)] * len(outs),
        out_shape=[jax.ShapeDtypeStruct(shape, kind) for shape, kind in outs],
        compiler_params=params(),
        name=name,
    )(place, *ins)


def cut_call(name, fn, place, ins, outs):
    return pl.pallas_call(
        functools.partial(local_kernel, fn, len(ins)),
        grid_spec=pltpu.PrefetchScalarGridSpec(
            num_scalar_prefetch=1,
            grid=(1,),
            in_specs=[
                pl.BlockSpec((v.shape[0] // 4, v.shape[1]), lambda _, p: (p[0], 0)) for v in ins
            ],
            out_specs=[pl.BlockSpec(shape, lambda _, p: (0, 0)) for shape in outs],
        ),
        out_shape=[jax.ShapeDtypeStruct(shape, F32) for shape in outs],
        compiler_params=params(),
        name=name,
    )(place, *ins)


def pack(place, ins, outs):
    wq, wk, wv, wo, wi, wu = ins
    local = wq.shape[1]
    for n, ref in enumerate((wq, wk, wv)):
        outs[0][:, n * local : (n + 1) * local] = ref[...].astype(F32)
    quarter, width = wi.shape[0], wo.shape[1]
    blocks = wi.shape[1] // width
    for n in range(blocks):
        outs[1][n * quarter : (n + 1) * quarter] = wi[:, n * width : (n + 1) * width].astype(F32)
    outs[1][blocks * quarter :] = wo[...].astype(F32)
    outs[2][...] = wu[...].astype(F32)


def embed_kernel(state, timing, out):
    out[...] = (state[...].astype(F32) + timing[...]).astype(BF)


def embed(state, timing):
    rows, width = state.shape
    tile = 512
    per = LEN // tile
    by_rows = pl.BlockSpec((tile, width), lambda p, s: (s * per + p, 0))
    return pl.pallas_call(
        embed_kernel,
        grid=(per, rows // LEN),
        in_specs=[by_rows, pl.BlockSpec((tile, width), lambda p, s: (p, 0))],
        out_specs=by_rows,
        out_shape=jax.ShapeDtypeStruct((rows, width), BF),
        compiler_params=params(),
        name="embed",
    )(state, timing)


def unpack_qkv(place, ins, outs):
    local = outs[0].shape[1]
    for p, ref in zip((0, 2, 1, 3), ins):
        rows = rows_at(place[p], ref.shape[0])
        for n, out in enumerate(outs):
            out[rows] = ref[:, n * local : (n + 1) * local].astype(BF)


def unpack_inner(place, ins, outs):
    wo, wi = outs
    width = wi.shape[0]
    quarter, blocks = width // 4, wi.shape[1] // width
    for p, ref in zip((0, 2, 1, 3), ins):
        rows = rows_at(place[p], quarter)
        for n in range(blocks):
            columns = slice(n * width, (n + 1) * width)
            wi[rows, columns] = ref[n * quarter : (n + 1) * quarter].astype(BF)
        wo[rows_at(place[p], wo.shape[0] // 4)] = ref[blocks * quarter :].astype(BF)


def finish_qkv(place, ins, outs):
    gq, gk, gv, go = outs
    width, local = gq.shape
    few, wide, half = ins[0].shape[0], 3 * local, width // 2
    for n, ref in enumerate(ins):
        core, y = jnp.bitwise_xor(place[4], n // 2), jnp.bitwise_xor(place[5], n % 2)
        rows = rows_at(2 * core + y, few)
        for k, out in enumerate((gq, gk, gv)):
            out[rows] = ref[:, k * local : (k + 1) * local]
        for k in range(2):

            @pl.when(y == k)
            def _():
                go[rows_at(core, few), k * half : (k + 1) * half] = ref[:, wide:]


def finish_ff_kernel(gu_in, vec_in, gi_in, gu, gi, *vec):
    gu[...] = gu_in[...]
    gi[...] = gi_in[...]

    @pl.when(pl.program_id(0) == 0)
    def _():
        for n, out in enumerate(vec):
            out[...] = vec_in[n]


def finish_ff(gu, gi):
    width, ff = gi.shape
    steps = 2
    upper = pl.BlockSpec((ff // steps, width), lambda i: (i, 0))
    inner = pl.BlockSpec((width // steps, ff), lambda i: (i, 0))
    return pl.pallas_call(
        finish_ff_kernel,
        grid=(steps,),
        in_specs=[upper, pl.BlockSpec((8, width), lambda i: (ff // 8, 0)), inner],
        out_specs=[upper, inner] + [whole((width,))] * 5,
        out_shape=[
            jax.ShapeDtypeStruct(shape, F32)
            for shape in [(ff, width), (width, ff)] + [(width,)] * 5
        ],
        compiler_params=params(),
        name="finish_ff",
    )(gu, gu, gi)


def flipped(size, even, odd):
    return [(i, i ^ (odd if i & 1 else even)) for i in range(size)]


def shards(
    dp, state, lengths, halt_mask, wq, wk, wv, wo, gain1, bias1, wi, wu, gain2, bias2,
    halt_weight, cotangent
):
    rows, width = state.shape
    local, ff = wq.shape[1], wi.shape[1]
    timing = jnp.asarray(timing_rows(width))
    me = lax.axis_index("dp").astype(jnp.int32)
    shift = np.array([0, 0, 0, 0, 0, 1], np.int32)
    mask = np.array([3, 3, 3, 3, 1, 1], np.int32)
    flip = np.array([0, 1, 2, 3, 0, 0], np.int32)
    place = jnp.bitwise_xor(jnp.bitwise_and(jnp.right_shift(me, shift), mask), flip)
    bits = dp.bit_length() - 1
    tie = lax.optimization_barrier
    call = functools.partial(local_call, place=place)

    def across(v):
        return lax.ppermute(v, "mp", [(0, 1), (1, 0)])

    def along(v, even, odd=None):
        return lax.ppermute(v, "dp", flipped(dp, even, odd or even))

    quarter = width // 4
    chunk_a, chunk_b, chunk_c = cut_call(
        "pack", pack, place, (wq, wk, wv, wo, wi, wu),
        [(quarter, 3 * local), (ff // 4 + local // 4, width), (ff // 4, width)],
    )
    qkv0 = across(chunk_a)
    x = embed(state, timing)
    in0 = across(chunk_b)
    fwd = attention_forward(0, lengths, x, wq, wk, wv)
    qkv0, chunk_c, fwd = tie((qkv0, chunk_c, fwd))
    qkv1 = along(qkv0, 2)
    out0 = across(chunk_c)
    fwd = attention_forward(1, lengths, x, wq, wk, wv, fwd)
    qkv1, in0, fwd = tie((qkv1, in0, fwd))
    qkv2, qkv3 = along(qkv0, 1), along(qkv1, 1)
    in1 = along(in0, 2)
    wq2, wk2, wv2 = call(
        "unpack_qkv", unpack_qkv, ins=(qkv0, qkv1, qkv2, qkv3),
        outs=[((width, local), BF)] * 3,
    )
    fwd2 = attention_forward(0, lengths, x, wq2, wk2, wv2)
    in1, out0, fwd2 = tie((in1, out0, fwd2))
    in2, in3 = along(in0, 1), along(in1, 1)
    out1 = along(out0, 2)
    out2 = along(out0, 1)
    fwd2 = attention_forward(1, lengths, x, wq2, wk2, wv2, fwd2)
    in2, in3, fwd2 = tie((in2, in3, fwd2))
    wo2, wi2 = call(
        "unpack_inner", unpack_inner, ins=(in0, in1, in2, in3),
        outs=[((local, width), BF), ((width, ff), BF)],
    )
    out1, out2, wo2, wi2 = tie((out1, out2, wo2, wi2))
    out3 = along(out1, 1)
    e_a, mix_a, r_a = fwd
    e_b, mix_b, r_b = fwd2
    new_state, gs, att, *grads = middle(
        place, state, timing, cotangent, halt_mask, mix_a, mix_b, wo, wo2, wi, wi2, wu,
        (gain1, bias1, gain2, bias2, halt_weight), (out0, out1, out2, out3)
    )

    grads = lax.psum(tuple(grads), "dp")
    own = dict(core=place[4:5], e=e_a, att=att, mix=mix_a, r=r_a, x=x, wq=wq, wk=wk, wv=wv, wo=wo)
    other = dict(
        core=place[4:5], e=e_b, att=att, mix=mix_b, r=r_b, x=x, wq=wq2, wk=wk2, wv=wv2, wo=wo2
    )

    def attention_and_sums(carry):
        step, gs, *_ = carry
        back = attention_backward
        gs, keep, send = back(0, rows // LEN, gs=gs, own=True, **own)
        g = keep + along(send, 1)
        g, gs = tie((g, gs))
        few = g.shape[0] // 2
        y = place[5]
        got = along(lax.dynamic_slice_in_dim(g, (1 - y) * few, few), 2)
        (gs,) = back(0, 1, gs=gs, own=False, **other)
        got, gs = tie((got, gs))
        g = lax.dynamic_slice_in_dim(g, y * few, few) + got
        g, gs = tie((g, gs))
        got = along(g, 4, 8)
        (gs,) = back(1, rows // LEN - 1, gs=gs, own=False, **other)
        got, gs = tie((got, gs))
        g = g + got
        g = g + along(g, 8, 4)
        for bit in range(4, bits):
            g = g + along(g, 1 << bit)
        got = along(g, 2)
        parts = call(
            "finish_qkv", finish_qkv, ins=(g, got, along(g, 1), along(got, 1)),
            outs=[((width, local), F32)] * 3 + [((local, width), F32)],
        )
        return (step + 1, gs, *parts)

    once = jnp.minimum(lengths[0], 1)
    empty = [jnp.zeros(shape, F32) for shape in [(width, local)] * 3 + [(local, width)]]
    _, gs, gq, gk, gv, go = lax.cond(
        once > 0, attention_and_sums, lambda c: c,
        (jnp.zeros_like(once), gs, *empty),
    )
    grads, gs, gq = tie((grads, gs, gq))
    gu, gi, *vec = finish_ff(*grads)
    return (
        new_state, gs, gq, gk, gv, go, vec[0], vec[1], gi, gu, vec[2], vec[3], vec[4]
    )


def solution(mesh):
    rows, columns, parts = P("dp", None), P(None, "mp"), P("mp", None)
    return jax.shard_map(
        functools.partial(shards, mesh.shape["dp"]),
        mesh=mesh,
        in_specs=(
            rows, P("dp"), P("dp"), columns, columns, columns, parts, P(), P(), columns,
            parts, P(), P(), P(), rows
        ),
        out_specs=(
            rows, rows, columns, columns, columns, parts, P(), P(), columns, parts, P(), P(),
            P()
        ),
        check_vma=False,
    )
```
